32 devices in a mesh: grp: 4 (over y, x), rows: 8 (over z, core).
Axes of the slice: x: 2, y: 2, z: 4, core: 2. Of those that a mesh axis runs over, the one named last changes fastest.
Arguments:
- single_rep: bfloat16 [4, 128, 512], P('grp', 'rows'), may hold values from -6 to 6
- pair_rep: bfloat16 [4, 128, 128, 128], P('grp', 'rows'), may hold values from -6 to 6
- residue_mask: int32 [4, 128], P('grp'), may hold values 0 or 1
- single_gains: bfloat16 [3, 512], replicated, may hold values from 0.25 to 1.75
- pair_gains: bfloat16 [6, 128], replicated, may hold values from 0.25 to 1.75
- mult_gains: bfloat16 [2, 128], replicated, may hold values from 0.25 to 1.75
- single_proj: bfloat16 [5, 512, 512], replicated, may hold values from -0.25 to 0.25
- single_bias: bfloat16 [128, 8], replicated, may hold values from -0.5 to 0.5
- single_up: bfloat16 [512, 2048], replicated, may hold values from -0.25 to 0.25
- single_down: bfloat16 [2048, 512], replicated, may hold values from -0.125 to 0.125
- opm_proj: bfloat16 [2, 512, 32], replicated, may hold values from -0.25 to 0.25
- opm_out: bfloat16 [32, 32, 128], replicated, may hold values from -0.1875 to 0.1875
- mult_proj: bfloat16 [2, 4, 128, 128], replicated, may hold values from -0.5 to 0.5
- mult_gate: bfloat16 [2, 128, 128], replicated, may hold values from -0.5 to 0.5
- mult_out: bfloat16 [2, 128, 128], replicated, may hold values from -0.5 to 0.5
- att_proj: bfloat16 [2, 4, 128, 128], replicated, may hold values from -0.5 to 0.5
- att_bias: bfloat16 [2, 128, 4], replicated, may hold values from -0.5 to 0.5
- att_out: bfloat16 [2, 128, 128], replicated, may hold values from -1 to 1
- pair_up: bfloat16 [128, 512], replicated, may hold values from -0.5 to 0.5
- pair_down: bfloat16 [512, 128], replicated, may hold values from -0.25 to 0.25
- single_cot: bfloat16 [4, 128, 512], P('grp', 'rows'), may hold values from -6 to 6
- pair_cot: bfloat16 [4, 128, 128, 128], P('grp', 'rows'), may hold values from -6 to 6
Outputs:
- single_out: bfloat16 [4, 128, 512], P('grp', 'rows')
- pair_out: bfloat16 [4, 128, 128, 128], P('grp', 'rows')
- single_grad: float32 [4, 128, 512], P('grp', 'rows')
- pair_grad: float32 [4, 128, 128, 128], P('grp', 'rows')
- single_gains_grad: float32 [3, 512], replicated
- pair_gains_grad: float32 [6, 128], replicated
- mult_gains_grad: float32 [2, 128], replicated
- single_proj_grad: float32 [5, 512, 512], replicated
- single_bias_grad: float32 [128, 8], replicated
- single_up_grad: float32 [512, 2048], replicated
- single_down_grad: float32 [2048, 512], replicated
- opm_proj_grad: float32 [2, 512, 32], replicated
- opm_out_grad: float32 [32, 32, 128], replicated
- mult_proj_grad: float32 [2, 4, 128, 128], replicated
- mult_gate_grad: float32 [2, 128, 128], replicated
- mult_out_grad: float32 [2, 128, 128], replicated
- att_proj_grad: float32 [2, 4, 128, 128], replicated
- att_bias_grad: float32 [2, 128, 4], replicated
- att_out_grad: float32 [2, 128, 128], replicated
- pair_up_grad: float32 [128, 512], replicated
- pair_down_grad: float32 [512, 128], replicated
The draws below stay inside these ranges and needn't reach their ends.
Inputs may be any that keep to these rules, and one draw needn't show every extreme that they name: `residue_mask`: 1 marks a residue that is present, 0 one that is missing.
All inputs are finite; a program needn't handle non-finite values. No bound on the sum of `residue_mask` on one device may be relied on, other than what follows from the above.
Results may differ from the reference program's by a relative error of at most 0.017.
Values may be sent and summed in bfloat16 or wider, within the bound.
No kernel may reach another device: no remote copies, remote signals or barrier semaphores. Data moves between devices by JAX's collectives and lax.ppermute only.
A program may use at most 128 MiB of HBM per device.

```python
from functools import partial
import jax
import jax.numpy as jnp
from jax import lax

S = 512
HEADS = 8
C = 128
MULT = 128
TH = 4
OPM = 32
FACTOR = 4
CROP = 128
CROPS = 4


def place_ends(entries, own_key, low, largest):
    longest = entries.shape.index(max(entries.shape))
    spots = []
    for shift in (0, 1):
        where = [jax.random.randint(jax.random.fold_in(own_key, axis), (), 0, length) for axis, length in enumerate(entries.shape)]
        where[longest] = (where[longest] + shift) % entries.shape[longest]
        spots.append(tuple(where))
    return entries.at[spots[0]].set(low).at[spots[1]].set(largest)


def level_of(key, shape, split, least, top_value):
    def one(position, parts):
        draws = jax.random.uniform(jax.random.fold_in(jax.random.fold_in(key, 6), position), (parts,), jnp.float32, least / len(split), top_value / len(split))
        return jnp.repeat(jnp.exp(draws), shape[position] // parts).reshape((-1,) + (1,) * (len(shape) - position - 1))

    level = one(*split[0])
    for cut in split[1:]:
        level = level * one(*cut)
    return level


def centred(own_key, dims, deviation, reach, pieces=(), dtype=jnp.bfloat16):
    result = jax.random.normal(own_key, dims, jnp.float32) * deviation
    if len(pieces) > 0:
        result = level_of(own_key, dims, pieces, -0.22, 0.18) * result
    return jnp.clip(result, min=-reach, max=reach).astype(dtype)


def setup_inputs(seed: int = 0) -> dict:
    streams_of = jax.random.split(jax.random.key(seed), 23)
    single_rep = centred(streams_of[0], (CROPS, CROP, S), 1.0, 6.0, ((0, 4), (1, 8)))
    pair_rep = centred(streams_of[1], (CROPS, CROP, CROP, C), 1.0, 6.0, ((0, 4), (1, 8)))
    residue_mask = place_ends((jax.random.randint(streams_of[2], (CROPS, CROP), 0, 8) < 7).astype(jnp.int32), jax.random.fold_in(streams_of[2], 1), 0, 1)
    single_gains = jnp.clip(1.0 + 0.15 * jax.random.normal(streams_of[3], (3, S), jnp.float32), 0.25, 1.75).astype(jnp.bfloat16)
    pair_gains = jnp.clip(1.0 + 0.15 * jax.random.normal(streams_of[4], (6, C), jnp.float32), 0.25, 1.75).astype(jnp.bfloat16)
    mult_gains = jnp.clip(1.0 + 0.15 * jax.random.normal(streams_of[5], (2, MULT), jnp.float32), 0.25, 1.75).astype(jnp.bfloat16)
    single_proj = centred(streams_of[6], (5, S, S), S ** -0.5, 0.25)
    single_bias = centred(streams_of[7], (C, HEADS), C ** -0.5, 0.5)
    single_up = centred(streams_of[8], (S, FACTOR * S), S ** -0.5, 0.25)
    single_down = centred(streams_of[9], (FACTOR * S, S), (FACTOR * S) ** -0.5, 0.125)
    opm_proj = centred(streams_of[10], (2, S, OPM), S ** -0.5, 0.25)
    opm_out = centred(streams_of[11], (OPM, OPM, C), (OPM * OPM) ** -0.5, 0.1875)
    mult_proj = centred(streams_of[12], (2, 4, C, MULT), C ** -0.5, 0.5)
    mult_gate = centred(streams_of[13], (2, C, C), C ** -0.5, 0.5)
    mult_out = centred(streams_of[14], (2, MULT, C), MULT ** -0.5, 0.5)
    att_proj = centred(streams_of[15], (2, 4, C, C), C ** -0.5, 0.5)
    att_bias = centred(streams_of[16], (2, C, TH), C ** -0.5, 0.5)
    att_out = centred(streams_of[17], (2, C, C), (C // 4) ** -0.5, 1.0)
    pair_up = centred(streams_of[18], (C, FACTOR * C), C ** -0.5, 0.5)
    pair_down = centred(streams_of[19], (FACTOR * C, C), (FACTOR * C) ** -0.5, 0.25)
    single_cot = centred(streams_of[20], (CROPS, CROP, S), 1.0, 6.0, ((0, 4), (1, 8)))
    pair_cot = centred(streams_of[21], (CROPS, CROP, CROP, C), 1.0, 6.0, ((0, 4), (1, 8)))
    return {"single_rep": single_rep, "pair_rep": pair_rep, "residue_mask": residue_mask, "single_gains": single_gains, "pair_gains": pair_gains, "mult_gains": mult_gains, "single_proj": single_proj, "single_bias": single_bias, "single_up": single_up, "single_down": single_down, "opm_proj": opm_proj, "opm_out": opm_out, "mult_proj": mult_proj, "mult_gate": mult_gate, "mult_out": mult_out, "att_proj": att_proj, "att_bias": att_bias, "att_out": att_out, "pair_up": pair_up, "pair_down": pair_down, "single_cot": single_cot, "pair_cot": pair_cot}


PRECISE = lax.Precision.HIGHEST
EPSILON = 1e-05
MASKED = 1000000000.0

@jax.custom_vjp
def low(v):
    return lax.optimization_barrier(v.astype(jnp.bfloat16)).astype(jnp.float32)

@jax.custom_vjp
def low_back(v):
    return v

def low_keep(v):
    return (low(v), None)

def low_pass(kept, grad):
    return (grad,)

def back_keep(v):
    return (v, None)

def back_low(kept, grad):
    return (low(grad),)
low.defvjp(low_keep, low_pass)
low_back.defvjp(back_keep, back_low)

def rounded_both(operand):
    return low_back(low(operand))

def contract(pattern, first_term, second_term):
    return jnp.einsum(pattern, first_term, second_term, precision=PRECISE)

def norm_last(operand, gain_vec):
    centre = operand - lax.optimization_barrier(jnp.mean(operand, -1, keepdims=True))
    spread = lax.optimization_barrier(jnp.mean(centre * centre, -1, keepdims=True))
    return centre * lax.rsqrt(spread + EPSILON) * gain_vec

def soft_weights(logits):
    highest = lax.optimization_barrier(jnp.max(logits, -1, keepdims=True))
    raised = jnp.exp(logits - highest)
    return raised / lax.optimization_barrier(jnp.sum(raised, -1, keepdims=True))

def single_attend(queries, key_rows, values, gate_value, pair_bias, key_bias, weight_out):
    head_count = pair_bias.shape[0]
    feature_width = queries.shape[-1]
    head_size = feature_width // head_count
    query_heads = queries.reshape(queries.shape[0], head_count, head_size)
    key_heads = key_rows.reshape(key_rows.shape[0], head_count, head_size)
    value_heads = values.reshape(values.shape[0], head_count, head_size)
    logits = contract('ihd,jhd->hij', query_heads, key_heads) * head_size ** (-0.5) + pair_bias + key_bias
    mixed = contract('hij,jhd->ihd', soft_weights(logits), value_heads).reshape(queries.shape[0], feature_width)
    return contract('is,st->it', mixed * jax.nn.sigmoid(gate_value), weight_out)

def tri_attend(normed, pair_bias, weight_four, weight_out, key_bias):
    head_count = pair_bias.shape[0]
    feature_width = normed.shape[-1]
    head_size = feature_width // head_count

    def one_row(row_in):
        projected = contract('lc,ncd->nld', row_in, weight_four)
        shaped = projected[:3].reshape(3, row_in.shape[0], head_count, head_size)
        logits = contract('jhd,khd->hjk', shaped[0], shaped[1]) * head_size ** (-0.5) + pair_bias + key_bias
        mixed = contract('hjk,khd->jhd', soft_weights(logits), shaped[2]).reshape(row_in.shape[0], feature_width)
        return contract('lc,cd->ld', mixed * jax.nn.sigmoid(projected[3]), weight_out)
    return lax.map(jax.checkpoint(one_row), normed)

def tri_mult(pair_in, gain_in, weight_four, weight_gate, gain_out, weight_out, pair_mask, pattern):
    normed = norm_last(pair_in, gain_in)
    projected = contract('ijc,ncm->nijm', normed, weight_four)
    left_side = rounded_both(jax.nn.sigmoid(projected[0]) * projected[1] * pair_mask[:, :, None])
    right_side = rounded_both(jax.nn.sigmoid(projected[2]) * projected[3] * pair_mask[:, :, None])
    product = rounded_both(contract(pattern, left_side, right_side))
    gate_value = jax.nn.sigmoid(contract('ijc,cd->ijd', normed, weight_gate))
    return pair_in + contract('ijm,mc->ijc', norm_last(product, gain_out), weight_out) * gate_value

def forward(mask_all, single_in, pair_in, single_gains, pair_gains, mult_gains, single_proj, single_bias, single_up, single_down, opm_proj, opm_out, mult_proj, mult_gate, mult_out, att_proj, att_bias, att_out, pair_up, pair_down):
    key_bias = (mask_all - 1.0) * MASKED
    pair_mask = mask_all[:, None] * mask_all[None, :]
    normed = norm_last(single_in, single_gains[0])
    queries = contract('is,st->it', normed, single_proj[0])
    key_rows = rounded_both(contract('is,st->it', normed, single_proj[1]))
    values = rounded_both(contract('is,st->it', normed, single_proj[2]))
    gate_value = contract('is,st->it', normed, single_proj[3])
    row_bias = contract('ijc,ch->hij', norm_last(pair_in, pair_gains[0]), single_bias)
    first_sum = single_in + single_attend(queries, key_rows, values, gate_value, row_bias, key_bias, single_proj[4])
    hidden = jax.nn.gelu(contract('is,st->it', norm_last(first_sum, single_gains[1]), single_up))
    single_next = first_sum + contract('it,ts->is', hidden, single_down)
    outer_in = norm_last(single_next, single_gains[2])
    left_side = rounded_both(contract('is,sa->ia', outer_in, opm_proj[0]) * mask_all[:, None])
    right_side = rounded_both(contract('is,sa->ia', outer_in, opm_proj[1]) * mask_all[:, None])
    pair_one = pair_in + contract('ibc,jb->ijc', contract('ia,abc->ibc', left_side, opm_out), right_side)
    pair_two = tri_mult(pair_one, pair_gains[1], mult_proj[0], mult_gate[0], mult_gains[0], mult_out[0], pair_mask, 'ikc,jkc->ijc')
    pair_three = tri_mult(pair_two, pair_gains[2], mult_proj[1], mult_gate[1], mult_gains[1], mult_out[1], pair_mask, 'kic,kjc->ijc')
    normed_start = norm_last(pair_three, pair_gains[3])
    bias_start = rounded_both(contract('ijc,ch->hij', normed_start, att_bias[0]))
    pair_four = pair_three + tri_attend(normed_start, bias_start, att_proj[0], att_out[0], key_bias)
    normed_end = rounded_both(norm_last(pair_four, pair_gains[4]))
    turned = jnp.swapaxes(normed_end, 0, 1)
    bias_end = rounded_both(contract('ijc,ch->hij', turned, att_bias[1]))
    update = rounded_both(tri_attend(turned, bias_end, att_proj[1], att_out[1], key_bias))
    pair_five = pair_four + jnp.swapaxes(update, 0, 1)
    hidden_pair = jax.nn.gelu(contract('ijc,cd->ijd', norm_last(pair_five, pair_gains[5]), pair_up))
    pair_six = pair_five + contract('ijd,dc->ijc', hidden_pair, pair_down)
    return (single_next, pair_six)

def reference(single_rep, pair_rep, residue_mask, single_gains, pair_gains, mult_gains, single_proj, single_bias, single_up, single_down, opm_proj, opm_out, mult_proj, mult_gate, mult_out, att_proj, att_bias, att_out, pair_up, pair_down, single_cot, pair_cot):
    params = tuple((member.astype(jnp.float32) for member in (single_gains, pair_gains, mult_gains, single_proj, single_bias, single_up, single_down, opm_proj, opm_out, mult_proj, mult_gate, mult_out, att_proj, att_bias, att_out, pair_up, pair_down)))
    single_outs = []
    pair_outs = []
    single_grads = []
    pair_grads = []
    summed = None
    for crop_index in range(CROPS):
        mask_all = residue_mask[crop_index].astype(jnp.float32)
        results, backward = jax.vjp(partial(forward, mask_all), single_rep[crop_index].astype(jnp.float32), pair_rep[crop_index].astype(jnp.float32), *params)
        gradients = backward((single_cot[crop_index].astype(jnp.float32), pair_cot[crop_index].astype(jnp.float32)))
        single_outs.append(results[0].astype(jnp.bfloat16))
        pair_outs.append(results[1].astype(jnp.bfloat16))
        single_grads.append(gradients[0])
        pair_grads.append(gradients[1])
        if summed is None:
            summed = tuple(gradients[2:])
        else:
            summed = tuple((running + addend for running, addend in zip(summed, gradients[2:])))
    grad_sg, grad_pg, grad_mg, grad_sp, grad_sb, grad_su, grad_sd, grad_op, grad_oo, grad_mp, grad_mgt, grad_mo, grad_ap, grad_ab, grad_ao, grad_pu, grad_pd = summed
    return (jnp.stack(single_outs), jnp.stack(pair_outs), jnp.stack(single_grads), jnp.stack(pair_grads), grad_sg, grad_pg, grad_mg, grad_sp, grad_sb, grad_su, grad_sd, grad_op, grad_oo, grad_mp, grad_mgt, grad_mo, grad_ap, grad_ab, grad_ao, grad_pu, grad_pd)
```

```python
import jax
import jax.numpy as jnp
from jax import lax
from jax.experimental import pallas as pl
from jax.experimental.pallas import tpu as pltpu
from jax.sharding import PartitionSpec as P

BF = jnp.bfloat16
F32 = jnp.float32
EPSILON = 1e-05
MASKED = 1000000000.0
AX = ("grp", "rows")
L = 128
C = 128
TH = 4
HD = 32
HPAD = 16


def dot(a, b):
    return lax.dot_general(a, b, (((1,), (0,)), ((), ())), preferred_element_type=F32)


def dot_nt(a, b):
    return lax.dot_general(a, b, (((1,), (1,)), ((), ())), preferred_element_type=F32)


def dot_tn(a, b):
    return lax.dot_general(a, b, (((0,), (0,)), ((), ())), preferred_element_type=F32)


def b16(x):
    return x.astype(BF)


def f32(x):
    return x.astype(F32)


def sig(x):
    return 0.5 * jnp.tanh(0.5 * x) + 0.5


GELU_A = 0.7978845608028654
GELU_B = 0.044715


def gelu_parts(x):
    t = jnp.tanh(GELU_A * (x + GELU_B * x * x * x))
    half = 0.5 * (1.0 + t)
    slope = half + 0.5 * x * (1.0 - t * t) * (GELU_A * (1.0 + 3.0 * GELU_B * x * x))
    return x * half, slope


def norm_cols(z):
    c = z - jnp.mean(z, 0, keepdims=True)
    scale = lax.rsqrt(jnp.mean(c * c, 0, keepdims=True) + EPSILON)
    return c * scale, scale


def norm_cols_back(dx, xh, scale):
    return scale * (
        dx - jnp.mean(dx, 0, keepdims=True) - xh * jnp.mean(dx * xh, 0, keepdims=True)
    )


def cols(r):
    return pl.ds(pl.multiple_of(r * L, L), L)


def each_row(count, body):
    def step(r, carry):
        body(r)
        return carry

    lax.fori_loop(0, count, step, 0)


def call(kernel, outs, scratch, args, flops=10**9):
    vm = pl.BlockSpec(memory_space=pltpu.VMEM)
    moved = sum(a.size * a.dtype.itemsize for a in args)
    return pl.pallas_call(
        kernel,
        out_shape=[jax.ShapeDtypeStruct(s, d) for s, d in outs],
        in_specs=[vm] * len(args),
        out_specs=[vm] * len(outs),
        scratch_shapes=[pltpu.VMEM(s, d) for s, d in scratch],
        compiler_params=pltpu.CompilerParams(vmem_limit_bytes=50 << 20),
        cost_estimate=pl.CostEstimate(flops=flops, bytes_accessed=moved, transcendentals=0),
    )(*args)


def prep_weights(gp, gm, mp, mg, mo, ap, ab, ao, pu, pd, sb):
    def kernel(
        gp, gm, mp, mg, mo, ap, ab, ao, pu, pd, sb,
        m5t, m5, mot, mof, a4t, a4, aot, abt, upt, up, dnt, sbt,
    ):
        gpv = f32(gp[...])
        gmv = f32(gm[...])
        for t in range(2):
            g = gpv[1 + t : 2 + t]
            for k in range(5):
                w = f32(mp[t, k] if k < 4 else mg[t]).T * g
                m5t[t, k * C : (k + 1) * C] = b16(w)
                m5[t, :, k * C : (k + 1) * C] = b16(w.T)
            w = f32(mo[t]).T * gmv[t : t + 1]
            mot[t] = b16(w)
            mof[t] = b16(w.T)
            g = gpv[3 + t : 4 + t]
            for k in range(4):
                w = f32(ap[t, k]).T * (g * HD**-0.5 if k == 0 else g)
                a4t[t, k * C : (k + 1) * C] = b16(w)
                a4[t, :, k * C : (k + 1) * C] = b16(w.T)
            aot[t] = b16(f32(ao[t]).T)
            abt[t] = b16(f32(ab[t]) * g)
        g = gpv[5:6]
        for k in range(4):
            s = slice(k * C, (k + 1) * C)
            w = f32(pu[:, s]).T * g
            upt[s] = b16(w)
            up[:, s] = b16(w.T)
            dnt[:, s] = b16(f32(pd[s]).T)
        sbt[...] = b16(f32(sb[...]) * gpv[0:1])

    outs = [
        ((2, 640, C), BF), ((2, C, 640), BF), ((2, C, C), BF), ((2, C, C), BF),
        ((2, 512, C), BF), ((2, C, 512), BF), ((2, C, C), BF), ((2, HPAD, C), BF),
        ((512, C), BF), ((C, 512), BF), ((C, 512), BF), ((HPAD, C), BF),
    ]
    return call(kernel, outs, [], (gp, gm, mp, mg, mo, ap, ab, ao, pu, pd, sb))


def row_bias(rows, pair, sbt):
    def kernel(pair, sbt, out, s):
        def body(r):
            xh, _ = norm_cols(f32(pair[r]).T)
            s[pl.ds(r, HPAD, stride=rows), :] = dot(sbt[...], b16(xh))

        each_row(rows, body)
        out[...] = b16(s[0 : 8 * rows])

    return call(kernel, [((8 * rows, L), BF)], [((HPAD * rows, L), F32)], (pair, sbt))[0]


def project_pair(z, r, rows, m5t, pmask, sa, sb):
    xh, _ = norm_cols(z)
    p = dot(m5t[0:512], b16(xh))
    mk = pmask[pl.ds(r, 1), :]
    sa[pl.ds(r, C, stride=rows), :] = sig(p[0:C]) * p[C : 2 * C] * mk
    sb[pl.ds(r, C, stride=rows), :] = sig(p[2 * C : 3 * C]) * p[3 * C : 4 * C] * mk


def put_pair(n, ab, sa, sb):
    part = sa.shape[0] // n
    for d in range(n):
        ab[d, 0:part] = b16(sa[d * part : (d + 1) * part])
        ab[d, part : 2 * part] = b16(sb[d * part : (d + 1) * part])


def gated_product(z, r, rows, gatet, mot, sp):
    xh, _ = norm_cols(z)
    gate = sig(dot(gatet[...], b16(xh)))
    ph, _ = norm_cols(sp[pl.ds(r, C, stride=rows), :])
    return z + dot(mot[...], b16(ph)) * gate


def front(n, rows, pair, inner, right, pmask, m5t):
    def kernel(pair, inner, right, pmask, m5t, z1, ab, sa, sb):
        def body(r):
            z = (f32(pair[r]) + dot(right[...], inner[r])).T
            z1[:, cols(r)] = z
            project_pair(z, r, rows, m5t, pmask, sa, sb)

        each_row(rows, body)
        put_pair(n, ab, sa, sb)

    part = C * rows // n
    return call(
        kernel,
        [((C, rows * L), F32), ((n, 2 * part, L), BF)],
        [((C * rows, L), F32)] * 2,
        (pair, inner, right, pmask, m5t),
    )


def middle(n, rows, z1, prod, gatet, mot, pmask, m5t):
    def kernel(z1, prod, gatet, mot, pmask, m5t, z2, ab, sa, sb, sp):
        sp[...] = f32(prod[...])

        def body(r):
            z = gated_product(z1[:, cols(r)], r, rows, gatet, mot, sp)
            z2[:, cols(r)] = z
            project_pair(z, r, rows, m5t, pmask, sa, sb)

        each_row(rows, body)
        put_pair(n, ab, sa, sb)

    part = C * rows // n
    return call(
        kernel,
        [((C, rows * L), F32), ((n, 2 * part, L), BF)],
        [((C * rows, L), F32)] * 3,
        (z1, prod, gatet, mot, pmask, m5t),
    )


def start_front(rows, z2, prod, gatet, mot, abt):
    def kernel(z2, prod, gatet, mot, abt, z3, tb, sp, st):
        sp[...] = f32(prod[...])

        def body(r):
            z = gated_product(z2[:, cols(r)], r, rows, gatet, mot, sp)
            z3[:, cols(r)] = z
            xh, _ = norm_cols(z)
            st[pl.ds(r, HPAD, stride=rows), :] = dot(abt[...], b16(xh))

        each_row(rows, body)
        tb[...] = b16(st[0 : TH * rows])

    return call(
        kernel,
        [((C, rows * L), F32), ((TH * rows, L), BF)],
        [((C * rows, L), F32), ((HPAD * rows, L), F32)],
        (z2, prod, gatet, mot, abt),
    )


def channel_product(n, rows, outgoing, ab):
    def kernel(ab, out):
        part = C * rows // n
        for ch in range(C // n):
            a = ab[:, ch * rows : (ch + 1) * rows, :].reshape(L, L)
            b = ab[:, part + ch * rows : part + (ch + 1) * rows, :].reshape(L, L)
            prod = dot_nt(a, b) if outgoing else dot_tn(a, b)
            out[:, ch * rows : (ch + 1) * rows, :] = b16(prod).reshape(n, rows, L)

    return call(kernel, [((n, C * rows // n, L), BF)], [], (ab,))[0]


def channel_product_back(n, rows, outgoing, ab, dprod):
    def kernel(ab, dprod, out):
        part = C * rows // n
        for ch in range(C // n):
            low, high = ch * rows, (ch + 1) * rows
            a = ab[:, low:high, :].reshape(L, L)
            b = ab[:, part + low : part + high, :].reshape(L, L)
            g = dprod[:, low:high, :].reshape(L, L)
            if outgoing:
                da, db = dot(g, b), dot_tn(g, a)
            else:
                da, db = dot_nt(b, g), dot(a, g)
            out[:, low:high, :] = b16(da).reshape(n, rows, L)
            out[:, part + low : part + high, :] = b16(db).reshape(n, rows, L)

    return call(kernel, [((n, 2 * C * rows // n, L), BF)], [], (ab, dprod))[0]


def head_masks():
    lane = lax.broadcasted_iota(jnp.int32, (1, C), 1)
    return [b16(jnp.where((lane >= h * HD) & (lane < (h + 1) * HD), 1.0, 0.0)) for h in range(TH)]


def by_head(x):
    pm = b16(x.T)
    return jnp.concatenate([pm * m for m in head_masks()], 0)


def attend(x16, a4t, bias):
    p4 = dot(a4t[...], x16)
    q, k, v = p4[0:C], p4[C : 2 * C], p4[2 * C : 3 * C]
    gate = sig(p4[3 * C : 4 * C])
    logits = dot(by_head(k), b16(q)) + bias[...]
    raised, outs = [], []
    v16 = b16(v)
    for h in range(TH):
        s = logits[h * L : (h + 1) * L]
        e = jnp.exp(s - jnp.max(s, 0, keepdims=True))
        inv = 1.0 / jnp.sum(e, 0, keepdims=True)
        raised.append((e, inv))
        outs.append(dot(v16[h * HD : (h + 1) * HD], b16(e)) * inv)
    mixed = jnp.concatenate(outs, 0)
    return (q, k, v, gate, raised, mixed)


def attend_back(state, dy16, ao, dbias):
    q, k, v, gate, raised, mixed = state
    du = dot(ao[...], dy16)
    do = du * gate
    dgate = du * mixed * gate * (1.0 - gate)
    do16, q16, k16 = b16(do), b16(q), b16(k)
    dp = dot(by_head(v), do16)
    row = do * mixed
    dq, dk, dv = [], [], []
    for h in range(TH):
        s = slice(h * HD, (h + 1) * HD)
        w = slice(h * L, (h + 1) * L)
        e, inv = raised[h]
        p = e * inv
        ds = p * (dp[w] - jnp.sum(row[s], 0, keepdims=True))
        dbias[w, :] += ds
        ds16, p16 = b16(ds), b16(p)
        dv.append(dot_nt(do16[s], p16))
        dq.append(dot(k16[s], ds16))
        dk.append(dot_nt(q16[s], ds16))
    return jnp.concatenate([b16(x) for x in dq + dk + dv] + [b16(dgate)], 0)


def start_attention(n, rows, z3, tb_all, key_row, a4t, aot, abt_end):
    def kernel(z3, tb_all, key_row, a4t, aot, abt, z4, send, bias, st, se):
        for h in range(TH):
            b = f32(tb_all[:, h * rows : (h + 1) * rows, :].reshape(L, L)) + key_row[...]
            bias[h * L : (h + 1) * L, :] = b.T

        def body(r):
            z = z3[:, cols(r)]
            xh, _ = norm_cols(z)
            q, k, v, gate, raised, mixed = attend(b16(xh), a4t, bias)
            z = z + dot(aot[...], b16(mixed * gate))
            z4[:, cols(r)] = z
            st[pl.ds(r, L, stride=rows), :] = z.T
            xe, _ = norm_cols(z)
            se[pl.ds(r, HPAD, stride=rows), :] = dot(abt[...], b16(xe))

        each_row(rows, body)
        part = L * rows // n
        for d in range(n):
            send[d, 0:part] = b16(st[d * part : (d + 1) * part])
            send[d, part : part + TH * rows] = b16(se[0 : TH * rows])

    part = L * rows // n
    return call(
        kernel,
        [((C, rows * L), F32), ((n, part + TH * rows, L), BF)],
        [((TH * L, L), F32), ((L * rows, C), F32), ((HPAD * rows, L), F32)],
        (z3, tb_all, key_row, a4t, aot, abt_end),
    )


def end_both(n, rows, recv, cot, key_row, a4t, a4, aot, ao, upt, up, dnt, dn):
    part = L * rows // n

    def kernel(
        recv, cot, key_row, a4t, a4, aot, ao, upt, up, dnt, dn,
        pout, send, m_up, m_dn, m_a4, m_ao,
        bias, dbias, sout, sdz, o_h, o_dh, o_x5, o_cot, o_x4, o_d4, o_u, o_dy,
    ):
        kb = jnp.broadcast_to(key_row[...], (L, L)).T
        for h in range(TH):
            b = recv[:, part + h * rows : part + (h + 1) * rows, :].reshape(L, L)
            bias[h * L : (h + 1) * L, :] = f32(b) + kb
        dbias[...] = jnp.zeros_like(dbias)

        def body(r):
            w = cols(r)
            z4 = f32(recv[:, pl.ds(pl.multiple_of(r * rows, rows), rows), :].reshape(L, C)).T
            x4, scale4 = norm_cols(z4)
            x16 = b16(x4)
            state = attend(x16, a4t, bias)
            gated = b16(state[5] * state[3])
            z5 = z4 + dot(aot[...], gated)
            x5, scale5 = norm_cols(z5)
            x516 = b16(x5)
            hid, slope = gelu_parts(dot(upt[...], x516))
            h16 = b16(hid)
            z6 = z5 + dot(dnt[...], h16)
            sout[pl.ds(r, L, stride=rows), :] = z6.T
            dz6 = f32(cot[r]).T
            c16 = b16(dz6)
            dh16 = b16(dot(dn[...], c16) * slope)
            dz5 = dz6 + norm_cols_back(dot(up[...], dh16), x5, scale5)
            dy16 = b16(dz5)
            d4 = attend_back(state, dy16, ao, dbias)
            dz4 = dz5 + norm_cols_back(dot(a4[...], d4), x4, scale4)
            sdz[pl.ds(r, L, stride=rows), :] = dz4.T
            o_h[:, w] = h16
            o_dh[:, w] = dh16
            o_x5[:, w] = x516
            o_cot[:, w] = c16
            o_x4[:, w] = x16
            o_d4[:, w] = d4
            o_u[:, w] = gated
            o_dy[:, w] = dy16

        each_row(rows, body)
        for d in range(n):
            pout[d] = b16(sout[d * part : (d + 1) * part])
            send[d, 0:part] = b16(sdz[d * part : (d + 1) * part])
            for h in range(TH):
                send[d, part + h * rows : part + (h + 1) * rows] = b16(
                    dbias[h * L + d * rows : h * L + (d + 1) * rows]
                )
        for k in range(4):
            s = slice(k * C, (k + 1) * C)
            m_up[s] = dot_nt(o_x5[...], o_dh[s])
            m_a4[s] = dot_nt(o_x4[...], o_d4[s])
        m_dn[...] = dot_nt(o_h[...], o_cot[...])
        m_ao[...] = dot_nt(o_u[...], o_dy[...])

    wide = rows * L
    return call(
        kernel,
        [
            ((n, part, C), BF), ((n, part + TH * rows, L), BF),
            ((512, C), F32), ((512, C), F32), ((512, C), F32), ((C, C), F32),
        ],
        [
            ((TH * L, L), F32), ((TH * L, L), F32), ((L * rows, C), F32), ((L * rows, C), F32),
            ((512, wide), BF), ((512, wide), BF), ((C, wide), BF), ((C, wide), BF),
            ((C, wide), BF), ((512, wide), BF), ((C, wide), BF), ((C, wide), BF),
        ],
        (recv, cot, key_row, a4t, a4, aot, ao, upt, up, dnt, dn),
    )


def start_back(n, rows, z3, z4, recv, tb_all, key_row, a4t, a4, ao, abt_end):
    part = L * rows // n

    def kernel(
        z3, z4, recv, tb_all, key_row, a4t, a4, ao, abt,
        dz4_out, dxs, dtb, m_a4, m_ao, m_ab,
        bias, dbias, seb, o_x3, o_d4, o_u, o_dy, o_x4, o_eb,
    ):
        for h in range(TH):
            b = f32(tb_all[:, h * rows : (h + 1) * rows, :].reshape(L, L)) + key_row[...]
            bias[h * L : (h + 1) * L, :] = b.T
        dbias[...] = jnp.zeros_like(dbias)
        seb[...] = jnp.zeros_like(seb)
        total = f32(recv[0, part : part + TH * rows])
        for d in range(1, n):
            total = total + f32(recv[d, part : part + TH * rows])
        seb[0 : TH * rows, :] = total

        def body(r):
            w = cols(r)
            x4, scale4 = norm_cols(z4[:, w])
            eb16 = b16(seb[pl.ds(r, HPAD, stride=rows), :])
            dz4 = f32(recv[:, pl.ds(pl.multiple_of(r * rows, rows), rows), :].reshape(L, C)).T
            dz4 = dz4 + norm_cols_back(dot_tn(abt[...], eb16), x4, scale4)
            dz4_out[:, w] = dz4
            x3, _ = norm_cols(z3[:, w])
            x16 = b16(x3)
            state = attend(x16, a4t, bias)
            dy16 = b16(dz4)
            d4 = attend_back(state, dy16, ao, dbias)
            dxs[:, w] = dot(a4[...], d4)
            o_x3[:, w] = x16
            o_d4[:, w] = d4
            o_u[:, w] = b16(state[5] * state[3])
            o_dy[:, w] = dy16
            o_x4[:, w] = b16(x4)
            o_eb[:, w] = eb16

        each_row(rows, body)
        for h in range(TH):
            turned = b16(dbias[h * L : (h + 1) * L, :].T)
            for d in range(n):
                dtb[d, h * rows : (h + 1) * rows] = turned[d * rows : (d + 1) * rows]
        for k in range(4):
            s = slice(k * C, (k + 1) * C)
            m_a4[s] = dot_nt(o_x3[...], o_d4[s])
        m_ao[...] = dot_nt(o_u[...], o_dy[...])
        m_ab[...] = dot_nt(o_eb[...], o_x4[...])

    wide = rows * L
    return call(
        kernel,
        [
            ((C, wide), F32), ((C, wide), F32), ((n, TH * rows, L), BF),
            ((512, C), F32), ((C, C), F32), ((HPAD, C), F32),
        ],
        [
            ((TH * L, L), F32), ((TH * L, L), F32), ((HPAD * rows, L), F32),
            ((C, wide), BF), ((512, wide), BF), ((C, wide), BF), ((C, wide), BF),
            ((C, wide), BF), ((HPAD, wide), BF),
        ],
        (z3, z4, recv, tb_all, key_row, a4t, a4, ao, abt_end),
    )


def product_back(z, dz, r, rows, sp, gatet, mot, mof, sdp, dgp_out, o_ph, o_do):
    w = cols(r)
    xh, _ = norm_cols(z)
    gate = sig(dot(gatet[...], b16(xh)))
    ph, scale = norm_cols(sp[pl.ds(r, C, stride=rows), :])
    ph16 = b16(ph)
    out = dot(mot[...], ph16)
    dgp_out[:, w] = b16(dz * out * gate * (1.0 - gate))
    do16 = b16(dz * gate)
    sdp[pl.ds(r, C, stride=rows), :] = norm_cols_back(dot(mof[...], do16), ph, scale)
    o_ph[:, w] = ph16
    o_do[:, w] = do16


def third_back(n, rows, z3, dz4, dxs, recv, abt, z2, prod, gatet, mot, mof):
    def kernel(
        z3, dz4, dxs, recv, abt, z2, prod, gatet, mot, mof,
        dz3, dgp, dp, m_ab, m_mo,
        stb, sp, sdp, o_x3, o_tb, o_ph, o_do,
    ):
        sp[...] = f32(prod[...])
        stb[...] = jnp.zeros_like(stb)
        total = f32(recv[0])
        for d in range(1, n):
            total = total + f32(recv[d])
        stb[0 : TH * rows, :] = total

        def body(r):
            w = cols(r)
            x3, scale3 = norm_cols(z3[:, w])
            tb16 = b16(stb[pl.ds(r, HPAD, stride=rows), :])
            dx = dxs[:, w] + dot_tn(abt[...], tb16)
            dz = dz4[:, w] + norm_cols_back(dx, x3, scale3)
            dz3[:, w] = dz
            o_x3[:, w] = b16(x3)
            o_tb[:, w] = tb16
            product_back(z2[:, w], dz, r, rows, sp, gatet, mot, mof, sdp, dgp, o_ph, o_do)

        each_row(rows, body)
        dp[...] = b16(sdp[...])
        m_ab[...] = dot_nt(o_tb[...], o_x3[...])
        m_mo[...] = dot_nt(o_ph[...], o_do[...])

    wide = rows * L
    return call(
        kernel,
        [
            ((C, wide), F32), ((C, wide), BF), ((C * rows, L), BF),
            ((HPAD, C), F32), ((C, C), F32),
        ],
        [
            ((HPAD * rows, L), F32), ((C * rows, L), F32), ((C * rows, L), F32),
            ((C, wide), BF), ((HPAD, wide), BF), ((C, wide), BF), ((C, wide), BF),
        ],
        (z3, dz4, dxs, recv, abt, z2, prod, gatet, mot, mof),
    )


def projections_back(n, rows, z, dz, dgp, r, pmask, m5t, m5, sa, sb, o_x, o_d5):
    w = cols(r)
    xh, scale = norm_cols(z)
    x16 = b16(xh)
    p = dot(m5t[0:512], x16)
    mk = pmask[pl.ds(r, 1), :]
    da = sa[pl.ds(r, C, stride=rows), :] * mk
    db = sb[pl.ds(r, C, stride=rows), :] * mk
    ga, gb = sig(p[0:C]), sig(p[2 * C : 3 * C])
    va, vb = p[C : 2 * C], p[3 * C : 4 * C]
    d5 = jnp.concatenate(
        [
            b16(da * va * ga * (1.0 - ga)),
            b16(da * ga),
            b16(db * vb * gb * (1.0 - gb)),
            b16(db * gb),
            dgp[:, w],
        ],
        0,
    )
    o_x[:, w] = x16
    o_d5[:, w] = d5
    return dz + norm_cols_back(dot(m5[...], d5), xh, scale)


def take_pair(n, dab, sa, sb):
    part = sa.shape[0] // n
    for d in range(n):
        sa[d * part : (d + 1) * part, :] = f32(dab[d, 0:part])
        sb[d * part : (d + 1) * part, :] = f32(dab[d, part : 2 * part])


def second_back(n, rows, z2, dz3, dgp, dab, pmask, m5t, m5, z1, prod, gatet, mot, mof):
    def kernel(
        z2, dz3, dgp, dab, pmask, m5t, m5, z1, prod, gatet, mot, mof,
        dz2, dgp_out, dp, m_m5, m_mo,
        sa, sb, sp, sdp, o_x, o_d5, o_ph, o_do,
    ):
        sp[...] = f32(prod[...])
        take_pair(n, dab, sa, sb)

        def body(r):
            w = cols(r)
            dz = projections_back(
                n, rows, z2[:, w], dz3[:, w], dgp, r, pmask, m5t, m5, sa, sb, o_x, o_d5
            )
            dz2[:, w] = dz
            product_back(z1[:, w], dz, r, rows, sp, gatet, mot, mof, sdp, dgp_out, o_ph, o_do)

        each_row(rows, body)
        dp[...] = b16(sdp[...])
        for k in range(5):
            s = slice(k * C, (k + 1) * C)
            m_m5[s] = dot_nt(o_x[...], o_d5[s])
        m_mo[...] = dot_nt(o_ph[...], o_do[...])

    wide = rows * L
    return call(
        kernel,
        [
            ((C, wide), F32), ((C, wide), BF), ((C * rows, L), BF),
            ((640, C), F32), ((C, C), F32),
        ],
        [
            ((C * rows, L), F32), ((C * rows, L), F32), ((C * rows, L), F32), ((C * rows, L), F32),
            ((C, wide), BF), ((640, wide), BF), ((C, wide), BF), ((C, wide), BF),
        ],
        (z2, dz3, dgp, dab, pmask, m5t, m5, z1, prod, gatet, mot, mof),
    )


def first_back(n, rows, z1, dz2, dgp, dab, pmask, m5t, m5, inner, right, right_t):
    def kernel(
        z1, dz2, dgp, dab, pmask, m5t, m5, inner, right, right_t,
        dz1, dinner, dright, m_m5,
        sa, sb, o_x, o_d5,
    ):
        take_pair(n, dab, sa, sb)
        dright[...] = jnp.zeros_like(dright)

        def body(r):
            w = cols(r)
            dz = projections_back(
                n, rows, z1[:, w], dz2[:, w], dgp, r, pmask, m5t, m5, sa, sb, o_x, o_d5
            ).T
            dz1[r] = b16(dz)
            dz16 = b16(dz)
            dinner[r] = dot(right_t[...], dz16)
            dright[...] += dot_nt(dz16, inner[r])

        each_row(rows, body)
        for k in range(5):
            s = slice(k * C, (k + 1) * C)
            m_m5[s] = dot_nt(o_x[...], o_d5[s])

    wide = rows * L
    opm = right.shape[1]
    return call(
        kernel,
        [
            ((rows, L, C), BF), ((rows, opm, C), F32), ((L, opm), F32), ((640, C), F32),
        ],
        [
            ((C * rows, L), F32), ((C * rows, L), F32), ((C, wide), BF), ((640, wide), BF),
        ],
        (z1, dz2, dgp, dab, pmask, m5t, m5, inner, right, right_t),
    )


def last_back(rows, pair, drb, dz1, sbt):
    def kernel(pair, drb, dz1, sbt, grad, m_sb, o_x, o_d):
        def body(r):
            w = cols(r)
            xh, scale = norm_cols(f32(pair[r]).T)
            d = drb[pl.ds(r, 8, stride=rows), :]
            d16 = b16(jnp.concatenate([d, jnp.zeros_like(d)], 0))
            back = norm_cols_back(dot_tn(sbt[...], d16), xh, scale)
            grad[r] = f32(dz1[r]) + back.T
            o_x[:, w] = b16(xh)
            o_d[:, w] = d16

        each_row(rows, body)
        m_sb[...] = dot_nt(o_d[...], o_x[...])

    wide = rows * L
    return call(
        kernel,
        [((rows, L, C), F32), ((HPAD, C), F32)],
        [((C, wide), BF), ((HPAD, wide), BF)],
        (pair, drb, dz1, sbt),
    )


PRECISE = lax.Precision.HIGHEST


def for_sending(shard):

    def short(part):
        return part.astype(jnp.bfloat16) if part.dtype == jnp.float32 else part

    return jax.tree.map(short, shard)


def widen(operand):
    return operand.astype(jnp.float32)


def narrow(operand):
    return operand.astype(jnp.bfloat16)


def rounded(operand):
    return lax.optimization_barrier(operand.astype(jnp.bfloat16)).astype(jnp.float32)


def contract(pattern, first_term, second_term):
    return jnp.einsum(pattern, first_term, second_term, precision=PRECISE)


def low_product(pattern, first_term, second_term):
    return jnp.einsum(pattern, first_term, second_term, preferred_element_type=jnp.float32)


def norm_rows(operand, gain_vec):
    centre = operand - jnp.mean(operand, -1, keepdims=True)
    spread = jnp.mean(centre * centre, -1, keepdims=True)
    return centre * lax.rsqrt(spread + EPSILON) * gain_vec


def soft_weights(logits):
    highest = jnp.max(logits, -1, keepdims=True)
    raised = jnp.exp(logits - highest)
    return raised / jnp.sum(raised, -1, keepdims=True)


def single_attend(queries, key_rows, values, gate_value, pair_bias, key_bias, weight_out):
    head_count = pair_bias.shape[0]
    feature_width = queries.shape[-1]
    head_size = feature_width // head_count
    query_heads = queries.reshape(queries.shape[0], head_count, head_size)
    key_heads = key_rows.reshape(key_rows.shape[0], head_count, head_size)
    value_heads = values.reshape(values.shape[0], head_count, head_size)
    logits = (
        contract("ihd,jhd->hij", query_heads, key_heads) * head_size ** (-0.5)
        + pair_bias
        + key_bias
    )
    mixed = contract("hij,jhd->ihd", soft_weights(logits), value_heads).reshape(
        queries.shape[0], feature_width
    )
    return contract("is,st->it", mixed * jax.nn.sigmoid(gate_value), weight_out)


def tri_attend(normed, pair_bias, weight_four, weight_out, key_bias):
    head_count = pair_bias.shape[0]
    feature_width = normed.shape[-1]
    head_size = feature_width // head_count

    def one_row(row_in):
        projected = contract("lc,ncd->nld", row_in, weight_four)
        shaped = projected[:3].reshape(3, row_in.shape[0], head_count, head_size)
        logits = (
            contract("jhd,khd->hjk", shaped[0], shaped[1]) * head_size ** (-0.5)
            + pair_bias
            + key_bias
        )
        mixed = contract("hjk,khd->jhd", soft_weights(logits), shaped[2]).reshape(
            row_in.shape[0], feature_width
        )
        return contract("lc,cd->ld", mixed * jax.nn.sigmoid(projected[3]), weight_out)

    return lax.map(jax.checkpoint(one_row), normed)


def mult_front(pair_in, gain_vec, weight_four, weight_gate, pair_mask):
    normed = norm_rows(pair_in, gain_vec)
    projected = contract("rlc,ncm->nmrl", normed, weight_four)
    left_side = jax.nn.sigmoid(projected[0]) * projected[1] * pair_mask
    right_side = jax.nn.sigmoid(projected[2]) * projected[3] * pair_mask
    gate_value = jax.nn.sigmoid(contract("rlc,cd->rld", normed, weight_gate))
    return (left_side, right_side, gate_value)


def mult_back(pair_in, product, gate_value, gain_vec, weight_out):
    centre = product - jnp.mean(product, 0, keepdims=True)
    spread = jnp.mean(centre * centre, 0, keepdims=True)
    scaled = centre * lax.rsqrt(spread + EPSILON) * gain_vec[:, None, None]
    return pair_in + contract("mrl,mc->rlc", scaled, weight_out) * gate_value


def outgoing_forward(left_chan, right_chan):
    return low_product("mik,mjk->mij", left_chan, right_chan)


def outgoing_backward(left_chan, right_chan, grad_out):
    return (
        low_product("mij,mjk->mik", grad_out, right_chan),
        low_product("mij,mik->mjk", grad_out, left_chan),
    )


def incoming_forward(left_chan, right_chan):
    return low_product("mki,mkj->mij", left_chan, right_chan)


def incoming_backward(left_chan, right_chan, grad_out):
    return (
        low_product("mij,mkj->mki", grad_out, right_chan),
        low_product("mij,mki->mkj", grad_out, left_chan),
    )


def to_channels(operand):
    return jax.tree.map(
        lambda part, own: part.astype(own.dtype),
        lax.all_to_all(for_sending(operand), "rows", split_axis=0, concat_axis=1, tiled=True),
        operand,
    )


def to_rows(operand):
    return jax.tree.map(
        lambda part, own: part.astype(own.dtype),
        lax.all_to_all(for_sending(operand), "rows", split_axis=1, concat_axis=0, tiled=True),
        operand,
    )


def turn_cols(operand):
    return jnp.swapaxes(
        lax.all_to_all(operand, "rows", split_axis=1, concat_axis=0, tiled=True), 0, 1
    )


def turn_rows(operand):
    return lax.all_to_all(
        jnp.swapaxes(operand, 0, 1), "rows", split_axis=0, concat_axis=1, tiled=True
    )


def gather_bias(operand):
    return lax.all_gather(operand, "rows", axis=1, tiled=True)


def scatter_bias(operand):
    return lax.psum_scatter(operand, "rows", scatter_dimension=1, tiled=True)


def general_local(
    single_rep,
    pair_rep,
    residue_mask,
    single_gains,
    pair_gains,
    mult_gains,
    single_proj,
    single_bias,
    single_up,
    single_down,
    opm_proj,
    opm_out,
    mult_proj,
    mult_gate,
    mult_out,
    att_proj,
    att_bias,
    att_out,
    pair_up,
    pair_down,
    single_cot,
    pair_cot,
):
    gains_s = widen(single_gains)
    gains_p = widen(pair_gains)
    gains_m = widen(mult_gains)
    proj_s = widen(single_proj)
    bias_sw = widen(single_bias)
    up_s = widen(single_up)
    down_s = widen(single_down)
    proj_o = widen(opm_proj)
    outer_w = widen(opm_out)
    proj_m = widen(mult_proj)
    gate_m = widen(mult_gate)
    out_m = widen(mult_out)
    proj_a = widen(att_proj)
    bias_a = widen(att_bias)
    out_a = widen(att_out)
    up_p = widen(pair_up)
    down_p = widen(pair_down)
    mask_all = widen(residue_mask[0])
    shard_rows = pair_rep.shape[1]
    first_row = lax.axis_index("rows") * shard_rows
    mask_own = lax.dynamic_slice_in_dim(mask_all, first_row, shard_rows, 0)
    key_bias = (mask_all - 1.0) * MASKED
    pair_mask = mask_own[:, None] * mask_all[None, :]
    single_own = widen(single_rep[0])
    pair_own = widen(pair_rep[0])

    def front_single(
        single_in, pair_in, gain_s, gain_z, proj_query, proj_key, proj_value, proj_gate, bias_w
    ):
        normed = norm_rows(single_in, gain_s)
        pair_normed = norm_rows(pair_in, gain_z)
        return (
            contract("rs,st->rt", normed, proj_query),
            contract("rs,st->rt", normed, proj_key),
            contract("rs,st->rt", normed, proj_value),
            contract("rs,st->rt", normed, proj_gate),
            contract("rlc,ch->hrl", pair_normed, bias_w),
        )

    def back_single(
        queries,
        key_rows,
        values,
        gate_value,
        row_bias,
        single_in,
        proj_out,
        gain_t,
        weight_up,
        weight_down,
        gain_o,
        left_w,
        right_w,
    ):
        first_sum = single_in + single_attend(
            queries, key_rows, values, gate_value, row_bias, key_bias, proj_out
        )
        hidden = jax.nn.gelu(contract("rs,st->rt", norm_rows(first_sum, gain_t), weight_up))
        second_sum = first_sum + contract("rt,ts->rs", hidden, weight_down)
        outer_in = norm_rows(second_sum, gain_o)
        left_side = contract("rs,sa->ra", outer_in, left_w) * mask_own[:, None]
        right_side = contract("rs,sa->ra", outer_in, right_w) * mask_own[:, None]
        return (second_sum, left_side, right_side)

    def outer_front(left_side, right_all, pair_in, weight_outer, gain_in, weight_four, weight_gate):
        inner = contract("ia,abc->ibc", left_side, weight_outer)
        updated = pair_in + contract("ibc,jb->ijc", inner, right_all)
        left_m, right_m, gate_value = mult_front(
            updated, gain_in, weight_four, weight_gate, pair_mask
        )
        return (updated, left_m, right_m, gate_value)

    def middle_mult(
        pair_in, product, gate_value, gain_out, weight_out, gain_in, weight_four, weight_gate
    ):
        updated = mult_back(pair_in, product, gate_value, gain_out, weight_out)
        left_m, right_m, gate_next = mult_front(
            updated, gain_in, weight_four, weight_gate, pair_mask
        )
        return (updated, left_m, right_m, gate_next)

    def start_front_general(pair_in, product, gate_value, gain_out, weight_out, gain_start, bias_w):
        updated = mult_back(pair_in, product, gate_value, gain_out, weight_out)
        normed = norm_rows(updated, gain_start)
        return (updated, normed, contract("rlc,ch->hrl", normed, bias_w))

    def start_core(pair_in, normed, bias_all, weight_four, weight_out, gain_end):
        updated = pair_in + tri_attend(normed, bias_all, weight_four, weight_out, key_bias)
        return (updated, norm_rows(updated, gain_end))

    def end_bias(turned, bias_w):
        return contract("rlc,ch->hrl", turned, bias_w)

    def end_core(turned, bias_all, weight_four, weight_out):
        return tri_attend(turned, bias_all, weight_four, weight_out, key_bias)

    def final_pair(pair_in, update, gain_vec, weight_up, weight_down):
        summed = pair_in + update
        hidden = jax.nn.gelu(contract("rlc,cd->rld", norm_rows(summed, gain_vec), weight_up))
        return summed + contract("rld,dc->rlc", hidden, weight_down)

    outs_one, back_one = jax.vjp(
        front_single,
        single_own,
        pair_own,
        gains_s[0],
        gains_p[0],
        proj_s[0],
        proj_s[1],
        proj_s[2],
        proj_s[3],
        bias_sw,
    )
    queries, keys_own, values_own, gate_single, row_bias = outs_one
    keys_all, values_all = (
        lax.all_gather(narrow(keys_own), "rows", axis=0, tiled=True),
        lax.all_gather(narrow(values_own), "rows", axis=0, tiled=True),
    )
    outs_two, back_two = jax.vjp(
        back_single,
        queries,
        widen(keys_all),
        widen(values_all),
        gate_single,
        row_bias,
        single_own,
        proj_s[4],
        gains_s[1],
        up_s,
        down_s,
        gains_s[2],
        proj_o[0],
        proj_o[1],
    )
    single_next, left_outer, right_outer = outs_two
    right_all = widen(lax.all_gather(narrow(right_outer), "rows", axis=0, tiled=True))
    outs_three, back_three = jax.vjp(
        outer_front,
        rounded(left_outer),
        right_all,
        pair_own,
        outer_w,
        gains_p[1],
        proj_m[0],
        gate_m[0],
    )
    pair_one, left_first, right_first, gate_first = outs_three
    chan_left, chan_right = to_channels((narrow(left_first), narrow(right_first)))
    product_one = outgoing_forward(chan_left, chan_right)
    rows_one = widen(to_rows(narrow(product_one)))
    outs_five, back_five = jax.vjp(
        middle_mult,
        pair_one,
        rows_one,
        gate_first,
        gains_m[0],
        out_m[0],
        gains_p[2],
        proj_m[1],
        gate_m[1],
    )
    pair_two, left_second, right_second, gate_second = outs_five
    chan_left_two, chan_right_two = to_channels((narrow(left_second), narrow(right_second)))
    product_two = incoming_forward(chan_left_two, chan_right_two)
    rows_two = widen(to_rows(narrow(product_two)))
    outs_seven, back_seven = jax.vjp(
        start_front_general, pair_two, rows_two, gate_second, gains_m[1], out_m[1], gains_p[3], bias_a[0]
    )
    pair_three, normed_start, bias_start = outs_seven
    bias_start_all = widen(gather_bias(narrow(bias_start)))
    outs_eight, back_eight = jax.vjp(
        start_core, pair_three, normed_start, bias_start_all, proj_a[0], out_a[0], gains_p[4]
    )
    pair_four, normed_end = outs_eight
    turned = widen(turn_cols(narrow(normed_end)))
    bias_end, back_nine = jax.vjp(end_bias, turned, bias_a[1])
    bias_end_all = widen(gather_bias(narrow(bias_end)))
    update_turned, back_ten = jax.vjp(end_core, turned, bias_end_all, proj_a[1], out_a[1])
    update = widen(turn_rows(narrow(update_turned)))
    pair_six, back_eleven = jax.vjp(final_pair, pair_four, update, gains_p[5], up_p, down_p)
    grad_four, grad_update, g_pg5, g_pu, g_pd = back_eleven(widen(pair_cot[0]))
    g_pg5, g_pu, g_pd = (g_pg5, g_pu, g_pd)
    grad_turned_update = widen(turn_cols(narrow(grad_update)))
    grad_turned_a, grad_bias_end_all, g_ap1, g_ao1 = back_ten(grad_turned_update)
    g_ap1, g_ao1 = (g_ap1, g_ao1)
    grad_bias_end = rounded(scatter_bias(grad_bias_end_all))
    grad_turned_b, g_ab1 = back_nine(grad_bias_end)
    grad_normed_end = widen(turn_rows(narrow(grad_turned_a + grad_turned_b)))
    grad_three, grad_normed_start, grad_bias_start_all, g_ap0, g_ao0, g_pg4 = back_eight(
        (grad_four, grad_normed_end)
    )
    g_ap0, g_ao0, g_pg4 = (g_ap0, g_ao0, g_pg4)
    grad_bias_start = rounded(scatter_bias(grad_bias_start_all))
    grad_two, grad_rows_two, grad_gate_second, g_mg1, g_mo1, g_pg3, g_ab0 = back_seven(
        (grad_three, grad_normed_start, grad_bias_start)
    )
    g_mg1, g_mo1, g_pg3, g_ab0 = (g_mg1, g_mo1, g_pg3, g_ab0)
    grad_chan_left_two, grad_chan_right_two = incoming_backward(
        chan_left_two, chan_right_two, to_channels(narrow(grad_rows_two))
    )
    grad_left_second, grad_right_second = to_rows(
        (narrow(grad_chan_left_two), narrow(grad_chan_right_two))
    )
    grad_one, grad_rows_one, grad_gate_first, g_mg0, g_mo0, g_pg2, g_mp1, g_mgt1 = back_five(
        (grad_two, widen(grad_left_second), widen(grad_right_second), grad_gate_second)
    )
    g_mg0, g_mo0, g_pg2, g_mp1, g_mgt1 = (g_mg0, g_mo0, g_pg2, g_mp1, g_mgt1)
    grad_chan_left, grad_chan_right = outgoing_backward(
        chan_left, chan_right, to_channels(narrow(grad_rows_one))
    )
    grad_left_first, grad_right_first = to_rows((narrow(grad_chan_left), narrow(grad_chan_right)))
    grad_left_outer, grad_right_all, grad_pair_a, g_oo, g_pg1, g_mp0, g_mgt0 = back_three(
        (grad_one, widen(grad_left_first), widen(grad_right_first), grad_gate_first)
    )
    g_oo, g_pg1, g_mp0, g_mgt0 = (g_oo, g_pg1, g_mp0, g_mgt0)
    grad_right_outer = rounded(
        lax.psum_scatter(grad_right_all, "rows", scatter_dimension=0, tiled=True)
    )
    two_grads = back_two((widen(single_cot[0]), rounded(grad_left_outer), grad_right_outer))
    grad_query, grad_keys_all, grad_values_all, grad_gate_single, grad_row_bias, grad_single_a = (
        two_grads[:6]
    )
    g_sp4, g_sg1, g_su, g_sd, g_sg2, g_op0, g_op1 = tuple(two_grads[6:])
    grad_keys, grad_values = (
        lax.psum_scatter(grad_keys_all, "rows", scatter_dimension=0, tiled=True),
        lax.psum_scatter(grad_values_all, "rows", scatter_dimension=0, tiled=True),
    )
    grad_single_b, grad_pair_b, g_sg0, g_pg0, g_sp0, g_sp1, g_sp2, g_sp3, g_sb = back_one(
        (grad_query, rounded(grad_keys), rounded(grad_values), grad_gate_single, grad_row_bias)
    )
    g_sg0, g_pg0, g_sp0, g_sp1, g_sp2, g_sp3, g_sb = (
        g_sg0,
        g_pg0,
        g_sp0,
        g_sp1,
        g_sp2,
        g_sp3,
        g_sb,
    )
    weight_totals = (
        jnp.stack([g_sg0, g_sg1, g_sg2]),
        jnp.stack([g_pg0, g_pg1, g_pg2, g_pg3, g_pg4, g_pg5]),
        jnp.stack([g_mg0, g_mg1]),
        jnp.stack([g_sp0, g_sp1, g_sp2, g_sp3, g_sp4]),
        g_sb,
        g_su,
        g_sd,
        jnp.stack([g_op0, g_op1]),
        g_oo,
        jnp.stack([g_mp0, g_mp1]),
        jnp.stack([g_mgt0, g_mgt1]),
        jnp.stack([g_mo0, g_mo1]),
        jnp.stack([g_ap0, g_ap1]),
        jnp.stack([g_ab0, g_ab1]),
        jnp.stack([g_ao0, g_ao1]),
        g_pu,
        g_pd,
    )
    weight_totals = lax.psum(
        (
            weight_totals[0],
            weight_totals[1],
            weight_totals[2],
            weight_totals[3],
            weight_totals[4],
            weight_totals[5],
            weight_totals[6],
            weight_totals[7],
            weight_totals[8],
            weight_totals[9],
            weight_totals[10],
            weight_totals[11],
            weight_totals[12],
            weight_totals[13],
            weight_totals[14],
            weight_totals[15],
            weight_totals[16],
        ),
        ("grp", "rows"),
    )
    return (
        narrow(single_next)[None],
        narrow(pair_six)[None],
        (grad_single_a + grad_single_b)[None],
        (grad_pair_a + grad_pair_b)[None],
    ) + tuple(weight_totals)


def norm_last(operand, gain_vec):
    centre = operand - jnp.mean(operand, -1, keepdims=True)
    spread = jnp.mean(centre * centre, -1, keepdims=True)
    return centre * lax.rsqrt(spread + EPSILON) * gain_vec


def single_track(single, row_bias, gains, proj, up, down, outer, mask):
    crops, tokens, width = single.shape
    heads = row_bias.shape[1]
    size = width // heads
    key_bias = (mask - 1.0) * MASKED

    def mm(x, w):
        return jnp.einsum("bis,st->bit", x, w)

    def split(x):
        return x.reshape(crops, tokens, heads, size)

    normed = norm_last(single, gains[0])
    query, keys, vals, sgate = (mm(normed, proj[k]) for k in range(4))
    logits = (
        jnp.einsum("bihd,bjhd->bhij", split(query), split(keys)) * size**-0.5
        + row_bias
        + key_bias[:, None, None, :]
    )
    raised = jnp.exp(logits - lax.stop_gradient(jnp.max(logits, -1, keepdims=True)))
    weights = raised / jnp.sum(raised, -1, keepdims=True)
    mixed = jnp.einsum("bhij,bjhd->bihd", weights, split(vals)).reshape(single.shape)
    first = single + mm(mixed * jax.nn.sigmoid(sgate), proj[4])
    hidden = jax.nn.gelu(mm(norm_last(first, gains[1]), up))
    second = first + mm(hidden, down)
    outer_in = norm_last(second, gains[2])
    left = mm(outer_in, outer[0]) * mask[:, :, None]
    right = mm(outer_in, outer[1]) * mask[:, :, None]
    return second, left, right


def pad_rows(x, count):
    return jnp.concatenate([x, jnp.zeros((count - x.shape[0],) + x.shape[1:], x.dtype)], 0)


def fast_local(plane, groups, row_count):
    n = row_count
    rows = L // n
    part = L * rows // n
    crops = 4
    total = crops * n

    def swap(x):
        if not plane:
            return x
        pairs = []
        for g in range(crops):
            for z in range(n // 2):
                for c in range(2):
                    pairs.append((g * n + z * 2 + c, z * n + g * 2 + c))
        return lax.ppermute(x, AX, pairs)

    def exchange(x):
        if plane:
            return lax.all_to_all(x, AX, 0, 0, tiled=True, axis_index_groups=groups)
        return lax.all_to_all(x, "rows", 0, 0, tiled=True)

    def to_all(x):
        return lax.all_to_all(jnp.broadcast_to(x, (total,) + x.shape), AX, 0, 0, tiled=True)

    def by_block(x):
        if plane:
            y = x.reshape((crops, n // 2, 2) + x.shape[1:])
            return jnp.swapaxes(y, 0, 1).reshape((crops, n) + x.shape[1:])
        return x.reshape((crops, n) + x.shape[1:])

    def reduce_rows(x):
        count = x.shape[0]
        whole = -(-count // (total * 16)) * total * 16
        x = b16(pad_rows(x, whole)).reshape(total, whole // total, 128)
        x = lax.all_to_all(x, AX, 0, 0, tiled=True)
        x = b16(jnp.sum(f32(x), 0))
        return f32(to_all(x)).reshape(whole, 128)[:count]

    def local(
        single_rep, pair_rep, residue_mask, single_gains, pair_gains, mult_gains, single_proj,
        single_bias, single_up, single_down, opm_proj, opm_out, mult_proj, mult_gate, mult_out,
        att_proj, att_bias, att_out, pair_up, pair_down, single_cot, pair_cot,
    ):
        grp, row = lax.axis_index("grp"), lax.axis_index("rows")
        if plane:
            crop, block = row // 2, grp * 2 + row % 2
        else:
            crop, block = grp, row
        ab_pad = jnp.pad(jnp.swapaxes(att_bias, 1, 2), ((0, 0), (0, HPAD - TH), (0, 0)))
        sb_pad = jnp.pad(single_bias.T, ((0, HPAD - single_bias.shape[1]), (0, 0)))
        m5t, m5, mot, mof, a4t, a4, aot, abt, upt, up, dnt, sbt = prep_weights(
            pair_gains, mult_gains, mult_proj, mult_gate, mult_out, att_proj, ab_pad, att_out,
            pair_up, pair_down, sb_pad,
        )
        gatet = m5t[:, 512:640]

        pair = swap(pair_rep[0])
        rb_own = row_bias(rows, pair_rep[0], sbt)
        mask_row = pad_rows(b16(residue_mask), 16)
        s_rows = rows * 4
        gathered = to_all(
            jnp.concatenate([single_rep[0].reshape(s_rows, 128), rb_own, mask_row], 0)
        )
        single_all = f32(gathered[:, :s_rows]).reshape(crops, L, 512)
        rb_all = f32(gathered[:, s_rows : s_rows + 8 * rows]).reshape(crops, n, 8, rows, L)
        rb_all = jnp.swapaxes(rb_all, 1, 2).reshape(crops, 8, L, L)
        masks = f32(gathered[:, s_rows + 8 * rows]).reshape(crops, n, L)[:, 0]
        cot_all = f32(to_all(single_cot[0].reshape(s_rows, 128))).reshape(crops, L, 512)

        (s2, left, right), single_pull = jax.vjp(
            lambda s, b, g, p, u, d, o: single_track(s, b, g, p, u, d, o, masks),
            single_all, rb_all, f32(single_gains), f32(single_proj), f32(single_up),
            f32(single_down), f32(opm_proj),
        )
        mask_crop = lax.dynamic_index_in_dim(masks, crop, 0, keepdims=False)
        mask_own = lax.dynamic_slice_in_dim(mask_crop, block * rows, rows, 0)
        pmask = mask_own[:, None] * mask_crop[None, :]
        key_row = ((mask_crop - 1.0) * MASKED)[None, :]
        right_own = b16(lax.dynamic_index_in_dim(right, crop, 0, keepdims=False))
        left_own = lax.dynamic_index_in_dim(left, crop, 0, keepdims=False)
        left_own = b16(lax.dynamic_slice_in_dim(left_own, block * rows, rows, 0))
        inner = b16(jnp.einsum("ia,abc->ibc", left_own, opm_out, preferred_element_type=F32))

        z1, ab1 = front(n, rows, pair, inner, right_own, pmask, m5t[0])
        ab1 = exchange(ab1)
        p1 = exchange(channel_product(n, rows, True, ab1)).reshape(C * rows, L)
        z2, ab2 = middle(n, rows, z1, p1, gatet[0], mot[0], pmask, m5t[1])
        ab2 = exchange(ab2)
        p2 = exchange(channel_product(n, rows, False, ab2)).reshape(C * rows, L)
        z3, tb = start_front(rows, z2, p2, gatet[1], mot[1], abt[0])
        tb_all = exchange(jnp.broadcast_to(tb, (n,) + tb.shape))
        z4, turn = start_attention(n, rows, z3, tb_all, key_row, a4t[0], aot[0], abt[1])
        turn = exchange(turn)

        cot = swap(pair_cot[0]).reshape(rows, n, rows, C)
        cot = exchange(jnp.transpose(cot, (1, 2, 0, 3)))
        cot = jnp.swapaxes(cot, 0, 1).reshape(rows, L, C)
        pout, back, m_up, m_dn, m_a41, m_ao1 = end_both(
            n, rows, turn, cot, key_row, a4t[1], a4[1], aot[1], att_out[1], upt, up, dnt,
            pair_down,
        )
        back = exchange(back)
        pout = exchange(pout).reshape(n, rows, rows, C)
        pair_six = swap(jnp.swapaxes(pout, 0, 1).reshape(rows, L, C))

        dz4, dxs, dtb, m_a40, m_ao0, m_ab1 = start_back(
            n, rows, z3, z4, back, tb_all, key_row, a4t[0], a4[0], att_out[0], abt[1]
        )
        dtb = exchange(dtb)
        dz3, dgp2, dp2, m_ab0, m_mo1 = third_back(
            n, rows, z3, dz4, dxs, dtb, abt[0], z2, p2, gatet[1], mot[1], mof[1]
        )
        dp2 = exchange(dp2.reshape(n, part, L))
        dab2 = exchange(channel_product_back(n, rows, False, ab2, dp2))
        dz2, dgp1, dp1, m_m51, m_mo0 = second_back(
            n, rows, z2, dz3, dgp2, dab2, pmask, m5t[1], m5[1], z1, p1, gatet[0], mot[0], mof[0]
        )
        dp1 = exchange(dp1.reshape(n, part, L))
        dab1 = exchange(channel_product_back(n, rows, True, ab1, dp1))
        dz1, dinner, dright, m_m50 = first_back(
            n, rows, z1, dz2, dgp1, dab1, pmask, m5t[0], m5[0], inner, right_own, right_own.T
        )
        dz1 = swap(dz1)
        dleft = jnp.einsum("ibc,abc->ia", dinner, f32(opm_out))
        m_oo = jnp.einsum("ia,ibc->abc", f32(left_own), dinner)

        opm = dleft.shape[1]
        ends = b16(jnp.concatenate([dleft, dright], 0)).reshape(-1, 128)
        ends = by_block(to_all(ends).reshape(total, rows + L, opm))
        dleft_all = f32(ends[:, :, :rows]).reshape(crops, L, opm)
        dright_all = jnp.sum(f32(ends[:, :, rows:]), 1)
        ds, drb, g_sg, g_sp, g_su, g_sd, g_op = single_pull((cot_all, dleft_all, dright_all))
        drb_own = lax.dynamic_index_in_dim(drb, grp, 0, keepdims=False)
        drb_own = lax.dynamic_slice_in_dim(drb_own, row * rows, rows, 1).reshape(8 * rows, L)
        pair_grad, m_sb = last_back(rows, pair_rep[0], drb_own, dz1, sbt)

        first = [m_up, m_dn, m_a41, m_ao1, m_a40, m_ao0, m_mo1, m_mo0, m_ab1, m_ab0, m_m51]
        second = [m_m50, m_oo.reshape(-1, 128)]

        def reduce_list(parts):
            summed = reduce_rows(jnp.concatenate(parts, 0))
            out, at = [], 0
            for p in parts:
                out.append(summed[at : at + p.shape[0]])
                at += p.shape[0]
            return out

        m_up, m_dn, m_a41, m_ao1, m_a40, m_ao0, m_mo1, m_mo0, m_ab1, m_ab0, m_m51 = reduce_list(
            first
        )
        m_m50, m_oo = reduce_list(second)
        m_sb = jnp.sum(to_all(m_sb), 0)[:8]

        gp, gm = f32(pair_gains), f32(mult_gains)
        scale = jnp.array([HD**-0.5, 1.0, 1.0, 1.0], F32)[:, None, None]
        g_pg = [jnp.sum(f32(single_bias) * m_sb.T, 1)]
        g_mp, g_mgt, g_mo, g_mg, g_ap, g_ab = [], [], [], [], [], []
        for t, (m, mo) in enumerate(((m_m50, m_mo0), (m_m51, m_mo1))):
            m = m.reshape(5, C, C)
            g = gp[1 + t][:, None]
            g_mp.append(m[:4] * g)
            g_mgt.append(m[4] * g)
            g_pg.append(
                jnp.sum(f32(mult_proj[t]) * m[:4], (0, 2)) + jnp.sum(f32(mult_gate[t]) * m[4], 1)
            )
            g_mo.append(mo * gm[t][:, None])
            g_mg.append(jnp.sum(f32(mult_out[t]) * mo, 1))
        for t, (m, mab) in enumerate(((m_a40, m_ab0), (m_a41, m_ab1))):
            m = m.reshape(4, C, C) * scale
            mab = mab[:TH].T
            g = gp[3 + t][:, None]
            g_ap.append(m * g)
            g_ab.append(mab * g)
            g_pg.append(
                jnp.sum(f32(att_proj[t]) * m, (0, 2)) + jnp.sum(f32(att_bias[t]) * mab, 1)
            )
        m_up = jnp.swapaxes(m_up.reshape(4, C, C), 0, 1).reshape(C, 512)
        g_pg.append(jnp.sum(f32(pair_up) * m_up, 1))

        own = lambda x: lax.dynamic_slice(x, (grp, row * rows, 0), (1, rows, 512))
        return (
            b16(own(s2)),
            pair_six[None],
            own(ds),
            pair_grad[None],
            g_sg,
            jnp.stack(g_pg),
            jnp.stack(g_mg),
            g_sp,
            m_sb.T * gp[0][:, None],
            g_su,
            g_sd,
            g_op,
            m_oo.reshape(opm, opm, C),
            jnp.stack(g_mp),
            jnp.stack(g_mgt),
            jnp.stack(g_mo),
            jnp.stack(g_ap),
            jnp.stack(g_ab),
            jnp.stack([m_ao0, m_ao1]),
            m_up * gp[5][:, None],
            m_dn,
        )

    return local


def solution(mesh):
    groups_of, n = mesh.shape["grp"], mesh.shape["rows"]
    whole = P()
    in_specs = (
        (P("grp", "rows", None), P("grp", "rows", None, None), P("grp", None))
        + (whole,) * 17
        + (P("grp", "rows", None), P("grp", "rows", None, None))
    )
    out_specs = (
        P("grp", "rows", None),
        P("grp", "rows", None, None),
        P("grp", "rows", None),
        P("grp", "rows", None, None),
    ) + (whole,) * 17
    if L % n == 0 and (L // n) % 16 == 0:
        plane = groups_of * 2 == n
        groups = [
            [g * n + z * 2 + c for g in range(groups_of) for c in range(2)]
            for z in range(n // 2)
        ]
        body = fast_local(plane, groups if plane else None, n)
    else:
        body = general_local
    return jax.shard_map(body, mesh=mesh, in_specs=in_specs, out_specs=out_specs, check_vma=False)
```

```python
import math

import jax
import jax.numpy as jnp
from jax import lax
from jax.experimental import pallas as pl
from jax.experimental.pallas import tpu as pltpu
from jax.sharding import PartitionSpec as P

BF = jnp.bfloat16
F32 = jnp.float32
EPSILON = 1e-05
MASKED = 1000000000.0
AX = ("grp", "rows")
L = 128
C = 128
TH = 4
HD = 32
HPAD = 16


def dot(a, b):
    return lax.dot_general(a, b, (((1,), (0,)), ((), ())), preferred_element_type=F32)


def dot_nt(a, b):
    return lax.dot_general(a, b, (((1,), (1,)), ((), ())), preferred_element_type=F32)


def dot_tn(a, b):
    return lax.dot_general(a, b, (((0,), (0,)), ((), ())), preferred_element_type=F32)


def b16(x):
    return x.astype(BF)


def f32(x):
    return x.astype(F32)


def sig(x):
    return 0.5 * jnp.tanh(0.5 * x) + 0.5


GELU_A = 0.7978845608028654
GELU_B = 0.044715


def gelu_parts(x):
    t = jnp.tanh(GELU_A * (x + GELU_B * x * x * x))
    half = 0.5 * (1.0 + t)
    slope = half + 0.5 * x * (1.0 - t * t) * (GELU_A * (1.0 + 3.0 * GELU_B * x * x))
    return x * half, slope


def norm_cols(z):
    c = z - jnp.mean(z, 0, keepdims=True)
    scale = lax.rsqrt(jnp.mean(c * c, 0, keepdims=True) + EPSILON)
    return c * scale, scale


def norm_cols_back(dx, xh, scale):
    return scale * (
        dx - jnp.mean(dx, 0, keepdims=True) - xh * jnp.mean(dx * xh, 0, keepdims=True)
    )


def cols(r):
    return pl.ds(pl.multiple_of(r * L, L), L)


def each_row(count, body):
    def step(r, carry):
        body(r)
        return carry

    lax.fori_loop(0, count, step, 0, unroll=4 if count > 4 else 2)


def call(kernel, outs, scratch, args, deps=(), raw=(), late=(), far=(), us=5):
    count, more, given = len(args), len(deps), len(outs)
    fetched = [args[k] for k in raw]

    def body(*refs):
        mine = list(refs[:count])
        results = list(refs[count + more : count + more + given])
        rest = list(refs[count + more + given :])
        sems = rest.pop() if raw or far else None
        stores = [rest.pop() for _ in far][::-1]
        held = [rest.pop() for _ in raw][::-1]
        moves = {}
        for i, k in enumerate(raw):
            moves[k] = pltpu.make_async_copy(mine[k], held[i], sems.at[i])
            moves[k].start()
        for k in raw:
            if k not in late:
                moves[k].wait()
        for i, k in enumerate(raw):
            mine[k] = held[i]
        ends = []
        for i, k in enumerate(far):
            ends.append(pltpu.make_async_copy(stores[i], results[k], sems.at[len(raw) + i]))
            results[k] = stores[i]
        if late:
            kernel(lambda k: moves[k].wait(), *mine, *results, *rest)
        else:
            kernel(*mine, *results, *rest)
        for end in ends:
            end.start()
        for end in ends:
            end.wait()

    vm = pl.BlockSpec(memory_space=pltpu.VMEM)
    sm = pl.BlockSpec(memory_space=pltpu.SMEM)
    away = pl.BlockSpec(memory_space=pl.ANY)
    moved = sum(a.size * a.dtype.itemsize for a in args)
    buffers = [pltpu.VMEM(s, d) for s, d in scratch]
    buffers += [pltpu.VMEM(a.shape, a.dtype) for a in fetched]
    buffers += [pltpu.VMEM(*outs[k]) for k in far]
    placed = sum(math.prod(b.shape) * jnp.dtype(b.dtype).itemsize for b in buffers)
    if raw or far:
        buffers.append(pltpu.SemaphoreType.DMA((len(raw) + len(far),)))
    return pl.pallas_call(
        body,
        out_shape=[
            pltpu.HBM(s, d) if k in far else jax.ShapeDtypeStruct(s, d)
            for k, (s, d) in enumerate(outs)
        ],
        in_specs=[
            away if k in raw else sm if a.dtype == jnp.int32 else vm for k, a in enumerate(args)
        ]
        + [away] * more,
        out_specs=[away if k in far else vm for k in range(given)],
        scratch_shapes=buffers,
        compiler_params=pltpu.CompilerParams(vmem_limit_bytes=(12 << 20) + placed),
        cost_estimate=pl.CostEstimate(flops=us * 10**9, bytes_accessed=moved, transcendentals=0),
    )(
        *[
            pltpu.with_memory_space_constraint(a, pltpu.HBM) if k in raw else a
            for k, a in enumerate(args)
        ],
        *deps,
    )


def prep_weights(gp, gm, mp, mg, mo, ap, ab, ao, pu, pd, sb):
    def kernel(
        gp, gm, mp, mg, mo, ap, ab, ao, pu, pd, sb,
        m5t, m5, mot, mof, a4t, a4, aot, abt, upt, up, dnt, sbt,
    ):
        gpv = f32(gp[...])
        gmv = f32(gm[...])

        def turned(w):
            shape = (HPAD, w.shape[1])
            row = lax.broadcasted_iota(jnp.int32, shape, 0)
            lane = lax.broadcasted_iota(jnp.int32, shape, 1)
            return dot_nt(b16(jnp.where(row == lane, 1.0, 0.0)), w)

        for t in range(2):
            g = gpv[1 + t : 2 + t]
            for k in range(5):
                w = f32(mp[t, k] if k < 4 else mg[t]).T * g
                m5t[t, k * C : (k + 1) * C] = b16(w)
                m5[t, :, k * C : (k + 1) * C] = b16(w.T)
            w = f32(mo[t]).T * gmv[t : t + 1]
            mot[t] = b16(w)
            mof[t] = b16(w.T)
            g = gpv[3 + t : 4 + t]
            for k in range(4):
                w = f32(ap[t, k]).T * (g * HD**-0.5 if k == 0 else g)
                a4t[t, k * C : (k + 1) * C] = b16(w)
                a4[t, :, k * C : (k + 1) * C] = b16(w.T)
            aot[t] = b16(f32(ao[t]).T)
            abt[t] = b16(turned(ab[t]) * g)
        g = gpv[5:6]
        for k in range(4):
            s = slice(k * C, (k + 1) * C)
            w = f32(pu[:, s]).T * g
            upt[s] = b16(w)
            up[:, s] = b16(w.T)
            dnt[:, s] = b16(f32(pd[s]).T)
        sbt[...] = b16(turned(sb[...]) * gpv[0:1])

    outs = [
        ((2, 640, C), BF), ((2, C, 640), BF), ((2, C, C), BF), ((2, C, C), BF),
        ((2, 512, C), BF), ((2, C, 512), BF), ((2, C, C), BF), ((2, HPAD, C), BF),
        ((512, C), BF), ((C, 512), BF), ((C, 512), BF), ((HPAD, C), BF),
    ]
    return call(kernel, outs, [], (gp, gm, mp, mg, mo, ap, ab, ao, pu, pd, sb), raw=(0, 1, 2, 3, 4, 5, 6, 7, 8, 9, 10), far=(0, 1, 2, 3, 4, 5, 6, 7, 8, 9, 10, 11), us=3)


def pack(rows, single, cot, pair, mask, sbt, where):
    def kernel(single, cot, pair, mask, sbt, where, mine, mask_col, s, sm):
        sm[...] = jnp.broadcast_to(mask[...], (L, L)).T
        mask_col[...] = sm[pl.ds(pl.multiple_of(where[3] * rows, rows), rows), :]
        key_row = (mask[...] - 1.0) * MASKED

        def body(r):
            xh, _ = norm_cols(f32(pair[r]).T)
            rb = dot(sbt[...], b16(xh)) + key_row
            s[pl.ds(r, HPAD, stride=rows), :] = rb

        each_row(rows, body)
        mine[0:rows] = single[...]
        mine[rows : 2 * rows] = cot[...]
        for h in range(8):
            mine[rows * (2 + h // 4) : rows * (3 + h // 4), (h % 4) * L : (h % 4 + 1) * L] = b16(
                s[h * rows : (h + 1) * rows]
            )

    width = single.shape[1]
    return call(
        kernel,
        [((4 * rows, width), BF), ((rows, L), F32)],
        [((HPAD * rows, L), F32), ((L, L), F32)],
        (single, cot, pair, mask, sbt, where), raw=(0, 1, 2, 4), us=2)


def copies_of(x, count, deps):
    def kernel(x, out):
        for d in range(count):
            out[d] = x[...]

    return call(kernel, [((count,) + x.shape, x.dtype)], [], (x,), deps=deps)[0]


def norm_rows16(x):
    c = x - jnp.mean(x, -1, keepdims=True)
    scale = lax.rsqrt(jnp.mean(c * c, -1, keepdims=True) + EPSILON)
    return c * scale, scale


def norm_rows16_back(dx, xh, scale):
    return scale * (
        dx - jnp.mean(dx, -1, keepdims=True) - xh * jnp.mean(dx * xh, -1, keepdims=True)
    )


def halves():
    lane = lax.broadcasted_iota(jnp.int32, (1, L), 1)
    low = jnp.where(lane < L // 2, 1.0, 0.0)
    return b16(low), b16(1.0 - low)


def pair_weights(q, k, bias0, bias1):
    out = []
    for m, bias in zip(halves(), (bias0, bias1)):
        s = dot_nt(q * m, k) + bias
        e = jnp.exp(s - jnp.max(s, -1, keepdims=True))
        out.append(b16(e / jnp.sum(e, -1, keepdims=True)))
    return out


def on_halves(x, axis=0):
    return jnp.concatenate([x * m for m in halves()], axis)


def single_own(n, rows, copies, gathered, mine, mask_col, gains, proj, up, down, outer):
    width = up.shape[0]
    opm2 = 64

    def kernel(arrive, gathered, mine, mask_col, gains, proj, up, down, outer, out, lr):
        g = f32(gains[...])
        sn = b16(norm_rows16(f32(gathered[...].reshape(n * rows, width)))[0] * g[0:1])
        arrive(4)
        keys, vals = b16(dot(sn, proj[1])), b16(dot(sn, proj[2]))
        x = f32(mine[0:rows])
        sn = b16(norm_rows16(x)[0] * g[0:1])
        query = b16(dot(sn, proj[0]) * 0.125)
        gate = sig(dot(sn, proj[3]))
        mixed = []
        for t in range(4):
            s = slice(t * L, (t + 1) * L)
            bias = [
                f32(mine[rows * (2 + h // 4) : rows * (3 + h // 4), (h % 4) * L : (h % 4 + 1) * L])
                for h in (2 * t, 2 * t + 1)
            ]
            p = pair_weights(query[:, s], keys[:, s], *bias)
            mixed.append(dot(jnp.concatenate(p, 1), on_halves(vals[:, s])))
        mixed = jnp.concatenate(mixed, 1)
        first = x + dot(b16(mixed * gate), proj[4])
        x1 = b16(norm_rows16(first)[0] * g[1:2])
        arrive(5)
        hidden = b16(gelu_parts(dot(x1, up[...]))[0])
        arrive(6)
        second = first + dot(hidden, down[...])
        out[...] = b16(second)
        x2 = b16(norm_rows16(second)[0] * g[2:3])
        both = dot(x2, outer[...]) * mask_col[...]
        lane = lax.broadcasted_iota(jnp.int32, (rows, L), 1)
        both = b16(jnp.where(lane >= opm2, mask_col[...], both))
        for d in range(copies):
            lr[d] = both

    return call(
        kernel,
        [((rows, width), BF), ((copies, rows, L), BF)],
        [],
        (gathered, mine, mask_col, gains, proj, up, down, outer), raw=(3, 4, 5, 6, 7), late=(4, 5, 6), us=6)


def single_every(n, rows, where, ga, gb, gains, proj, up, down, deps=()):
    width, wide = up.shape
    tokens = 4 * L
    half = ga.shape[0]

    def kernel(
        arrive, where, ga, gb, gains, proj, up, down,
        x_all, cot_all, xs, qkv, gm, probs, slope, first_out, second_out, held,
    ):
        core = where[3] % 2
        for k in range(half):
            held[2 * k + core] = ga[k]
            held[2 * k + 1 - core] = gb[k]
        g = f32(gains[...])

        def body(crop):
            rs = pl.ds(pl.multiple_of(crop * L, L), L)
            ds = pl.ds(crop * n, n)
            x16 = held[ds, 0:rows, :].reshape(L, width)
            x_all[rs, :] = x16
            cot_all[rs, :] = held[ds, rows : 2 * rows, :].reshape(L, width)
            x = f32(x16)
            sn = b16(norm_rows16(x)[0] * g[0:1])
            xs[rs, 0:width] = sn

            @pl.when(crop == 0)
            def _():
                arrive(4)

            query = b16(dot(sn, proj[0]) * 0.125)
            keys, vals = b16(dot(sn, proj[1])), b16(dot(sn, proj[2]))
            qkv[rs, 0:width] = query
            qkv[rs, width : 2 * width] = keys
            qkv[rs, 2 * width : 3 * width] = vals
            gate = sig(dot(sn, proj[3]))
            mixed = []
            for t in range(4):
                s = slice(t * L, (t + 1) * L)
                bias = [
                    f32(
                        held[
                            ds,
                            rows * (2 + h // 4) : rows * (3 + h // 4),
                            (h % 4) * L : (h % 4 + 1) * L,
                        ].reshape(L, L)
                    )
                    for h in (2 * t, 2 * t + 1)
                ]
                p = pair_weights(query[:, s], keys[:, s], *bias)
                for k in range(2):
                    at = pl.multiple_of((crop * 8 + 2 * t + k) * L, L)
                    probs[pl.ds(at, L), :] = p[k]
                mixed.append(dot(jnp.concatenate(p, 1), on_halves(vals[:, s])))
            mixed = jnp.concatenate(mixed, 1)
            gm[rs, 0:width] = b16(gate)
            gm[rs, width : 2 * width] = b16(mixed)
            u = b16(mixed * gate)
            xs[rs, width : 2 * width] = u
            first = x + dot(u, proj[4])
            first_out[rs, :] = first
            x1 = b16(norm_rows16(first)[0] * g[1:2])
            xs[rs, 2 * width : 3 * width] = x1

            @pl.when(crop == 0)
            def _():
                arrive(5)
                arrive(6)

            hid, slp = gelu_parts(dot(x1, up[...]))
            h16 = b16(hid)
            xs[rs, 3 * width : 3 * width + wide] = h16
            slope[rs, :] = b16(slp)
            second_out[rs, :] = first + dot(h16, down[...])

        each_row(4, body)

    return call(
        kernel,
        [
            ((tokens, width), BF), ((tokens, width), BF), ((tokens, 3 * width + wide), BF),
            ((tokens, 3 * width), BF), ((tokens, 2 * width), BF), ((4 * 8 * L, L), BF),
            ((tokens, wide), BF), ((tokens, width), F32), ((tokens, width), F32),
        ],
        [((2 * half, 4 * rows, width), BF)],
        (where, ga, gb, gains, proj, up, down),
        deps=deps, raw=(1, 2, 3, 4, 5, 6), late=(4, 5, 6), far=(0, 1, 2, 3, 4, 5, 6, 7, 8), us=19)


def single_back(members, rows, where, ea, eb, kept, gains, proj, up, down, outer, deps=()):
    width, wide = up.shape
    tokens = 4 * L
    x_all, cot_all, _, qkv, gm, probs, slope, first_in, second_in = kept

    def kernel(
        arrive, where, ea, eb, x_all, cot_all, qkv, gm, probs, slope, first_in, second_in,
        gains, proj, up, down, outer,
        ys, gain_grad, d_own, drb, m_op,
        dlr, o_x2, sdrb, sds,
    ):
        g = f32(gains[...])
        gain_grad[...] = jnp.zeros_like(gain_grad)
        for crop in range(4):
            total = f32(ea[members[crop][0]]) + f32(eb[members[crop][0]])
            for k in members[crop][1:]:
                total = total + (f32(ea[k]) + f32(eb[k]))
            total = jnp.concatenate([total, jnp.zeros_like(total)], 0)
            dlr[crop * L : (crop + 1) * L] = b16(total.T)

        def body(crop):
            rs = pl.ds(pl.multiple_of(crop * L, L), L)
            x2, sc2 = norm_rows16(second_in[rs, :])
            o_x2[rs, :] = b16(x2 * g[2:3])
            dx = dot_nt(dlr[rs, :], outer[...])
            gain_grad[2:3] += jnp.sum(dx * x2, 0, keepdims=True)
            ds2 = f32(cot_all[rs, :]) + norm_rows16_back(dx * g[2:3], x2, sc2)
            ds2_16 = b16(ds2)
            ys[rs, 5 * width + wide :] = ds2_16

            @pl.when(crop == 0)
            def _():
                for k in (14, 8, 13, 9):
                    arrive(k)

            dhp = b16(dot_nt(ds2_16, down[...]) * f32(slope[rs, :]))
            ys[rs, 5 * width : 5 * width + wide] = dhp
            dx = dot_nt(dhp, up[...])
            x1, sc1 = norm_rows16(first_in[rs, :])
            gain_grad[1:2] += jnp.sum(dx * x1, 0, keepdims=True)
            df = ds2 + norm_rows16_back(dx * g[1:2], x1, sc1)
            df16 = b16(df)
            ys[rs, 4 * width : 5 * width] = df16

            @pl.when(crop == 0)
            def _():
                for k in (12, 6, 5, 7):
                    arrive(k)

            du = dot_nt(df16, proj[4])
            gate, mixed = f32(gm[rs, 0:width]), f32(gm[rs, width : 2 * width])
            do = du * gate
            do16 = b16(do)
            row = do * mixed
            dgate = b16(du * mixed * gate * (1.0 - gate))
            ys[rs, 3 * width : 4 * width] = dgate
            lane = lax.broadcasted_iota(jnp.int32, (1, L), 1)
            low = jnp.where(lane < L // 2, 1.0, 0.0)
            for t in range(4):
                s = slice(t * L, (t + 1) * L)
                q = qkv[rs, t * L : (t + 1) * L]
                k = qkv[rs, width + t * L : width + (t + 1) * L]
                v = qkv[rs, 2 * width + t * L : 2 * width + (t + 1) * L]
                grads, weights = [], []
                for j, (m, mf) in enumerate(zip(halves(), (low, 1.0 - low))):
                    at = pl.multiple_of((crop * 8 + 2 * t + j) * L, L)
                    p16 = probs[pl.ds(at, L), :]
                    dp = dot_nt(do16[:, s] * m, v)
                    e = f32(p16) * (dp - jnp.sum(row[:, s] * mf, -1, keepdims=True))
                    sdrb[pl.ds(at, L), :] = e
                    grads.append(b16(e))
                    weights.append(p16)
                dq = dot(jnp.concatenate(grads, 1), on_halves(k)) * 0.125
                dk = dot_tn(jnp.concatenate(grads, 0), on_halves(q))
                dv = dot_tn(jnp.concatenate(weights, 0), on_halves(do16[:, s]))
                ys[rs, t * L : (t + 1) * L] = b16(dq)
                ys[rs, width + t * L : width + (t + 1) * L] = b16(dk)
                ys[rs, 2 * width + t * L : 2 * width + (t + 1) * L] = b16(dv)
            dx = dot_nt(ys[rs, 0:width], proj[0])
            for k in range(1, 4):
                dx = dx + dot_nt(ys[rs, k * width : (k + 1) * width], proj[k])
            x0, sc0 = norm_rows16(f32(x_all[rs, :]))
            gain_grad[0:1] += jnp.sum(dx * x0, 0, keepdims=True)
            sds[rs, :] = df + norm_rows16_back(dx * g[0:1], x0, sc0)

        each_row(4, body)
        grp, row = where[2], where[3]
        d_own[...] = sds[pl.ds(pl.multiple_of(grp * L + row * rows, rows), rows), :]
        for h in range(8):
            at = pl.multiple_of((grp * 8 + h) * L + row * rows, rows)
            drb[h * rows : (h + 1) * rows] = sdrb[pl.ds(at, rows), :]
        m_op[...] = dot_tn(o_x2[...], dlr[...])

    return call(
        kernel,
        [
            ((tokens, 6 * width + wide), BF), ((3, width), F32), ((rows, width), F32),
            ((8 * rows, L), F32), ((width, L), F32),
        ],
        [
            ((tokens, L), BF), ((tokens, width), BF), ((4 * 8 * L, L), F32), ((tokens, width), F32),
        ],
        (
            where, ea, eb, x_all, cot_all, qkv, gm, probs, slope, first_in, second_in,
            gains, proj, up, down, outer,
        ), deps=deps, raw=(3, 4, 5, 6, 7, 8, 9, 10, 11, 12, 13, 14, 15), late=(5, 6, 7, 8, 9, 12, 13, 14), far=(0, 1, 2, 3, 4), us=22)


def weight_grads(xs, ys, width, wide):
    tokens = xs.shape[0]
    blocks = wide // width

    def kernel(x, y, out):
        out[...] = dot_tn(x[...], y[...]).reshape(out.shape)

    def run(steps, x_at, y_at, shape, block, out_at):
        return pl.pallas_call(
            kernel,
            grid=(steps,),
            out_shape=jax.ShapeDtypeStruct(shape, F32),
            in_specs=[
                pl.BlockSpec((tokens, width), x_at),
                pl.BlockSpec((tokens, width), y_at),
            ],
            out_specs=pl.BlockSpec(block, out_at),
            compiler_params=pltpu.CompilerParams(vmem_limit_bytes=32 << 20),
            cost_estimate=pl.CostEstimate(
                flops=4 * 10**9,
                bytes_accessed=steps * width * width * 8,
                transcendentals=0,
            ),
        )(pltpu.with_memory_space_constraint(xs, pltpu.HBM), pltpu.with_memory_space_constraint(ys, pltpu.HBM))

    proj = run(
        5, lambda i: (0, i // 4), lambda i: (0, i), (5, width, width), (1, width, width),
        lambda i: (i, 0, 0),
    )
    up = run(
        blocks, lambda i: (0, 2), lambda i: (0, 5 + i), (width, wide), (width, width),
        lambda i: (0, i),
    )
    down = run(
        blocks, lambda i: (0, 3 + i), lambda i: (0, 5 + blocks), (wide, width), (width, width),
        lambda i: (i, 0),
    )
    return proj, up, down


def project_pair(z, r, rows, m5t, pmask, sa, sb):
    xh, _ = norm_cols(z)
    p = dot(m5t[0:512], b16(xh))
    mk = pmask[pl.ds(r, 1), :]
    sa[pl.ds(r, C, stride=rows), :] = sig(p[0:C]) * p[C : 2 * C] * mk
    sb[pl.ds(r, C, stride=rows), :] = sig(p[2 * C : 3 * C]) * p[3 * C : 4 * C] * mk


def put_pair(n, ab, sa, sb):
    part = sa.shape[0] // n
    for d in range(n):
        ab[d, 0:part] = b16(sa[d * part : (d + 1) * part])
        ab[d, part : 2 * part] = b16(sb[d * part : (d + 1) * part])


def gated_product(z, r, rows, gatet, mot, sp):
    xh, _ = norm_cols(z)
    gate = sig(dot(gatet[...], b16(xh)))
    ph, _ = norm_cols(sp[pl.ds(r, C, stride=rows), :])
    return z + dot(mot[...], b16(ph)) * gate


def front(n, rows, where, lr_all, pair, outer_w, m5ts, deps=()):
    opm = outer_w.shape[0]

    def kernel(
        where, lr_all, pair, outer_w, m5ts,
        z1, ab, pmask, key_row, inner, lrt, left_own, sa, sb, slr, spm,
    ):
        m5t = m5ts.at[0]
        crop, block = where[0], where[1]
        lr16 = lr_all[pl.ds(crop * n, n)].reshape(L, C)
        lr = f32(lr16)
        turned = lr.T
        lrt[...] = turned
        mrow = turned[2 * opm : 2 * opm + 1]
        key_row[...] = (mrow - 1.0) * MASKED
        first = pl.multiple_of(block * rows, rows)
        spm[...] = jnp.broadcast_to(mrow, (L, L)).T * mrow
        pmask[...] = spm[pl.ds(first, rows), :]
        slr[...] = lr
        left = b16(slr[pl.ds(first, rows), :])
        left_own[...] = left
        for b in range(opm):
            inner[b * rows : (b + 1) * rows] = dot(left[:, 0:opm], outer_w[b])
        edge = jnp.zeros((opm, C), BF)

        def body(r):
            mine = b16(inner[pl.ds(r, opm, stride=rows), :])
            mine = jnp.concatenate([edge, mine, edge, edge], 0)
            z = (f32(pair[r]) + dot(lr16, mine)).T
            z1[:, cols(r)] = z
            project_pair(z, r, rows, m5t, pmask, sa, sb)

        each_row(rows, body)
        put_pair(n, ab, sa, sb)

    part = C * rows // n
    return call(
        kernel,
        [
            ((C, rows * L), F32), ((n, 2 * part, L), BF), ((rows, L), F32), ((1, L), F32),
            ((opm * rows, C), F32), ((C, L), F32), ((rows, C), BF),
        ],
        [((C * rows, L), F32)] * 2 + [((L, C), F32), ((L, L), F32)],
        (where, lr_all, pair, outer_w, m5ts), deps=deps, raw=(2, 3, 4), far=(0, 2, 3, 4, 5, 6), us=5)


def middle(n, rows, z1, prod, mots, pmask, m5ts):
    def kernel(z1, prod, mots, pmask, m5ts, z2, ab, sa, sb, sp):
        gatet, mot, m5t = m5ts.at[0, 512:640], mots.at[0], m5ts.at[1]
        sp[...] = f32(prod[...])

        def body(r):
            z = gated_product(z1[:, cols(r)], r, rows, gatet, mot, sp)
            z2[:, cols(r)] = z
            project_pair(z, r, rows, m5t, pmask, sa, sb)

        each_row(rows, body)
        put_pair(n, ab, sa, sb)

    part = C * rows // n
    return call(
        kernel,
        [((C, rows * L), F32), ((n, 2 * part, L), BF)],
        [((C * rows, L), F32)] * 3,
        (z1, prod, mots, pmask, m5ts), raw=(0, 1, 2, 3, 4), far=(0,), us=4)


def start_front(n, rows, z2, prod, m5ts, mots, abts, deps=()):
    def kernel(z2, prod, m5ts, mots, abts, z3, tb, sp, st):
        gatet, mot, abt = m5ts.at[1, 512:640], mots.at[1], abts.at[0]
        sp[...] = f32(prod[...])

        def body(r):
            z = gated_product(z2[:, cols(r)], r, rows, gatet, mot, sp)
            z3[:, cols(r)] = z
            xh, _ = norm_cols(z)
            st[pl.ds(r, HPAD, stride=rows), :] = dot(abt[...], b16(xh))

        each_row(rows, body)
        for d in range(n):
            tb[d] = b16(st[0 : TH * rows])

    return call(
        kernel,
        [((C, rows * L), F32), ((n, TH * rows, L), BF)],
        [((C * rows, L), F32), ((HPAD * rows, L), F32)],
        (z2, prod, m5ts, mots, abts), deps=deps, raw=(0, 1, 2, 3, 4), far=(0,), us=4)


def channel_product(n, rows, outgoing, ab):
    def kernel(ab, out):
        part = C * rows // n
        for ch in range(C // n):
            a = ab[:, ch * rows : (ch + 1) * rows, :].reshape(L, L)
            b = ab[:, part + ch * rows : part + (ch + 1) * rows, :].reshape(L, L)
            prod = dot_nt(a, b) if outgoing else dot_tn(a, b)
            out[:, ch * rows : (ch + 1) * rows, :] = b16(prod).reshape(n, rows, L)

    return call(kernel, [((n, C * rows // n, L), BF)], [], (ab,), raw=(0,), us=1)[0]


def channel_product_back(n, rows, outgoing, ab, dprod, deps=()):
    def kernel(ab, dprod, out):
        part = C * rows // n
        for ch in range(C // n):
            low, high = ch * rows, (ch + 1) * rows
            a = ab[:, low:high, :].reshape(L, L)
            b = ab[:, part + low : part + high, :].reshape(L, L)
            g = dprod[:, low:high, :].reshape(L, L)
            if outgoing:
                da, db = dot(g, b), dot_tn(g, a)
            else:
                da, db = dot_nt(b, g), dot(a, g)
            out[:, low:high, :] = b16(da).reshape(n, rows, L)
            out[:, part + low : part + high, :] = b16(db).reshape(n, rows, L)

    return call(kernel, [((n, 2 * C * rows // n, L), BF)], [], (ab, dprod), deps=deps, raw=(0,), us=2)[0]


def head_masks():
    lane = lax.broadcasted_iota(jnp.int32, (1, C), 1)
    return [b16(jnp.where((lane >= h * HD) & (lane < (h + 1) * HD), 1.0, 0.0)) for h in range(TH)]


def by_head(x):
    pm = b16(x.T)
    return jnp.concatenate([pm * m for m in head_masks()], 0)


def attend(x16, a4t, bias):
    p4 = dot(a4t[...], x16)
    q, k, v = p4[0:C], p4[C : 2 * C], p4[2 * C : 3 * C]
    gate = sig(p4[3 * C : 4 * C])
    logits = dot(by_head(k), b16(q)) + bias[...]
    raised, outs = [], []
    v16 = b16(v)
    for h in range(TH):
        s = logits[h * L : (h + 1) * L]
        e = jnp.exp(s - jnp.max(s, 0, keepdims=True))
        inv = 1.0 / jnp.sum(e, 0, keepdims=True)
        raised.append((e, inv))
        outs.append(dot(v16[h * HD : (h + 1) * HD], b16(e)) * inv)
    mixed = jnp.concatenate(outs, 0)
    return (q, k, v, gate, raised, mixed)


def attend_back(state, dy16, ao, dbias):
    q, k, v, gate, raised, mixed = state
    du = dot(ao[...], dy16)
    do = du * gate
    dgate = du * mixed * gate * (1.0 - gate)
    do16, q16, k16 = b16(do), b16(q), b16(k)
    dp = dot(by_head(v), do16)
    row = do * mixed
    dq, dk, dv = [], [], []
    for h in range(TH):
        s = slice(h * HD, (h + 1) * HD)
        w = slice(h * L, (h + 1) * L)
        e, inv = raised[h]
        p = e * inv
        ds = p * (dp[w] - jnp.sum(row[s], 0, keepdims=True))
        dbias[w, :] += ds
        ds16, p16 = b16(ds), b16(p)
        dv.append(dot_nt(do16[s], p16))
        dq.append(dot(k16[s], ds16))
        dk.append(dot_nt(q16[s], ds16))
    return jnp.concatenate([b16(x) for x in dq + dk + dv] + [b16(dgate)], 0)


def start_attention(n, rows, z3, tb_all, key_row, a4ts, aots, abts, deps=()):
    def kernel(z3, tb_all, key_row, a4ts, aots, abts, z4, send, bias, st, se):
        a4t, aot, abt = a4ts.at[0], aots.at[0], abts.at[1]
        for h in range(TH):
            b = f32(tb_all[:, h * rows : (h + 1) * rows, :].reshape(L, L)) + key_row[...]
            bias[h * L : (h + 1) * L, :] = b.T

        def body(r):
            z = z3[:, cols(r)]
            xh, _ = norm_cols(z)
            q, k, v, gate, raised, mixed = attend(b16(xh), a4t, bias)
            z = z + dot(aot[...], b16(mixed * gate))
            z4[:, cols(r)] = z
            st[pl.ds(r, L, stride=rows), :] = z.T
            xe, _ = norm_cols(z)
            se[pl.ds(r, HPAD, stride=rows), :] = dot(abt[...], b16(xe))

        each_row(rows, body)
        part = L * rows // n
        for d in range(n):
            send[d, 0:part] = b16(st[d * part : (d + 1) * part])
            send[d, part : part + TH * rows] = b16(se[0 : TH * rows])

    part = L * rows // n
    return call(
        kernel,
        [((C, rows * L), F32), ((n, part + TH * rows, L), BF)],
        [((TH * L, L), F32), ((L * rows, C), F32), ((HPAD * rows, L), F32)],
        (z3, tb_all, key_row, a4ts, aots, abts), deps=deps, raw=(0, 1, 2, 3, 4, 5), far=(0,), us=12)


def end_both(n, rows, recv, cot, key_row, a4ts, a4s, aots, aos, upt, up, dnt, dn, deps=()):
    part = L * rows // n

    def kernel(
        recv, cot, key_row, a4ts, a4s, aots, aos, upt, up, dnt, dn,
        pout, send, m_up, m_dn, m_a4, m_ao,
        bias, dbias, sout, sdz, o_h, o_dh, o_x5, o_cot, o_x4, o_d4, o_u, o_dy,
    ):
        a4t, a4, aot, ao = a4ts.at[1], a4s.at[1], aots.at[1], aos.at[1]
        kb = jnp.broadcast_to(key_row[...], (L, L)).T
        for h in range(TH):
            b = recv[:, part + h * rows : part + (h + 1) * rows, :].reshape(L, L)
            bias[h * L : (h + 1) * L, :] = f32(b) + kb
        dbias[...] = jnp.zeros_like(dbias)

        def body(r):
            w = cols(r)
            z4 = f32(recv[:, pl.ds(pl.multiple_of(r * rows, rows), rows), :].reshape(L, C)).T
            x4, scale4 = norm_cols(z4)
            x16 = b16(x4)
            state = attend(x16, a4t, bias)
            gated = b16(state[5] * state[3])
            z5 = z4 + dot(aot[...], gated)
            x5, scale5 = norm_cols(z5)
            x516 = b16(x5)
            hid, slope = gelu_parts(dot(upt[...], x516))
            h16 = b16(hid)
            z6 = z5 + dot(dnt[...], h16)
            sout[pl.ds(r, L, stride=rows), :] = z6.T
            dz6 = f32(cot[r]).T
            c16 = b16(dz6)
            dh16 = b16(dot(dn[...], c16) * slope)
            dz5 = dz6 + norm_cols_back(dot(up[...], dh16), x5, scale5)
            dy16 = b16(dz5)
            d4 = attend_back(state, dy16, ao, dbias)
            dz4 = dz5 + norm_cols_back(dot(a4[...], d4), x4, scale4)
            sdz[pl.ds(r, L, stride=rows), :] = dz4.T
            o_h[:, w] = h16
            o_dh[:, w] = dh16
            o_x5[:, w] = x516
            o_cot[:, w] = c16
            o_x4[:, w] = x16
            o_d4[:, w] = d4
            o_u[:, w] = gated
            o_dy[:, w] = dy16

        each_row(rows, body)
        for d in range(n):
            pout[d] = b16(sout[d * part : (d + 1) * part])
            send[d, 0:part] = b16(sdz[d * part : (d + 1) * part])
            for h in range(TH):
                send[d, part + h * rows : part + (h + 1) * rows] = b16(
                    dbias[h * L + d * rows : h * L + (d + 1) * rows]
                )
        for k in range(4):
            s = slice(k * C, (k + 1) * C)
            m_up[s] = dot_nt(o_x5[...], o_dh[s])
            m_a4[s] = dot_nt(o_x4[...], o_d4[s])
        m_dn[...] = dot_nt(o_h[...], o_cot[...])
        m_ao[...] = dot_nt(o_u[...], o_dy[...])

    wide = rows * L
    return call(
        kernel,
        [
            ((n, part, C), BF), ((n, part + TH * rows, L), BF),
            ((512, C), F32), ((512, C), F32), ((512, C), F32), ((C, C), F32),
        ],
        [
            ((TH * L, L), F32), ((TH * L, L), F32), ((L * rows, C), F32), ((L * rows, C), F32),
            ((512, wide), BF), ((512, wide), BF), ((C, wide), BF), ((C, wide), BF),
            ((C, wide), BF), ((512, wide), BF), ((C, wide), BF), ((C, wide), BF),
        ],
        (recv, cot, key_row, a4ts, a4s, aots, aos, upt, up, dnt, dn),
        deps=deps, raw=(1, 2, 3, 4, 5, 6, 7, 8, 9, 10), far=(2, 3, 4, 5), us=36)


def start_back(n, rows, z3, z4, recv, tb_all, key_row, a4ts, a4s, aos, abts, deps=()):
    part = L * rows // n

    def kernel(
        z3, z4, recv, tb_all, key_row, a4ts, a4s, aos, abts,
        dz4_out, dxs, dtb, m_a4, m_ao, m_ab,
        bias, dbias, seb, o_x3, o_d4, o_u, o_dy, o_x4, o_eb,
    ):
        a4t, a4, ao, abt = a4ts.at[0], a4s.at[0], aos.at[0], abts.at[1]
        for h in range(TH):
            b = f32(tb_all[:, h * rows : (h + 1) * rows, :].reshape(L, L)) + key_row[...]
            bias[h * L : (h + 1) * L, :] = b.T
        dbias[...] = jnp.zeros_like(dbias)
        seb[...] = jnp.zeros_like(seb)
        total = f32(recv[0, part : part + TH * rows])
        for d in range(1, n):
            total = total + f32(recv[d, part : part + TH * rows])
        seb[0 : TH * rows, :] = total

        def body(r):
            w = cols(r)
            x4, scale4 = norm_cols(z4[:, w])
            eb16 = b16(seb[pl.ds(r, HPAD, stride=rows), :])
            dz4 = f32(recv[:, pl.ds(pl.multiple_of(r * rows, rows), rows), :].reshape(L, C)).T
            dz4 = dz4 + norm_cols_back(dot_tn(abt[...], eb16), x4, scale4)
            dz4_out[:, w] = dz4
            x3, _ = norm_cols(z3[:, w])
            x16 = b16(x3)
            state = attend(x16, a4t, bias)
            dy16 = b16(dz4)
            d4 = attend_back(state, dy16, ao, dbias)
            dxs[:, w] = dot(a4[...], d4)
            o_x3[:, w] = x16
            o_d4[:, w] = d4
            o_u[:, w] = b16(state[5] * state[3])
            o_dy[:, w] = dy16
            o_x4[:, w] = b16(x4)
            o_eb[:, w] = eb16

        each_row(rows, body)
        for h in range(TH):
            turned = b16(dbias[h * L : (h + 1) * L, :].T)
            for d in range(n):
                dtb[d, h * rows : (h + 1) * rows] = turned[d * rows : (d + 1) * rows]
        for k in range(4):
            s = slice(k * C, (k + 1) * C)
            m_a4[s] = dot_nt(o_x3[...], o_d4[s])
        m_ao[...] = dot_nt(o_u[...], o_dy[...])
        m_ab[...] = dot_nt(o_eb[...], o_x4[...])

    wide = rows * L
    return call(
        kernel,
        [
            ((C, wide), F32), ((C, wide), F32), ((n, TH * rows, L), BF),
            ((512, C), F32), ((C, C), F32), ((HPAD, C), F32),
        ],
        [
            ((TH * L, L), F32), ((TH * L, L), F32), ((HPAD * rows, L), F32),
            ((C, wide), BF), ((512, wide), BF), ((C, wide), BF), ((C, wide), BF),
            ((C, wide), BF), ((HPAD, wide), BF),
        ],
        (z3, z4, recv, tb_all, key_row, a4ts, a4s, aos, abts),
        deps=deps, raw=(0, 1, 3, 4, 5, 6, 7, 8), far=(0, 1, 3, 4, 5), us=20)


def product_back(z, dz, r, rows, sp, gatet, mot, mof, sdp, dgp_out, o_ph, o_do):
    w = cols(r)
    xh, _ = norm_cols(z)
    gate = sig(dot(gatet[...], b16(xh)))
    ph, scale = norm_cols(sp[pl.ds(r, C, stride=rows), :])
    ph16 = b16(ph)
    out = dot(mot[...], ph16)
    dgp_out[:, w] = b16(dz * out * gate * (1.0 - gate))
    do16 = b16(dz * gate)
    sdp[pl.ds(r, C, stride=rows), :] = norm_cols_back(dot(mof[...], do16), ph, scale)
    o_ph[:, w] = ph16
    o_do[:, w] = do16


def third_back(n, rows, z3, dz4, dxs, recv, abts, z2, prod, m5ts, mots, mofs, deps=()):
    def kernel(
        z3, dz4, dxs, recv, abts, z2, prod, m5ts, mots, mofs,
        dz3, dgp, dp, m_ab, m_mo,
        stb, sp, sdp, o_x3, o_tb, o_ph, o_do,
    ):
        abt, gatet, mot, mof = abts.at[0], m5ts.at[1, 512:640], mots.at[1], mofs.at[1]
        sp[...] = f32(prod[...])
        stb[...] = jnp.zeros_like(stb)
        total = f32(recv[0])
        for d in range(1, n):
            total = total + f32(recv[d])
        stb[0 : TH * rows, :] = total

        def body(r):
            w = cols(r)
            x3, scale3 = norm_cols(z3[:, w])
            tb16 = b16(stb[pl.ds(r, HPAD, stride=rows), :])
            dx = dxs[:, w] + dot_tn(abt[...], tb16)
            dz = dz4[:, w] + norm_cols_back(dx, x3, scale3)
            dz3[:, w] = dz
            o_x3[:, w] = b16(x3)
            o_tb[:, w] = tb16
            product_back(z2[:, w], dz, r, rows, sp, gatet, mot, mof, sdp, dgp, o_ph, o_do)

        each_row(rows, body)
        dp[...] = b16(sdp[...])
        m_ab[...] = dot_nt(o_tb[...], o_x3[...])
        m_mo[...] = dot_nt(o_ph[...], o_do[...])

    wide = rows * L
    return call(
        kernel,
        [
            ((C, wide), F32), ((C, wide), BF), ((C * rows, L), BF),
            ((HPAD, C), F32), ((C, C), F32),
        ],
        [
            ((HPAD * rows, L), F32), ((C * rows, L), F32), ((C * rows, L), F32),
            ((C, wide), BF), ((HPAD, wide), BF), ((C, wide), BF), ((C, wide), BF),
        ],
        (z3, dz4, dxs, recv, abts, z2, prod, m5ts, mots, mofs), deps=deps, raw=(0, 1, 2, 4, 5, 6, 7, 8, 9), far=(0, 1, 3, 4), us=7)


def projections_back(n, rows, z, dz, dgp, r, pmask, m5t, m5, sa, sb, o_x, o_d5):
    w = cols(r)
    xh, scale = norm_cols(z)
    x16 = b16(xh)
    p = dot(m5t[0:512], x16)
    mk = pmask[pl.ds(r, 1), :]
    da = sa[pl.ds(r, C, stride=rows), :] * mk
    db = sb[pl.ds(r, C, stride=rows), :] * mk
    ga, gb = sig(p[0:C]), sig(p[2 * C : 3 * C])
    va, vb = p[C : 2 * C], p[3 * C : 4 * C]
    d5 = jnp.concatenate(
        [
            b16(da * va * ga * (1.0 - ga)),
            b16(da * ga),
            b16(db * vb * gb * (1.0 - gb)),
            b16(db * gb),
            dgp[:, w],
        ],
        0,
    )
    o_x[:, w] = x16
    o_d5[:, w] = d5
    return dz + norm_cols_back(dot(m5[...], d5), xh, scale)


def take_pair(n, dab, sa, sb):
    part = sa.shape[0] // n
    for d in range(n):
        sa[d * part : (d + 1) * part, :] = f32(dab[d, 0:part])
        sb[d * part : (d + 1) * part, :] = f32(dab[d, part : 2 * part])


def second_back(n, rows, z2, dz3, dgp, dab, pmask, m5ts, m5s, z1, prod, mots, mofs, deps=()):
    def kernel(
        z2, dz3, dgp, dab, pmask, m5ts, m5s, z1, prod, mots, mofs,
        dz2, dgp_out, dp, m_m5, m_mo,
        sa, sb, sp, sdp, o_x, o_d5, o_ph, o_do,
    ):
        m5t, m5, gatet = m5ts.at[1], m5s.at[1], m5ts.at[0, 512:640]
        mot, mof = mots.at[0], mofs.at[0]
        sp[...] = f32(prod[...])
        take_pair(n, dab, sa, sb)

        def body(r):
            w = cols(r)
            dz = projections_back(
                n, rows, z2[:, w], dz3[:, w], dgp, r, pmask, m5t, m5, sa, sb, o_x, o_d5
            )
            dz2[:, w] = dz
            product_back(z1[:, w], dz, r, rows, sp, gatet, mot, mof, sdp, dgp_out, o_ph, o_do)

        each_row(rows, body)
        dp[...] = b16(sdp[...])
        for k in range(5):
            s = slice(k * C, (k + 1) * C)
            m_m5[s] = dot_nt(o_x[...], o_d5[s])
        m_mo[...] = dot_nt(o_ph[...], o_do[...])

    wide = rows * L
    return call(
        kernel,
        [
            ((C, wide), F32), ((C, wide), BF), ((C * rows, L), BF),
            ((640, C), F32), ((C, C), F32),
        ],
        [
            ((C * rows, L), F32), ((C * rows, L), F32), ((C * rows, L), F32), ((C * rows, L), F32),
            ((C, wide), BF), ((640, wide), BF), ((C, wide), BF), ((C, wide), BF),
        ],
        (z2, dz3, dgp, dab, pmask, m5ts, m5s, z1, prod, mots, mofs), deps=deps, raw=(0, 1, 2, 4, 5, 6, 7, 8, 9, 10), far=(0, 1, 3, 4), us=11)


def first_back(n, rows, copies, where, z1, dz2, dgp, dab, pmask, m5ts, m5s, inner, lrt, left_own, outer_w, deps=()):
    opm = outer_w.shape[0]

    def kernel(
        where, z1, dz2, dgp, dab, pmask, m5ts, m5s, inner, lrt, left_own, outer_w,
        dz1, ends, m_oo, m_m5,
        sa, sb, o_x, o_d5, sdi, sdr,
    ):
        m5t, m5 = m5ts.at[0], m5s.at[0]
        take_pair(n, dab, sa, sb)
        sdr[...] = jnp.zeros_like(sdr)
        right_t = b16(lrt[opm : 2 * opm])

        def body(r):
            w = cols(r)
            dz = projections_back(
                n, rows, z1[:, w], dz2[:, w], dgp, r, pmask, m5t, m5, sa, sb, o_x, o_d5
            ).T
            dz16 = b16(dz)
            dz1[r] = dz16
            sdi[pl.ds(r, opm, stride=rows), :] = dot(right_t, dz16)
            sdr[...] += dot_nt(b16(inner[pl.ds(r, opm, stride=rows), :]), dz16)

        each_row(rows, body)
        left = left_own[:, 0:opm]
        dleft = jnp.zeros((opm, rows), F32)
        for b in range(opm):
            d16 = b16(sdi[b * rows : (b + 1) * rows])
            m_oo[b * opm : (b + 1) * opm] = dot_tn(left, d16)
            dleft = dleft + dot_nt(outer_w[b], d16)
        lane = lax.broadcasted_iota(jnp.int32, (rows, L), 1)
        spot = lax.broadcasted_iota(jnp.int32, (rows, L), 0) + where[1] * rows
        dleft = dot(b16(dleft), b16(jnp.where(lane == spot, 1.0, 0.0)))
        both = jnp.concatenate([dleft, sdr[...]], 0) * lrt[2 * opm : 2 * opm + 1]
        for d in range(copies):
            ends[d] = b16(both)
        for k in range(5):
            s = slice(k * C, (k + 1) * C)
            m_m5[s] = dot_nt(o_x[...], o_d5[s])

    wide = rows * L
    return call(
        kernel,
        [
            ((rows, L, C), BF), ((copies, 2 * opm, L), BF), ((opm * opm, C), F32), ((640, C), F32),
        ],
        [
            ((C * rows, L), F32), ((C * rows, L), F32), ((C, wide), BF), ((640, wide), BF),
            ((opm * rows, C), F32), ((opm, L), F32),
        ],
        (where, z1, dz2, dgp, dab, pmask, m5ts, m5s, inner, lrt, left_own, outer_w), deps=deps, raw=(1, 2, 3, 5, 6, 7, 8, 9, 10, 11), far=(2, 3), us=11)


def last_back(rows, pair, drb, dz1, sbt, deps=()):
    def kernel(pair, drb, dz1, sbt, grad, m_sb, o_x, o_d):
        def body(r):
            w = cols(r)
            xh, scale = norm_cols(f32(pair[r]).T)
            d = drb[pl.ds(r, 8, stride=rows), :]
            d16 = b16(jnp.concatenate([d, jnp.zeros_like(d)], 0))
            back = norm_cols_back(dot_tn(sbt[...], d16), xh, scale)
            grad[r] = f32(dz1[r]) + back.T
            o_x[:, w] = b16(xh)
            o_d[:, w] = d16

        each_row(rows, body)
        m_sb[...] = dot_nt(o_d[...], o_x[...])

    wide = rows * L
    return call(
        kernel,
        [((rows, L, C), F32), ((HPAD, C), F32)],
        [((C, wide), BF), ((HPAD, wide), BF)],
        (pair, drb, dz1, sbt), deps=deps, raw=(0, 1, 2, 3), us=3)


def collect(where, parts, half, deps):
    def kernel(where, *refs):
        sources, (kept, given, rows) = refs[: len(parts)], refs[len(parts) :]
        core = where[3] % 2
        at = 0
        for ref in sources:
            rows[at : at + ref.shape[0]] = ref[...]
            at += ref.shape[0]
        if at < 2 * half:
            rows[at : 2 * half] = jnp.zeros((2 * half - at, C), F32)
        kept[...] = rows[pl.ds(pl.multiple_of(core * half, half), half), :]
        given[...] = b16(rows[pl.ds(pl.multiple_of((1 - core) * half, half), half), :])

    return call(
        kernel,
        [((half, C), F32), ((half, C), BF)],
        [((2 * half, C), F32)],
        (where, *parts),
        deps=deps,
        us=3,
    )


def sum_copies(x, count, deps):
    def kernel(x, out):
        total = b16(jnp.sum(f32(x[...]), 0))
        for d in range(count):
            out[d] = total

    return call(kernel, [((count,) + x.shape[1:], BF)], [], (x,), deps=deps, us=2)[0]


def finish(where, near, far, m_sb, gp, gm, mp, mg, mo, ap, ab, pu, sb, places, half, opm, n_all, deps):
    def kernel(
        where, near, far, m_sb, gp, gm, mp, mg, mo, ap, ab, pu, sb,
        g_pg, g_mg, g_sb, g_oo, g_mp, g_mgt, g_mo, g_ap, g_ab, g_ao, g_pu, g_pd,
        rows,
    ):
        core = where[3] % 2
        rows[pl.ds(pl.multiple_of(core * half, half), half), :] = f32(near[...])
        rows[pl.ds(pl.multiple_of((1 - core) * half, half), half), :] = f32(far[...])

        def take(name, count, skip=0):
            at = places[name] + skip
            return rows[at : at + count]

        gpv, gmv = f32(gp[...]), f32(gm[...])

        def column(row):
            return jnp.broadcast_to(row, (C, C)).T

        def over_lanes(x):
            return jnp.sum(x.T, 0, keepdims=True)

        def turned(w):
            shape = (HPAD, w.shape[1])
            row = lax.broadcasted_iota(jnp.int32, shape, 0)
            lane = lax.broadcasted_iota(jnp.int32, shape, 1)
            return dot_nt(b16(jnp.where(row == lane, 1.0, 0.0)), w)

        total = m_sb[0]
        for d in range(1, n_all):
            total = total + m_sb[d]
        g_pg[0:1] = jnp.sum(turned(sb[...]) * total, 0, keepdims=True)
        wide = jnp.concatenate([total * gpv[0:1], jnp.zeros((C - HPAD, C), F32)], 0)
        g_sb[...] = wide.T[:, 0:8]
        for t in range(2):
            g = column(gpv[1 + t : 2 + t])
            both = jnp.zeros((C, C), F32)
            for k in range(5):
                m = take("m5%d" % t, C, k * C)
                both = both + m * f32(mp[t, k] if k < 4 else mg[t])
                if k < 4:
                    g_mp[t, k] = m * g
                else:
                    g_mgt[t] = m * g
            g_pg[1 + t : 2 + t] = over_lanes(both)
            m = take("mo%d" % t, C)
            g_mo[t] = m * column(gmv[t : t + 1])
            g_mg[t : t + 1] = over_lanes(m * f32(mo[t]))
            g = column(gpv[3 + t : 4 + t])
            both = jnp.zeros((C, C), F32)
            for k in range(4):
                m = take("a4%d" % t, C, k * C)
                if k == 0:
                    m = m * HD**-0.5
                both = both + m * f32(ap[t, k])
                g_ap[t, k] = m * g
            m = take("ab%d" % t, HPAD)
            g_pg[3 + t : 4 + t] = over_lanes(both) + jnp.sum(turned(ab[t]) * m, 0, keepdims=True)
            wide = jnp.concatenate(
                [m * gpv[3 + t : 4 + t], jnp.zeros((C - HPAD, C), F32)], 0
            )
            g_ab[t] = wide.T[:, 0:TH]
            g_ao[t] = take("ao%d" % t, C)
        g = column(gpv[5:6])
        both = jnp.zeros((C, C), F32)
        for k in range(4):
            s = slice(k * C, (k + 1) * C)
            m = take("up", C, k * C)
            both = both + m * f32(pu[:, s])
            g_pu[:, s] = m * g
        g_pg[5:6] = over_lanes(both)
        g_pd[...] = take("dn", 512)
        for b in range(opm):
            g_oo[:, b, :] = take("oo", opm, b * opm)

    outs = [
        (6, C), (2, C), (C, 8), (opm, opm, C), (2, 4, C, C), (2, C, C), (2, C, C), (2, 4, C, C),
        (2, C, TH), (2, C, C), (C, 512), (512, C),
    ]
    return call(
        kernel,
        [(s, F32) for s in outs],
        [((2 * half, C), F32)],
        (where, near, far, m_sb, gp, gm, mp, mg, mo, ap, ab, pu, sb),

        raw=(4, 5, 6, 7, 8, 9, 10, 11, 12), deps=deps, us=4,
    )


PRECISE = lax.Precision.HIGHEST


def for_sending(shard):

    def short(part):
        return part.astype(jnp.bfloat16) if part.dtype == jnp.float32 else part

    return jax.tree.map(short, shard)


def widen(operand):
    return operand.astype(jnp.float32)


def narrow(operand):
    return operand.astype(jnp.bfloat16)


def rounded(operand):
    return lax.optimization_barrier(operand.astype(jnp.bfloat16)).astype(jnp.float32)


def contract(pattern, first_term, second_term):
    return jnp.einsum(pattern, first_term, second_term, precision=PRECISE)


def low_product(pattern, first_term, second_term):
    return jnp.einsum(pattern, first_term, second_term, preferred_element_type=jnp.float32)


def norm_rows(operand, gain_vec):
    centre = operand - jnp.mean(operand, -1, keepdims=True)
    spread = jnp.mean(centre * centre, -1, keepdims=True)
    return centre * lax.rsqrt(spread + EPSILON) * gain_vec


def soft_weights(logits):
    highest = jnp.max(logits, -1, keepdims=True)
    raised = jnp.exp(logits - highest)
    return raised / jnp.sum(raised, -1, keepdims=True)


def single_attend(queries, key_rows, values, gate_value, pair_bias, key_bias, weight_out):
    head_count = pair_bias.shape[0]
    feature_width = queries.shape[-1]
    head_size = feature_width // head_count
    query_heads = queries.reshape(queries.shape[0], head_count, head_size)
    key_heads = key_rows.reshape(key_rows.shape[0], head_count, head_size)
    value_heads = values.reshape(values.shape[0], head_count, head_size)
    logits = (
        contract("ihd,jhd->hij", query_heads, key_heads) * head_size ** (-0.5)
        + pair_bias
        + key_bias
    )
    mixed = contract("hij,jhd->ihd", soft_weights(logits), value_heads).reshape(
        queries.shape[0], feature_width
    )
    return contract("is,st->it", mixed * jax.nn.sigmoid(gate_value), weight_out)


def tri_attend(normed, pair_bias, weight_four, weight_out, key_bias):
    head_count = pair_bias.shape[0]
    feature_width = normed.shape[-1]
    head_size = feature_width // head_count

    def one_row(row_in):
        projected = contract("lc,ncd->nld", row_in, weight_four)
        shaped = projected[:3].reshape(3, row_in.shape[0], head_count, head_size)
        logits = (
            contract("jhd,khd->hjk", shaped[0], shaped[1]) * head_size ** (-0.5)
            + pair_bias
            + key_bias
        )
        mixed = contract("hjk,khd->jhd", soft_weights(logits), shaped[2]).reshape(
            row_in.shape[0], feature_width
        )
        return contract("lc,cd->ld", mixed * jax.nn.sigmoid(projected[3]), weight_out)

    return lax.map(jax.checkpoint(one_row), normed)


def mult_front(pair_in, gain_vec, weight_four, weight_gate, pair_mask):
    normed = norm_rows(pair_in, gain_vec)
    projected = contract("rlc,ncm->nmrl", normed, weight_four)
    left_side = jax.nn.sigmoid(projected[0]) * projected[1] * pair_mask
    right_side = jax.nn.sigmoid(projected[2]) * projected[3] * pair_mask
    gate_value = jax.nn.sigmoid(contract("rlc,cd->rld", normed, weight_gate))
    return (left_side, right_side, gate_value)


def mult_back(pair_in, product, gate_value, gain_vec, weight_out):
    centre = product - jnp.mean(product, 0, keepdims=True)
    spread = jnp.mean(centre * centre, 0, keepdims=True)
    scaled = centre * lax.rsqrt(spread + EPSILON) * gain_vec[:, None, None]
    return pair_in + contract("mrl,mc->rlc", scaled, weight_out) * gate_value


def outgoing_forward(left_chan, right_chan):
    return low_product("mik,mjk->mij", left_chan, right_chan)


def outgoing_backward(left_chan, right_chan, grad_out):
    return (
        low_product("mij,mjk->mik", grad_out, right_chan),
        low_product("mij,mik->mjk", grad_out, left_chan),
    )


def incoming_forward(left_chan, right_chan):
    return low_product("mki,mkj->mij", left_chan, right_chan)


def incoming_backward(left_chan, right_chan, grad_out):
    return (
        low_product("mij,mkj->mki", grad_out, right_chan),
        low_product("mij,mki->mkj", grad_out, left_chan),
    )


def to_channels(operand):
    return jax.tree.map(
        lambda part, own: part.astype(own.dtype),
        lax.all_to_all(for_sending(operand), "rows", split_axis=0, concat_axis=1, tiled=True),
        operand,
    )


def to_rows(operand):
    return jax.tree.map(
        lambda part, own: part.astype(own.dtype),
        lax.all_to_all(for_sending(operand), "rows", split_axis=1, concat_axis=0, tiled=True),
        operand,
    )


def turn_cols(operand):
    return jnp.swapaxes(
        lax.all_to_all(operand, "rows", split_axis=1, concat_axis=0, tiled=True), 0, 1
    )


def turn_rows(operand):
    return lax.all_to_all(
        jnp.swapaxes(operand, 0, 1), "rows", split_axis=0, concat_axis=1, tiled=True
    )


def gather_bias(operand):
    return lax.all_gather(operand, "rows", axis=1, tiled=True)


def scatter_bias(operand):
    return lax.psum_scatter(operand, "rows", scatter_dimension=1, tiled=True)


def general_local(
    single_rep,
    pair_rep,
    residue_mask,
    single_gains,
    pair_gains,
    mult_gains,
    single_proj,
    single_bias,
    single_up,
    single_down,
    opm_proj,
    opm_out,
    mult_proj,
    mult_gate,
    mult_out,
    att_proj,
    att_bias,
    att_out,
    pair_up,
    pair_down,
    single_cot,
    pair_cot,
):
    gains_s = widen(single_gains)
    gains_p = widen(pair_gains)
    gains_m = widen(mult_gains)
    proj_s = widen(single_proj)
    bias_sw = widen(single_bias)
    up_s = widen(single_up)
    down_s = widen(single_down)
    proj_o = widen(opm_proj)
    outer_w = widen(opm_out)
    proj_m = widen(mult_proj)
    gate_m = widen(mult_gate)
    out_m = widen(mult_out)
    proj_a = widen(att_proj)
    bias_a = widen(att_bias)
    out_a = widen(att_out)
    up_p = widen(pair_up)
    down_p = widen(pair_down)
    mask_all = widen(residue_mask[0])
    shard_rows = pair_rep.shape[1]
    first_row = lax.axis_index("rows") * shard_rows
    mask_own = lax.dynamic_slice_in_dim(mask_all, first_row, shard_rows, 0)
    key_bias = (mask_all - 1.0) * MASKED
    pair_mask = mask_own[:, None] * mask_all[None, :]
    single_own = widen(single_rep[0])
    pair_own = widen(pair_rep[0])

    def front_single(
        single_in, pair_in, gain_s, gain_z, proj_query, proj_key, proj_value, proj_gate, bias_w
    ):
        normed = norm_rows(single_in, gain_s)
        pair_normed = norm_rows(pair_in, gain_z)
        return (
            contract("rs,st->rt", normed, proj_query),
            contract("rs,st->rt", normed, proj_key),
            contract("rs,st->rt", normed, proj_value),
            contract("rs,st->rt", normed, proj_gate),
            contract("rlc,ch->hrl", pair_normed, bias_w),
        )

    def back_single(
        queries,
        key_rows,
        values,
        gate_value,
        row_bias,
        single_in,
        proj_out,
        gain_t,
        weight_up,
        weight_down,
        gain_o,
        left_w,
        right_w,
    ):
        first_sum = single_in + single_attend(
            queries, key_rows, values, gate_value, row_bias, key_bias, proj_out
        )
        hidden = jax.nn.gelu(contract("rs,st->rt", norm_rows(first_sum, gain_t), weight_up))
        second_sum = first_sum + contract("rt,ts->rs", hidden, weight_down)
        outer_in = norm_rows(second_sum, gain_o)
        left_side = contract("rs,sa->ra", outer_in, left_w) * mask_own[:, None]
        right_side = contract("rs,sa->ra", outer_in, right_w) * mask_own[:, None]
        return (second_sum, left_side, right_side)

    def outer_front(left_side, right_all, pair_in, weight_outer, gain_in, weight_four, weight_gate):
        inner = contract("ia,abc->ibc", left_side, weight_outer)
        updated = pair_in + contract("ibc,jb->ijc", inner, right_all)
        left_m, right_m, gate_value = mult_front(
            updated, gain_in, weight_four, weight_gate, pair_mask
        )
        return (updated, left_m, right_m, gate_value)

    def middle_mult(
        pair_in, product, gate_value, gain_out, weight_out, gain_in, weight_four, weight_gate
    ):
        updated = mult_back(pair_in, product, gate_value, gain_out, weight_out)
        left_m, right_m, gate_next = mult_front(
            updated, gain_in, weight_four, weight_gate, pair_mask
        )
        return (updated, left_m, right_m, gate_next)

    def start_front_general(pair_in, product, gate_value, gain_out, weight_out, gain_start, bias_w):
        updated = mult_back(pair_in, product, gate_value, gain_out, weight_out)
        normed = norm_rows(updated, gain_start)
        return (updated, normed, contract("rlc,ch->hrl", normed, bias_w))

    def start_core(pair_in, normed, bias_all, weight_four, weight_out, gain_end):
        updated = pair_in + tri_attend(normed, bias_all, weight_four, weight_out, key_bias)
        return (updated, norm_rows(updated, gain_end))

    def end_bias(turned, bias_w):
        return contract("rlc,ch->hrl", turned, bias_w)

    def end_core(turned, bias_all, weight_four, weight_out):
        return tri_attend(turned, bias_all, weight_four, weight_out, key_bias)

    def final_pair(pair_in, update, gain_vec, weight_up, weight_down):
        summed = pair_in + update
        hidden = jax.nn.gelu(contract("rlc,cd->rld", norm_rows(summed, gain_vec), weight_up))
        return summed + contract("rld,dc->rlc", hidden, weight_down)

    outs_one, back_one = jax.vjp(
        front_single,
        single_own,
        pair_own,
        gains_s[0],
        gains_p[0],
        proj_s[0],
        proj_s[1],
        proj_s[2],
        proj_s[3],
        bias_sw,
    )
    queries, keys_own, values_own, gate_single, row_bias = outs_one
    keys_all, values_all = (
        lax.all_gather(narrow(keys_own), "rows", axis=0, tiled=True),
        lax.all_gather(narrow(values_own), "rows", axis=0, tiled=True),
    )
    outs_two, back_two = jax.vjp(
        back_single,
        queries,
        widen(keys_all),
        widen(values_all),
        gate_single,
        row_bias,
        single_own,
        proj_s[4],
        gains_s[1],
        up_s,
        down_s,
        gains_s[2],
        proj_o[0],
        proj_o[1],
    )
    single_next, left_outer, right_outer = outs_two
    right_all = widen(lax.all_gather(narrow(right_outer), "rows", axis=0, tiled=True))
    outs_three, back_three = jax.vjp(
        outer_front,
        rounded(left_outer),
        right_all,
        pair_own,
        outer_w,
        gains_p[1],
        proj_m[0],
        gate_m[0],
    )
    pair_one, left_first, right_first, gate_first = outs_three
    chan_left, chan_right = to_channels((narrow(left_first), narrow(right_first)))
    product_one = outgoing_forward(chan_left, chan_right)
    rows_one = widen(to_rows(narrow(product_one)))
    outs_five, back_five = jax.vjp(
        middle_mult,
        pair_one,
        rows_one,
        gate_first,
        gains_m[0],
        out_m[0],
        gains_p[2],
        proj_m[1],
        gate_m[1],
    )
    pair_two, left_second, right_second, gate_second = outs_five
    chan_left_two, chan_right_two = to_channels((narrow(left_second), narrow(right_second)))
    product_two = incoming_forward(chan_left_two, chan_right_two)
    rows_two = widen(to_rows(narrow(product_two)))
    outs_seven, back_seven = jax.vjp(
        start_front_general, pair_two, rows_two, gate_second, gains_m[1], out_m[1], gains_p[3], bias_a[0]
    )
    pair_three, normed_start, bias_start = outs_seven
    bias_start_all = widen(gather_bias(narrow(bias_start)))
    outs_eight, back_eight = jax.vjp(
        start_core, pair_three, normed_start, bias_start_all, proj_a[0], out_a[0], gains_p[4]
    )
    pair_four, normed_end = outs_eight
    turned = widen(turn_cols(narrow(normed_end)))
    bias_end, back_nine = jax.vjp(end_bias, turned, bias_a[1])
    bias_end_all = widen(gather_bias(narrow(bias_end)))
    update_turned, back_ten = jax.vjp(end_core, turned, bias_end_all, proj_a[1], out_a[1])
    update = widen(turn_rows(narrow(update_turned)))
    pair_six, back_eleven = jax.vjp(final_pair, pair_four, update, gains_p[5], up_p, down_p)
    grad_four, grad_update, g_pg5, g_pu, g_pd = back_eleven(widen(pair_cot[0]))
    g_pg5, g_pu, g_pd = (g_pg5, g_pu, g_pd)
    grad_turned_update = widen(turn_cols(narrow(grad_update)))
    grad_turned_a, grad_bias_end_all, g_ap1, g_ao1 = back_ten(grad_turned_update)
    g_ap1, g_ao1 = (g_ap1, g_ao1)
    grad_bias_end = rounded(scatter_bias(grad_bias_end_all))
    grad_turned_b, g_ab1 = back_nine(grad_bias_end)
    grad_normed_end = widen(turn_rows(narrow(grad_turned_a + grad_turned_b)))
    grad_three, grad_normed_start, grad_bias_start_all, g_ap0, g_ao0, g_pg4 = back_eight(
        (grad_four, grad_normed_end)
    )
    g_ap0, g_ao0, g_pg4 = (g_ap0, g_ao0, g_pg4)
    grad_bias_start = rounded(scatter_bias(grad_bias_start_all))
    grad_two, grad_rows_two, grad_gate_second, g_mg1, g_mo1, g_pg3, g_ab0 = back_seven(
        (grad_three, grad_normed_start, grad_bias_start)
    )
    g_mg1, g_mo1, g_pg3, g_ab0 = (g_mg1, g_mo1, g_pg3, g_ab0)
    grad_chan_left_two, grad_chan_right_two = incoming_backward(
        chan_left_two, chan_right_two, to_channels(narrow(grad_rows_two))
    )
    grad_left_second, grad_right_second = to_rows(
        (narrow(grad_chan_left_two), narrow(grad_chan_right_two))
    )
    grad_one, grad_rows_one, grad_gate_first, g_mg0, g_mo0, g_pg2, g_mp1, g_mgt1 = back_five(
        (grad_two, widen(grad_left_second), widen(grad_right_second), grad_gate_second)
    )
    g_mg0, g_mo0, g_pg2, g_mp1, g_mgt1 = (g_mg0, g_mo0, g_pg2, g_mp1, g_mgt1)
    grad_chan_left, grad_chan_right = outgoing_backward(
        chan_left, chan_right, to_channels(narrow(grad_rows_one))
    )
    grad_left_first, grad_right_first = to_rows((narrow(grad_chan_left), narrow(grad_chan_right)))
    grad_left_outer, grad_right_all, grad_pair_a, g_oo, g_pg1, g_mp0, g_mgt0 = back_three(
        (grad_one, widen(grad_left_first), widen(grad_right_first), grad_gate_first)
    )
    g_oo, g_pg1, g_mp0, g_mgt0 = (g_oo, g_pg1, g_mp0, g_mgt0)
    grad_right_outer = rounded(
        lax.psum_scatter(grad_right_all, "rows", scatter_dimension=0, tiled=True)
    )
    two_grads = back_two((widen(single_cot[0]), rounded(grad_left_outer), grad_right_outer))
    grad_query, grad_keys_all, grad_values_all, grad_gate_single, grad_row_bias, grad_single_a = (
        two_grads[:6]
    )
    g_sp4, g_sg1, g_su, g_sd, g_sg2, g_op0, g_op1 = tuple(two_grads[6:])
    grad_keys, grad_values = (
        lax.psum_scatter(grad_keys_all, "rows", scatter_dimension=0, tiled=True),
        lax.psum_scatter(grad_values_all, "rows", scatter_dimension=0, tiled=True),
    )
    grad_single_b, grad_pair_b, g_sg0, g_pg0, g_sp0, g_sp1, g_sp2, g_sp3, g_sb = back_one(
        (grad_query, rounded(grad_keys), rounded(grad_values), grad_gate_single, grad_row_bias)
    )
    g_sg0, g_pg0, g_sp0, g_sp1, g_sp2, g_sp3, g_sb = (
        g_sg0,
        g_pg0,
        g_sp0,
        g_sp1,
        g_sp2,
        g_sp3,
        g_sb,
    )
    weight_totals = (
        jnp.stack([g_sg0, g_sg1, g_sg2]),
        jnp.stack([g_pg0, g_pg1, g_pg2, g_pg3, g_pg4, g_pg5]),
        jnp.stack([g_mg0, g_mg1]),
        jnp.stack([g_sp0, g_sp1, g_sp2, g_sp3, g_sp4]),
        g_sb,
        g_su,
        g_sd,
        jnp.stack([g_op0, g_op1]),
        g_oo,
        jnp.stack([g_mp0, g_mp1]),
        jnp.stack([g_mgt0, g_mgt1]),
        jnp.stack([g_mo0, g_mo1]),
        jnp.stack([g_ap0, g_ap1]),
        jnp.stack([g_ab0, g_ab1]),
        jnp.stack([g_ao0, g_ao1]),
        g_pu,
        g_pd,
    )
    weight_totals = lax.psum(
        (
            weight_totals[0],
            weight_totals[1],
            weight_totals[2],
            weight_totals[3],
            weight_totals[4],
            weight_totals[5],
            weight_totals[6],
            weight_totals[7],
            weight_totals[8],
            weight_totals[9],
            weight_totals[10],
            weight_totals[11],
            weight_totals[12],
            weight_totals[13],
            weight_totals[14],
            weight_totals[15],
            weight_totals[16],
        ),
        ("grp", "rows"),
    )
    return (
        narrow(single_next)[None],
        narrow(pair_six)[None],
        (grad_single_a + grad_single_b)[None],
        (grad_pair_a + grad_pair_b)[None],
    ) + tuple(weight_totals)


def pad_rows(x, count):
    return jnp.concatenate([x, jnp.zeros((count - x.shape[0],) + x.shape[1:], x.dtype)], 0)


def fast_local(square, row_count):
    n = row_count
    rows = L // n
    part = L * rows // n
    crops = 4
    total = crops * n

    def home(g, r):
        if square and (r // 2) // 2 != g % 2:
            g, r = g ^ 1, ((r // 2) ^ 2) * 2 + r % 2
        return g * n + r

    groups = [[home(g, r) for r in range(n)] for g in range(crops)]

    def swap(x):
        if not square:
            return x
        return lax.ppermute(x, AX, [(g * n + r, home(g, r)) for g in range(crops) for r in range(n)])

    def exchange(x):
        if square:
            return lax.all_to_all(x, AX, 0, 0, tiled=True, axis_index_groups=groups)
        return lax.all_to_all(x, "rows", 0, 0, tiled=True)

    def to_all(copies):
        return lax.all_to_all(copies, AX, 0, 0, tiled=True)

    chips = total // 2
    same_core = [[g * n + z * 2 + c for g in range(crops) for z in range(n // 2)] for c in range(2)]
    members = [sorted(set(d // 2 for d in group)) for group in groups]

    def other_core(x):
        return lax.ppermute(x, "rows", [(i, i ^ 1) for i in range(n)])

    def to_chips(copies):
        return lax.all_to_all(copies, AX, 0, 0, tiled=True, axis_index_groups=same_core)

    def local(
        single_rep, pair_rep, residue_mask, single_gains, pair_gains, mult_gains, single_proj,
        single_bias, single_up, single_down, opm_proj, opm_out, mult_proj, mult_gate, mult_out,
        att_proj, att_bias, att_out, pair_up, pair_down, single_cot, pair_cot,
    ):
        grp, row = lax.axis_index("grp"), lax.axis_index("rows")
        crop, block = grp, row
        if square:
            moved = (row // 4) != grp % 2
            crop = jnp.where(moved, grp ^ 1, grp)
            block = jnp.where(moved, row ^ 4, row)
        where = jnp.stack([crop, block, grp, row]).astype(jnp.int32)
        single, width = single_rep[0], single_rep.shape[2]
        gathered = lax.all_to_all(
            jnp.broadcast_to(single, (n,) + single.shape), "rows", 0, 0, tiled=True
        )
        pair = swap(pair_rep[0])
        cot = swap(pair_cot[0])
        m5t, m5, mot, mof, a4t, a4, aot, abt, upt, up, dnt, sbt = prep_weights(
            pair_gains, mult_gains, mult_proj, mult_gate, mult_out, att_proj, att_bias, att_out,
            pair_up, pair_down, single_bias,
        )
        opm = opm_proj.shape[2]
        outer = jnp.swapaxes(opm_proj, 0, 1).reshape(width, 2 * opm)
        outer = jnp.pad(outer, ((0, 0), (0, L - 2 * opm)))
        outer_w = jnp.swapaxes(opm_out, 0, 1)
        mask_row = f32(residue_mask)
        mine, mask_col = pack(rows, single, single_cot[0], pair_rep[0], mask_row, sbt, where)
        single_out, lr = single_own(
            n, rows, total, gathered, mine, mask_col, single_gains, single_proj, single_up,
            single_down, outer,
        )
        lr = to_all(lr)

        z1, ab1, pmask, key_row, inner, lrt, left_own = front(
            n, rows, where, lr, pair, outer_w, m5t, deps=(cot,)
        )
        ab1 = exchange(ab1)
        p1 = exchange(channel_product(n, rows, True, ab1)).reshape(C * rows, L)
        z2, ab2 = middle(n, rows, z1, p1, mot, pmask, m5t)
        ab2 = exchange(ab2)
        p2 = exchange(channel_product(n, rows, False, ab2)).reshape(C * rows, L)
        z3, tb = start_front(n, rows, z2, p2, m5t, mot, abt)
        tb_all = exchange(tb)
        cot = exchange(jnp.transpose(cot.reshape(rows, n, rows, C), (1, 2, 0, 3)))
        cot = jnp.swapaxes(cot, 0, 1).reshape(rows, L, C)
        z4, turn = start_attention(n, rows, z3, tb_all, key_row, a4t, aot, abt, deps=(cot,))
        turn = exchange(turn)
        copies = to_chips(copies_of(mine, chips, (turn,)))
        others = other_core(copies)

        pout, back, m_up, m_dn, m_a41, m_ao1 = end_both(
            n, rows, turn, cot, key_row, a4t, a4, aot, att_out, upt, up, dnt, pair_down
        )
        back = exchange(back)
        pout = exchange(pout).reshape(n, rows, rows, C)
        pair_six = swap(jnp.swapaxes(pout, 0, 1).reshape(rows, L, C))

        dz4, dxs, dtb, m_a40, m_ao0, m_ab1 = start_back(
            n, rows, z3, z4, back, tb_all, key_row, a4t, a4, att_out, abt, deps=(copies, others)
        )
        dtb = exchange(dtb)
        dz3, dgp2, dp2, m_ab0, m_mo1 = third_back(
            n, rows, z3, dz4, dxs, dtb, abt, z2, p2, m5t, mot, mof, deps=(pout,)
        )
        dp2 = exchange(dp2.reshape(n, part, L))
        dab2 = channel_product_back(n, rows, False, ab2, dp2)
        kept = single_every(
            n, rows, where, copies, others, single_gains, single_proj, single_up, single_down,
            deps=(dab2,),
        )
        dab2 = exchange(dab2)
        dz2, dgp1, dp1, m_m51, m_mo0 = second_back(
            n, rows, z2, dz3, dgp2, dab2, pmask, m5t, m5, z1, p1, mot, mof, deps=(pair_six, kept[0])
        )
        dp1 = exchange(dp1.reshape(n, part, L))
        dab1 = exchange(channel_product_back(n, rows, True, ab1, dp1))
        dz1, ends, m_oo, m_m50 = first_back(
            n, rows, chips, where, z1, dz2, dgp1, dab1, pmask, m5t, m5, inner, lrt, left_own,
            outer_w,
        )
        ends = to_chips(ends)
        others_ends = other_core(ends)
        dz1 = swap(copies_of(dz1, 1, (others_ends,))[0])
        names = "up dn a41 ao1 a40 ao0 m51 mo1 mo0 m50 oo ab1 ab0".split()
        sums = [
            m_up, m_dn, m_a41, m_ao1, m_a40, m_ao0, m_m51, m_mo1, m_mo0, m_m50, m_oo, m_ab1, m_ab0,
        ]
        places, at = {}, 0
        for name, m in zip(names, sums):
            places[name] = at
            at += m.shape[0]
        half = -(-at // (total * 16)) * total * 8
        near, far = collect(where, sums, half, (ends, others_ends))
        near = b16(near + f32(other_core(far)))
        near = to_chips(near.reshape(chips, half // chips, C))
        ys, g_sg, d_own, drb, m_op = single_back(
            members, rows, where, ends, others_ends, kept, single_gains, single_proj,
            single_up, single_down, outer,
        )
        pair_grad, m_sb = last_back(rows, pair_rep[0], drb, dz1, sbt)
        m_sb = to_all(copies_of(m_sb, total, ()))
        g_sp, g_su, g_sd = weight_grads(kept[2], ys, width, single_up.shape[1])
        g_op = jnp.swapaxes(m_op[:, : 2 * opm].reshape(width, 2, opm), 0, 1)

        near = to_chips(sum_copies(near, chips, (drb,))).reshape(half, C)
        grads = finish(
            where, near, other_core(near), m_sb, pair_gains, mult_gains, mult_proj, mult_gate,
            mult_out, att_proj, att_bias, pair_up, single_bias, places, half, opm, total,
            (g_sd, g_su, g_sp),
        )
        g_pg, g_mg, g_sb, g_oo, g_mp, g_mgt, g_mo, g_ap, g_ab, g_ao, g_pu, g_pd = grads
        return (
            single_out[None],
            pair_six[None],
            d_own[None],
            pair_grad[None],
            g_sg,
            g_pg,
            g_mg,
            g_sp,
            g_sb,
            g_su,
            g_sd,
            g_op,
            g_oo,
            g_mp,
            g_mgt,
            g_mo,
            g_ap,
            g_ab,
            g_ao,
            g_pu,
            g_pd,
        )

    return local


def solution(mesh):
    groups_of, n = mesh.shape["grp"], mesh.shape["rows"]
    whole = P()
    in_specs = (
        (P("grp", "rows", None), P("grp", "rows", None, None), P("grp", None))
        + (whole,) * 17
        + (P("grp", "rows", None), P("grp", "rows", None, None))
    )
    out_specs = (
        P("grp", "rows", None),
        P("grp", "rows", None, None),
        P("grp", "rows", None),
        P("grp", "rows", None, None),
    ) + (whole,) * 17
    if L % n == 0 and (L // n) % 16 == 0:
        body = fast_local((groups_of, n) == (4, 8), n)
    else:
        body = general_local
    return jax.shard_map(body, mesh=mesh, in_specs=in_specs, out_specs=out_specs, check_vma=False)
```

```python
import math

import jax
import jax.numpy as jnp
from jax import lax
from jax.experimental import pallas as pl
from jax.experimental.pallas import tpu as pltpu
from jax.sharding import PartitionSpec as P

BF = jnp.bfloat16
F32 = jnp.float32
EPSILON = 1e-05
MASKED = 1000000000.0
AX = ("grp", "rows")
L = 128
C = 128
TH = 4
HD = 32
HPAD = 16


def dot(a, b):
    return lax.dot_general(a, b, (((1,), (0,)), ((), ())), preferred_element_type=F32)


def dot_nt(a, b):
    return lax.dot_general(a, b, (((1,), (1,)), ((), ())), preferred_element_type=F32)


def dot_tn(a, b):
    return lax.dot_general(a, b, (((0,), (0,)), ((), ())), preferred_element_type=F32)


def b16(x):
    return x.astype(BF)


def f32(x):
    return x.astype(F32)


def sig(x):
    return 0.5 * jnp.tanh(0.5 * x) + 0.5


GELU_A = 0.7978845608028654
GELU_B = 0.044715


def gelu_parts(x):
    t = jnp.tanh(GELU_A * (x + GELU_B * x * x * x))
    half = 0.5 * (1.0 + t)
    slope = half + 0.5 * x * (1.0 - t * t) * (GELU_A * (1.0 + 3.0 * GELU_B * x * x))
    return x * half, slope


def norm_cols(z):
    c = z - jnp.mean(z, 0, keepdims=True)
    scale = lax.rsqrt(jnp.mean(c * c, 0, keepdims=True) + EPSILON)
    return c * scale, scale


def norm_cols_back(dx, xh, scale):
    return scale * (
        dx - jnp.mean(dx, 0, keepdims=True) - xh * jnp.mean(dx * xh, 0, keepdims=True)
    )


U = 2


def cols(r):
    return pl.ds(pl.multiple_of(r * U * L, U * L), U * L)


def side(parts):
    return jnp.concatenate(parts, 1)


def lanes(x, u):
    return x[:, u * L : (u + 1) * L]


def get_rows(ref, r, count, rows):
    return side([ref[pl.ds(r * U + u, count, stride=rows), :] for u in range(U)])


def put_rows(ref, r, count, rows, x):
    for u in range(U):
        ref[pl.ds(r * U + u, count, stride=rows), :] = lanes(x, u)


def put_turned(ref, r, rows, x):
    for u in range(U):
        ref[pl.ds(r * U + u, L, stride=rows), :] = lanes(x, u).T


def get_turned(ref, r, rows):
    return side(
        [
            f32(ref[:, pl.ds(pl.multiple_of((r * U + u) * rows, rows), rows), :].reshape(L, C)).T
            for u in range(U)
        ]
    )


def each_row(count, body):
    def step(r, carry):
        body(r)
        return carry

    lax.fori_loop(0, count, step, 0, unroll=2)


def call(kernel, outs, scratch, args, deps=(), raw=(), late=(), far=(), us=5):
    count, more, given = len(args), len(deps), len(outs)
    fetched = [args[k] for k in raw]

    def body(*refs):
        mine = list(refs[:count])
        results = list(refs[count + more : count + more + given])
        rest = list(refs[count + more + given :])
        sems = rest.pop() if raw or far else None
        stores = [rest.pop() for _ in far][::-1]
        held = [rest.pop() for _ in raw][::-1]
        moves = {}
        for i, k in enumerate(raw):
            moves[k] = pltpu.make_async_copy(mine[k], held[i], sems.at[i])
            moves[k].start()
        for k in raw:
            if k not in late:
                moves[k].wait()
        for i, k in enumerate(raw):
            mine[k] = held[i]
        ends = []
        for i, k in enumerate(far):
            ends.append(pltpu.make_async_copy(stores[i], results[k], sems.at[len(raw) + i]))
            results[k] = stores[i]
        if late:
            kernel(lambda k: moves[k].wait(), *mine, *results, *rest)
        else:
            kernel(*mine, *results, *rest)
        for end in ends:
            end.start()
        for end in ends:
            end.wait()

    vm = pl.BlockSpec(memory_space=pltpu.VMEM)
    sm = pl.BlockSpec(memory_space=pltpu.SMEM)
    away = pl.BlockSpec(memory_space=pl.ANY)
    moved = sum(a.size * a.dtype.itemsize for a in args)
    buffers = [pltpu.VMEM(s, d) for s, d in scratch]
    buffers += [pltpu.VMEM(a.shape, a.dtype) for a in fetched]
    buffers += [pltpu.VMEM(*outs[k]) for k in far]
    placed = sum(math.prod(b.shape) * jnp.dtype(b.dtype).itemsize for b in buffers)
    if raw or far:
        buffers.append(pltpu.SemaphoreType.DMA((len(raw) + len(far),)))
    return pl.pallas_call(
        body,
        out_shape=[
            pltpu.HBM(s, d) if k in far else jax.ShapeDtypeStruct(s, d)
            for k, (s, d) in enumerate(outs)
        ],
        in_specs=[
            away if k in raw else sm if a.dtype == jnp.int32 else vm for k, a in enumerate(args)
        ]
        + [away] * more,
        out_specs=[away if k in far else vm for k in range(given)],
        scratch_shapes=buffers,
        compiler_params=pltpu.CompilerParams(vmem_limit_bytes=(12 << 20) + placed),
        cost_estimate=pl.CostEstimate(flops=us * 10**9, bytes_accessed=moved, transcendentals=0),
    )(
        *[
            pltpu.with_memory_space_constraint(a, pltpu.HBM) if k in raw else a
            for k, a in enumerate(args)
        ],
        *[pltpu.with_memory_space_constraint(d, pltpu.HBM) for d in deps],
    )


def prep_weights(gp, gm, mp, mg, mo, ap, ab, ao, pu, pd, sb):
    def kernel(
        gp, gm, mp, mg, mo, ap, ab, ao, pu, pd, sb,
        m5t, m5, mot, mof, a4t, a4, aot, abt, upt, up, dnt, sbt,
    ):
        gpv = f32(gp[...])
        gmv = f32(gm[...])

        def padded(w):
            return jnp.concatenate([f32(w), jnp.zeros((HPAD - w.shape[0], C), F32)], 0)

        for t in range(2):
            g = gpv[1 + t : 2 + t]
            for k in range(5):
                w = f32(mp[t, k] if k < 4 else mg[t]).T * g
                m5t[t, k * C : (k + 1) * C] = b16(w)
                m5[t, :, k * C : (k + 1) * C] = b16(w.T)
            w = f32(mo[t]).T * gmv[t : t + 1]
            mot[t] = b16(w)
            mof[t] = b16(w.T)
            g = gpv[3 + t : 4 + t]
            for k in range(4):
                w = f32(ap[t, k]).T * (g * HD**-0.5 if k == 0 else g)
                a4t[t, k * C : (k + 1) * C] = b16(w)
                a4[t, :, k * C : (k + 1) * C] = b16(w.T)
            aot[t] = b16(f32(ao[t]).T)
            abt[t] = b16(padded(ab[t]) * g)
        g = gpv[5:6]
        for k in range(4):
            s = slice(k * C, (k + 1) * C)
            w = f32(pu[:, s]).T * g
            upt[s] = b16(w)
            up[:, s] = b16(w.T)
            dnt[:, s] = b16(f32(pd[s]).T)
        sbt[...] = b16(padded(sb[...]) * gpv[0:1])

    outs = [
        ((2, 640, C), BF), ((2, C, 640), BF), ((2, C, C), BF), ((2, C, C), BF),
        ((2, 512, C), BF), ((2, C, 512), BF), ((2, C, C), BF), ((2, HPAD, C), BF),
        ((512, C), BF), ((C, 512), BF), ((C, 512), BF), ((HPAD, C), BF),
    ]
    return call(kernel, outs, [], (gp, gm, mp, mg, mo, ap, ab, ao, pu, pd, sb), raw=(0, 1, 2, 3, 4, 5, 6, 7, 8, 9, 10), far=(0, 1, 2, 3, 4, 5, 6, 7, 8, 9, 10, 11), us=3)


def pack(rows, single, cot, pair, mask, sbt, where):
    def kernel(single, cot, pair, mask, sbt, where, mine, mask_col, s, sm):
        sm[...] = jnp.broadcast_to(mask[...], (L, L)).T
        mask_col[...] = sm[pl.ds(pl.multiple_of(where[3] * rows, rows), rows), :]
        key_row = (mask[...] - 1.0) * MASKED

        def body(r):
            xh, _ = norm_cols(side([f32(pair[r * U + u]).T for u in range(U)]))
            put_rows(s, r, HPAD, rows, dot(sbt[...], b16(xh)) + side([key_row] * U))

        each_row(rows // U, body)
        mine[0:rows] = single[...]
        mine[rows : 2 * rows] = cot[...]
        for h in range(8):
            mine[rows * (2 + h // 4) : rows * (3 + h // 4), (h % 4) * L : (h % 4 + 1) * L] = b16(
                s[h * rows : (h + 1) * rows]
            )

    width = single.shape[1]
    return call(
        kernel,
        [((4 * rows, width), BF), ((rows, L), F32)],
        [((HPAD * rows, L), F32), ((L, L), F32)],
        (single, cot, pair, mask, sbt, where), raw=(0, 1, 2, 4), us=2)


def copies_of(x, count, deps):
    def kernel(x, out):
        for d in range(count):
            out[d] = x[...]

    return call(kernel, [((count,) + x.shape, x.dtype)], [], (x,), deps=deps)[0]


def part_of(x, first, last, deps):
    def kernel(x, out):
        out[...] = x[first:last]

    return call(
        kernel, [((last - first,) + x.shape[1:], x.dtype)], [], (x,), deps=deps, raw=(0,), us=1
    )[0]


def norm_rows16(x):
    c = x - jnp.mean(x, -1, keepdims=True)
    scale = lax.rsqrt(jnp.mean(c * c, -1, keepdims=True) + EPSILON)
    return c * scale, scale


def norm_rows16_back(dx, xh, scale):
    return scale * (
        dx - jnp.mean(dx, -1, keepdims=True) - xh * jnp.mean(dx * xh, -1, keepdims=True)
    )


def halves():
    lane = lax.broadcasted_iota(jnp.int32, (1, L), 1)
    low = jnp.where(lane < L // 2, 1.0, 0.0)
    return b16(low), b16(1.0 - low)


def pair_weights(q, k, bias0, bias1):
    out = []
    for m, bias in zip(halves(), (bias0, bias1)):
        s = dot_nt(q * m, k) + bias
        e = jnp.exp(s - jnp.max(s, -1, keepdims=True))
        out.append(b16(e / jnp.sum(e, -1, keepdims=True)))
    return out


def on_halves(x, axis=0):
    return jnp.concatenate([x * m for m in halves()], axis)


def single_own(n, rows, copies, gathered, mine, mask_col, gains, proj, up, down, outer):
    width = up.shape[0]
    opm2 = 64

    def kernel(arrive, gathered, mine, mask_col, gains, proj, up, down, outer, out, lr):
        g = f32(gains[...])
        sn = b16(norm_rows16(f32(gathered[...].reshape(n * rows, width)))[0] * g[0:1])
        arrive(4)
        keys, vals = b16(dot(sn, proj[1])), b16(dot(sn, proj[2]))
        x = f32(mine[0:rows])
        sn = b16(norm_rows16(x)[0] * g[0:1])
        query = b16(dot(sn, proj[0]) * 0.125)
        gate = sig(dot(sn, proj[3]))
        mixed = []
        for t in range(4):
            s = slice(t * L, (t + 1) * L)
            bias = [
                f32(mine[rows * (2 + h // 4) : rows * (3 + h // 4), (h % 4) * L : (h % 4 + 1) * L])
                for h in (2 * t, 2 * t + 1)
            ]
            p = pair_weights(query[:, s], keys[:, s], *bias)
            mixed.append(dot(jnp.concatenate(p, 1), on_halves(vals[:, s])))
        mixed = jnp.concatenate(mixed, 1)
        first = x + dot(b16(mixed * gate), proj[4])
        x1 = b16(norm_rows16(first)[0] * g[1:2])
        arrive(5)
        hidden = b16(gelu_parts(dot(x1, up[...]))[0])
        arrive(6)
        second = first + dot(hidden, down[...])
        out[...] = b16(second)
        x2 = b16(norm_rows16(second)[0] * g[2:3])
        both = dot(x2, outer[...]) * mask_col[...]
        lane = lax.broadcasted_iota(jnp.int32, (rows, L), 1)
        both = b16(jnp.where(lane >= opm2, mask_col[...], both))
        for d in range(copies):
            lr[d] = both

    return call(
        kernel,
        [((rows, width), BF), ((copies, rows, L), BF)],
        [],
        (gathered, mine, mask_col, gains, proj, up, down, outer), raw=(3, 4, 5, 6, 7), late=(4, 5, 6), us=6)


def single_every(n, rows, where, ga, gb, gains, proj, up, down, deps=()):
    width, wide = up.shape
    tokens = 4 * L
    half = ga.shape[0]

    def kernel(
        arrive, where, ga, gb, gains, proj, up, down,
        x_all, cot_all, xs, qkv, gm, probs, slope, first_out, second_out, held,
    ):
        core = where[3] % 2
        for k in range(half):
            held[2 * k + core] = ga[k]
            held[2 * k + 1 - core] = gb[k]
        g = f32(gains[...])

        def body(step):
            rs = pl.ds(pl.multiple_of(step * 2 * L, 2 * L), 2 * L)
            ds = pl.ds(step * 2 * n, 2 * n)
            x16 = held[ds, 0:rows, :].reshape(2 * L, width)
            x_all[rs, :] = x16
            cot_all[rs, :] = held[ds, rows : 2 * rows, :].reshape(2 * L, width)
            x = f32(x16)
            sn = b16(norm_rows16(x)[0] * g[0:1])
            xs[rs, 0:width] = sn

            if step == 0:
                arrive(4)

            query = b16(dot(sn, proj[0]) * 0.125)
            keys, vals = b16(dot(sn, proj[1])), b16(dot(sn, proj[2]))
            qkv[rs, 0:width] = query
            qkv[rs, width : 2 * width] = keys
            qkv[rs, 2 * width : 3 * width] = vals
            gate = sig(dot(sn, proj[3]))
            mixed = []
            for u in range(2):
                crop = step * 2 + u
                own = pl.ds(crop * n, n)
                part = slice(u * L, (u + 1) * L)
                outs = []
                for t in range(4):
                    s = slice(t * L, (t + 1) * L)
                    bias = [
                        f32(
                            held[
                                own,
                                rows * (2 + h // 4) : rows * (3 + h // 4),
                                (h % 4) * L : (h % 4 + 1) * L,
                            ].reshape(L, L)
                        )
                        for h in (2 * t, 2 * t + 1)
                    ]
                    p = pair_weights(query[part, s], keys[part, s], *bias)
                    for k in range(2):
                        at = pl.multiple_of((crop * 8 + 2 * t + k) * L, L)
                        probs[pl.ds(at, L), :] = p[k]
                    outs.append(dot(jnp.concatenate(p, 1), on_halves(vals[part, s])))
                mixed.append(jnp.concatenate(outs, 1))
            mixed = jnp.concatenate(mixed, 0)
            gm[rs, 0:width] = b16(gate)
            gm[rs, width : 2 * width] = b16(mixed)
            u = b16(mixed * gate)
            xs[rs, width : 2 * width] = u
            first = x + dot(u, proj[4])
            first_out[rs, :] = first
            x1 = b16(norm_rows16(first)[0] * g[1:2])
            xs[rs, 2 * width : 3 * width] = x1

            if step == 0:
                arrive(5)
                arrive(6)

            hid, slp = gelu_parts(dot(x1, up[...]))
            h16 = b16(hid)
            xs[rs, 3 * width : 3 * width + wide] = h16
            slope[rs, :] = b16(slp)
            second_out[rs, :] = first + dot(h16, down[...])

        for step in range(2):
            body(step)

    return call(
        kernel,
        [
            ((tokens, width), BF), ((tokens, width), BF), ((tokens, 3 * width + wide), BF),
            ((tokens, 3 * width), BF), ((tokens, 2 * width), BF), ((4 * 8 * L, L), BF),
            ((tokens, wide), BF), ((tokens, width), F32), ((tokens, width), F32),
        ],
        [((2 * half, 4 * rows, width), BF)],
        (where, ga, gb, gains, proj, up, down),
        deps=deps, raw=(1, 2, 3, 4, 5, 6), late=(4, 5, 6), far=(0, 1, 2, 3, 4, 5, 6, 7, 8), us=19)


def single_back(members, rows, where, ea, eb, kept, gains, proj, up, down, outer, deps=()):
    width, wide = up.shape
    tokens = 4 * L
    x_all, cot_all, _, qkv, gm, probs, slope, first_in, second_in = kept

    def kernel(
        arrive, where, ea, eb, x_all, cot_all, qkv, gm, probs, slope, first_in, second_in,
        gains, proj, up, down, outer,
        ys, gain_grad, d_own, drb, m_op,
        dlr, o_x2, sdrb, sds,
    ):
        g = f32(gains[...])
        gain_grad[...] = jnp.zeros_like(gain_grad)
        for crop in range(4):
            total = f32(ea[members[crop][0]]) + f32(eb[members[crop][0]])
            for k in members[crop][1:]:
                total = total + (f32(ea[k]) + f32(eb[k]))
            total = jnp.concatenate([total, jnp.zeros_like(total)], 0)
            dlr[crop * L : (crop + 1) * L] = b16(total.T)

        def body(step):
            rs = pl.ds(pl.multiple_of(step * 2 * L, 2 * L), 2 * L)
            x2, sc2 = norm_rows16(second_in[rs, :])
            o_x2[rs, :] = b16(x2 * g[2:3])
            dx = dot_nt(dlr[rs, :], outer[...])
            gain_grad[2:3] += jnp.sum(dx * x2, 0, keepdims=True)
            ds2 = f32(cot_all[rs, :]) + norm_rows16_back(dx * g[2:3], x2, sc2)
            ds2_16 = b16(ds2)
            ys[rs, 5 * width + wide :] = ds2_16

            if step == 0:
                for k in (14, 8, 13, 9):
                    arrive(k)

            dhp = b16(dot_nt(ds2_16, down[...]) * f32(slope[rs, :]))
            ys[rs, 5 * width : 5 * width + wide] = dhp
            dx = dot_nt(dhp, up[...])
            x1, sc1 = norm_rows16(first_in[rs, :])
            gain_grad[1:2] += jnp.sum(dx * x1, 0, keepdims=True)
            df = ds2 + norm_rows16_back(dx * g[1:2], x1, sc1)
            df16 = b16(df)
            ys[rs, 4 * width : 5 * width] = df16

            if step == 0:
                for k in (12, 6, 5, 7):
                    arrive(k)

            du = dot_nt(df16, proj[4])
            gate, mixed = f32(gm[rs, 0:width]), f32(gm[rs, width : 2 * width])
            do = du * gate
            do16 = b16(do)
            row = do * mixed
            dgate = b16(du * mixed * gate * (1.0 - gate))
            ys[rs, 3 * width : 4 * width] = dgate
            lane = lax.broadcasted_iota(jnp.int32, (1, L), 1)
            low = jnp.where(lane < L // 2, 1.0, 0.0)
            for u in range(2):
                crop = step * 2 + u
                own = pl.ds(pl.multiple_of(crop * L, L), L)
                part = slice(u * L, (u + 1) * L)
                for t in range(4):
                    s = slice(t * L, (t + 1) * L)
                    q = qkv[own, t * L : (t + 1) * L]
                    k = qkv[own, width + t * L : width + (t + 1) * L]
                    v = qkv[own, 2 * width + t * L : 2 * width + (t + 1) * L]
                    grads, weights = [], []
                    for j, (m, mf) in enumerate(zip(halves(), (low, 1.0 - low))):
                        at = pl.multiple_of((crop * 8 + 2 * t + j) * L, L)
                        p16 = probs[pl.ds(at, L), :]
                        dp = dot_nt(do16[part, s] * m, v)
                        e = f32(p16) * (dp - jnp.sum(row[part, s] * mf, -1, keepdims=True))
                        sdrb[pl.ds(at, L), :] = e
                        grads.append(b16(e))
                        weights.append(p16)
                    dq = dot(jnp.concatenate(grads, 1), on_halves(k)) * 0.125
                    dk = dot_tn(jnp.concatenate(grads, 0), on_halves(q))
                    dv = dot_tn(jnp.concatenate(weights, 0), on_halves(do16[part, s]))
                    ys[own, t * L : (t + 1) * L] = b16(dq)
                    ys[own, width + t * L : width + (t + 1) * L] = b16(dk)
                    ys[own, 2 * width + t * L : 2 * width + (t + 1) * L] = b16(dv)
            dx = dot_nt(ys[rs, 0:width], proj[0])
            for k in range(1, 4):
                dx = dx + dot_nt(ys[rs, k * width : (k + 1) * width], proj[k])
            x0, sc0 = norm_rows16(f32(x_all[rs, :]))
            gain_grad[0:1] += jnp.sum(dx * x0, 0, keepdims=True)
            sds[rs, :] = df + norm_rows16_back(dx * g[0:1], x0, sc0)

        for step in range(2):
            body(step)
        grp, row = where[2], where[3]
        d_own[...] = sds[pl.ds(pl.multiple_of(grp * L + row * rows, rows), rows), :]
        for h in range(8):
            at = pl.multiple_of((grp * 8 + h) * L + row * rows, rows)
            drb[h * rows : (h + 1) * rows] = sdrb[pl.ds(at, rows), :]
        m_op[...] = dot_tn(o_x2[...], dlr[...])

    return call(
        kernel,
        [
            ((tokens, 6 * width + wide), BF), ((3, width), F32), ((rows, width), F32),
            ((8 * rows, L), F32), ((width, L), F32),
        ],
        [
            ((tokens, L), BF), ((tokens, width), BF), ((4 * 8 * L, L), F32), ((tokens, width), F32),
        ],
        (
            where, ea, eb, x_all, cot_all, qkv, gm, probs, slope, first_in, second_in,
            gains, proj, up, down, outer,
        ), deps=deps, raw=(10, 15, 4, 11, 14, 8, 13, 9, 12, 6, 5, 7, 3), late=(5, 6, 7, 8, 9, 12, 13, 14), far=(0, 1, 2, 3, 4), us=22)


def weight_grads(xs, ys, width, wide, after):
    tokens = xs.shape[0]
    blocks = wide // width

    def kernel(x, y, after, out):
        out[...] = dot_tn(x[...], y[...]).reshape(out.shape)

    def run(steps, x_at, y_at, shape, block, out_at):
        return pl.pallas_call(
            kernel,
            grid=(steps,),
            out_shape=pltpu.HBM(shape, F32),
            in_specs=[
                pl.BlockSpec((tokens, width), x_at),
                pl.BlockSpec((tokens, width), y_at),
                pl.BlockSpec(memory_space=pl.ANY),
            ],
            out_specs=pl.BlockSpec(block, out_at),
            compiler_params=pltpu.CompilerParams(vmem_limit_bytes=32 << 20),
            cost_estimate=pl.CostEstimate(
                flops=2 * 10**9,
                bytes_accessed=steps * width * width * 8,
                transcendentals=0,
            ),
        )(
            pltpu.with_memory_space_constraint(xs, pltpu.HBM),
            pltpu.with_memory_space_constraint(ys, pltpu.HBM),
            pltpu.with_memory_space_constraint(after, pltpu.HBM),
        )

    proj = run(
        5, lambda i: (0, i // 4), lambda i: (0, i), (5, width, width), (1, width, width),
        lambda i: (i, 0, 0),
    )
    up = run(
        blocks, lambda i: (0, 2), lambda i: (0, 5 + i), (width, wide), (width, width),
        lambda i: (0, i),
    )
    down = run(
        blocks, lambda i: (0, 3 + i), lambda i: (0, 5 + blocks), (wide, width), (width, width),
        lambda i: (i, 0),
    )
    return proj, up, down


def project_pair(z, r, rows, m5t, pmask, sa, sb):
    xh, _ = norm_cols(z)
    p = dot(m5t[0:512], b16(xh))
    mk = get_rows(pmask, r, 1, 1)
    put_rows(sa, r, C, rows, sig(p[0:C]) * p[C : 2 * C] * mk)
    put_rows(sb, r, C, rows, sig(p[2 * C : 3 * C]) * p[3 * C : 4 * C] * mk)


def put_pair(n, ab, sa, sb):
    part = sa.shape[0] // n
    for d in range(n):
        ab[d, 0:part] = b16(sa[d * part : (d + 1) * part])
        ab[d, part : 2 * part] = b16(sb[d * part : (d + 1) * part])


def gated_product(z, r, rows, gatet, mot, sp):
    xh, _ = norm_cols(z)
    gate = sig(dot(gatet[...], b16(xh)))
    ph, _ = norm_cols(get_rows(sp, r, C, rows))
    return z + dot(mot[...], b16(ph)) * gate


def front(n, rows, where, lr_all, pair, outer_w, m5ts, deps=()):
    opm = outer_w.shape[0]

    def kernel(
        where, lr_all, pair, outer_w, m5ts,
        z1, ab, pmask, key_row, inner, lrt, left_own, sa, sb, slr, spm,
    ):
        m5t = m5ts.at[0]
        crop, block = where[0], where[1]
        lr16 = lr_all[pl.ds(crop * n, n)].reshape(L, C)
        lr = f32(lr16)
        turned = lr.T
        lrt[...] = turned
        mrow = turned[2 * opm : 2 * opm + 1]
        key_row[...] = (mrow - 1.0) * MASKED
        first = pl.multiple_of(block * rows, rows)
        spm[...] = jnp.broadcast_to(mrow, (L, L)).T * mrow
        pmask[...] = spm[pl.ds(first, rows), :]
        slr[...] = lr
        left = b16(slr[pl.ds(first, rows), :])
        left_own[...] = left
        for b in range(opm):
            inner[b * rows : (b + 1) * rows] = dot(left[:, 0:opm], outer_w[b])
        edge = jnp.zeros((opm, C), BF)

        def body(r):
            parts = []
            for u in range(U):
                mine = b16(inner[pl.ds(r * U + u, opm, stride=rows), :])
                mine = jnp.concatenate([edge, mine, edge, edge], 0)
                parts.append((f32(pair[r * U + u]) + dot(lr16, mine)).T)
            z = side(parts)
            z1[:, cols(r)] = z
            project_pair(z, r, rows, m5t, pmask, sa, sb)

        each_row(rows // U, body)
        put_pair(n, ab, sa, sb)

    part = C * rows // n
    return call(
        kernel,
        [
            ((C, rows * L), F32), ((n, 2 * part, L), BF), ((rows, L), F32), ((1, L), F32),
            ((opm * rows, C), F32), ((C, L), F32), ((rows, C), BF),
        ],
        [((C * rows, L), F32)] * 2 + [((L, C), F32), ((L, L), F32)],
        (where, lr_all, pair, outer_w, m5ts), deps=deps, raw=(2, 3, 4), far=(0, 2, 3, 4, 5, 6), us=5)


def middle(n, rows, z1, prod, mots, pmask, m5ts, deps=()):
    def kernel(z1, prod, mots, pmask, m5ts, z2, ab, sa, sb, sp):
        gatet, mot, m5t = m5ts.at[0, 512:640], mots.at[0], m5ts.at[1]
        sp[...] = f32(prod[...])

        def body(r):
            z = gated_product(z1[:, cols(r)], r, rows, gatet, mot, sp)
            z2[:, cols(r)] = z
            project_pair(z, r, rows, m5t, pmask, sa, sb)

        each_row(rows // U, body)
        put_pair(n, ab, sa, sb)

    part = C * rows // n
    return call(
        kernel,
        [((C, rows * L), F32), ((n, 2 * part, L), BF)],
        [((C * rows, L), F32)] * 3,
        (z1, prod, mots, pmask, m5ts), deps=deps, raw=(0, 1, 2, 3, 4), far=(0,), us=4)


def start_front(n, rows, z2, prod, m5ts, mots, abts, deps=()):
    def kernel(z2, prod, m5ts, mots, abts, z3, tb, sp, st):
        gatet, mot, abt = m5ts.at[1, 512:640], mots.at[1], abts.at[0]
        sp[...] = f32(prod[...])

        def body(r):
            z = gated_product(z2[:, cols(r)], r, rows, gatet, mot, sp)
            z3[:, cols(r)] = z
            xh, _ = norm_cols(z)
            put_rows(st, r, HPAD, rows, dot(abt[...], b16(xh)))

        each_row(rows // U, body)
        for d in range(n):
            tb[d] = b16(st[0 : TH * rows])

    return call(
        kernel,
        [((C, rows * L), F32), ((n, TH * rows, L), BF)],
        [((C * rows, L), F32), ((HPAD * rows, L), F32)],
        (z2, prod, m5ts, mots, abts), deps=deps, raw=(0, 1, 2, 3, 4), far=(0,), us=4)


def channel_product(n, rows, outgoing, ab):
    def kernel(ab, out):
        part = C * rows // n
        for ch in range(C // n):
            a = ab[:, ch * rows : (ch + 1) * rows, :].reshape(L, L)
            b = ab[:, part + ch * rows : part + (ch + 1) * rows, :].reshape(L, L)
            prod = dot_nt(a, b) if outgoing else dot_tn(a, b)
            out[:, ch * rows : (ch + 1) * rows, :] = b16(prod).reshape(n, rows, L)

    return call(kernel, [((n, C * rows // n, L), BF)], [], (ab,), raw=(0,), us=1)[0]


def channel_product_back(n, rows, outgoing, ab, dprod, deps=()):
    def kernel(ab, dprod, out):
        part = C * rows // n
        for ch in range(C // n):
            low, high = ch * rows, (ch + 1) * rows
            a = ab[:, low:high, :].reshape(L, L)
            b = ab[:, part + low : part + high, :].reshape(L, L)
            g = dprod[:, low:high, :].reshape(L, L)
            if outgoing:
                da, db = dot(g, b), dot_tn(g, a)
            else:
                da, db = dot_nt(b, g), dot(a, g)
            out[:, low:high, :] = b16(da).reshape(n, rows, L)
            out[:, part + low : part + high, :] = b16(db).reshape(n, rows, L)

    return call(kernel, [((n, 2 * C * rows // n, L), BF)], [], (ab, dprod), deps=deps, raw=(0,), us=2)[0]


def head_masks():
    lane = lax.broadcasted_iota(jnp.int32, (1, C), 1)
    return [b16(jnp.where((lane >= h * HD) & (lane < (h + 1) * HD), 1.0, 0.0)) for h in range(TH)]


def by_head(x):
    pm = b16(x.T)
    return jnp.concatenate([pm * m for m in head_masks()], 0)


def attend(x16, a4t, bias):
    p4 = dot(a4t[...], x16)
    gate = sig(p4[3 * C : 4 * C])
    each, mixed = [], []
    for u in range(U):
        q, k, v = (lanes(p4[m * C : (m + 1) * C], u) for m in range(3))
        logits = dot(by_head(k), b16(q)) + bias[...]
        raised, outs = [], []
        v16 = b16(v)
        for h in range(TH):
            s = logits[h * L : (h + 1) * L]
            e = jnp.exp(s - jnp.max(s, 0, keepdims=True))
            inv = 1.0 / jnp.sum(e, 0, keepdims=True)
            raised.append((e, inv))
            outs.append(dot(v16[h * HD : (h + 1) * HD], b16(e)) * inv)
        each.append((q, k, v, raised))
        mixed.append(jnp.concatenate(outs, 0))
    return each, gate, side(mixed)


def attend_back(state, dy16, ao, dbias):
    each, gate, mixed = state
    du = dot(ao[...], dy16)
    do = du * gate
    dgate = du * mixed * gate * (1.0 - gate)
    both = do * mixed
    parts = []
    for u in range(U):
        q, k, v, raised = each[u]
        do16, q16, k16 = b16(lanes(do, u)), b16(q), b16(k)
        dp = dot(by_head(v), do16)
        row = lanes(both, u)
        dq, dk, dv = [], [], []
        for h in range(TH):
            s = slice(h * HD, (h + 1) * HD)
            w = slice(h * L, (h + 1) * L)
            e, inv = raised[h]
            p = e * inv
            ds = p * (dp[w] - jnp.sum(row[s], 0, keepdims=True))
            dbias[w, :] += ds
            ds16, p16 = b16(ds), b16(p)
            dv.append(dot_nt(do16[s], p16))
            dq.append(dot(k16[s], ds16))
            dk.append(dot_nt(q16[s], ds16))
        parts.append(jnp.concatenate([b16(x) for x in dq + dk + dv], 0))
    return jnp.concatenate([side(parts), b16(dgate)], 0)


def start_attention(n, rows, z3, tb_all, key_row, a4ts, aots, abts, deps=()):
    def kernel(z3, tb_all, key_row, a4ts, aots, abts, z4, send, bias, st, se):
        a4t, aot, abt = a4ts.at[0], aots.at[0], abts.at[1]
        for h in range(TH):
            b = f32(tb_all[:, h * rows : (h + 1) * rows, :].reshape(L, L)) + key_row[...]
            bias[h * L : (h + 1) * L, :] = b.T

        def body(r):
            z = z3[:, cols(r)]
            xh, _ = norm_cols(z)
            _, gate, mixed = attend(b16(xh), a4t, bias)
            z = z + dot(aot[...], b16(mixed * gate))
            z4[:, cols(r)] = z
            put_turned(st, r, rows, z)
            xe, _ = norm_cols(z)
            put_rows(se, r, HPAD, rows, dot(abt[...], b16(xe)))

        each_row(rows // U, body)
        part = L * rows // n
        for d in range(n):
            send[d, 0:part] = b16(st[d * part : (d + 1) * part])
            send[d, part : part + TH * rows] = b16(se[0 : TH * rows])

    part = L * rows // n
    return call(
        kernel,
        [((C, rows * L), F32), ((n, part + TH * rows, L), BF)],
        [((TH * L, L), F32), ((L * rows, C), F32), ((HPAD * rows, L), F32)],
        (z3, tb_all, key_row, a4ts, aots, abts), deps=deps, raw=(0, 1, 2, 3, 4, 5), far=(0,), us=12)


def end_both(n, rows, recv, cot, key_row, a4ts, a4s, aots, aos, upt, up, dnt, dn, deps=()):
    part = L * rows // n

    def kernel(
        recv, cot, key_row, a4ts, a4s, aots, aos, upt, up, dnt, dn,
        pout, send, m_up, m_dn, m_a4, m_ao,
        bias, dbias, sout, sdz, o_h, o_dh, o_x5, o_cot, o_x4, o_d4, o_u, o_dy,
    ):
        a4t, a4, aot, ao = a4ts.at[1], a4s.at[1], aots.at[1], aos.at[1]
        kb = jnp.broadcast_to(key_row[...], (L, L)).T
        for h in range(TH):
            b = recv[:, part + h * rows : part + (h + 1) * rows, :].reshape(L, L)
            bias[h * L : (h + 1) * L, :] = f32(b) + kb
        dbias[...] = jnp.zeros_like(dbias)

        def body(r):
            w = cols(r)
            z4 = get_turned(recv, r, rows)
            x4, scale4 = norm_cols(z4)
            x16 = b16(x4)
            state = attend(x16, a4t, bias)
            gated = b16(state[2] * state[1])
            z5 = z4 + dot(aot[...], gated)
            x5, scale5 = norm_cols(z5)
            x516 = b16(x5)
            hid, slope = gelu_parts(dot(upt[...], x516))
            h16 = b16(hid)
            z6 = z5 + dot(dnt[...], h16)
            put_turned(sout, r, rows, z6)
            dz6 = side([f32(cot[r * U + u]).T for u in range(U)])
            c16 = b16(dz6)
            dh16 = b16(dot(dn[...], c16) * slope)
            dz5 = dz6 + norm_cols_back(dot(up[...], dh16), x5, scale5)
            dy16 = b16(dz5)
            d4 = attend_back(state, dy16, ao, dbias)
            dz4 = dz5 + norm_cols_back(dot(a4[...], d4), x4, scale4)
            put_turned(sdz, r, rows, dz4)
            o_h[:, w] = h16
            o_dh[:, w] = dh16
            o_x5[:, w] = x516
            o_cot[:, w] = c16
            o_x4[:, w] = x16
            o_d4[:, w] = d4
            o_u[:, w] = gated
            o_dy[:, w] = dy16

        each_row(rows // U, body)
        for d in range(n):
            pout[d] = b16(sout[d * part : (d + 1) * part])
            send[d, 0:part] = b16(sdz[d * part : (d + 1) * part])
            for h in range(TH):
                send[d, part + h * rows : part + (h + 1) * rows] = b16(
                    dbias[h * L + d * rows : h * L + (d + 1) * rows]
                )
        for k in range(4):
            s = slice(k * C, (k + 1) * C)
            m_up[s] = dot_nt(o_x5[...], o_dh[s])
            m_a4[s] = dot_nt(o_x4[...], o_d4[s])
        m_dn[...] = dot_nt(o_h[...], o_cot[...])
        m_ao[...] = dot_nt(o_u[...], o_dy[...])

    wide = rows * L
    return call(
        kernel,
        [
            ((n, part, C), BF), ((n, part + TH * rows, L), BF),
            ((512, C), F32), ((512, C), F32), ((512, C), F32), ((C, C), F32),
        ],
        [
            ((TH * L, L), F32), ((TH * L, L), F32), ((L * rows, C), F32), ((L * rows, C), F32),
            ((512, wide), BF), ((512, wide), BF), ((C, wide), BF), ((C, wide), BF),
            ((C, wide), BF), ((512, wide), BF), ((C, wide), BF), ((C, wide), BF),
        ],
        (recv, cot, key_row, a4ts, a4s, aots, aos, upt, up, dnt, dn),
        deps=deps, raw=(1, 2, 3, 4, 5, 6, 7, 8, 9, 10), far=(2, 3, 4, 5), us=36)


def start_back(n, rows, z3, z4, recv, tb_all, key_row, a4ts, a4s, aos, abts, deps=()):
    part = L * rows // n

    def kernel(
        z3, z4, recv, tb_all, key_row, a4ts, a4s, aos, abts,
        dz4_out, dxs, dtb, m_a4, m_ao, m_ab,
        bias, dbias, seb, o_x3, o_d4, o_u, o_dy, o_x4, o_eb,
    ):
        a4t, a4, ao, abt = a4ts.at[0], a4s.at[0], aos.at[0], abts.at[1]
        for h in range(TH):
            b = f32(tb_all[:, h * rows : (h + 1) * rows, :].reshape(L, L)) + key_row[...]
            bias[h * L : (h + 1) * L, :] = b.T
        dbias[...] = jnp.zeros_like(dbias)
        seb[...] = jnp.zeros_like(seb)
        total = f32(recv[0, part : part + TH * rows])
        for d in range(1, n):
            total = total + f32(recv[d, part : part + TH * rows])
        seb[0 : TH * rows, :] = total

        def body(r):
            w = cols(r)
            x4, scale4 = norm_cols(z4[:, w])
            eb16 = b16(get_rows(seb, r, HPAD, rows))
            dz4 = get_turned(recv, r, rows)
            dz4 = dz4 + norm_cols_back(dot_tn(abt[...], eb16), x4, scale4)
            dz4_out[:, w] = dz4
            x3, _ = norm_cols(z3[:, w])
            x16 = b16(x3)
            state = attend(x16, a4t, bias)
            dy16 = b16(dz4)
            d4 = attend_back(state, dy16, ao, dbias)
            dxs[:, w] = dot(a4[...], d4)
            o_x3[:, w] = x16
            o_d4[:, w] = d4
            o_u[:, w] = b16(state[2] * state[1])
            o_dy[:, w] = dy16
            o_x4[:, w] = b16(x4)
            o_eb[:, w] = eb16

        each_row(rows // U, body)
        for h in range(TH):
            turned = b16(dbias[h * L : (h + 1) * L, :].T)
            for d in range(n):
                dtb[d, h * rows : (h + 1) * rows] = turned[d * rows : (d + 1) * rows]
        for k in range(4):
            s = slice(k * C, (k + 1) * C)
            m_a4[s] = dot_nt(o_x3[...], o_d4[s])
        m_ao[...] = dot_nt(o_u[...], o_dy[...])
        m_ab[...] = dot_nt(o_eb[...], o_x4[...])

    wide = rows * L
    return call(
        kernel,
        [
            ((C, wide), F32), ((C, wide), F32), ((n, TH * rows, L), BF),
            ((512, C), F32), ((C, C), F32), ((HPAD, C), F32),
        ],
        [
            ((TH * L, L), F32), ((TH * L, L), F32), ((HPAD * rows, L), F32),
            ((C, wide), BF), ((512, wide), BF), ((C, wide), BF), ((C, wide), BF),
            ((C, wide), BF), ((HPAD, wide), BF),
        ],
        (z3, z4, recv, tb_all, key_row, a4ts, a4s, aos, abts),
        deps=deps, raw=(0, 1, 3, 4, 5, 6, 7, 8), far=(0, 1, 3, 4, 5), us=20)


def product_back(z, dz, r, rows, sp, gatet, mot, mof, sdp, dgp_out, o_ph, o_do):
    w = cols(r)
    xh, _ = norm_cols(z)
    gate = sig(dot(gatet[...], b16(xh)))
    ph, scale = norm_cols(get_rows(sp, r, C, rows))
    ph16 = b16(ph)
    out = dot(mot[...], ph16)
    dgp_out[:, w] = b16(dz * out * gate * (1.0 - gate))
    do16 = b16(dz * gate)
    put_rows(sdp, r, C, rows, norm_cols_back(dot(mof[...], do16), ph, scale))
    o_ph[:, w] = ph16
    o_do[:, w] = do16


def third_back(n, rows, z3, dz4, dxs, recv, abts, z2, prod, m5ts, mots, mofs, deps=()):
    def kernel(
        z3, dz4, dxs, recv, abts, z2, prod, m5ts, mots, mofs,
        dz3, dgp, dp, m_ab, m_mo,
        stb, sp, sdp, o_x3, o_tb, o_ph, o_do,
    ):
        abt, gatet, mot, mof = abts.at[0], m5ts.at[1, 512:640], mots.at[1], mofs.at[1]
        sp[...] = f32(prod[...])
        stb[...] = jnp.zeros_like(stb)
        total = f32(recv[0])
        for d in range(1, n):
            total = total + f32(recv[d])
        stb[0 : TH * rows, :] = total

        def body(r):
            w = cols(r)
            x3, scale3 = norm_cols(z3[:, w])
            tb16 = b16(get_rows(stb, r, HPAD, rows))
            dx = dxs[:, w] + dot_tn(abt[...], tb16)
            dz = dz4[:, w] + norm_cols_back(dx, x3, scale3)
            dz3[:, w] = dz
            o_x3[:, w] = b16(x3)
            o_tb[:, w] = tb16
            product_back(z2[:, w], dz, r, rows, sp, gatet, mot, mof, sdp, dgp, o_ph, o_do)

        each_row(rows // U, body)
        dp[...] = b16(sdp[...])
        m_ab[...] = dot_nt(o_tb[...], o_x3[...])
        m_mo[...] = dot_nt(o_ph[...], o_do[...])

    wide = rows * L
    return call(
        kernel,
        [
            ((C, wide), F32), ((C, wide), BF), ((C * rows, L), BF),
            ((HPAD, C), F32), ((C, C), F32),
        ],
        [
            ((HPAD * rows, L), F32), ((C * rows, L), F32), ((C * rows, L), F32),
            ((C, wide), BF), ((HPAD, wide), BF), ((C, wide), BF), ((C, wide), BF),
        ],
        (z3, dz4, dxs, recv, abts, z2, prod, m5ts, mots, mofs), deps=deps, raw=(0, 1, 2, 4, 5, 6, 7, 8, 9), far=(0, 1, 3, 4), us=7)


def projections_back(n, rows, z, dz, dgp, r, pmask, m5t, m5, sa, sb, o_x, o_d5):
    w = cols(r)
    xh, scale = norm_cols(z)
    x16 = b16(xh)
    p = dot(m5t[0:512], x16)
    mk = get_rows(pmask, r, 1, 1)
    da = get_rows(sa, r, C, rows) * mk
    db = get_rows(sb, r, C, rows) * mk
    ga, gb = sig(p[0:C]), sig(p[2 * C : 3 * C])
    va, vb = p[C : 2 * C], p[3 * C : 4 * C]
    d5 = jnp.concatenate(
        [
            b16(da * va * ga * (1.0 - ga)),
            b16(da * ga),
            b16(db * vb * gb * (1.0 - gb)),
            b16(db * gb),
            dgp[:, w],
        ],
        0,
    )
    o_x[:, w] = x16
    o_d5[:, w] = d5
    return dz + norm_cols_back(dot(m5[...], d5), xh, scale)


def take_pair(n, dab, sa, sb):
    part = sa.shape[0] // n
    for d in range(n):
        sa[d * part : (d + 1) * part, :] = f32(dab[d, 0:part])
        sb[d * part : (d + 1) * part, :] = f32(dab[d, part : 2 * part])


def second_back(n, rows, z2, dz3, dgp, dab, pmask, m5ts, m5s, z1, prod, mots, mofs, deps=()):
    def kernel(
        z2, dz3, dgp, dab, pmask, m5ts, m5s, z1, prod, mots, mofs,
        dz2, dgp_out, dp, m_m5, m_mo,
        sa, sb, sp, sdp, o_x, o_d5, o_ph, o_do,
    ):
        m5t, m5, gatet = m5ts.at[1], m5s.at[1], m5ts.at[0, 512:640]
        mot, mof = mots.at[0], mofs.at[0]
        sp[...] = f32(prod[...])
        take_pair(n, dab, sa, sb)

        def body(r):
            w = cols(r)
            dz = projections_back(
                n, rows, z2[:, w], dz3[:, w], dgp, r, pmask, m5t, m5, sa, sb, o_x, o_d5
            )
            dz2[:, w] = dz
            product_back(z1[:, w], dz, r, rows, sp, gatet, mot, mof, sdp, dgp_out, o_ph, o_do)

        each_row(rows // U, body)
        dp[...] = b16(sdp[...])
        for k in range(5):
            s = slice(k * C, (k + 1) * C)
            m_m5[s] = dot_nt(o_x[...], o_d5[s])
        m_mo[...] = dot_nt(o_ph[...], o_do[...])

    wide = rows * L
    return call(
        kernel,
        [
            ((C, wide), F32), ((C, wide), BF), ((C * rows, L), BF),
            ((640, C), F32), ((C, C), F32),
        ],
        [
            ((C * rows, L), F32), ((C * rows, L), F32), ((C * rows, L), F32), ((C * rows, L), F32),
            ((C, wide), BF), ((640, wide), BF), ((C, wide), BF), ((C, wide), BF),
        ],
        (z2, dz3, dgp, dab, pmask, m5ts, m5s, z1, prod, mots, mofs), deps=deps, raw=(0, 1, 2, 4, 5, 6, 7, 8, 9, 10), far=(0, 1, 3, 4), us=11)


def first_back(n, rows, copies, where, z1, dz2, dgp, dab, pmask, m5ts, m5s, inner, lrt, left_own, outer_w, deps=()):
    opm = outer_w.shape[0]

    def kernel(
        where, z1, dz2, dgp, dab, pmask, m5ts, m5s, inner, lrt, left_own, outer_w,
        dz1, ends, m_oo, m_m5,
        sa, sb, o_x, o_d5, sdi, sdr,
    ):
        m5t, m5 = m5ts.at[0], m5s.at[0]
        take_pair(n, dab, sa, sb)
        sdr[...] = jnp.zeros_like(sdr)
        right_t = b16(lrt[opm : 2 * opm])

        def body(r):
            w = cols(r)
            dz = projections_back(
                n, rows, z1[:, w], dz2[:, w], dgp, r, pmask, m5t, m5, sa, sb, o_x, o_d5
            )
            for u in range(U):
                dz16 = b16(lanes(dz, u).T)
                dz1[r * U + u] = dz16
                at = pl.ds(r * U + u, opm, stride=rows)
                sdi[at, :] = dot(right_t, dz16)
                sdr[...] += dot_nt(b16(inner[at, :]), dz16)

        each_row(rows // U, body)
        left = left_own[:, 0:opm]
        dleft = jnp.zeros((opm, rows), F32)
        for b in range(opm):
            d16 = b16(sdi[b * rows : (b + 1) * rows])
            m_oo[b * opm : (b + 1) * opm] = dot_tn(left, d16)
            dleft = dleft + dot_nt(outer_w[b], d16)
        lane = lax.broadcasted_iota(jnp.int32, (rows, L), 1)
        spot = lax.broadcasted_iota(jnp.int32, (rows, L), 0) + where[1] * rows
        dleft = dot(b16(dleft), b16(jnp.where(lane == spot, 1.0, 0.0)))
        both = jnp.concatenate([dleft, sdr[...]], 0) * lrt[2 * opm : 2 * opm + 1]
        for d in range(copies):
            ends[d] = b16(both)
        for k in range(5):
            s = slice(k * C, (k + 1) * C)
            m_m5[s] = dot_nt(o_x[...], o_d5[s])

    wide = rows * L
    return call(
        kernel,
        [
            ((rows, L, C), BF), ((copies, 2 * opm, L), BF), ((opm * opm, C), F32), ((640, C), F32),
        ],
        [
            ((C * rows, L), F32), ((C * rows, L), F32), ((C, wide), BF), ((640, wide), BF),
            ((opm * rows, C), F32), ((opm, L), F32),
        ],
        (where, z1, dz2, dgp, dab, pmask, m5ts, m5s, inner, lrt, left_own, outer_w), deps=deps, raw=(1, 2, 3, 5, 6, 7, 8, 9, 10, 11), far=(2, 3), us=11)


def last_back(rows, pair, drb, sbt, deps=()):
    def kernel(pair, drb, sbt, grad, m_sb, o_x, o_d):
        def body(r):
            w = cols(r)
            xh, scale = norm_cols(side([f32(pair[r * U + u]).T for u in range(U)]))
            d = get_rows(drb, r, 8, rows)
            d16 = b16(jnp.concatenate([d, jnp.zeros_like(d)], 0))
            back = norm_cols_back(dot_tn(sbt[...], d16), xh, scale)
            for u in range(U):
                grad[r * U + u] = lanes(back, u).T
            o_x[:, w] = b16(xh)
            o_d[:, w] = d16

        each_row(rows // U, body)
        m_sb[...] = dot_nt(o_d[...], o_x[...])

    wide = rows * L
    return call(
        kernel,
        [((rows, L, C), F32), ((HPAD, C), F32)],
        [((C, wide), BF), ((HPAD, wide), BF)],
        (pair, drb, sbt), deps=deps, raw=(0, 1, 2), us=3)


def collect(where, parts, half, deps):
    def kernel(where, *refs):
        sources, (kept, given, rows) = refs[: len(parts)], refs[len(parts) :]
        core = where[3] % 2
        at = 0
        for ref in sources:
            rows[at : at + ref.shape[0]] = ref[...]
            at += ref.shape[0]
        if at < 2 * half:
            rows[at : 2 * half] = jnp.zeros((2 * half - at, C), F32)
        kept[...] = rows[pl.ds(pl.multiple_of(core * half, half), half), :]
        given[...] = b16(rows[pl.ds(pl.multiple_of((1 - core) * half, half), half), :])

    return call(
        kernel,
        [((half, C), F32), ((half, C), BF)],
        [((2 * half, C), F32)],
        (where, *parts),
        deps=deps,
        raw=tuple(range(1, len(parts) + 1)),
        us=3,
    )


def sum_copies(x, extra, count):
    rows, more = x.shape[1], extra.shape[0]

    def kernel(x, extra, out):
        total = b16(jnp.sum(f32(x[...]), 0))
        for d in range(count):
            out[d, 0:rows] = total
            out[d, rows : rows + more] = b16(extra[...])

    return call(kernel, [((count, rows + more, C), BF)], [], (x, extra), us=2)[0]


def finish(where, near, far, gp, gm, mp, mg, mo, ap, ab, pu, sb, places, half, opm, deps):
    def kernel(
        where, near, far, gp, gm, mp, mg, mo, ap, ab, pu, sb,
        g_pg, g_mg, g_sb, g_oo, g_mp, g_mgt, g_mo, g_ap, g_ab, g_ao, g_pu, g_pd,
        rows,
    ):
        core = where[3] % 2
        chips = near.shape[0]
        size = half // chips
        for k in range(chips):
            at = pl.multiple_of(core * half + k * size, 8)
            rows[pl.ds(at, size), :] = f32(near[k, 0:size])
            at = pl.multiple_of((1 - core) * half + k * size, 8)
            rows[pl.ds(at, size), :] = f32(far[k, 0:size])

        def take(name, count, skip=0):
            at = places[name] + skip
            return rows[at : at + count]

        gpv, gmv = f32(gp[...]), f32(gm[...])

        def column(row):
            return jnp.broadcast_to(row, (C, C)).T

        def over_lanes(x):
            return jnp.sum(x.T, 0, keepdims=True)

        def padded(w):
            return jnp.concatenate([f32(w), jnp.zeros((HPAD - w.shape[0], C), F32)], 0)

        total = jnp.zeros((8, C), F32)
        for k in range(chips):
            total = total + (f32(near[k, size : size + 8]) + f32(far[k, size : size + 8]))
        g_pg[0:1] = jnp.sum(f32(sb[...]) * total, 0, keepdims=True)
        g_sb[...] = total * gpv[0:1]
        for t in range(2):
            g = column(gpv[1 + t : 2 + t])
            both = jnp.zeros((C, C), F32)
            for k in range(5):
                m = take("m5%d" % t, C, k * C)
                both = both + m * f32(mp[t, k] if k < 4 else mg[t])
                if k < 4:
                    g_mp[t, k] = m * g
                else:
                    g_mgt[t] = m * g
            g_pg[1 + t : 2 + t] = over_lanes(both)
            m = take("mo%d" % t, C)
            g_mo[t] = m * column(gmv[t : t + 1])
            g_mg[t : t + 1] = over_lanes(m * f32(mo[t]))
            g = column(gpv[3 + t : 4 + t])
            both = jnp.zeros((C, C), F32)
            for k in range(4):
                m = take("a4%d" % t, C, k * C)
                if k == 0:
                    m = m * HD**-0.5
                both = both + m * f32(ap[t, k])
                g_ap[t, k] = m * g
            m = take("ab%d" % t, HPAD)
            g_pg[3 + t : 4 + t] = over_lanes(both) + jnp.sum(padded(ab[t]) * m, 0, keepdims=True)
            g_ab[t] = (m * gpv[3 + t : 4 + t])[0:TH]
            g_ao[t] = take("ao%d" % t, C)
        g = column(gpv[5:6])
        both = jnp.zeros((C, C), F32)
        for k in range(4):
            s = slice(k * C, (k + 1) * C)
            m = take("up", C, k * C)
            both = both + m * f32(pu[:, s])
            g_pu[:, s] = m * g
        g_pg[5:6] = over_lanes(both)
        g_pd[...] = take("dn", 512)
        for b in range(opm):
            g_oo[:, b, :] = take("oo", opm, b * opm)

    outs = [
        (6, C), (2, C), (8, C), (opm, opm, C), (2, 4, C, C), (2, C, C), (2, C, C), (2, 4, C, C),
        (2, TH, C), (2, C, C), (C, 512), (512, C),
    ]
    return call(
        kernel,
        [(s, F32) for s in outs],
        [((2 * half, C), F32)],
        (where, near, far, gp, gm, mp, mg, mo, ap, ab, pu, sb),

        raw=(3, 4, 5, 6, 7, 8, 9, 10, 11), deps=deps, far=tuple(range(12)), us=4,
    )


PRECISE = lax.Precision.HIGHEST


def for_sending(shard):

    def short(part):
        return part.astype(jnp.bfloat16) if part.dtype == jnp.float32 else part

    return jax.tree.map(short, shard)


def widen(operand):
    return operand.astype(jnp.float32)


def narrow(operand):
    return operand.astype(jnp.bfloat16)


def rounded(operand):
    return lax.optimization_barrier(operand.astype(jnp.bfloat16)).astype(jnp.float32)


def contract(pattern, first_term, second_term):
    return jnp.einsum(pattern, first_term, second_term, precision=PRECISE)


def low_product(pattern, first_term, second_term):
    return jnp.einsum(pattern, first_term, second_term, preferred_element_type=jnp.float32)


def norm_rows(operand, gain_vec):
    centre = operand - jnp.mean(operand, -1, keepdims=True)
    spread = jnp.mean(centre * centre, -1, keepdims=True)
    return centre * lax.rsqrt(spread + EPSILON) * gain_vec


def soft_weights(logits):
    highest = jnp.max(logits, -1, keepdims=True)
    raised = jnp.exp(logits - highest)
    return raised / jnp.sum(raised, -1, keepdims=True)


def single_attend(queries, key_rows, values, gate_value, pair_bias, key_bias, weight_out):
    head_count = pair_bias.shape[0]
    feature_width = queries.shape[-1]
    head_size = feature_width // head_count
    query_heads = queries.reshape(queries.shape[0], head_count, head_size)
    key_heads = key_rows.reshape(key_rows.shape[0], head_count, head_size)
    value_heads = values.reshape(values.shape[0], head_count, head_size)
    logits = (
        contract("ihd,jhd->hij", query_heads, key_heads) * head_size ** (-0.5)
        + pair_bias
        + key_bias
    )
    mixed = contract("hij,jhd->ihd", soft_weights(logits), value_heads).reshape(
        queries.shape[0], feature_width
    )
    return contract("is,st->it", mixed * jax.nn.sigmoid(gate_value), weight_out)


def tri_attend(normed, pair_bias, weight_four, weight_out, key_bias):
    head_count = pair_bias.shape[0]
    feature_width = normed.shape[-1]
    head_size = feature_width // head_count

    def one_row(row_in):
        projected = contract("lc,ncd->nld", row_in, weight_four)
        shaped = projected[:3].reshape(3, row_in.shape[0], head_count, head_size)
        logits = (
            contract("jhd,khd->hjk", shaped[0], shaped[1]) * head_size ** (-0.5)
            + pair_bias
            + key_bias
        )
        mixed = contract("hjk,khd->jhd", soft_weights(logits), shaped[2]).reshape(
            row_in.shape[0], feature_width
        )
        return contract("lc,cd->ld", mixed * jax.nn.sigmoid(projected[3]), weight_out)

    return lax.map(jax.checkpoint(one_row), normed)


def mult_front(pair_in, gain_vec, weight_four, weight_gate, pair_mask):
    normed = norm_rows(pair_in, gain_vec)
    projected = contract("rlc,ncm->nmrl", normed, weight_four)
    left_side = jax.nn.sigmoid(projected[0]) * projected[1] * pair_mask
    right_side = jax.nn.sigmoid(projected[2]) * projected[3] * pair_mask
    gate_value = jax.nn.sigmoid(contract("rlc,cd->rld", normed, weight_gate))
    return (left_side, right_side, gate_value)


def mult_back(pair_in, product, gate_value, gain_vec, weight_out):
    centre = product - jnp.mean(product, 0, keepdims=True)
    spread = jnp.mean(centre * centre, 0, keepdims=True)
    scaled = centre * lax.rsqrt(spread + EPSILON) * gain_vec[:, None, None]
    return pair_in + contract("mrl,mc->rlc", scaled, weight_out) * gate_value


def outgoing_forward(left_chan, right_chan):
    return low_product("mik,mjk->mij", left_chan, right_chan)


def outgoing_backward(left_chan, right_chan, grad_out):
    return (
        low_product("mij,mjk->mik", grad_out, right_chan),
        low_product("mij,mik->mjk", grad_out, left_chan),
    )


def incoming_forward(left_chan, right_chan):
    return low_product("mki,mkj->mij", left_chan, right_chan)


def incoming_backward(left_chan, right_chan, grad_out):
    return (
        low_product("mij,mkj->mki", grad_out, right_chan),
        low_product("mij,mki->mkj", grad_out, left_chan),
    )


def to_channels(operand):
    return jax.tree.map(
        lambda part, own: part.astype(own.dtype),
        lax.all_to_all(for_sending(operand), "rows", split_axis=0, concat_axis=1, tiled=True),
        operand,
    )


def to_rows(operand):
    return jax.tree.map(
        lambda part, own: part.astype(own.dtype),
        lax.all_to_all(for_sending(operand), "rows", split_axis=1, concat_axis=0, tiled=True),
        operand,
    )


def turn_cols(operand):
    return jnp.swapaxes(
        lax.all_to_all(operand, "rows", split_axis=1, concat_axis=0, tiled=True), 0, 1
    )


def turn_rows(operand):
    return lax.all_to_all(
        jnp.swapaxes(operand, 0, 1), "rows", split_axis=0, concat_axis=1, tiled=True
    )


def gather_bias(operand):
    return lax.all_gather(operand, "rows", axis=1, tiled=True)


def scatter_bias(operand):
    return lax.psum_scatter(operand, "rows", scatter_dimension=1, tiled=True)


def general_local(
    single_rep,
    pair_rep,
    residue_mask,
    single_gains,
    pair_gains,
    mult_gains,
    single_proj,
    single_bias,
    single_up,
    single_down,
    opm_proj,
    opm_out,
    mult_proj,
    mult_gate,
    mult_out,
    att_proj,
    att_bias,
    att_out,
    pair_up,
    pair_down,
    single_cot,
    pair_cot,
):
    gains_s = widen(single_gains)
    gains_p = widen(pair_gains)
    gains_m = widen(mult_gains)
    proj_s = widen(single_proj)
    bias_sw = widen(single_bias)
    up_s = widen(single_up)
    down_s = widen(single_down)
    proj_o = widen(opm_proj)
    outer_w = widen(opm_out)
    proj_m = widen(mult_proj)
    gate_m = widen(mult_gate)
    out_m = widen(mult_out)
    proj_a = widen(att_proj)
    bias_a = widen(att_bias)
    out_a = widen(att_out)
    up_p = widen(pair_up)
    down_p = widen(pair_down)
    mask_all = widen(residue_mask[0])
    shard_rows = pair_rep.shape[1]
    first_row = lax.axis_index("rows") * shard_rows
    mask_own = lax.dynamic_slice_in_dim(mask_all, first_row, shard_rows, 0)
    key_bias = (mask_all - 1.0) * MASKED
    pair_mask = mask_own[:, None] * mask_all[None, :]
    single_own = widen(single_rep[0])
    pair_own = widen(pair_rep[0])

    def front_single(
        single_in, pair_in, gain_s, gain_z, proj_query, proj_key, proj_value, proj_gate, bias_w
    ):
        normed = norm_rows(single_in, gain_s)
        pair_normed = norm_rows(pair_in, gain_z)
        return (
            contract("rs,st->rt", normed, proj_query),
            contract("rs,st->rt", normed, proj_key),
            contract("rs,st->rt", normed, proj_value),
            contract("rs,st->rt", normed, proj_gate),
            contract("rlc,ch->hrl", pair_normed, bias_w),
        )

    def back_single(
        queries,
        key_rows,
        values,
        gate_value,
        row_bias,
        single_in,
        proj_out,
        gain_t,
        weight_up,
        weight_down,
        gain_o,
        left_w,
        right_w,
    ):
        first_sum = single_in + single_attend(
            queries, key_rows, values, gate_value, row_bias, key_bias, proj_out
        )
        hidden = jax.nn.gelu(contract("rs,st->rt", norm_rows(first_sum, gain_t), weight_up))
        second_sum = first_sum + contract("rt,ts->rs", hidden, weight_down)
        outer_in = norm_rows(second_sum, gain_o)
        left_side = contract("rs,sa->ra", outer_in, left_w) * mask_own[:, None]
        right_side = contract("rs,sa->ra", outer_in, right_w) * mask_own[:, None]
        return (second_sum, left_side, right_side)

    def outer_front(left_side, right_all, pair_in, weight_outer, gain_in, weight_four, weight_gate):
        inner = contract("ia,abc->ibc", left_side, weight_outer)
        updated = pair_in + contract("ibc,jb->ijc", inner, right_all)
        left_m, right_m, gate_value = mult_front(
            updated, gain_in, weight_four, weight_gate, pair_mask
        )
        return (updated, left_m, right_m, gate_value)

    def middle_mult(
        pair_in, product, gate_value, gain_out, weight_out, gain_in, weight_four, weight_gate
    ):
        updated = mult_back(pair_in, product, gate_value, gain_out, weight_out)
        left_m, right_m, gate_next = mult_front(
            updated, gain_in, weight_four, weight_gate, pair_mask
        )
        return (updated, left_m, right_m, gate_next)

    def start_front_general(pair_in, product, gate_value, gain_out, weight_out, gain_start, bias_w):
        updated = mult_back(pair_in, product, gate_value, gain_out, weight_out)
        normed = norm_rows(updated, gain_start)
        return (updated, normed, contract("rlc,ch->hrl", normed, bias_w))

    def start_core(pair_in, normed, bias_all, weight_four, weight_out, gain_end):
        updated = pair_in + tri_attend(normed, bias_all, weight_four, weight_out, key_bias)
        return (updated, norm_rows(updated, gain_end))

    def end_bias(turned, bias_w):
        return contract("rlc,ch->hrl", turned, bias_w)

    def end_core(turned, bias_all, weight_four, weight_out):
        return tri_attend(turned, bias_all, weight_four, weight_out, key_bias)

    def final_pair(pair_in, update, gain_vec, weight_up, weight_down):
        summed = pair_in + update
        hidden = jax.nn.gelu(contract("rlc,cd->rld", norm_rows(summed, gain_vec), weight_up))
        return summed + contract("rld,dc->rlc", hidden, weight_down)

    outs_one, back_one = jax.vjp(
        front_single,
        single_own,
        pair_own,
        gains_s[0],
        gains_p[0],
        proj_s[0],
        proj_s[1],
        proj_s[2],
        proj_s[3],
        bias_sw,
    )
    queries, keys_own, values_own, gate_single, row_bias = outs_one
    keys_all, values_all = (
        lax.all_gather(narrow(keys_own), "rows", axis=0, tiled=True),
        lax.all_gather(narrow(values_own), "rows", axis=0, tiled=True),
    )
    outs_two, back_two = jax.vjp(
        back_single,
        queries,
        widen(keys_all),
        widen(values_all),
        gate_single,
        row_bias,
        single_own,
        proj_s[4],
        gains_s[1],
        up_s,
        down_s,
        gains_s[2],
        proj_o[0],
        proj_o[1],
    )
    single_next, left_outer, right_outer = outs_two
    right_all = widen(lax.all_gather(narrow(right_outer), "rows", axis=0, tiled=True))
    outs_three, back_three = jax.vjp(
        outer_front,
        rounded(left_outer),
        right_all,
        pair_own,
        outer_w,
        gains_p[1],
        proj_m[0],
        gate_m[0],
    )
    pair_one, left_first, right_first, gate_first = outs_three
    chan_left, chan_right = to_channels((narrow(left_first), narrow(right_first)))
    product_one = outgoing_forward(chan_left, chan_right)
    rows_one = widen(to_rows(narrow(product_one)))
    outs_five, back_five = jax.vjp(
        middle_mult,
        pair_one,
        rows_one,
        gate_first,
        gains_m[0],
        out_m[0],
        gains_p[2],
        proj_m[1],
        gate_m[1],
    )
    pair_two, left_second, right_second, gate_second = outs_five
    chan_left_two, chan_right_two = to_channels((narrow(left_second), narrow(right_second)))
    product_two = incoming_forward(chan_left_two, chan_right_two)
    rows_two = widen(to_rows(narrow(product_two)))
    outs_seven, back_seven = jax.vjp(
        start_front_general, pair_two, rows_two, gate_second, gains_m[1], out_m[1], gains_p[3], bias_a[0]
    )
    pair_three, normed_start, bias_start = outs_seven
    bias_start_all = widen(gather_bias(narrow(bias_start)))
    outs_eight, back_eight = jax.vjp(
        start_core, pair_three, normed_start, bias_start_all, proj_a[0], out_a[0], gains_p[4]
    )
    pair_four, normed_end = outs_eight
    turned = widen(turn_cols(narrow(normed_end)))
    bias_end, back_nine = jax.vjp(end_bias, turned, bias_a[1])
    bias_end_all = widen(gather_bias(narrow(bias_end)))
    update_turned, back_ten = jax.vjp(end_core, turned, bias_end_all, proj_a[1], out_a[1])
    update = widen(turn_rows(narrow(update_turned)))
    pair_six, back_eleven = jax.vjp(final_pair, pair_four, update, gains_p[5], up_p, down_p)
    grad_four, grad_update, g_pg5, g_pu, g_pd = back_eleven(widen(pair_cot[0]))
    g_pg5, g_pu, g_pd = (g_pg5, g_pu, g_pd)
    grad_turned_update = widen(turn_cols(narrow(grad_update)))
    grad_turned_a, grad_bias_end_all, g_ap1, g_ao1 = back_ten(grad_turned_update)
    g_ap1, g_ao1 = (g_ap1, g_ao1)
    grad_bias_end = rounded(scatter_bias(grad_bias_end_all))
    grad_turned_b, g_ab1 = back_nine(grad_bias_end)
    grad_normed_end = widen(turn_rows(narrow(grad_turned_a + grad_turned_b)))
    grad_three, grad_normed_start, grad_bias_start_all, g_ap0, g_ao0, g_pg4 = back_eight(
        (grad_four, grad_normed_end)
    )
    g_ap0, g_ao0, g_pg4 = (g_ap0, g_ao0, g_pg4)
    grad_bias_start = rounded(scatter_bias(grad_bias_start_all))
    grad_two, grad_rows_two, grad_gate_second, g_mg1, g_mo1, g_pg3, g_ab0 = back_seven(
        (grad_three, grad_normed_start, grad_bias_start)
    )
    g_mg1, g_mo1, g_pg3, g_ab0 = (g_mg1, g_mo1, g_pg3, g_ab0)
    grad_chan_left_two, grad_chan_right_two = incoming_backward(
        chan_left_two, chan_right_two, to_channels(narrow(grad_rows_two))
    )
    grad_left_second, grad_right_second = to_rows(
        (narrow(grad_chan_left_two), narrow(grad_chan_right_two))
    )
    grad_one, grad_rows_one, grad_gate_first, g_mg0, g_mo0, g_pg2, g_mp1, g_mgt1 = back_five(
        (grad_two, widen(grad_left_second), widen(grad_right_second), grad_gate_second)
    )
    g_mg0, g_mo0, g_pg2, g_mp1, g_mgt1 = (g_mg0, g_mo0, g_pg2, g_mp1, g_mgt1)
    grad_chan_left, grad_chan_right = outgoing_backward(
        chan_left, chan_right, to_channels(narrow(grad_rows_one))
    )
    grad_left_first, grad_right_first = to_rows((narrow(grad_chan_left), narrow(grad_chan_right)))
    grad_left_outer, grad_right_all, grad_pair_a, g_oo, g_pg1, g_mp0, g_mgt0 = back_three(
        (grad_one, widen(grad_left_first), widen(grad_right_first), grad_gate_first)
    )
    g_oo, g_pg1, g_mp0, g_mgt0 = (g_oo, g_pg1, g_mp0, g_mgt0)
    grad_right_outer = rounded(
        lax.psum_scatter(grad_right_all, "rows", scatter_dimension=0, tiled=True)
    )
    two_grads = back_two((widen(single_cot[0]), rounded(grad_left_outer), grad_right_outer))
    grad_query, grad_keys_all, grad_values_all, grad_gate_single, grad_row_bias, grad_single_a = (
        two_grads[:6]
    )
    g_sp4, g_sg1, g_su, g_sd, g_sg2, g_op0, g_op1 = tuple(two_grads[6:])
    grad_keys, grad_values = (
        lax.psum_scatter(grad_keys_all, "rows", scatter_dimension=0, tiled=True),
        lax.psum_scatter(grad_values_all, "rows", scatter_dimension=0, tiled=True),
    )
    grad_single_b, grad_pair_b, g_sg0, g_pg0, g_sp0, g_sp1, g_sp2, g_sp3, g_sb = back_one(
        (grad_query, rounded(grad_keys), rounded(grad_values), grad_gate_single, grad_row_bias)
    )
    g_sg0, g_pg0, g_sp0, g_sp1, g_sp2, g_sp3, g_sb = (
        g_sg0,
        g_pg0,
        g_sp0,
        g_sp1,
        g_sp2,
        g_sp3,
        g_sb,
    )
    weight_totals = (
        jnp.stack([g_sg0, g_sg1, g_sg2]),
        jnp.stack([g_pg0, g_pg1, g_pg2, g_pg3, g_pg4, g_pg5]),
        jnp.stack([g_mg0, g_mg1]),
        jnp.stack([g_sp0, g_sp1, g_sp2, g_sp3, g_sp4]),
        g_sb,
        g_su,
        g_sd,
        jnp.stack([g_op0, g_op1]),
        g_oo,
        jnp.stack([g_mp0, g_mp1]),
        jnp.stack([g_mgt0, g_mgt1]),
        jnp.stack([g_mo0, g_mo1]),
        jnp.stack([g_ap0, g_ap1]),
        jnp.stack([g_ab0, g_ab1]),
        jnp.stack([g_ao0, g_ao1]),
        g_pu,
        g_pd,
    )
    weight_totals = lax.psum(
        (
            weight_totals[0],
            weight_totals[1],
            weight_totals[2],
            weight_totals[3],
            weight_totals[4],
            weight_totals[5],
            weight_totals[6],
            weight_totals[7],
            weight_totals[8],
            weight_totals[9],
            weight_totals[10],
            weight_totals[11],
            weight_totals[12],
            weight_totals[13],
            weight_totals[14],
            weight_totals[15],
            weight_totals[16],
        ),
        ("grp", "rows"),
    )
    return (
        narrow(single_next)[None],
        narrow(pair_six)[None],
        (grad_single_a + grad_single_b)[None],
        (grad_pair_a + grad_pair_b)[None],
    ) + tuple(weight_totals)


def pad_rows(x, count):
    return jnp.concatenate([x, jnp.zeros((count - x.shape[0],) + x.shape[1:], x.dtype)], 0)


def fast_local(square, row_count):
    n = row_count
    rows = L // n
    part = L * rows // n
    crops = 4
    total = crops * n

    def home(g, r):
        if square and (r // 2) // 2 != g % 2:
            g, r = g ^ 1, ((r // 2) ^ 2) * 2 + r % 2
        return g * n + r

    groups = [[home(g, r) for r in range(n)] for g in range(crops)]

    def swap(x):
        if not square:
            return x
        return lax.ppermute(x, AX, [(g * n + r, home(g, r)) for g in range(crops) for r in range(n)])

    def exchange(x):
        if square:
            return lax.all_to_all(x, AX, 0, 0, tiled=True, axis_index_groups=groups)
        return lax.all_to_all(x, "rows", 0, 0, tiled=True)

    def to_all(copies):
        return lax.all_to_all(copies, AX, 0, 0, tiled=True)

    chips = total // 2
    same_core = [[g * n + z * 2 + c for g in range(crops) for z in range(n // 2)] for c in range(2)]
    members = [sorted(set(d // 2 for d in group)) for group in groups]

    def other_core(x):
        return lax.ppermute(x, "rows", [(i, i ^ 1) for i in range(n)])

    def to_chips(copies):
        return lax.all_to_all(copies, AX, 0, 0, tiled=True, axis_index_groups=same_core)

    def local(
        single_rep, pair_rep, residue_mask, single_gains, pair_gains, mult_gains, single_proj,
        single_bias, single_up, single_down, opm_proj, opm_out, mult_proj, mult_gate, mult_out,
        att_proj, att_bias, att_out, pair_up, pair_down, single_cot, pair_cot,
    ):
        grp, row = lax.axis_index("grp"), lax.axis_index("rows")
        crop, block = grp, row
        if square:
            moved = (row // 4) != grp % 2
            crop = jnp.where(moved, grp ^ 1, grp)
            block = jnp.where(moved, row ^ 4, row)
        where = jnp.stack([crop, block, grp, row]).astype(jnp.int32)
        single, width = single_rep[0], single_rep.shape[2]
        gathered = lax.all_to_all(
            jnp.broadcast_to(single, (n,) + single.shape), "rows", 0, 0, tiled=True
        )
        pair = swap(pair_rep[0])
        att_b, single_b = jnp.swapaxes(att_bias, 1, 2), single_bias.T
        m5t, m5, mot, mof, a4t, a4, aot, abt, upt, up, dnt, sbt = prep_weights(
            pair_gains, mult_gains, mult_proj, mult_gate, mult_out, att_proj, att_b, att_out,
            pair_up, pair_down, single_b,
        )
        opm = opm_proj.shape[2]
        outer = jnp.swapaxes(opm_proj, 0, 1).reshape(width, 2 * opm)
        outer = jnp.pad(outer, ((0, 0), (0, L - 2 * opm)))
        outer_w = jnp.swapaxes(opm_out, 0, 1)
        mask_row = f32(residue_mask)
        mine, mask_col = pack(rows, single, single_cot[0], pair_rep[0], mask_row, sbt, where)
        single_out, lr = single_own(
            n, rows, total, gathered, mine, mask_col, single_gains, single_proj, single_up,
            single_down, outer,
        )
        lr = to_all(lr)

        z1, ab1, pmask, key_row, inner, lrt, left_own = front(
            n, rows, where, lr, pair, outer_w, m5t
        )
        ab1 = exchange(ab1)
        p1 = exchange(channel_product(n, rows, True, ab1)).reshape(C * rows, L)
        z2, ab2 = middle(n, rows, z1, p1, mot, pmask, m5t)
        ab2 = exchange(ab2)
        p2 = exchange(channel_product(n, rows, False, ab2)).reshape(C * rows, L)
        z3, tb = start_front(n, rows, z2, p2, m5t, mot, abt)
        cot = swap(copies_of(pair_cot[0], 1, (p2,))[0])
        tb, cot = lax.optimization_barrier((tb, cot))
        tb_all = exchange(tb)
        cot = jnp.transpose(cot.reshape(rows, n, rows, C), (1, 2, 0, 3))
        tb_all, cot = lax.optimization_barrier((tb_all, cot))
        cot = exchange(cot)
        z4, turn = start_attention(n, rows, z3, tb_all, key_row, a4t, aot, abt)
        turn, cot = lax.optimization_barrier((turn, cot))
        cot = jnp.swapaxes(cot, 0, 1).reshape(rows, L, C)
        turn = exchange(turn)
        copies = to_chips(copies_of(mine, chips, (turn,)))
        others = other_core(copies)

        pout, back, m_up, m_dn, m_a41, m_ao1 = end_both(
            n, rows, turn, cot, key_row, a4t, a4, aot, att_out, upt, up, dnt, pair_down
        )
        back = exchange(back)
        pout = exchange(pout).reshape(n, rows, rows, C)
        pair_six = swap(jnp.swapaxes(pout, 0, 1).reshape(rows, L, C))

        dz4, dxs, dtb, m_a40, m_ao0, m_ab1 = start_back(
            n, rows, z3, z4, back, tb_all, key_row, a4t, a4, att_out, abt, deps=(copies, others)
        )
        dtb = exchange(dtb)
        dz3, dgp2, dp2, m_ab0, m_mo1 = third_back(
            n, rows, z3, dz4, dxs, dtb, abt, z2, p2, m5t, mot, mof, deps=(pout,)
        )
        dp2 = exchange(dp2.reshape(n, part, L))
        dab2 = channel_product_back(n, rows, False, ab2, dp2)
        kept = single_every(
            n, rows, where, copies, others, single_gains, single_proj, single_up, single_down,
            deps=(dab2,),
        )
        dab2 = exchange(dab2)
        dz2, dgp1, dp1, m_m51, m_mo0 = second_back(
            n, rows, z2, dz3, dgp2, dab2, pmask, m5t, m5, z1, p1, mot, mof, deps=(pair_six, kept[0])
        )
        dp1 = exchange(dp1.reshape(n, part, L))
        dab1 = exchange(channel_product_back(n, rows, True, ab1, dp1))
        dz1, ends, m_oo, m_m50 = first_back(
            n, rows, chips, where, z1, dz2, dgp1, dab1, pmask, m5t, m5, inner, lrt, left_own,
            outer_w,
        )
        ends = to_chips(ends)
        others_ends = other_core(ends)
        dz1 = swap(copies_of(dz1, 1, (others_ends,))[0])
        names = [
            "up", "dn", "a41", "ao1", "a40", "ao0", "m51", "mo1", "mo0", "m50", "oo", "ab1", "ab0",
        ]
        sums = [
            m_up, m_dn, m_a41, m_ao1, m_a40, m_ao0, m_m51, m_mo1, m_mo0, m_m50, m_oo, m_ab1, m_ab0,
        ]
        places, at = {}, 0
        for name, m in zip(names, sums):
            places[name] = at
            at += m.shape[0]
        half = -(-at // (total * 16)) * total * 8
        near, far = collect(where, sums, half, (ends, others_ends))
        near = b16(near + f32(other_core(far)))
        near = to_chips(near.reshape(chips, half // chips, C))
        ys, g_sg, d_own, drb, m_op = single_back(
            members, rows, where, ends, others_ends, kept, single_gains, single_proj,
            single_up, single_down, outer,
        )
        pair_grad, m_sb = last_back(rows, pair_rep[0], drb, sbt, deps=(dz1,))
        near_sums = sum_copies(near, m_sb, chips)
        g_sp, g_su, g_sd = weight_grads(kept[2], ys, width, single_up.shape[1], near_sums)
        pair_grad = pair_grad + f32(dz1)
        g_op = jnp.swapaxes(m_op[:, : 2 * opm].reshape(width, 2, opm), 0, 1)

        near = copies_of(to_chips(near_sums), 1, (g_sp, g_su, g_sd))[0]
        grads = finish(
            where, near, other_core(near), pair_gains, mult_gains, mult_proj, mult_gate,
            mult_out, att_proj, att_b, pair_up, single_b, places, half, opm, (),
        )
        g_pg, g_mg, g_sb, g_oo, g_mp, g_mgt, g_mo, g_ap, g_ab, g_ao, g_pu, g_pd = grads
        return (
            single_out[None],
            pair_six[None],
            d_own[None],
            pair_grad[None],
            g_sg,
            g_pg,
            g_mg,
            g_sp,
            g_sb.T,
            g_su,
            g_sd,
            g_op,
            g_oo,
            g_mp,
            g_mgt,
            g_mo,
            g_ap,
            jnp.swapaxes(g_ab, 1, 2),
            g_ao,
            g_pu,
            g_pd,
        )

    return local


def solution(mesh):
    groups_of, n = mesh.shape["grp"], mesh.shape["rows"]
    whole = P()
    in_specs = (
        (P("grp", "rows", None), P("grp", "rows", None, None), P("grp", None))
        + (whole,) * 17
        + (P("grp", "rows", None), P("grp", "rows", None, None))
    )
    out_specs = (
        P("grp", "rows", None),
        P("grp", "rows", None, None),
        P("grp", "rows", None),
        P("grp", "rows", None, None),
    ) + (whole,) * 17
    if L % n == 0 and (L // n) % 16 == 0:
        body = fast_local((groups_of, n) == (4, 8), n)
    else:
        body = general_local
    return jax.shard_map(body, mesh=mesh, in_specs=in_specs, out_specs=out_specs, check_vma=False)
```

```python
import math

import jax
import jax.numpy as jnp
from jax import lax
from jax.experimental import pallas as pl
from jax.experimental.pallas import tpu as pltpu
from jax.sharding import PartitionSpec as P

BF = jnp.bfloat16
F32 = jnp.float32
EPSILON = 1e-05
MASKED = 1000000000.0
AX = ("grp", "rows")
L = 128
C = 128
TH = 4
HD = 32
HPAD = 16


def dot(a, b):
    return lax.dot_general(a, b, (((1,), (0,)), ((), ())), preferred_element_type=F32)


def dot_nt(a, b):
    return lax.dot_general(a, b, (((1,), (1,)), ((), ())), preferred_element_type=F32)


def dot_tn(a, b):
    return lax.dot_general(a, b, (((0,), (0,)), ((), ())), preferred_element_type=F32)


def b16(x):
    return x.astype(BF)


def f32(x):
    return x.astype(F32)


def sig(x):
    return 0.5 * jnp.tanh(0.5 * x) + 0.5


GELU_A = 0.7978845608028654
GELU_B = 0.044715


def gelu_parts(x):
    t = jnp.tanh(GELU_A * (x + GELU_B * x * x * x))
    half = 0.5 * (1.0 + t)
    slope = half + 0.5 * x * (1.0 - t * t) * (GELU_A * (1.0 + 3.0 * GELU_B * x * x))
    return x * half, slope


def norm_cols(z):
    c = z - jnp.mean(z, 0, keepdims=True)
    scale = lax.rsqrt(jnp.mean(c * c, 0, keepdims=True) + EPSILON)
    return c * scale, scale


def norm_cols_back(dx, xh, scale):
    return scale * (
        dx - jnp.mean(dx, 0, keepdims=True) - xh * jnp.mean(dx * xh, 0, keepdims=True)
    )


U = 16


def cols(r):
    return pl.ds(pl.multiple_of(r * U * L, U * L), U * L)


def side(parts):
    return jnp.concatenate(parts, 1)


def lanes(x, u):
    return x[:, u * L : (u + 1) * L]


def get_rows(ref, r, count, rows):
    return side([ref[pl.ds(r * U + u, count, stride=rows), :] for u in range(U)])


def put_rows(ref, r, count, rows, x):
    for u in range(U):
        ref[pl.ds(r * U + u, count, stride=rows), :] = lanes(x, u)


def put_turned(ref, r, rows, x):
    for u in range(U):
        ref[pl.ds(r * U + u, L, stride=rows), :] = lanes(x, u).T


def get_turned(ref, r, rows):
    return side(
        [
            f32(ref[:, pl.ds(pl.multiple_of((r * U + u) * rows, rows), rows), :].reshape(L, C)).T
            for u in range(U)
        ]
    )


def each_row(count, body):
    def step(r, carry):
        body(r)
        return carry

    lax.fori_loop(0, count, step, 0, unroll=1)


def call(kernel, outs, scratch, args, deps=(), raw=(), late=(), far=(), us=5):
    count, more, given = len(args), len(deps), len(outs)
    fetched = [args[k] for k in raw]

    def body(*refs):
        mine = list(refs[:count])
        results = list(refs[count + more : count + more + given])
        rest = list(refs[count + more + given :])
        sems = rest.pop() if raw or far else None
        stores = [rest.pop() for _ in far][::-1]
        held = [rest.pop() for _ in raw][::-1]
        moves = {}
        for i, k in enumerate(raw):
            moves[k] = pltpu.make_async_copy(mine[k], held[i], sems.at[i])
            moves[k].start()
        for k in raw:
            if k not in late:
                moves[k].wait()
        for i, k in enumerate(raw):
            mine[k] = held[i]
        ends = []
        for i, k in enumerate(far):
            ends.append(pltpu.make_async_copy(stores[i], results[k], sems.at[len(raw) + i]))
            results[k] = stores[i]
        if late:
            kernel(lambda k: moves[k].wait(), *mine, *results, *rest)
        else:
            kernel(*mine, *results, *rest)
        for end in ends:
            end.start()
        for end in ends:
            end.wait()

    vm = pl.BlockSpec(memory_space=pltpu.VMEM)
    sm = pl.BlockSpec(memory_space=pltpu.SMEM)
    away = pl.BlockSpec(memory_space=pl.ANY)
    moved = sum(a.size * a.dtype.itemsize for a in args)
    buffers = [pltpu.VMEM(s, d) for s, d in scratch]
    buffers += [pltpu.VMEM(a.shape, a.dtype) for a in fetched]
    buffers += [pltpu.VMEM(*outs[k]) for k in far]
    placed = sum(math.prod(b.shape) * jnp.dtype(b.dtype).itemsize for b in buffers)
    if raw or far:
        buffers.append(pltpu.SemaphoreType.DMA((len(raw) + len(far),)))
    return pl.pallas_call(
        body,
        out_shape=[
            pltpu.HBM(s, d) if k in far else jax.ShapeDtypeStruct(s, d)
            for k, (s, d) in enumerate(outs)
        ],
        in_specs=[
            away if k in raw else sm if a.dtype == jnp.int32 else vm for k, a in enumerate(args)
        ]
        + [away] * more,
        out_specs=[away if k in far else vm for k in range(given)],
        scratch_shapes=buffers,
        compiler_params=pltpu.CompilerParams(vmem_limit_bytes=(30 << 20) + placed),
        cost_estimate=pl.CostEstimate(flops=us * 10**9, bytes_accessed=moved if us else 0, transcendentals=0),
    )(
        *[
            pltpu.with_memory_space_constraint(a, pltpu.HBM) if k in raw else a
            for k, a in enumerate(args)
        ],
        *[pltpu.with_memory_space_constraint(d, pltpu.HBM) for d in deps],
    )


def prep_weights(gp, gm, mp, mg, mo, ap, ab, ao, pu, pd, sb):
    def kernel(
        gp, gm, mp, mg, mo, ap, ab, ao, pu, pd, sb,
        m5t, m5, mot, mof, a4t, a4, aot, abt, upt, up, dnt, sbt,
    ):
        gpv = f32(gp[...])
        gmv = f32(gm[...])

        def padded(w):
            return jnp.concatenate([f32(w), jnp.zeros((HPAD - w.shape[0], C), F32)], 0)

        for t in range(2):
            g = gpv[1 + t : 2 + t]
            for k in range(5):
                w = f32(mp[t, k] if k < 4 else mg[t]).T * g
                m5t[t, k * C : (k + 1) * C] = b16(w)
                m5[t, :, k * C : (k + 1) * C] = b16(w.T)
            w = f32(mo[t]).T * gmv[t : t + 1]
            mot[t] = b16(w)
            mof[t] = b16(w.T)
            g = gpv[3 + t : 4 + t]
            for k in range(4):
                w = f32(ap[t, k]).T * (g * HD**-0.5 if k == 0 else g)
                a4t[t, k * C : (k + 1) * C] = b16(w)
                a4[t, :, k * C : (k + 1) * C] = b16(w.T)
            aot[t] = b16(f32(ao[t]).T)
            abt[t] = b16(padded(ab[t]) * g)
        g = gpv[5:6]
        for k in range(4):
            s = slice(k * C, (k + 1) * C)
            w = f32(pu[:, s]).T * g
            upt[s] = b16(w)
            up[:, s] = b16(w.T)
            dnt[:, s] = b16(f32(pd[s]).T)
        sbt[...] = b16(padded(sb[...]) * gpv[0:1])

    outs = [
        ((2, 640, C), BF), ((2, C, 640), BF), ((2, C, C), BF), ((2, C, C), BF),
        ((2, 512, C), BF), ((2, C, 512), BF), ((2, C, C), BF), ((2, HPAD, C), BF),
        ((512, C), BF), ((C, 512), BF), ((C, 512), BF), ((HPAD, C), BF),
    ]
    return call(kernel, outs, [], (gp, gm, mp, mg, mo, ap, ab, ao, pu, pd, sb), raw=(0, 1, 2, 3, 4, 5, 6, 7, 8, 9, 10), far=(0, 1, 2, 3, 4, 5, 6, 7, 8, 9, 10, 11), us=3)


def pack(rows, single, cot, pair, mask, sbt, where):
    def kernel(single, cot, pair, mask, sbt, where, mine, mask_col, s, sm):
        sm[...] = jnp.broadcast_to(mask[...], (L, L)).T
        mask_col[...] = sm[pl.ds(pl.multiple_of(where[3] * rows, rows), rows), :]
        key_row = (mask[...] - 1.0) * MASKED

        def body(r):
            xh, _ = norm_cols(side([f32(pair[r * U + u]).T for u in range(U)]))
            put_rows(s, r, HPAD, rows, dot(sbt[...], b16(xh)) + side([key_row] * U))

        each_row(rows // U, body)
        mine[0:rows] = single[...]
        mine[rows : 2 * rows] = cot[...]
        for h in range(8):
            mine[rows * (2 + h // 4) : rows * (3 + h // 4), (h % 4) * L : (h % 4 + 1) * L] = b16(
                s[h * rows : (h + 1) * rows]
            )

    width = single.shape[1]
    return call(
        kernel,
        [((4 * rows, width), BF), ((rows, L), F32)],
        [((HPAD * rows, L), F32), ((L, L), F32)],
        (single, cot, pair, mask, sbt, where), raw=(0, 1, 2, 4), us=2)


def copies_of(x, count, deps):
    def kernel(x, out):
        for d in range(count):
            out[d] = x[...]

    return call(kernel, [((count,) + x.shape, x.dtype)], [], (x,), deps=deps)[0]


def deal(n, rows, where, x, deps):
    def kernel(where, x, *outs):
        for k in range(n):
            block = lax.rem(where[3] + k, n)
            at = pl.ds(pl.multiple_of(block * rows, rows), rows)
            outs[k][...] = x[:, at, :].reshape(rows * rows, C)

    return call(
        kernel, [((rows * rows, C), BF)] * n, [], (where, x), deps=deps, raw=(1,),
        far=tuple(range(n)), us=1,
    )


def undeal(n, rows, where, parts):
    def kernel(where, *refs):
        out = refs[n]
        for k in range(n):
            block = lax.rem(where[3] + n - k, n)
            at = pl.ds(pl.multiple_of(block * rows, rows), rows)
            out[:, at, :] = refs[k][...].reshape(rows, rows, C)

    return call(
        kernel, [((rows, L, C), BF)], [], (where, *parts), raw=tuple(range(1, n + 1)), far=(0,),
        us=1,
    )[0]


def part_of(x, first, last, deps):
    def kernel(x, out):
        out[...] = x[first:last]

    return call(
        kernel, [((last - first,) + x.shape[1:], x.dtype)], [], (x,), deps=deps, raw=(0,), us=1
    )[0]


def norm_rows16(x):
    c = x - jnp.mean(x, -1, keepdims=True)
    scale = lax.rsqrt(jnp.mean(c * c, -1, keepdims=True) + EPSILON)
    return c * scale, scale


def norm_rows16_back(dx, xh, scale):
    return scale * (
        dx - jnp.mean(dx, -1, keepdims=True) - xh * jnp.mean(dx * xh, -1, keepdims=True)
    )


def halves():
    lane = lax.broadcasted_iota(jnp.int32, (1, L), 1)
    low = jnp.where(lane < L // 2, 1.0, 0.0)
    return b16(low), b16(1.0 - low)


def pair_weights(q, k, bias0, bias1):
    out = []
    for m, bias in zip(halves(), (bias0, bias1)):
        s = dot_nt(q * m, k) + bias
        e = jnp.exp(s - jnp.max(s, -1, keepdims=True))
        out.append(b16(e / jnp.sum(e, -1, keepdims=True)))
    return out


def on_halves(x, axis=0):
    return jnp.concatenate([x * m for m in halves()], axis)


def single_own(n, rows, copies, gathered, mine, mask_col, gains, proj, up, down, outer):
    width = up.shape[0]
    opm2 = 64

    def kernel(arrive, gathered, mine, mask_col, gains, proj, up, down, outer, out, lr):
        g = f32(gains[...])
        sn = b16(norm_rows16(f32(gathered[...].reshape(n * rows, width)))[0] * g[0:1])
        arrive(4)
        keys, vals = b16(dot(sn, proj[1])), b16(dot(sn, proj[2]))
        x = f32(mine[0:rows])
        sn = b16(norm_rows16(x)[0] * g[0:1])
        query = b16(dot(sn, proj[0]) * 0.125)
        gate = sig(dot(sn, proj[3]))
        mixed = []
        for t in range(4):
            s = slice(t * L, (t + 1) * L)
            bias = [
                f32(mine[rows * (2 + h // 4) : rows * (3 + h // 4), (h % 4) * L : (h % 4 + 1) * L])
                for h in (2 * t, 2 * t + 1)
            ]
            p = pair_weights(query[:, s], keys[:, s], *bias)
            mixed.append(dot(jnp.concatenate(p, 1), on_halves(vals[:, s])))
        mixed = jnp.concatenate(mixed, 1)
        first = x + dot(b16(mixed * gate), proj[4])
        x1 = b16(norm_rows16(first)[0] * g[1:2])
        arrive(5)
        hidden = b16(gelu_parts(dot(x1, up[...]))[0])
        arrive(6)
        second = first + dot(hidden, down[...])
        out[...] = b16(second)
        x2 = b16(norm_rows16(second)[0] * g[2:3])
        both = dot(x2, outer[...]) * mask_col[...]
        lane = lax.broadcasted_iota(jnp.int32, (rows, L), 1)
        both = b16(jnp.where(lane >= opm2, mask_col[...], both))
        for d in range(copies):
            lr[d] = both

    return call(
        kernel,
        [((rows, width), BF), ((copies, rows, L), BF)],
        [],
        (gathered, mine, mask_col, gains, proj, up, down, outer), raw=(3, 4, 5, 6, 7), late=(4, 5, 6), us=6)


def single_every(n, rows, where, ga, gb, gains, proj, up, down, deps=()):
    width, wide = up.shape
    tokens = 4 * L
    half = ga.shape[0]

    def kernel(
        arrive, where, ga, gb, gains, proj, up, down,
        x_all, cot_all, xs, qkv, gm, probs, slope, first_out, second_out, held,
    ):
        core = where[3] % 2
        for k in range(half):
            held[2 * k + core] = ga[k]
            held[2 * k + 1 - core] = gb[k]
        g = f32(gains[...])

        def body(step):
            rs = pl.ds(pl.multiple_of(step * 2 * L, 2 * L), 2 * L)
            ds = pl.ds(step * 2 * n, 2 * n)
            x16 = held[ds, 0:rows, :].reshape(2 * L, width)
            x_all[rs, :] = x16
            cot_all[rs, :] = held[ds, rows : 2 * rows, :].reshape(2 * L, width)
            x = f32(x16)
            sn = b16(norm_rows16(x)[0] * g[0:1])
            xs[rs, 0:width] = sn

            if step == 0:
                arrive(4)

            query = b16(dot(sn, proj[0]) * 0.125)
            keys, vals = b16(dot(sn, proj[1])), b16(dot(sn, proj[2]))
            qkv[rs, 0:width] = query
            qkv[rs, width : 2 * width] = keys
            qkv[rs, 2 * width : 3 * width] = vals
            gate = sig(dot(sn, proj[3]))
            mixed = []
            for u in range(2):
                crop = step * 2 + u
                own = pl.ds(crop * n, n)
                part = slice(u * L, (u + 1) * L)
                outs = []
                for t in range(4):
                    s = slice(t * L, (t + 1) * L)
                    bias = [
                        f32(
                            held[
                                own,
                                rows * (2 + h // 4) : rows * (3 + h // 4),
                                (h % 4) * L : (h % 4 + 1) * L,
                            ].reshape(L, L)
                        )
                        for h in (2 * t, 2 * t + 1)
                    ]
                    p = pair_weights(query[part, s], keys[part, s], *bias)
                    for k in range(2):
                        at = pl.multiple_of((crop * 8 + 2 * t + k) * L, L)
                        probs[pl.ds(at, L), :] = p[k]
                    outs.append(dot(jnp.concatenate(p, 1), on_halves(vals[part, s])))
                mixed.append(jnp.concatenate(outs, 1))
            mixed = jnp.concatenate(mixed, 0)
            gm[rs, 0:width] = b16(gate)
            gm[rs, width : 2 * width] = b16(mixed)
            u = b16(mixed * gate)
            xs[rs, width : 2 * width] = u
            first = x + dot(u, proj[4])
            first_out[rs, :] = first
            x1 = b16(norm_rows16(first)[0] * g[1:2])
            xs[rs, 2 * width : 3 * width] = x1

            if step == 0:
                arrive(5)
                arrive(6)

            hid, slp = gelu_parts(dot(x1, up[...]))
            h16 = b16(hid)
            xs[rs, 3 * width : 3 * width + wide] = h16
            slope[rs, :] = b16(slp)
            second_out[rs, :] = first + dot(h16, down[...])

        for step in range(2):
            body(step)

    return call(
        kernel,
        [
            ((tokens, width), BF), ((tokens, width), BF), ((tokens, 3 * width + wide), BF),
            ((tokens, 3 * width), BF), ((tokens, 2 * width), BF), ((4 * 8 * L, L), BF),
            ((tokens, wide), BF), ((tokens, width), F32), ((tokens, width), F32),
        ],
        [((2 * half, 4 * rows, width), BF)],
        (where, ga, gb, gains, proj, up, down),
        deps=deps, raw=(1, 2, 3, 4, 5, 6), late=(4, 5, 6), far=(0, 1, 2, 3, 4, 5, 6, 7, 8), us=19)


def single_back(members, rows, where, ea, eb, kept, gains, proj, up, down, outer, deps=()):
    width, wide = up.shape
    tokens = 4 * L
    x_all, cot_all, _, qkv, gm, probs, slope, first_in, second_in = kept

    def kernel(
        arrive, where, ea, eb, x_all, cot_all, qkv, gm, probs, slope, first_in, second_in,
        gains, proj, up, down, outer,
        ys, gain_grad, d_own, drb, m_op,
        dlr, o_x2, sdrb, sds,
    ):
        g = f32(gains[...])
        gain_grad[...] = jnp.zeros_like(gain_grad)
        for crop in range(4):
            total = f32(ea[members[crop][0]]) + f32(eb[members[crop][0]])
            for k in members[crop][1:]:
                total = total + (f32(ea[k]) + f32(eb[k]))
            total = jnp.concatenate([total, jnp.zeros_like(total)], 0)
            dlr[crop * L : (crop + 1) * L] = b16(total.T)

        def body(step):
            rs = pl.ds(pl.multiple_of(step * 2 * L, 2 * L), 2 * L)
            x2, sc2 = norm_rows16(second_in[rs, :])
            o_x2[rs, :] = b16(x2 * g[2:3])
            dx = dot_nt(dlr[rs, :], outer[...])
            gain_grad[2:3] += jnp.sum(dx * x2, 0, keepdims=True)
            ds2 = f32(cot_all[rs, :]) + norm_rows16_back(dx * g[2:3], x2, sc2)
            ds2_16 = b16(ds2)
            ys[rs, 5 * width + wide :] = ds2_16

            if step == 0:
                for k in (14, 8, 13, 9):
                    arrive(k)

            dhp = b16(dot_nt(ds2_16, down[...]) * f32(slope[rs, :]))
            ys[rs, 5 * width : 5 * width + wide] = dhp
            dx = dot_nt(dhp, up[...])
            x1, sc1 = norm_rows16(first_in[rs, :])
            gain_grad[1:2] += jnp.sum(dx * x1, 0, keepdims=True)
            df = ds2 + norm_rows16_back(dx * g[1:2], x1, sc1)
            df16 = b16(df)
            ys[rs, 4 * width : 5 * width] = df16

            if step == 0:
                for k in (12, 6, 5, 7):
                    arrive(k)

            du = dot_nt(df16, proj[4])
            gate, mixed = f32(gm[rs, 0:width]), f32(gm[rs, width : 2 * width])
            do = du * gate
            do16 = b16(do)
            row = do * mixed
            dgate = b16(du * mixed * gate * (1.0 - gate))
            ys[rs, 3 * width : 4 * width] = dgate
            lane = lax.broadcasted_iota(jnp.int32, (1, L), 1)
            low = jnp.where(lane < L // 2, 1.0, 0.0)
            for u in range(2):
                crop = step * 2 + u
                own = pl.ds(pl.multiple_of(crop * L, L), L)
                part = slice(u * L, (u + 1) * L)
                for t in range(4):
                    s = slice(t * L, (t + 1) * L)
                    q = qkv[own, t * L : (t + 1) * L]
                    k = qkv[own, width + t * L : width + (t + 1) * L]
                    v = qkv[own, 2 * width + t * L : 2 * width + (t + 1) * L]
                    grads, weights = [], []
                    for j, (m, mf) in enumerate(zip(halves(), (low, 1.0 - low))):
                        at = pl.multiple_of((crop * 8 + 2 * t + j) * L, L)
                        p16 = probs[pl.ds(at, L), :]
                        dp = dot_nt(do16[part, s] * m, v)
                        e = f32(p16) * (dp - jnp.sum(row[part, s] * mf, -1, keepdims=True))
                        sdrb[pl.ds(at, L), :] = e
                        grads.append(b16(e))
                        weights.append(p16)
                    dq = dot(jnp.concatenate(grads, 1), on_halves(k)) * 0.125
                    dk = dot_tn(jnp.concatenate(grads, 0), on_halves(q))
                    dv = dot_tn(jnp.concatenate(weights, 0), on_halves(do16[part, s]))
                    ys[own, t * L : (t + 1) * L] = b16(dq)
                    ys[own, width + t * L : width + (t + 1) * L] = b16(dk)
                    ys[own, 2 * width + t * L : 2 * width + (t + 1) * L] = b16(dv)
            dx = dot_nt(ys[rs, 0:width], proj[0])
            for k in range(1, 4):
                dx = dx + dot_nt(ys[rs, k * width : (k + 1) * width], proj[k])
            x0, sc0 = norm_rows16(f32(x_all[rs, :]))
            gain_grad[0:1] += jnp.sum(dx * x0, 0, keepdims=True)
            sds[rs, :] = df + norm_rows16_back(dx * g[0:1], x0, sc0)

        for step in range(2):
            body(step)
        grp, row = where[2], where[3]
        d_own[...] = sds[pl.ds(pl.multiple_of(grp * L + row * rows, rows), rows), :]
        for h in range(8):
            at = pl.multiple_of((grp * 8 + h) * L + row * rows, rows)
            drb[h * rows : (h + 1) * rows] = sdrb[pl.ds(at, rows), :]
        m_op[...] = dot_tn(o_x2[...], dlr[...])

    return call(
        kernel,
        [
            ((tokens, 6 * width + wide), BF), ((3, width), F32), ((rows, width), F32),
            ((8 * rows, L), F32), ((width, L), F32),
        ],
        [
            ((tokens, L), BF), ((tokens, width), BF), ((4 * 8 * L, L), F32), ((tokens, width), F32),
        ],
        (
            where, ea, eb, x_all, cot_all, qkv, gm, probs, slope, first_in, second_in,
            gains, proj, up, down, outer,
        ), deps=deps, raw=(10, 15, 4, 11, 14, 8, 13, 9, 12, 6, 5, 7, 3), late=(5, 6, 7, 8, 9, 12, 13, 14), far=(0, 1, 2, 3, 4), us=22)


def weight_grads(xs, ys, width, wide, after):
    tokens = xs.shape[0]
    blocks = wide // width

    def kernel(x, y, after, out):
        out[...] = dot_tn(x[...], y[...]).reshape(out.shape)

    def run(steps, x_at, y_at, shape, block, out_at):
        return pl.pallas_call(
            kernel,
            grid=(steps,),
            out_shape=pltpu.HBM(shape, F32),
            in_specs=[
                pl.BlockSpec((tokens, width), x_at),
                pl.BlockSpec((tokens, width), y_at),
                pl.BlockSpec(memory_space=pl.ANY),
            ],
            out_specs=pl.BlockSpec(block, out_at),
            compiler_params=pltpu.CompilerParams(vmem_limit_bytes=32 << 20),
            cost_estimate=pl.CostEstimate(
                flops=2 * 10**9,
                bytes_accessed=steps * width * width * 8,
                transcendentals=0,
            ),
        )(
            pltpu.with_memory_space_constraint(xs, pltpu.HBM),
            pltpu.with_memory_space_constraint(ys, pltpu.HBM),
            pltpu.with_memory_space_constraint(after, pltpu.HBM),
        )

    proj = run(
        5, lambda i: (0, i // 4), lambda i: (0, i), (5, width, width), (1, width, width),
        lambda i: (i, 0, 0),
    )
    up = run(
        blocks, lambda i: (0, 2), lambda i: (0, 5 + i), (width, wide), (width, width),
        lambda i: (0, i),
    )
    down = run(
        blocks, lambda i: (0, 3 + i), lambda i: (0, 5 + blocks), (wide, width), (width, width),
        lambda i: (i, 0),
    )
    return proj, up, down


def project_pair(z, r, rows, m5t, pmask, sa, sb):
    xh, _ = norm_cols(z)
    p = dot(m5t[0:512], b16(xh))
    mk = get_rows(pmask, r, 1, 1)
    put_rows(sa, r, C, rows, sig(p[0:C]) * p[C : 2 * C] * mk)
    put_rows(sb, r, C, rows, sig(p[2 * C : 3 * C]) * p[3 * C : 4 * C] * mk)


def put_pair(n, ab, sa, sb):
    part = sa.shape[0] // n
    for d in range(n):
        ab[d, 0:part] = b16(sa[d * part : (d + 1) * part])
        ab[d, part : 2 * part] = b16(sb[d * part : (d + 1) * part])


def gated_product(z, r, rows, gatet, mot, sp):
    xh, _ = norm_cols(z)
    gate = sig(dot(gatet[...], b16(xh)))
    ph, _ = norm_cols(get_rows(sp, r, C, rows))
    return z + dot(mot[...], b16(ph)) * gate


def front(n, rows, where, lr_all, pair, outer_w, m5ts, deps=()):
    opm = outer_w.shape[0]

    def kernel(
        where, lr_all, pair, outer_w, m5ts,
        z1, ab, pmask, key_row, inner, lrt, left_own, sa, sb, slr, spm,
    ):
        m5t = m5ts.at[0]
        crop, block = where[0], where[1]
        lr16 = lr_all[pl.ds(crop * n, n)].reshape(L, C)
        lr = f32(lr16)
        turned = lr.T
        lrt[...] = turned
        mrow = turned[2 * opm : 2 * opm + 1]
        key_row[...] = (mrow - 1.0) * MASKED
        first = pl.multiple_of(block * rows, rows)
        spm[...] = jnp.broadcast_to(mrow, (L, L)).T * mrow
        pmask[...] = spm[pl.ds(first, rows), :]
        slr[...] = lr
        left = b16(slr[pl.ds(first, rows), :])
        left_own[...] = left
        inners = dot(left[:, 0:opm], side([outer_w[b] for b in range(opm)]))
        for b in range(opm):
            inner[b * rows : (b + 1) * rows] = lanes(inners, b)
        edge = jnp.zeros((opm, C), BF)

        def body(r):
            parts = []
            for u in range(U):
                mine = b16(inner[pl.ds(r * U + u, opm, stride=rows), :])
                mine = jnp.concatenate([edge, mine, edge, edge], 0)
                parts.append((f32(pair[r * U + u]) + dot(lr16, mine)).T)
            z = side(parts)
            z1[:, cols(r)] = z
            project_pair(z, r, rows, m5t, pmask, sa, sb)

        each_row(rows // U, body)
        put_pair(n, ab, sa, sb)

    part = C * rows // n
    return call(
        kernel,
        [
            ((C, rows * L), F32), ((n, 2 * part, L), BF), ((rows, L), F32), ((1, L), F32),
            ((opm * rows, C), F32), ((C, L), F32), ((rows, C), BF),
        ],
        [((C * rows, L), F32)] * 2 + [((L, C), F32), ((L, L), F32)],
        (where, lr_all, pair, outer_w, m5ts), deps=deps, raw=(2, 3, 4), far=(0, 2, 3, 4, 5, 6), us=5)


def middle(n, rows, z1, prod, mots, pmask, m5ts, deps=()):
    def kernel(z1, prod, mots, pmask, m5ts, z2, ab, sa, sb, sp):
        gatet, mot, m5t = m5ts.at[0, 512:640], mots.at[0], m5ts.at[1]
        sp[...] = f32(prod[...])

        def body(r):
            z = gated_product(z1[:, cols(r)], r, rows, gatet, mot, sp)
            z2[:, cols(r)] = z
            project_pair(z, r, rows, m5t, pmask, sa, sb)

        each_row(rows // U, body)
        put_pair(n, ab, sa, sb)

    part = C * rows // n
    return call(
        kernel,
        [((C, rows * L), F32), ((n, 2 * part, L), BF)],
        [((C * rows, L), F32)] * 3,
        (z1, prod, mots, pmask, m5ts), deps=deps, raw=(0, 1, 2, 3, 4), far=(0,), us=4)


def start_front(n, rows, z2, prod, m5ts, mots, abts, deps=()):
    def kernel(z2, prod, m5ts, mots, abts, z3, tb, sp, st):
        gatet, mot, abt = m5ts.at[1, 512:640], mots.at[1], abts.at[0]
        sp[...] = f32(prod[...])

        def body(r):
            z = gated_product(z2[:, cols(r)], r, rows, gatet, mot, sp)
            z3[:, cols(r)] = z
            xh, _ = norm_cols(z)
            put_rows(st, r, HPAD, rows, dot(abt[...], b16(xh)))

        each_row(rows // U, body)
        for d in range(n):
            tb[d] = b16(st[0 : TH * rows])

    return call(
        kernel,
        [((C, rows * L), F32), ((n, TH * rows, L), BF)],
        [((C * rows, L), F32), ((HPAD * rows, L), F32)],
        (z2, prod, m5ts, mots, abts), deps=deps, raw=(0, 1, 2, 3, 4), far=(0,), us=4)


def channel_product(n, rows, outgoing, ab):
    def kernel(ab, out):
        part = C * rows // n
        for ch in range(C // n):
            a = ab[:, ch * rows : (ch + 1) * rows, :].reshape(L, L)
            b = ab[:, part + ch * rows : part + (ch + 1) * rows, :].reshape(L, L)
            prod = dot_nt(a, b) if outgoing else dot_tn(a, b)
            out[:, ch * rows : (ch + 1) * rows, :] = b16(prod).reshape(n, rows, L)

    return call(kernel, [((n, C * rows // n, L), BF)], [], (ab,), raw=(0,), us=1)[0]


def channel_product_back(n, rows, outgoing, ab, dprod, deps=()):
    def kernel(ab, dprod, out):
        part = C * rows // n
        for ch in range(C // n):
            low, high = ch * rows, (ch + 1) * rows
            a = ab[:, low:high, :].reshape(L, L)
            b = ab[:, part + low : part + high, :].reshape(L, L)
            g = dprod[:, low:high, :].reshape(L, L)
            if outgoing:
                da, db = dot(g, b), dot_tn(g, a)
            else:
                da, db = dot_nt(b, g), dot(a, g)
            out[:, low:high, :] = b16(da).reshape(n, rows, L)
            out[:, part + low : part + high, :] = b16(db).reshape(n, rows, L)

    return call(kernel, [((n, 2 * C * rows // n, L), BF)], [], (ab, dprod), deps=deps, raw=(0,), us=2)[0]


def head_masks():
    lane = lax.broadcasted_iota(jnp.int32, (1, C), 1)
    return [b16(jnp.where((lane >= h * HD) & (lane < (h + 1) * HD), 1.0, 0.0)) for h in range(TH)]


def by_head(x):
    pm = b16(x.T)
    return jnp.concatenate([pm * m for m in head_masks()], 0)


def attend(x16, a4t, bias):
    p4 = dot(a4t[...], x16)
    gate = sig(p4[3 * C : 4 * C])
    each, mixed = [], []
    for u in range(U):
        q, k, v = (lanes(p4[m * C : (m + 1) * C], u) for m in range(3))
        logits = dot(by_head(k), b16(q)) + bias[...]
        raised, outs = [], []
        v16 = b16(v)
        for h in range(TH):
            s = logits[h * L : (h + 1) * L]
            e = jnp.exp(s - jnp.max(s, 0, keepdims=True))
            inv = 1.0 / jnp.sum(e, 0, keepdims=True)
            raised.append((e, inv))
            outs.append(dot(v16[h * HD : (h + 1) * HD], b16(e)) * inv)
        each.append((q, k, v, raised))
        mixed.append(jnp.concatenate(outs, 0))
    return each, gate, side(mixed)


def attend_back(state, dy16, ao, dbias):
    each, gate, mixed = state
    du = dot(ao[...], dy16)
    do = du * gate
    dgate = du * mixed * gate * (1.0 - gate)
    both = do * mixed
    parts = []
    for u in range(U):
        q, k, v, raised = each[u]
        do16, q16, k16 = b16(lanes(do, u)), b16(q), b16(k)
        dp = dot(by_head(v), do16)
        row = lanes(both, u)
        dq, dk, dv = [], [], []
        for h in range(TH):
            s = slice(h * HD, (h + 1) * HD)
            w = slice(h * L, (h + 1) * L)
            e, inv = raised[h]
            p = e * inv
            ds = p * (dp[w] - jnp.sum(row[s], 0, keepdims=True))
            dbias[w, :] += ds
            ds16, p16 = b16(ds), b16(p)
            dv.append(dot_nt(do16[s], p16))
            dq.append(dot(k16[s], ds16))
            dk.append(dot_nt(q16[s], ds16))
        parts.append(jnp.concatenate([b16(x) for x in dq + dk + dv], 0))
    return jnp.concatenate([side(parts), b16(dgate)], 0)


def start_attention(n, rows, z3, tb_all, key_row, a4ts, aots, abts, deps=()):
    def kernel(z3, tb_all, key_row, a4ts, aots, abts, z4, send, bias, st, se):
        a4t, aot, abt = a4ts.at[0], aots.at[0], abts.at[1]
        for h in range(TH):
            b = f32(tb_all[:, h * rows : (h + 1) * rows, :].reshape(L, L)) + key_row[...]
            bias[h * L : (h + 1) * L, :] = b.T

        def body(r):
            z = z3[:, cols(r)]
            xh, _ = norm_cols(z)
            _, gate, mixed = attend(b16(xh), a4t, bias)
            z = z + dot(aot[...], b16(mixed * gate))
            z4[:, cols(r)] = z
            put_turned(st, r, rows, z)
            xe, _ = norm_cols(z)
            put_rows(se, r, HPAD, rows, dot(abt[...], b16(xe)))

        each_row(rows // U, body)
        part = L * rows // n
        for d in range(n):
            send[d, 0:part] = b16(st[d * part : (d + 1) * part])
            send[d, part : part + TH * rows] = b16(se[0 : TH * rows])

    part = L * rows // n
    return call(
        kernel,
        [((C, rows * L), F32), ((n, part + TH * rows, L), BF)],
        [((TH * L, L), F32), ((L * rows, C), F32), ((HPAD * rows, L), F32)],
        (z3, tb_all, key_row, a4ts, aots, abts), deps=deps, raw=(0, 1, 2, 3, 4, 5), far=(0,), us=12)


def end_both(n, rows, where, recv, cots, key_row, a4ts, a4s, aots, aos, upt, up, dnt, dn, deps=()):
    part = L * rows // n

    def kernel(where, recv, *refs):
        cots, refs = refs[:n], refs[n:]
        run(where, recv, cots, *refs)

    def run(
        where, recv, cots, key_row, a4ts, a4s, aots, aos, upt, up, dnt, dn,
        p0, p1, p2, p3, p4, p5, p6, p7, send, m_up, m_dn, m_a4, m_ao,
        bias, dbias, scot, sout, sdz, o_h, o_dh, o_x5, o_cot, o_x4, o_d4, o_u, o_dy,
    ):
        a4t, a4, aot, ao = a4ts.at[1], a4s.at[1], aots.at[1], aos.at[1]
        kb = jnp.broadcast_to(key_row[...], (L, L)).T
        for h in range(TH):
            b = recv[:, part + h * rows : part + (h + 1) * rows, :].reshape(L, L)
            bias[h * L : (h + 1) * L, :] = f32(b) + kb
        dbias[...] = jnp.zeros_like(dbias)
        for k in range(n):
            block = lax.rem(where[1] + n - k, n)
            scot[pl.ds(pl.multiple_of(block * part, part), part), :] = f32(cots[k][...])

        def body(r):
            w = cols(r)
            z4 = get_turned(recv, r, rows)
            x4, scale4 = norm_cols(z4)
            x16 = b16(x4)
            state = attend(x16, a4t, bias)
            gated = b16(state[2] * state[1])
            z5 = z4 + dot(aot[...], gated)
            x5, scale5 = norm_cols(z5)
            x516 = b16(x5)
            hid, slope = gelu_parts(dot(upt[...], x516))
            h16 = b16(hid)
            z6 = z5 + dot(dnt[...], h16)
            put_turned(sout, r, rows, z6)
            dz6 = side([scot[pl.ds(r * U + u, L, stride=rows), :].T for u in range(U)])
            c16 = b16(dz6)
            dh16 = b16(dot(dn[...], c16) * slope)
            dz5 = dz6 + norm_cols_back(dot(up[...], dh16), x5, scale5)
            dy16 = b16(dz5)
            d4 = attend_back(state, dy16, ao, dbias)
            dz4 = dz5 + norm_cols_back(dot(a4[...], d4), x4, scale4)
            put_turned(sdz, r, rows, dz4)
            o_h[:, w] = h16
            o_dh[:, w] = dh16
            o_x5[:, w] = x516
            o_cot[:, w] = c16
            o_x4[:, w] = x16
            o_d4[:, w] = d4
            o_u[:, w] = gated
            o_dy[:, w] = dy16

        each_row(rows // U, body)
        for d in range(n):
            send[d, 0:part] = b16(sdz[d * part : (d + 1) * part])
            for h in range(TH):
                send[d, part + h * rows : part + (h + 1) * rows] = b16(
                    dbias[h * L + d * rows : h * L + (d + 1) * rows]
                )
        for k, pout in enumerate((p0, p1, p2, p3, p4, p5, p6, p7)):
            block = lax.rem(where[1] + k, n)
            pout[...] = b16(sout[pl.ds(pl.multiple_of(block * part, part), part), :])
        for k in range(4):
            s = slice(k * C, (k + 1) * C)
            m_up[s] = dot_nt(o_x5[...], o_dh[s])
            m_a4[s] = dot_nt(o_x4[...], o_d4[s])
        m_dn[...] = dot_nt(o_h[...], o_cot[...])
        m_ao[...] = dot_nt(o_u[...], o_dy[...])

    wide = rows * L
    return call(
        kernel,
        [
            *[((part, C), BF)] * n, ((n, part + TH * rows, L), BF),
            ((512, C), F32), ((512, C), F32), ((512, C), F32), ((C, C), F32),
        ],
        [
            ((TH * L, L), F32), ((TH * L, L), F32), ((L * rows, C), F32), ((L * rows, C), F32),
            ((L * rows, C), F32),
            ((512, wide), BF), ((512, wide), BF), ((C, wide), BF), ((C, wide), BF),
            ((C, wide), BF), ((512, wide), BF), ((C, wide), BF), ((C, wide), BF),
        ],
        (where, recv, *cots, key_row, a4ts, a4s, aots, aos, upt, up, dnt, dn),
        deps=deps,
        raw=tuple(range(2, n + 11)),
        far=(0, 1, 2, 3, 4, 5, 6, 7, 9, 10, 11, 12),
        us=18,
    )


def start_back(n, rows, z3, z4, recv, tb_all, key_row, a4ts, a4s, aos, abts, deps=()):
    part = L * rows // n

    def kernel(
        z3, z4, recv, tb_all, key_row, a4ts, a4s, aos, abts,
        dz4_out, dxs, dtb, m_a4, m_ao, m_ab,
        bias, dbias, seb, o_x3, o_d4, o_u, o_dy, o_x4, o_eb,
    ):
        a4t, a4, ao, abt = a4ts.at[0], a4s.at[0], aos.at[0], abts.at[1]
        for h in range(TH):
            b = f32(tb_all[:, h * rows : (h + 1) * rows, :].reshape(L, L)) + key_row[...]
            bias[h * L : (h + 1) * L, :] = b.T
        dbias[...] = jnp.zeros_like(dbias)
        seb[...] = jnp.zeros_like(seb)
        total = f32(recv[0, part : part + TH * rows])
        for d in range(1, n):
            total = total + f32(recv[d, part : part + TH * rows])
        seb[0 : TH * rows, :] = total

        def body(r):
            w = cols(r)
            x4, scale4 = norm_cols(z4[:, w])
            eb16 = b16(get_rows(seb, r, HPAD, rows))
            dz4 = get_turned(recv, r, rows)
            dz4 = dz4 + norm_cols_back(dot_tn(abt[...], eb16), x4, scale4)
            dz4_out[:, w] = dz4
            x3, _ = norm_cols(z3[:, w])
            x16 = b16(x3)
            state = attend(x16, a4t, bias)
            dy16 = b16(dz4)
            d4 = attend_back(state, dy16, ao, dbias)
            dxs[:, w] = dot(a4[...], d4)
            o_x3[:, w] = x16
            o_d4[:, w] = d4
            o_u[:, w] = b16(state[2] * state[1])
            o_dy[:, w] = dy16
            o_x4[:, w] = b16(x4)
            o_eb[:, w] = eb16

        each_row(rows // U, body)
        for h in range(TH):
            turned = b16(dbias[h * L : (h + 1) * L, :].T)
            for d in range(n):
                dtb[d, h * rows : (h + 1) * rows] = turned[d * rows : (d + 1) * rows]
        for k in range(4):
            s = slice(k * C, (k + 1) * C)
            m_a4[s] = dot_nt(o_x3[...], o_d4[s])
        m_ao[...] = dot_nt(o_u[...], o_dy[...])
        m_ab[...] = dot_nt(o_eb[...], o_x4[...])

    wide = rows * L
    return call(
        kernel,
        [
            ((C, wide), F32), ((C, wide), F32), ((n, TH * rows, L), BF),
            ((512, C), F32), ((C, C), F32), ((HPAD, C), F32),
        ],
        [
            ((TH * L, L), F32), ((TH * L, L), F32), ((HPAD * rows, L), F32),
            ((C, wide), BF), ((512, wide), BF), ((C, wide), BF), ((C, wide), BF),
            ((C, wide), BF), ((HPAD, wide), BF),
        ],
        (z3, z4, recv, tb_all, key_row, a4ts, a4s, aos, abts),
        deps=deps, raw=(0, 1, 3, 4, 5, 6, 7, 8), far=(0, 1, 3, 4, 5), us=20)


def product_back(z, dz, r, rows, sp, gatet, mot, mof, sdp, dgp_out, o_ph, o_do):
    w = cols(r)
    xh, _ = norm_cols(z)
    gate = sig(dot(gatet[...], b16(xh)))
    ph, scale = norm_cols(get_rows(sp, r, C, rows))
    ph16 = b16(ph)
    out = dot(mot[...], ph16)
    dgp_out[:, w] = b16(dz * out * gate * (1.0 - gate))
    do16 = b16(dz * gate)
    put_rows(sdp, r, C, rows, norm_cols_back(dot(mof[...], do16), ph, scale))
    o_ph[:, w] = ph16
    o_do[:, w] = do16


def third_back(n, rows, z3, dz4, dxs, recv, abts, z2, prod, m5ts, mots, mofs, deps=()):
    def kernel(
        z3, dz4, dxs, recv, abts, z2, prod, m5ts, mots, mofs,
        dz3, dgp, dp, m_ab, m_mo,
        stb, sp, sdp, o_x3, o_tb, o_ph, o_do,
    ):
        abt, gatet, mot, mof = abts.at[0], m5ts.at[1, 512:640], mots.at[1], mofs.at[1]
        sp[...] = f32(prod[...])
        stb[...] = jnp.zeros_like(stb)
        total = f32(recv[0])
        for d in range(1, n):
            total = total + f32(recv[d])
        stb[0 : TH * rows, :] = total

        def body(r):
            w = cols(r)
            x3, scale3 = norm_cols(z3[:, w])
            tb16 = b16(get_rows(stb, r, HPAD, rows))
            dx = dxs[:, w] + dot_tn(abt[...], tb16)
            dz = dz4[:, w] + norm_cols_back(dx, x3, scale3)
            dz3[:, w] = dz
            o_x3[:, w] = b16(x3)
            o_tb[:, w] = tb16
            product_back(z2[:, w], dz, r, rows, sp, gatet, mot, mof, sdp, dgp, o_ph, o_do)

        each_row(rows // U, body)
        dp[...] = b16(sdp[...])
        m_ab[...] = dot_nt(o_tb[...], o_x3[...])
        m_mo[...] = dot_nt(o_ph[...], o_do[...])

    wide = rows * L
    return call(
        kernel,
        [
            ((C, wide), F32), ((C, wide), BF), ((C * rows, L), BF),
            ((HPAD, C), F32), ((C, C), F32),
        ],
        [
            ((HPAD * rows, L), F32), ((C * rows, L), F32), ((C * rows, L), F32),
            ((C, wide), BF), ((HPAD, wide), BF), ((C, wide), BF), ((C, wide), BF),
        ],
        (z3, dz4, dxs, recv, abts, z2, prod, m5ts, mots, mofs), deps=deps, raw=(0, 1, 2, 4, 5, 6, 7, 8, 9), far=(0, 1, 3, 4), us=7)


def projections_back(n, rows, z, dz, dgp, r, pmask, m5t, m5, sa, sb, o_x, o_d5):
    w = cols(r)
    xh, scale = norm_cols(z)
    x16 = b16(xh)
    p = dot(m5t[0:512], x16)
    mk = get_rows(pmask, r, 1, 1)
    da = get_rows(sa, r, C, rows) * mk
    db = get_rows(sb, r, C, rows) * mk
    ga, gb = sig(p[0:C]), sig(p[2 * C : 3 * C])
    va, vb = p[C : 2 * C], p[3 * C : 4 * C]
    d5 = jnp.concatenate(
        [
            b16(da * va * ga * (1.0 - ga)),
            b16(da * ga),
            b16(db * vb * gb * (1.0 - gb)),
            b16(db * gb),
            dgp[:, w],
        ],
        0,
    )
    o_x[:, w] = x16
    o_d5[:, w] = d5
    return dz + norm_cols_back(dot(m5[...], d5), xh, scale)


def take_pair(n, dab, sa, sb):
    part = sa.shape[0] // n
    for d in range(n):
        sa[d * part : (d + 1) * part, :] = f32(dab[d, 0:part])
        sb[d * part : (d + 1) * part, :] = f32(dab[d, part : 2 * part])


def second_back(n, rows, z2, dz3, dgp, dab, pmask, m5ts, m5s, z1, prod, mots, mofs, deps=()):
    def kernel(
        z2, dz3, dgp, dab, pmask, m5ts, m5s, z1, prod, mots, mofs,
        dz2, dgp_out, dp, m_m5, m_mo,
        sa, sb, sp, sdp, o_x, o_d5, o_ph, o_do,
    ):
        m5t, m5, gatet = m5ts.at[1], m5s.at[1], m5ts.at[0, 512:640]
        mot, mof = mots.at[0], mofs.at[0]
        sp[...] = f32(prod[...])
        take_pair(n, dab, sa, sb)

        def body(r):
            w = cols(r)
            dz = projections_back(
                n, rows, z2[:, w], dz3[:, w], dgp, r, pmask, m5t, m5, sa, sb, o_x, o_d5
            )
            dz2[:, w] = dz
            product_back(z1[:, w], dz, r, rows, sp, gatet, mot, mof, sdp, dgp_out, o_ph, o_do)

        each_row(rows // U, body)
        dp[...] = b16(sdp[...])
        for k in range(5):
            s = slice(k * C, (k + 1) * C)
            m_m5[s] = dot_nt(o_x[...], o_d5[s])
        m_mo[...] = dot_nt(o_ph[...], o_do[...])

    wide = rows * L
    return call(
        kernel,
        [
            ((C, wide), F32), ((C, wide), BF), ((C * rows, L), BF),
            ((640, C), F32), ((C, C), F32),
        ],
        [
            ((C * rows, L), F32), ((C * rows, L), F32), ((C * rows, L), F32), ((C * rows, L), F32),
            ((C, wide), BF), ((640, wide), BF), ((C, wide), BF), ((C, wide), BF),
        ],
        (z2, dz3, dgp, dab, pmask, m5ts, m5s, z1, prod, mots, mofs), deps=deps, raw=(0, 1, 2, 4, 5, 6, 7, 8, 9, 10), far=(0, 1, 3, 4), us=11)


def first_back(n, rows, copies, where, z1, dz2, dgp, dab, pmask, m5ts, m5s, inner, lrt, left_own, outer_w, deps=()):
    opm = outer_w.shape[0]

    def kernel(
        where, z1, dz2, dgp, dab, pmask, m5ts, m5s, inner, lrt, left_own, outer_w,
        dz1, ends, m_oo, m_m5,
        sa, sb, o_x, o_d5, sdi, sdr,
    ):
        m5t, m5 = m5ts.at[0], m5s.at[0]
        take_pair(n, dab, sa, sb)
        sdr[...] = jnp.zeros_like(sdr)
        right_t = b16(lrt[opm : 2 * opm])

        def body(r):
            w = cols(r)
            dz = projections_back(
                n, rows, z1[:, w], dz2[:, w], dgp, r, pmask, m5t, m5, sa, sb, o_x, o_d5
            )
            for u in range(U):
                dz16 = b16(lanes(dz, u).T)
                dz1[r * U + u] = dz16
                at = pl.ds(r * U + u, opm, stride=rows)
                sdi[at, :] = dot(right_t, dz16)
                sdr[...] += dot_nt(b16(inner[at, :]), dz16)

        each_row(rows // U, body)
        left = left_own[:, 0:opm]
        d16 = side([b16(sdi[b * rows : (b + 1) * rows]) for b in range(opm)])
        outers = dot_tn(left, d16)
        for b in range(opm):
            m_oo[b * opm : (b + 1) * opm] = lanes(outers, b)
        dleft = dot_nt(side([outer_w[b] for b in range(opm)]), d16)
        lane = lax.broadcasted_iota(jnp.int32, (rows, L), 1)
        spot = lax.broadcasted_iota(jnp.int32, (rows, L), 0) + where[1] * rows
        dleft = dot(b16(dleft), b16(jnp.where(lane == spot, 1.0, 0.0)))
        both = jnp.concatenate([dleft, sdr[...]], 0) * lrt[2 * opm : 2 * opm + 1]
        for d in range(copies):
            ends[d] = b16(both)
        for k in range(5):
            s = slice(k * C, (k + 1) * C)
            m_m5[s] = dot_nt(o_x[...], o_d5[s])

    wide = rows * L
    return call(
        kernel,
        [
            ((rows, L, C), BF), ((copies, 2 * opm, L), BF), ((opm * opm, C), F32), ((640, C), F32),
        ],
        [
            ((C * rows, L), F32), ((C * rows, L), F32), ((C, wide), BF), ((640, wide), BF),
            ((opm * rows, C), F32), ((opm, L), F32),
        ],
        (where, z1, dz2, dgp, dab, pmask, m5ts, m5s, inner, lrt, left_own, outer_w), deps=deps, raw=(1, 2, 3, 5, 6, 7, 8, 9, 10, 11), far=(2, 3), us=11)


def last_back(rows, pair, drb, dz1, sbt, deps=()):
    def kernel(pair, drb, dz1, sbt, grad, m_sb, o_x, o_d):
        def body(r):
            w = cols(r)
            xh, scale = norm_cols(side([f32(pair[r * U + u]).T for u in range(U)]))
            d = get_rows(drb, r, 8, rows)
            d16 = b16(jnp.concatenate([d, jnp.zeros_like(d)], 0))
            back = norm_cols_back(dot_tn(sbt[...], d16), xh, scale)
            for u in range(U):
                grad[r * U + u] = f32(dz1[r * U + u]) + lanes(back, u).T
            o_x[:, w] = b16(xh)
            o_d[:, w] = d16

        each_row(rows // U, body)
        m_sb[...] = dot_nt(o_d[...], o_x[...])

    wide = rows * L
    return call(
        kernel,
        [((rows, L, C), F32), ((HPAD, C), F32)],
        [((C, wide), BF), ((HPAD, wide), BF)],
        (pair, drb, dz1, sbt), deps=deps, raw=(0, 1, 2, 3), far=(0,), us=3)


def collect(where, parts, half, deps):
    def kernel(where, *refs):
        sources, (kept, given, rows) = refs[: len(parts)], refs[len(parts) :]
        core = where[3] % 2
        at = 0
        for ref in sources:
            rows[at : at + ref.shape[0]] = ref[...]
            at += ref.shape[0]
        if at < 2 * half:
            rows[at : 2 * half] = jnp.zeros((2 * half - at, C), F32)
        kept[...] = rows[pl.ds(pl.multiple_of(core * half, half), half), :]
        given[...] = b16(rows[pl.ds(pl.multiple_of((1 - core) * half, half), half), :])

    return call(
        kernel,
        [((half, C), F32), ((half, C), BF)],
        [((2 * half, C), F32)],
        (where, *parts),
        deps=deps,
        raw=tuple(range(1, len(parts) + 1)),
        us=0,
    )


def sum_copies(x, extra, count):
    rows, more = x.shape[1], extra.shape[0]

    def kernel(x, extra, out):
        total = b16(jnp.sum(f32(x[...]), 0))
        for d in range(count):
            out[d, 0:rows] = total
            out[d, rows : rows + more] = b16(extra[...])

    return call(kernel, [((count, rows + more, C), BF)], [], (x, extra), us=2)[0]


def finish(where, near, far, gp, gm, mp, mg, mo, ap, ab, pu, sb, places, half, opm, deps):
    def kernel(
        where, near, far, gp, gm, mp, mg, mo, ap, ab, pu, sb,
        g_pg, g_mg, g_sb, g_oo, g_mp, g_mgt, g_mo, g_ap, g_ab, g_ao, g_pu, g_pd,
        rows,
    ):
        core = where[3] % 2
        chips = near.shape[0]
        size = half // chips
        for k in range(chips):
            at = pl.multiple_of(core * half + k * size, 8)
            rows[pl.ds(at, size), :] = f32(near[k, 0:size])
            at = pl.multiple_of((1 - core) * half + k * size, 8)
            rows[pl.ds(at, size), :] = f32(far[k, 0:size])

        def take(name, count, skip=0):
            at = places[name] + skip
            return rows[at : at + count]

        gpv, gmv = f32(gp[...]), f32(gm[...])

        def column(row):
            return jnp.broadcast_to(row, (C, C)).T

        def over_lanes(x):
            return jnp.sum(x.T, 0, keepdims=True)

        def padded(w):
            return jnp.concatenate([f32(w), jnp.zeros((HPAD - w.shape[0], C), F32)], 0)

        total = jnp.zeros((8, C), F32)
        for k in range(chips):
            total = total + (f32(near[k, size : size + 8]) + f32(far[k, size : size + 8]))
        g_pg[0:1] = jnp.sum(f32(sb[...]) * total, 0, keepdims=True)
        g_sb[...] = total * gpv[0:1]
        for t in range(2):
            g = column(gpv[1 + t : 2 + t])
            both = jnp.zeros((C, C), F32)
            for k in range(5):
                m = take("m5%d" % t, C, k * C)
                both = both + m * f32(mp[t, k] if k < 4 else mg[t])
                if k < 4:
                    g_mp[t, k] = m * g
                else:
                    g_mgt[t] = m * g
            g_pg[1 + t : 2 + t] = over_lanes(both)
            m = take("mo%d" % t, C)
            g_mo[t] = m * column(gmv[t : t + 1])
            g_mg[t : t + 1] = over_lanes(m * f32(mo[t]))
            g = column(gpv[3 + t : 4 + t])
            both = jnp.zeros((C, C), F32)
            for k in range(4):
                m = take("a4%d" % t, C, k * C)
                if k == 0:
                    m = m * HD**-0.5
                both = both + m * f32(ap[t, k])
                g_ap[t, k] = m * g
            m = take("ab%d" % t, HPAD)
            g_pg[3 + t : 4 + t] = over_lanes(both) + jnp.sum(padded(ab[t]) * m, 0, keepdims=True)
            g_ab[t] = (m * gpv[3 + t : 4 + t])[0:TH]
            g_ao[t] = take("ao%d" % t, C)
        g = column(gpv[5:6])
        both = jnp.zeros((C, C), F32)
        for k in range(4):
            s = slice(k * C, (k + 1) * C)
            m = take("up", C, k * C)
            both = both + m * f32(pu[:, s])
            g_pu[:, s] = m * g
        g_pg[5:6] = over_lanes(both)
        g_pd[...] = take("dn", 512)
        for b in range(opm):
            g_oo[:, b, :] = take("oo", opm, b * opm)

    outs = [
        (6, C), (2, C), (8, C), (opm, opm, C), (2, 4, C, C), (2, C, C), (2, C, C), (2, 4, C, C),
        (2, TH, C), (2, C, C), (C, 512), (512, C),
    ]
    return call(
        kernel,
        [(s, F32) for s in outs],
        [((2 * half, C), F32)],
        (where, near, far, gp, gm, mp, mg, mo, ap, ab, pu, sb),

        raw=(3, 4, 5, 6, 7, 8, 9, 10, 11), deps=deps, far=tuple(range(12)), us=4,
    )


PRECISE = lax.Precision.HIGHEST


def for_sending(shard):

    def short(part):
        return part.astype(jnp.bfloat16) if part.dtype == jnp.float32 else part

    return jax.tree.map(short, shard)


def widen(operand):
    return operand.astype(jnp.float32)


def narrow(operand):
    return operand.astype(jnp.bfloat16)


def rounded(operand):
    return lax.optimization_barrier(operand.astype(jnp.bfloat16)).astype(jnp.float32)


def contract(pattern, first_term, second_term):
    return jnp.einsum(pattern, first_term, second_term, precision=PRECISE)


def low_product(pattern, first_term, second_term):
    return jnp.einsum(pattern, first_term, second_term, preferred_element_type=jnp.float32)


def norm_rows(operand, gain_vec):
    centre = operand - jnp.mean(operand, -1, keepdims=True)
    spread = jnp.mean(centre * centre, -1, keepdims=True)
    return centre * lax.rsqrt(spread + EPSILON) * gain_vec


def soft_weights(logits):
    highest = jnp.max(logits, -1, keepdims=True)
    raised = jnp.exp(logits - highest)
    return raised / jnp.sum(raised, -1, keepdims=True)


def single_attend(queries, key_rows, values, gate_value, pair_bias, key_bias, weight_out):
    head_count = pair_bias.shape[0]
    feature_width = queries.shape[-1]
    head_size = feature_width // head_count
    query_heads = queries.reshape(queries.shape[0], head_count, head_size)
    key_heads = key_rows.reshape(key_rows.shape[0], head_count, head_size)
    value_heads = values.reshape(values.shape[0], head_count, head_size)
    logits = (
        contract("ihd,jhd->hij", query_heads, key_heads) * head_size ** (-0.5)
        + pair_bias
        + key_bias
    )
    mixed = contract("hij,jhd->ihd", soft_weights(logits), value_heads).reshape(
        queries.shape[0], feature_width
    )
    return contract("is,st->it", mixed * jax.nn.sigmoid(gate_value), weight_out)


def tri_attend(normed, pair_bias, weight_four, weight_out, key_bias):
    head_count = pair_bias.shape[0]
    feature_width = normed.shape[-1]
    head_size = feature_width // head_count

    def one_row(row_in):
        projected = contract("lc,ncd->nld", row_in, weight_four)
        shaped = projected[:3].reshape(3, row_in.shape[0], head_count, head_size)
        logits = (
            contract("jhd,khd->hjk", shaped[0], shaped[1]) * head_size ** (-0.5)
            + pair_bias
            + key_bias
        )
        mixed = contract("hjk,khd->jhd", soft_weights(logits), shaped[2]).reshape(
            row_in.shape[0], feature_width
        )
        return contract("lc,cd->ld", mixed * jax.nn.sigmoid(projected[3]), weight_out)

    return lax.map(jax.checkpoint(one_row), normed)


def mult_front(pair_in, gain_vec, weight_four, weight_gate, pair_mask):
    normed = norm_rows(pair_in, gain_vec)
    projected = contract("rlc,ncm->nmrl", normed, weight_four)
    left_side = jax.nn.sigmoid(projected[0]) * projected[1] * pair_mask
    right_side = jax.nn.sigmoid(projected[2]) * projected[3] * pair_mask
    gate_value = jax.nn.sigmoid(contract("rlc,cd->rld", normed, weight_gate))
    return (left_side, right_side, gate_value)


def mult_back(pair_in, product, gate_value, gain_vec, weight_out):
    centre = product - jnp.mean(product, 0, keepdims=True)
    spread = jnp.mean(centre * centre, 0, keepdims=True)
    scaled = centre * lax.rsqrt(spread + EPSILON) * gain_vec[:, None, None]
    return pair_in + contract("mrl,mc->rlc", scaled, weight_out) * gate_value


def outgoing_forward(left_chan, right_chan):
    return low_product("mik,mjk->mij", left_chan, right_chan)


def outgoing_backward(left_chan, right_chan, grad_out):
    return (
        low_product("mij,mjk->mik", grad_out, right_chan),
        low_product("mij,mik->mjk", grad_out, left_chan),
    )


def incoming_forward(left_chan, right_chan):
    return low_product("mki,mkj->mij", left_chan, right_chan)


def incoming_backward(left_chan, right_chan, grad_out):
    return (
        low_product("mij,mkj->mki", grad_out, right_chan),
        low_product("mij,mki->mkj", grad_out, left_chan),
    )


def to_channels(operand):
    return jax.tree.map(
        lambda part, own: part.astype(own.dtype),
        lax.all_to_all(for_sending(operand), "rows", split_axis=0, concat_axis=1, tiled=True),
        operand,
    )


def to_rows(operand):
    return jax.tree.map(
        lambda part, own: part.astype(own.dtype),
        lax.all_to_all(for_sending(operand), "rows", split_axis=1, concat_axis=0, tiled=True),
        operand,
    )


def turn_cols(operand):
    return jnp.swapaxes(
        lax.all_to_all(operand, "rows", split_axis=1, concat_axis=0, tiled=True), 0, 1
    )


def turn_rows(operand):
    return lax.all_to_all(
        jnp.swapaxes(operand, 0, 1), "rows", split_axis=0, concat_axis=1, tiled=True
    )


def gather_bias(operand):
    return lax.all_gather(operand, "rows", axis=1, tiled=True)


def scatter_bias(operand):
    return lax.psum_scatter(operand, "rows", scatter_dimension=1, tiled=True)


def general_local(
    single_rep,
    pair_rep,
    residue_mask,
    single_gains,
    pair_gains,
    mult_gains,
    single_proj,
    single_bias,
    single_up,
    single_down,
    opm_proj,
    opm_out,
    mult_proj,
    mult_gate,
    mult_out,
    att_proj,
    att_bias,
    att_out,
    pair_up,
    pair_down,
    single_cot,
    pair_cot,
):
    gains_s = widen(single_gains)
    gains_p = widen(pair_gains)
    gains_m = widen(mult_gains)
    proj_s = widen(single_proj)
    bias_sw = widen(single_bias)
    up_s = widen(single_up)
    down_s = widen(single_down)
    proj_o = widen(opm_proj)
    outer_w = widen(opm_out)
    proj_m = widen(mult_proj)
    gate_m = widen(mult_gate)
    out_m = widen(mult_out)
    proj_a = widen(att_proj)
    bias_a = widen(att_bias)
    out_a = widen(att_out)
    up_p = widen(pair_up)
    down_p = widen(pair_down)
    mask_all = widen(residue_mask[0])
    shard_rows = pair_rep.shape[1]
    first_row = lax.axis_index("rows") * shard_rows
    mask_own = lax.dynamic_slice_in_dim(mask_all, first_row, shard_rows, 0)
    key_bias = (mask_all - 1.0) * MASKED
    pair_mask = mask_own[:, None] * mask_all[None, :]
    single_own = widen(single_rep[0])
    pair_own = widen(pair_rep[0])

    def front_single(
        single_in, pair_in, gain_s, gain_z, proj_query, proj_key, proj_value, proj_gate, bias_w
    ):
        normed = norm_rows(single_in, gain_s)
        pair_normed = norm_rows(pair_in, gain_z)
        return (
            contract("rs,st->rt", normed, proj_query),
            contract("rs,st->rt", normed, proj_key),
            contract("rs,st->rt", normed, proj_value),
            contract("rs,st->rt", normed, proj_gate),
            contract("rlc,ch->hrl", pair_normed, bias_w),
        )

    def back_single(
        queries,
        key_rows,
        values,
        gate_value,
        row_bias,
        single_in,
        proj_out,
        gain_t,
        weight_up,
        weight_down,
        gain_o,
        left_w,
        right_w,
    ):
        first_sum = single_in + single_attend(
            queries, key_rows, values, gate_value, row_bias, key_bias, proj_out
        )
        hidden = jax.nn.gelu(contract("rs,st->rt", norm_rows(first_sum, gain_t), weight_up))
        second_sum = first_sum + contract("rt,ts->rs", hidden, weight_down)
        outer_in = norm_rows(second_sum, gain_o)
        left_side = contract("rs,sa->ra", outer_in, left_w) * mask_own[:, None]
        right_side = contract("rs,sa->ra", outer_in, right_w) * mask_own[:, None]
        return (second_sum, left_side, right_side)

    def outer_front(left_side, right_all, pair_in, weight_outer, gain_in, weight_four, weight_gate):
        inner = contract("ia,abc->ibc", left_side, weight_outer)
        updated = pair_in + contract("ibc,jb->ijc", inner, right_all)
        left_m, right_m, gate_value = mult_front(
            updated, gain_in, weight_four, weight_gate, pair_mask
        )
        return (updated, left_m, right_m, gate_value)

    def middle_mult(
        pair_in, product, gate_value, gain_out, weight_out, gain_in, weight_four, weight_gate
    ):
        updated = mult_back(pair_in, product, gate_value, gain_out, weight_out)
        left_m, right_m, gate_next = mult_front(
            updated, gain_in, weight_four, weight_gate, pair_mask
        )
        return (updated, left_m, right_m, gate_next)

    def start_front_general(pair_in, product, gate_value, gain_out, weight_out, gain_start, bias_w):
        updated = mult_back(pair_in, product, gate_value, gain_out, weight_out)
        normed = norm_rows(updated, gain_start)
        return (updated, normed, contract("rlc,ch->hrl", normed, bias_w))

    def start_core(pair_in, normed, bias_all, weight_four, weight_out, gain_end):
        updated = pair_in + tri_attend(normed, bias_all, weight_four, weight_out, key_bias)
        return (updated, norm_rows(updated, gain_end))

    def end_bias(turned, bias_w):
        return contract("rlc,ch->hrl", turned, bias_w)

    def end_core(turned, bias_all, weight_four, weight_out):
        return tri_attend(turned, bias_all, weight_four, weight_out, key_bias)

    def final_pair(pair_in, update, gain_vec, weight_up, weight_down):
        summed = pair_in + update
        hidden = jax.nn.gelu(contract("rlc,cd->rld", norm_rows(summed, gain_vec), weight_up))
        return summed + contract("rld,dc->rlc", hidden, weight_down)

    outs_one, back_one = jax.vjp(
        front_single,
        single_own,
        pair_own,
        gains_s[0],
        gains_p[0],
        proj_s[0],
        proj_s[1],
        proj_s[2],
        proj_s[3],
        bias_sw,
    )
    queries, keys_own, values_own, gate_single, row_bias = outs_one
    keys_all, values_all = (
        lax.all_gather(narrow(keys_own), "rows", axis=0, tiled=True),
        lax.all_gather(narrow(values_own), "rows", axis=0, tiled=True),
    )
    outs_two, back_two = jax.vjp(
        back_single,
        queries,
        widen(keys_all),
        widen(values_all),
        gate_single,
        row_bias,
        single_own,
        proj_s[4],
        gains_s[1],
        up_s,
        down_s,
        gains_s[2],
        proj_o[0],
        proj_o[1],
    )
    single_next, left_outer, right_outer = outs_two
    right_all = widen(lax.all_gather(narrow(right_outer), "rows", axis=0, tiled=True))
    outs_three, back_three = jax.vjp(
        outer_front,
        rounded(left_outer),
        right_all,
        pair_own,
        outer_w,
        gains_p[1],
        proj_m[0],
        gate_m[0],
    )
    pair_one, left_first, right_first, gate_first = outs_three
    chan_left, chan_right = to_channels((narrow(left_first), narrow(right_first)))
    product_one = outgoing_forward(chan_left, chan_right)
    rows_one = widen(to_rows(narrow(product_one)))
    outs_five, back_five = jax.vjp(
        middle_mult,
        pair_one,
        rows_one,
        gate_first,
        gains_m[0],
        out_m[0],
        gains_p[2],
        proj_m[1],
        gate_m[1],
    )
    pair_two, left_second, right_second, gate_second = outs_five
    chan_left_two, chan_right_two = to_channels((narrow(left_second), narrow(right_second)))
    product_two = incoming_forward(chan_left_two, chan_right_two)
    rows_two = widen(to_rows(narrow(product_two)))
    outs_seven, back_seven = jax.vjp(
        start_front_general, pair_two, rows_two, gate_second, gains_m[1], out_m[1], gains_p[3], bias_a[0]
    )
    pair_three, normed_start, bias_start = outs_seven
    bias_start_all = widen(gather_bias(narrow(bias_start)))
    outs_eight, back_eight = jax.vjp(
        start_core, pair_three, normed_start, bias_start_all, proj_a[0], out_a[0], gains_p[4]
    )
    pair_four, normed_end = outs_eight
    turned = widen(turn_cols(narrow(normed_end)))
    bias_end, back_nine = jax.vjp(end_bias, turned, bias_a[1])
    bias_end_all = widen(gather_bias(narrow(bias_end)))
    update_turned, back_ten = jax.vjp(end_core, turned, bias_end_all, proj_a[1], out_a[1])
    update = widen(turn_rows(narrow(update_turned)))
    pair_six, back_eleven = jax.vjp(final_pair, pair_four, update, gains_p[5], up_p, down_p)
    grad_four, grad_update, g_pg5, g_pu, g_pd = back_eleven(widen(pair_cot[0]))
    g_pg5, g_pu, g_pd = (g_pg5, g_pu, g_pd)
    grad_turned_update = widen(turn_cols(narrow(grad_update)))
    grad_turned_a, grad_bias_end_all, g_ap1, g_ao1 = back_ten(grad_turned_update)
    g_ap1, g_ao1 = (g_ap1, g_ao1)
    grad_bias_end = rounded(scatter_bias(grad_bias_end_all))
    grad_turned_b, g_ab1 = back_nine(grad_bias_end)
    grad_normed_end = widen(turn_rows(narrow(grad_turned_a + grad_turned_b)))
    grad_three, grad_normed_start, grad_bias_start_all, g_ap0, g_ao0, g_pg4 = back_eight(
        (grad_four, grad_normed_end)
    )
    g_ap0, g_ao0, g_pg4 = (g_ap0, g_ao0, g_pg4)
    grad_bias_start = rounded(scatter_bias(grad_bias_start_all))
    grad_two, grad_rows_two, grad_gate_second, g_mg1, g_mo1, g_pg3, g_ab0 = back_seven(
        (grad_three, grad_normed_start, grad_bias_start)
    )
    g_mg1, g_mo1, g_pg3, g_ab0 = (g_mg1, g_mo1, g_pg3, g_ab0)
    grad_chan_left_two, grad_chan_right_two = incoming_backward(
        chan_left_two, chan_right_two, to_channels(narrow(grad_rows_two))
    )
    grad_left_second, grad_right_second = to_rows(
        (narrow(grad_chan_left_two), narrow(grad_chan_right_two))
    )
    grad_one, grad_rows_one, grad_gate_first, g_mg0, g_mo0, g_pg2, g_mp1, g_mgt1 = back_five(
        (grad_two, widen(grad_left_second), widen(grad_right_second), grad_gate_second)
    )
    g_mg0, g_mo0, g_pg2, g_mp1, g_mgt1 = (g_mg0, g_mo0, g_pg2, g_mp1, g_mgt1)
    grad_chan_left, grad_chan_right = outgoing_backward(
        chan_left, chan_right, to_channels(narrow(grad_rows_one))
    )
    grad_left_first, grad_right_first = to_rows((narrow(grad_chan_left), narrow(grad_chan_right)))
    grad_left_outer, grad_right_all, grad_pair_a, g_oo, g_pg1, g_mp0, g_mgt0 = back_three(
        (grad_one, widen(grad_left_first), widen(grad_right_first), grad_gate_first)
    )
    g_oo, g_pg1, g_mp0, g_mgt0 = (g_oo, g_pg1, g_mp0, g_mgt0)
    grad_right_outer = rounded(
        lax.psum_scatter(grad_right_all, "rows", scatter_dimension=0, tiled=True)
    )
    two_grads = back_two((widen(single_cot[0]), rounded(grad_left_outer), grad_right_outer))
    grad_query, grad_keys_all, grad_values_all, grad_gate_single, grad_row_bias, grad_single_a = (
        two_grads[:6]
    )
    g_sp4, g_sg1, g_su, g_sd, g_sg2, g_op0, g_op1 = tuple(two_grads[6:])
    grad_keys, grad_values = (
        lax.psum_scatter(grad_keys_all, "rows", scatter_dimension=0, tiled=True),
        lax.psum_scatter(grad_values_all, "rows", scatter_dimension=0, tiled=True),
    )
    grad_single_b, grad_pair_b, g_sg0, g_pg0, g_sp0, g_sp1, g_sp2, g_sp3, g_sb = back_one(
        (grad_query, rounded(grad_keys), rounded(grad_values), grad_gate_single, grad_row_bias)
    )
    g_sg0, g_pg0, g_sp0, g_sp1, g_sp2, g_sp3, g_sb = (
        g_sg0,
        g_pg0,
        g_sp0,
        g_sp1,
        g_sp2,
        g_sp3,
        g_sb,
    )
    weight_totals = (
        jnp.stack([g_sg0, g_sg1, g_sg2]),
        jnp.stack([g_pg0, g_pg1, g_pg2, g_pg3, g_pg4, g_pg5]),
        jnp.stack([g_mg0, g_mg1]),
        jnp.stack([g_sp0, g_sp1, g_sp2, g_sp3, g_sp4]),
        g_sb,
        g_su,
        g_sd,
        jnp.stack([g_op0, g_op1]),
        g_oo,
        jnp.stack([g_mp0, g_mp1]),
        jnp.stack([g_mgt0, g_mgt1]),
        jnp.stack([g_mo0, g_mo1]),
        jnp.stack([g_ap0, g_ap1]),
        jnp.stack([g_ab0, g_ab1]),
        jnp.stack([g_ao0, g_ao1]),
        g_pu,
        g_pd,
    )
    weight_totals = lax.psum(
        (
            weight_totals[0],
            weight_totals[1],
            weight_totals[2],
            weight_totals[3],
            weight_totals[4],
            weight_totals[5],
            weight_totals[6],
            weight_totals[7],
            weight_totals[8],
            weight_totals[9],
            weight_totals[10],
            weight_totals[11],
            weight_totals[12],
            weight_totals[13],
            weight_totals[14],
            weight_totals[15],
            weight_totals[16],
        ),
        ("grp", "rows"),
    )
    return (
        narrow(single_next)[None],
        narrow(pair_six)[None],
        (grad_single_a + grad_single_b)[None],
        (grad_pair_a + grad_pair_b)[None],
    ) + tuple(weight_totals)


def pad_rows(x, count):
    return jnp.concatenate([x, jnp.zeros((count - x.shape[0],) + x.shape[1:], x.dtype)], 0)


def fast_local(square, row_count):
    n = row_count
    rows = L // n
    part = L * rows // n
    crops = 4
    total = crops * n

    def home(g, r):
        if square:
            x, z = g % 2, r // 2
            near = 3 - z if x else z
            side_of, level = ((x, 0), (1 - x, 1), (x, 1), (1 - x, 0))[near]
            g, r = g - x + side_of, (3 - level if x else level) * 2 + r % 2
        return g * n + r

    groups = [[home(g, r) for r in range(n)] for g in range(crops)]

    def swap(x, back=False):
        if not square:
            return x
        pairs = [(g * n + r, home(g, r)) for g in range(crops) for r in range(n)]
        return lax.ppermute(x, AX, [(b, a) for a, b in pairs] if back else pairs)

    def to_home(k, x):
        pairs = [(g * n + r, home(g, (r + k) % n)) for g in range(crops) for r in range(n)]
        return lax.ppermute(x, AX, pairs)

    def from_home(k, x):
        pairs = [(home(g, r), g * n + (r + k) % n) for g in range(crops) for r in range(n)]
        return lax.ppermute(x, AX, pairs)

    def exchange(x):
        if square:
            return lax.all_to_all(x, AX, 0, 0, tiled=True, axis_index_groups=groups)
        return lax.all_to_all(x, "rows", 0, 0, tiled=True)

    def to_all(copies):
        return lax.all_to_all(copies, AX, 0, 0, tiled=True)

    chips = total // 2
    same_core = [[g * n + z * 2 + c for g in range(crops) for z in range(n // 2)] for c in range(2)]
    members = [sorted(set(d // 2 for d in group)) for group in groups]

    def other_core(x):
        return lax.ppermute(x, "rows", [(i, i ^ 1) for i in range(n)])

    def to_chips(copies):
        return lax.all_to_all(copies, AX, 0, 0, tiled=True, axis_index_groups=same_core)

    def local(
        single_rep, pair_rep, residue_mask, single_gains, pair_gains, mult_gains, single_proj,
        single_bias, single_up, single_down, opm_proj, opm_out, mult_proj, mult_gate, mult_out,
        att_proj, att_bias, att_out, pair_up, pair_down, single_cot, pair_cot,
    ):
        grp, row = lax.axis_index("grp"), lax.axis_index("rows")
        crop, block = grp, row
        if square:
            half = row // 4
            level = jnp.where(half == 1, 3 - row // 2, row // 2)
            near = jnp.where(grp % 2 == half, 2 * level, 3 - 2 * level)
            crop = grp - grp % 2 + half
            block = jnp.where(half == 1, 3 - near, near) * 2 + row % 2
        where = jnp.stack([crop, block, grp, row]).astype(jnp.int32)
        single, width = single_rep[0], single_rep.shape[2]
        gathered = lax.all_to_all(
            jnp.broadcast_to(single, (n,) + single.shape), "rows", 0, 0, tiled=True
        )
        pair = swap(pair_rep[0])
        att_b, single_b = jnp.swapaxes(att_bias, 1, 2), single_bias.T
        m5t, m5, mot, mof, a4t, a4, aot, abt, upt, up, dnt, sbt = prep_weights(
            pair_gains, mult_gains, mult_proj, mult_gate, mult_out, att_proj, att_b, att_out,
            pair_up, pair_down, single_b,
        )
        opm = opm_proj.shape[2]
        outer = jnp.swapaxes(opm_proj, 0, 1).reshape(width, 2 * opm)
        outer = jnp.pad(outer, ((0, 0), (0, L - 2 * opm)))
        outer_w = jnp.swapaxes(opm_out, 0, 1)
        mask_row = f32(residue_mask)
        mine, mask_col = pack(rows, single, single_cot[0], pair_rep[0], mask_row, sbt, where)
        single_out, lr = single_own(
            n, rows, total, gathered, mine, mask_col, single_gains, single_proj, single_up,
            single_down, outer,
        )
        lr = to_all(lr)

        z1, ab1, pmask, key_row, inner, lrt, left_own = front(
            n, rows, where, lr, pair, outer_w, m5t
        )
        dealt = deal(n, rows, where, pair_cot[0], (mine,))
        cots = {}

        def send_cots(offsets, ahead, behind):
            for k in offsets:
                block, _ = lax.optimization_barrier((dealt[k], behind))
                cots[k] = to_home(k, block)
            return lax.optimization_barrier((ahead, *[cots[k] for k in offsets]))[0]

        ab1 = send_cots((0, 1), ab1, lr)
        ab1 = exchange(ab1)
        p1 = exchange(channel_product(n, rows, True, ab1)).reshape(C * rows, L)
        z2, ab2 = middle(n, rows, z1, p1, mot, pmask, m5t)
        ab2 = send_cots((2, 3), ab2, p1)
        ab2 = exchange(ab2)
        p2 = exchange(channel_product(n, rows, False, ab2)).reshape(C * rows, L)
        z3, tb = start_front(n, rows, z2, p2, m5t, mot, abt)
        tb = send_cots((4, 5), tb, p2)
        tb_all = exchange(tb)
        z4, turn = start_attention(n, rows, z3, tb_all, key_row, a4t, aot, abt)
        turn = send_cots((6, 7), turn, tb_all)
        turn = exchange(turn)
        copies = to_chips(copies_of(mine, chips, (turn,)))
        others = other_core(copies)

        *pouts, back, m_up, m_dn, m_a41, m_ao1 = end_both(
            n, rows, where, turn, [cots[k] for k in range(n)], key_row, a4t, a4, aot, att_out, upt,
            up, dnt, pair_down,
        )
        back = exchange(back)
        sent = {}

        def send_pouts(offsets, ahead, behind):
            for k in offsets:
                block, _ = lax.optimization_barrier((pouts[k], behind))
                sent[k] = from_home(k, block)
            return lax.optimization_barrier((ahead, *[sent[k] for k in offsets]))[0]

        dz4, dxs, dtb, m_a40, m_ao0, m_ab1 = start_back(
            n, rows, z3, z4, back, tb_all, key_row, a4t, a4, att_out, abt, deps=(copies, others)
        )
        dtb = send_pouts((0, 1, 2, 3), dtb, back)
        dtb = exchange(dtb)
        dz3, dgp2, dp2, m_ab0, m_mo1 = third_back(
            n, rows, z3, dz4, dxs, dtb, abt, z2, p2, m5t, mot, mof
        )
        dp2 = send_pouts((4, 5), dp2, dtb)
        dp2 = exchange(dp2.reshape(n, part, L))
        dab2 = channel_product_back(n, rows, False, ab2, dp2)
        kept = single_every(
            n, rows, where, copies, others, single_gains, single_proj, single_up, single_down,
            deps=(dab2,),
        )
        dab2 = exchange(dab2)
        dz2, dgp1, dp1, m_m51, m_mo0 = second_back(
            n, rows, z2, dz3, dgp2, dab2, pmask, m5t, m5, z1, p1, mot, mof, deps=(kept[0],)
        )
        dp1 = send_pouts((6, 7), dp1, dab2)
        pair_six = undeal(n, rows, where, [sent[k] for k in range(n)])
        dp1 = exchange(dp1.reshape(n, part, L))
        dab1 = exchange(channel_product_back(n, rows, True, ab1, dp1))
        dz1, ends, m_oo, m_m50 = first_back(
            n, rows, chips, where, z1, dz2, dgp1, dab1, pmask, m5t, m5, inner, lrt, left_own,
            outer_w,
        )
        names = [
            "up", "dn", "a41", "ao1", "a40", "ao0", "m51", "mo1", "mo0", "m50", "oo", "ab1", "ab0",
        ]
        sums = [
            m_up, m_dn, m_a41, m_ao1, m_a40, m_ao0, m_m51, m_mo1, m_mo0, m_m50, m_oo, m_ab1, m_ab0,
        ]
        places, at = {}, 0
        for name, m in zip(names, sums):
            places[name] = at
            at += m.shape[0]
        half = -(-at // (total * 16)) * total * 8
        near, far = collect(where, sums, half, ())
        near = b16(near + f32(other_core(far)))
        ends = to_chips(ends)
        ends, near = lax.optimization_barrier((ends, near))
        others_ends = other_core(ends)
        dz1 = swap(copies_of(dz1, 1, (others_ends,))[0], True)
        near, others_ends = lax.optimization_barrier((near, others_ends))
        near = to_chips(near.reshape(chips, half // chips, C))
        ys, g_sg, d_own, drb, m_op = single_back(
            members, rows, where, ends, others_ends, kept, single_gains, single_proj,
            single_up, single_down, outer,
        )
        pair_grad, m_sb = last_back(rows, pair_rep[0], drb, dz1, sbt)
        near_sums = sum_copies(near, m_sb, chips)
        g_sp, g_su, g_sd = weight_grads(kept[2], ys, width, single_up.shape[1], near_sums)
        g_op = jnp.swapaxes(m_op[:, : 2 * opm].reshape(width, 2, opm), 0, 1)

        near = copies_of(to_chips(near_sums), 1, (g_sp, g_su, g_sd, pair_six))[0]
        grads = finish(
            where, near, other_core(near), pair_gains, mult_gains, mult_proj, mult_gate,
            mult_out, att_proj, att_b, pair_up, single_b, places, half, opm, (),
        )
        g_pg, g_mg, g_sb, g_oo, g_mp, g_mgt, g_mo, g_ap, g_ab, g_ao, g_pu, g_pd = grads
        return (
            single_out[None],
            pair_six[None],
            d_own[None],
            pair_grad[None],
            g_sg,
            g_pg,
            g_mg,
            g_sp,
            g_sb.T,
            g_su,
            g_sd,
            g_op,
            g_oo,
            g_mp,
            g_mgt,
            g_mo,
            g_ap,
            jnp.swapaxes(g_ab, 1, 2),
            g_ao,
            g_pu,
            g_pd,
        )

    return local


def solution(mesh):
    groups_of, n = mesh.shape["grp"], mesh.shape["rows"]
    whole = P()
    in_specs = (
        (P("grp", "rows", None), P("grp", "rows", None, None), P("grp", None))
        + (whole,) * 17
        + (P("grp", "rows", None), P("grp", "rows", None, None))
    )
    out_specs = (
        P("grp", "rows", None),
        P("grp", "rows", None, None),
        P("grp", "rows", None),
        P("grp", "rows", None, None),
    ) + (whole,) * 17
    if L % n == 0 and (L // n) % 16 == 0:
        body = fast_local((groups_of, n) == (4, 8), n)
    else:
        body = general_local
    return jax.shard_map(body, mesh=mesh, in_specs=in_specs, out_specs=out_specs, check_vma=False)
```

```python
import math

import jax
import jax.numpy as jnp
from jax import lax
from jax.experimental import pallas as pl
from jax.experimental.pallas import tpu as pltpu
from jax.sharding import PartitionSpec as P

BF = jnp.bfloat16
F32 = jnp.float32
EPSILON = 1e-05
MASKED = 1000000000.0
AX = ("grp", "rows")
L = 128
C = 128
TH = 4
HD = 32
HPAD = 16


def dot(a, b):
    return lax.dot_general(a, b, (((1,), (0,)), ((), ())), preferred_element_type=F32)


def dot_nt(a, b):
    return lax.dot_general(a, b, (((1,), (1,)), ((), ())), preferred_element_type=F32)


def dot_tn(a, b):
    return lax.dot_general(a, b, (((0,), (0,)), ((), ())), preferred_element_type=F32)


def b16(x):
    return x.astype(BF)


def f32(x):
    return x.astype(F32)


def sig(x):
    return 0.5 * jnp.tanh(0.5 * x) + 0.5


GELU_A = 0.7978845608028654
GELU_B = 0.044715


def gelu_parts(x):
    t = jnp.tanh(GELU_A * (x + GELU_B * x * x * x))
    half = 0.5 * (1.0 + t)
    slope = half + 0.5 * x * (1.0 - t * t) * (GELU_A * (1.0 + 3.0 * GELU_B * x * x))
    return x * half, slope


def norm_cols(z):
    c = z - jnp.mean(z, 0, keepdims=True)
    scale = lax.rsqrt(jnp.mean(c * c, 0, keepdims=True) + EPSILON)
    return c * scale, scale


def norm_cols_back(dx, xh, scale):
    return scale * (
        dx - jnp.mean(dx, 0, keepdims=True) - xh * jnp.mean(dx * xh, 0, keepdims=True)
    )


U = 16


def cols(r):
    return pl.ds(pl.multiple_of(r * U * L, U * L), U * L)


def side(parts):
    return jnp.concatenate(parts, 1)


def lanes(x, u):
    return x[:, u * L : (u + 1) * L]


def get_rows(ref, r, count, rows):
    return side([ref[pl.ds(r * U + u, count, stride=rows), :] for u in range(U)])


def put_rows(ref, r, count, rows, x):
    for u in range(U):
        ref[pl.ds(r * U + u, count, stride=rows), :] = lanes(x, u)


def put_turned(ref, r, rows, x):
    for u in range(U):
        ref[pl.ds(r * U + u, L, stride=rows), :] = lanes(x, u).T


def get_turned(ref, r, rows):
    return side(
        [
            f32(ref[:, pl.ds(pl.multiple_of((r * U + u) * rows, rows), rows), :].reshape(L, C)).T
            for u in range(U)
        ]
    )


def each_row(count, body):
    def step(r, carry):
        body(r)
        return carry

    lax.fori_loop(0, count, step, 0, unroll=4 if count == 4 else 1)


def call(kernel, outs, scratch, args, deps=(), raw=(), late=(), far=(), step=16, us=5):
    global U
    U = step
    count, more, given = len(args), len(deps), len(outs)
    fetched = [args[k] for k in raw]

    def body(*refs):
        mine = list(refs[:count])
        results = list(refs[count + more : count + more + given])
        rest = list(refs[count + more + given :])
        sems = rest.pop() if raw or far else None
        stores = [rest.pop() for _ in far][::-1]
        held = [rest.pop() for _ in raw][::-1]
        moves = {}
        for i, k in enumerate(raw):
            moves[k] = pltpu.make_async_copy(mine[k], held[i], sems.at[i])
            moves[k].start()
        for k in raw:
            if k not in late:
                moves[k].wait()
        for i, k in enumerate(raw):
            mine[k] = held[i]
        ends = []
        for i, k in enumerate(far):
            ends.append(pltpu.make_async_copy(stores[i], results[k], sems.at[len(raw) + i]))
            results[k] = stores[i]
        early = set()

        def arrive(k):
            moves[k].wait()

        def leave(k):
            early.add(far.index(k))
            ends[far.index(k)].start()

        if late:
            kernel((arrive, leave), *mine, *results, *rest)
        else:
            kernel(*mine, *results, *rest)
        for i, end in enumerate(ends):
            if i not in early:
                end.start()
        for end in ends:
            end.wait()

    vm = pl.BlockSpec(memory_space=pltpu.VMEM)
    sm = pl.BlockSpec(memory_space=pltpu.SMEM)
    away = pl.BlockSpec(memory_space=pl.ANY)
    moved = sum(a.size * a.dtype.itemsize for a in args)
    buffers = [pltpu.VMEM(s, d) for s, d in scratch]
    buffers += [pltpu.VMEM(a.shape, a.dtype) for a in fetched]
    buffers += [pltpu.VMEM(*outs[k]) for k in far]
    placed = sum(math.prod(b.shape) * jnp.dtype(b.dtype).itemsize for b in buffers)
    if raw or far:
        buffers.append(pltpu.SemaphoreType.DMA((len(raw) + len(far),)))
    return pl.pallas_call(
        body,
        out_shape=[
            pltpu.HBM(s, d) if k in far else jax.ShapeDtypeStruct(s, d)
            for k, (s, d) in enumerate(outs)
        ],
        in_specs=[
            away if k in raw else sm if a.dtype == jnp.int32 else vm for k, a in enumerate(args)
        ]
        + [away] * more,
        out_specs=[away if k in far else vm for k in range(given)],
        scratch_shapes=buffers,
        compiler_params=pltpu.CompilerParams(vmem_limit_bytes=(30 << 20) + placed),
        cost_estimate=pl.CostEstimate(flops=us * 10**9, bytes_accessed=moved if us else 0, transcendentals=0),
    )(
        *[
            pltpu.with_memory_space_constraint(a, pltpu.HBM) if k in raw else a
            for k, a in enumerate(args)
        ],
        *[pltpu.with_memory_space_constraint(d, pltpu.HBM) for d in deps],
    )


def prep_weights(gp, gm, mp, mg, mo, ap, ab, ao, pu, pd, sb):
    def kernel(
        gp, gm, mp, mg, mo, ap, ab, ao, pu, pd, sb,
        m5t, m5, mot, mof, a4t, a4, aot, abt, upt, up, dnt, sbt,
    ):
        gpv = f32(gp[...])
        gmv = f32(gm[...])

        def padded(w):
            return jnp.concatenate([f32(w), jnp.zeros((HPAD - w.shape[0], C), F32)], 0)

        for t in range(2):
            g = gpv[1 + t : 2 + t]
            for k in range(5):
                w = f32(mp[t, k] if k < 4 else mg[t]).T * g
                m5t[t, k * C : (k + 1) * C] = b16(w)
                m5[t, :, k * C : (k + 1) * C] = b16(w.T)
            w = f32(mo[t]).T * gmv[t : t + 1]
            mot[t] = b16(w)
            mof[t] = b16(w.T)
            g = gpv[3 + t : 4 + t]
            for k in range(4):
                w = f32(ap[t, k]).T * (g * HD**-0.5 if k == 0 else g)
                a4t[t, k * C : (k + 1) * C] = b16(w)
                a4[t, :, k * C : (k + 1) * C] = b16(w.T)
            aot[t] = b16(f32(ao[t]).T)
            abt[t] = b16(padded(ab[t]) * g)
        g = gpv[5:6]
        for k in range(4):
            s = slice(k * C, (k + 1) * C)
            w = f32(pu[:, s]).T * g
            upt[s] = b16(w)
            up[:, s] = b16(w.T)
            dnt[:, s] = b16(f32(pd[s]).T)
        sbt[...] = b16(padded(sb[...]) * gpv[0:1])

    outs = [
        ((2, 640, C), BF), ((2, C, 640), BF), ((2, C, C), BF), ((2, C, C), BF),
        ((2, 512, C), BF), ((2, C, 512), BF), ((2, C, C), BF), ((2, HPAD, C), BF),
        ((512, C), BF), ((C, 512), BF), ((C, 512), BF), ((HPAD, C), BF),
    ]
    return call(kernel, outs, [], (gp, gm, mp, mg, mo, ap, ab, ao, pu, pd, sb), raw=(0, 1, 2, 3, 4, 5, 6, 7, 8, 9, 10), far=(0, 1, 2, 3, 4, 5, 6, 7, 8, 9, 10, 11), us=3)


def pack(rows, single, cot, pair, mask, sbt, where):
    def kernel(single, cot, pair, mask, sbt, where, mine, mask_col, s, sm):
        sm[...] = jnp.broadcast_to(mask[...], (L, L)).T
        mask_col[...] = sm[pl.ds(pl.multiple_of(where[3] * rows, rows), rows), :]
        key_row = (mask[...] - 1.0) * MASKED

        def body(r):
            xh, _ = norm_cols(side([f32(pair[r * U + u]).T for u in range(U)]))
            put_rows(s, r, HPAD, rows, dot(sbt[...], b16(xh)) + side([key_row] * U))

        each_row(rows // U, body)
        mine[0:rows] = single[...]
        mine[rows : 2 * rows] = cot[...]
        for h in range(8):
            mine[rows * (2 + h // 4) : rows * (3 + h // 4), (h % 4) * L : (h % 4 + 1) * L] = b16(
                s[h * rows : (h + 1) * rows]
            )

    width = single.shape[1]
    return call(
        kernel,
        [((4 * rows, width), BF), ((rows, L), F32)],
        [((HPAD * rows, L), F32), ((L, L), F32)],
        (single, cot, pair, mask, sbt, where), raw=(0, 1, 2, 4), us=2)


def copies_of(x, count, deps):
    def kernel(x, out):
        for d in range(count):
            out[d] = x[...]

    return call(kernel, [((count,) + x.shape, x.dtype)], [], (x,), deps=deps)[0]


def deal(n, rows, where, x, deps):
    def kernel(where, x, *outs):
        for k in range(n):
            block = lax.rem(where[3] + k, n)
            at = pl.ds(pl.multiple_of(block * rows, rows), rows)
            outs[k][...] = x[:, at, :].reshape(rows * rows, C)

    return call(
        kernel, [((rows * rows, C), BF)] * n, [], (where, x), deps=deps, raw=(1,),
        far=tuple(range(n)), us=1,
    )


def undeal(n, rows, where, parts):
    def kernel(where, *refs):
        out = refs[n]
        for k in range(n):
            block = lax.rem(where[3] + n - k, n)
            at = pl.ds(pl.multiple_of(block * rows, rows), rows)
            out[:, at, :] = refs[k][...].reshape(rows, rows, C)

    return call(
        kernel, [((rows, L, C), BF)], [], (where, *parts), raw=tuple(range(1, n + 1)), far=(0,),
        us=1,
    )[0]


def part_of(x, first, last, deps):
    def kernel(x, out):
        out[...] = x[first:last]

    return call(
        kernel, [((last - first,) + x.shape[1:], x.dtype)], [], (x,), deps=deps, raw=(0,), us=1
    )[0]


def norm_rows16(x):
    c = x - jnp.mean(x, -1, keepdims=True)
    scale = lax.rsqrt(jnp.mean(c * c, -1, keepdims=True) + EPSILON)
    return c * scale, scale


def norm_rows16_back(dx, xh, scale):
    return scale * (
        dx - jnp.mean(dx, -1, keepdims=True) - xh * jnp.mean(dx * xh, -1, keepdims=True)
    )


def halves():
    lane = lax.broadcasted_iota(jnp.int32, (1, L), 1)
    low = jnp.where(lane < L // 2, 1.0, 0.0)
    return b16(low), b16(1.0 - low)


def pair_weights(q, k, bias0, bias1):
    out = []
    for m, bias in zip(halves(), (bias0, bias1)):
        s = dot_nt(q * m, k) + bias
        e = jnp.exp(s - jnp.max(s, -1, keepdims=True))
        out.append(b16(e / jnp.sum(e, -1, keepdims=True)))
    return out


def on_halves(x, axis=0):
    return jnp.concatenate([x * m for m in halves()], axis)


def single_own(n, rows, copies, gathered, mine, mask_col, gains, proj, up, down, outer):
    width = up.shape[0]
    opm2 = 64

    def kernel(moves, gathered, mine, mask_col, gains, proj, up, down, outer, out, lr):
        g = f32(gains[...])
        sn = b16(norm_rows16(f32(gathered[...].reshape(n * rows, width)))[0] * g[0:1])
        arrive, _ = moves
        arrive(4)
        keys, vals = b16(dot(sn, proj[1])), b16(dot(sn, proj[2]))
        x = f32(mine[0:rows])
        sn = b16(norm_rows16(x)[0] * g[0:1])
        query = b16(dot(sn, proj[0]) * 0.125)
        gate = sig(dot(sn, proj[3]))
        mixed = []
        for t in range(4):
            s = slice(t * L, (t + 1) * L)
            bias = [
                f32(mine[rows * (2 + h // 4) : rows * (3 + h // 4), (h % 4) * L : (h % 4 + 1) * L])
                for h in (2 * t, 2 * t + 1)
            ]
            p = pair_weights(query[:, s], keys[:, s], *bias)
            mixed.append(dot(jnp.concatenate(p, 1), on_halves(vals[:, s])))
        mixed = jnp.concatenate(mixed, 1)
        first = x + dot(b16(mixed * gate), proj[4])
        x1 = b16(norm_rows16(first)[0] * g[1:2])
        arrive(5)
        hidden = b16(gelu_parts(dot(x1, up[...]))[0])
        arrive(6)
        second = first + dot(hidden, down[...])
        out[...] = b16(second)
        x2 = b16(norm_rows16(second)[0] * g[2:3])
        both = dot(x2, outer[...]) * mask_col[...]
        lane = lax.broadcasted_iota(jnp.int32, (rows, L), 1)
        both = b16(jnp.where(lane >= opm2, mask_col[...], both))
        for d in range(copies):
            lr[d] = both

    return call(
        kernel,
        [((rows, width), BF), ((copies, rows, L), BF)],
        [],
        (gathered, mine, mask_col, gains, proj, up, down, outer), raw=(3, 4, 5, 6, 7), late=(4, 5, 6), us=6)


def single_every(n, rows, where, ga, gb, gains, proj, up, down, deps=()):
    width, wide = up.shape
    tokens = 4 * L
    half = ga.shape[0]

    def kernel(
        moves, where, ga, gb, gains, proj, up, down,
        x_all, cot_all, xs, qkv, gm, probs, slope, first_out, second_out, held,
    ):
        arrive, leave = moves
        core = where[3] % 2
        for k in range(half):
            held[2 * k + core] = ga[k]
            held[2 * k + 1 - core] = gb[k]
        g = f32(gains[...])
        x16 = held[:, 0:rows, :].reshape(tokens, width)
        x_all[...] = x16
        cot_all[...] = held[:, rows : 2 * rows, :].reshape(tokens, width)
        leave(0)
        leave(1)
        x = f32(x16)
        sn = b16(norm_rows16(x)[0] * g[0:1])
        xs[:, 0:width] = sn
        arrive(4)
        qkv[:, 0:width] = b16(dot(sn, proj[0]) * 0.125)
        qkv[:, width : 2 * width] = b16(dot(sn, proj[1]))
        qkv[:, 2 * width : 3 * width] = b16(dot(sn, proj[2]))
        leave(3)
        gate = sig(dot(sn, proj[3]))
        gm[:, 0:width] = b16(gate)

        def body(crop):
            own = pl.ds(pl.multiple_of(crop * L, L), L)
            part = pl.ds(crop * n, n)
            for t in range(4):
                q = qkv[own, t * L : (t + 1) * L]
                k = qkv[own, width + t * L : width + (t + 1) * L]
                v = qkv[own, 2 * width + t * L : 2 * width + (t + 1) * L]
                bias = [
                    f32(
                        held[
                            part,
                            rows * (2 + h // 4) : rows * (3 + h // 4),
                            (h % 4) * L : (h % 4 + 1) * L,
                        ].reshape(L, L)
                    )
                    for h in (2 * t, 2 * t + 1)
                ]
                p = pair_weights(q, k, *bias)
                for m in range(2):
                    at = pl.multiple_of((crop * 8 + 2 * t + m) * L, L)
                    probs[pl.ds(at, L), :] = p[m]
                mixed = dot(jnp.concatenate(p, 1), on_halves(v))
                gm[own, width + t * L : width + (t + 1) * L] = b16(mixed)

        each_row(4, body)
        leave(5)
        leave(4)
        u = b16(f32(gm[:, width : 2 * width]) * f32(gm[:, 0:width]))
        xs[:, width : 2 * width] = u
        first = x + dot(u, proj[4])
        first_out[...] = first
        leave(7)
        x1 = b16(norm_rows16(first)[0] * g[1:2])
        xs[:, 2 * width : 3 * width] = x1
        arrive(5)
        total = first
        arrive(6)
        for m in range(wide // width):
            s = slice(m * width, (m + 1) * width)
            hid, slp = gelu_parts(dot(x1, up[:, s]))
            h16 = b16(hid)
            xs[:, (3 + m) * width : (4 + m) * width] = h16
            slope[:, s] = b16(slp)
            total = total + dot(h16, down[s])
        second_out[...] = total

    return call(
        kernel,
        [
            ((tokens, width), BF), ((tokens, width), BF), ((tokens, 3 * width + wide), BF),
            ((tokens, 3 * width), BF), ((tokens, 2 * width), BF), ((4 * 8 * L, L), BF),
            ((tokens, wide), BF), ((tokens, width), F32), ((tokens, width), F32),
        ],
        [((2 * half, 4 * rows, width), BF)],
        (where, ga, gb, gains, proj, up, down),
        deps=deps, raw=(1, 2, 3, 4, 5, 6), late=(4, 5, 6), far=(0, 1, 2, 3, 4, 5, 6, 7, 8), us=19)


def single_back(members, rows, where, ea, eb, kept, gains, proj, up, down, outer, deps=()):
    width, wide = up.shape
    tokens = 4 * L
    x_all, cot_all, _, qkv, gm, probs, slope, first_in, second_in = kept

    def kernel(
        moves, where, ea, eb, x_all, cot_all, qkv, gm, probs, slope, first_in, second_in,
        gains, proj, up, down, outer,
        ys, gain_grad, d_own, drb, m_op,
        dlr, o_do, sdrb, sds, srow,
    ):
        arrive, _ = moves
        g = f32(gains[...])
        for crop in range(4):
            total = f32(ea[members[crop][0]]) + f32(eb[members[crop][0]])
            for k in members[crop][1:]:
                total = total + (f32(ea[k]) + f32(eb[k]))
            total = jnp.concatenate([total, jnp.zeros_like(total)], 0)
            dlr[crop * L : (crop + 1) * L] = b16(total.T)
        x2, sc2 = norm_rows16(second_in[...])
        m_op[...] = dot_tn(b16(x2 * g[2:3]), dlr[...])
        dx = dot_nt(dlr[...], outer[...])
        gain_grad[2:3] = jnp.sum(dx * x2, 0, keepdims=True)
        ds2 = f32(cot_all[...]) + norm_rows16_back(dx * g[2:3], x2, sc2)
        ds2_16 = b16(ds2)
        ys[:, 5 * width + wide :] = ds2_16
        for k in (14, 8, 13, 9):
            arrive(k)
        dx = jnp.zeros((tokens, width), F32)
        for m in range(wide // width):
            s = slice(m * width, (m + 1) * width)
            dhp = b16(dot_nt(ds2_16, down[s]) * f32(slope[:, s]))
            ys[:, (5 + m) * width : (6 + m) * width] = dhp
            dx = dx + dot_nt(dhp, up[:, s])
        x1, sc1 = norm_rows16(first_in[...])
        gain_grad[1:2] = jnp.sum(dx * x1, 0, keepdims=True)
        df = ds2 + norm_rows16_back(dx * g[1:2], x1, sc1)
        sds[...] = df
        df16 = b16(df)
        ys[:, 4 * width : 5 * width] = df16
        for k in (12, 6, 5, 7):
            arrive(k)
        du = dot_nt(df16, proj[4])
        gate, mixed = f32(gm[:, 0:width]), f32(gm[:, width : 2 * width])
        do = du * gate
        o_do[...] = b16(do)
        srow[...] = do * mixed
        ys[:, 3 * width : 4 * width] = b16(du * mixed * gate * (1.0 - gate))
        lane = lax.broadcasted_iota(jnp.int32, (1, L), 1)
        low = jnp.where(lane < L // 2, 1.0, 0.0)

        def body(crop):
            own = pl.ds(pl.multiple_of(crop * L, L), L)
            for t in range(4):
                s = slice(t * L, (t + 1) * L)
                q = qkv[own, t * L : (t + 1) * L]
                k = qkv[own, width + t * L : width + (t + 1) * L]
                v = qkv[own, 2 * width + t * L : 2 * width + (t + 1) * L]
                do16, row = o_do[own, s], srow[own, s]
                grads, weights = [], []
                for j, (m, mf) in enumerate(zip(halves(), (low, 1.0 - low))):
                    at = pl.multiple_of((crop * 8 + 2 * t + j) * L, L)
                    p16 = probs[pl.ds(at, L), :]
                    dp = dot_nt(do16 * m, v)
                    e = f32(p16) * (dp - jnp.sum(row * mf, -1, keepdims=True))
                    sdrb[pl.ds(at, L), :] = e
                    grads.append(b16(e))
                    weights.append(p16)
                dq = dot(jnp.concatenate(grads, 1), on_halves(k)) * 0.125
                dk = dot_tn(jnp.concatenate(grads, 0), on_halves(q))
                dv = dot_tn(jnp.concatenate(weights, 0), on_halves(do16))
                ys[own, t * L : (t + 1) * L] = b16(dq)
                ys[own, width + t * L : width + (t + 1) * L] = b16(dk)
                ys[own, 2 * width + t * L : 2 * width + (t + 1) * L] = b16(dv)

        each_row(4, body)
        dx = dot_nt(ys[:, 0:width], proj[0])
        for k in range(1, 4):
            dx = dx + dot_nt(ys[:, k * width : (k + 1) * width], proj[k])
        x0, sc0 = norm_rows16(f32(x_all[...]))
        gain_grad[0:1] = jnp.sum(dx * x0, 0, keepdims=True)
        sds[...] = sds[...] + norm_rows16_back(dx * g[0:1], x0, sc0)
        grp, row = where[2], where[3]
        d_own[...] = sds[pl.ds(pl.multiple_of(grp * L + row * rows, rows), rows), :]
        for h in range(8):
            at = pl.multiple_of((grp * 8 + h) * L + row * rows, rows)
            drb[h * rows : (h + 1) * rows] = sdrb[pl.ds(at, rows), :]

    return call(
        kernel,
        [
            ((tokens, 6 * width + wide), BF), ((3, width), F32), ((rows, width), F32),
            ((8 * rows, L), F32), ((width, L), F32),
        ],
        [
            ((tokens, L), BF), ((tokens, width), BF), ((4 * 8 * L, L), F32), ((tokens, width), F32),
            ((tokens, width), F32),
        ],
        (
            where, ea, eb, x_all, cot_all, qkv, gm, probs, slope, first_in, second_in,
            gains, proj, up, down, outer,
        ), deps=deps, raw=(10, 15, 4, 11, 14, 8, 13, 9, 12, 6, 5, 7, 3), late=(5, 6, 7, 8, 9, 12, 13, 14), far=(0, 1, 2, 3, 4), us=22)


def weight_grads(xs, ys, width, wide, after):
    tokens = xs.shape[0]
    blocks = wide // width

    def kernel(x, y, after, out):
        out[...] = dot_tn(x[...], y[...]).reshape(out.shape)

    def run(steps, x_at, y_at, shape, block, out_at):
        return pl.pallas_call(
            kernel,
            grid=(steps,),
            out_shape=pltpu.HBM(shape, F32),
            in_specs=[
                pl.BlockSpec((tokens, width), x_at),
                pl.BlockSpec((tokens, width), y_at),
                pl.BlockSpec(memory_space=pl.ANY),
            ],
            out_specs=pl.BlockSpec(block, out_at),
            compiler_params=pltpu.CompilerParams(vmem_limit_bytes=32 << 20),
            cost_estimate=pl.CostEstimate(
                flops=2 * 10**9,
                bytes_accessed=steps * width * width * 8,
                transcendentals=0,
            ),
        )(
            pltpu.with_memory_space_constraint(xs, pltpu.HBM),
            pltpu.with_memory_space_constraint(ys, pltpu.HBM),
            pltpu.with_memory_space_constraint(after, pltpu.HBM),
        )

    proj = run(
        5, lambda i: (0, i // 4), lambda i: (0, i), (5, width, width), (1, width, width),
        lambda i: (i, 0, 0),
    )
    up = run(
        blocks, lambda i: (0, 2), lambda i: (0, 5 + i), (width, wide), (width, width),
        lambda i: (0, i),
    )
    down = run(
        blocks, lambda i: (0, 3 + i), lambda i: (0, 5 + blocks), (wide, width), (width, width),
        lambda i: (i, 0),
    )
    return proj, up, down


def project_pair(z, r, rows, m5t, pmask, sa, sb):
    xh, _ = norm_cols(z)
    p = dot(m5t[0:512], b16(xh))
    mk = get_rows(pmask, r, 1, 1)
    put_rows(sa, r, C, rows, sig(p[0:C]) * p[C : 2 * C] * mk)
    put_rows(sb, r, C, rows, sig(p[2 * C : 3 * C]) * p[3 * C : 4 * C] * mk)


def put_pair(n, ab, sa, sb):
    part = sa.shape[0] // n
    for d in range(n):
        ab[d, 0:part] = b16(sa[d * part : (d + 1) * part])
        ab[d, part : 2 * part] = b16(sb[d * part : (d + 1) * part])


def gated_product(z, r, rows, gatet, mot, sp):
    xh, _ = norm_cols(z)
    gate = sig(dot(gatet[...], b16(xh)))
    ph, _ = norm_cols(get_rows(sp, r, C, rows))
    return z + dot(mot[...], b16(ph)) * gate


def front(n, rows, where, lr_all, pair, outer_w, m5ts, deps=()):
    opm = outer_w.shape[0]

    def kernel(
        where, lr_all, pair, outer_w, m5ts,
        z1, ab, pmask, key_row, inner, lrt, left_own, sa, sb, slr, spm,
    ):
        m5t = m5ts.at[0]
        crop, block = where[0], where[1]
        lr16 = lr_all[pl.ds(crop * n, n)].reshape(L, C)
        lr = f32(lr16)
        turned = lr.T
        lrt[...] = turned
        mrow = turned[2 * opm : 2 * opm + 1]
        key_row[...] = (mrow - 1.0) * MASKED
        first = pl.multiple_of(block * rows, rows)
        spm[...] = jnp.broadcast_to(mrow, (L, L)).T * mrow
        pmask[...] = spm[pl.ds(first, rows), :]
        slr[...] = lr
        left = b16(slr[pl.ds(first, rows), :])
        left_own[...] = left
        inners = dot(left[:, 0:opm], side([outer_w[b] for b in range(opm)]))
        for b in range(opm):
            inner[b * rows : (b + 1) * rows] = lanes(inners, b)
        edge = jnp.zeros((opm, C), BF)

        def body(r):
            parts = []
            for u in range(U):
                mine = b16(inner[pl.ds(r * U + u, opm, stride=rows), :])
                mine = jnp.concatenate([edge, mine, edge, edge], 0)
                parts.append((f32(pair[r * U + u]) + dot(lr16, mine)).T)
            z = side(parts)
            z1[:, cols(r)] = z
            project_pair(z, r, rows, m5t, pmask, sa, sb)

        each_row(rows // U, body)
        put_pair(n, ab, sa, sb)

    part = C * rows // n
    return call(
        kernel,
        [
            ((C, rows * L), F32), ((n, 2 * part, L), BF), ((rows, L), F32), ((1, L), F32),
            ((opm * rows, C), F32), ((C, L), F32), ((rows, C), BF),
        ],
        [((C * rows, L), F32)] * 2 + [((L, C), F32), ((L, L), F32)],
        (where, lr_all, pair, outer_w, m5ts), deps=deps, raw=(2, 3, 4), far=(0, 2, 3, 4, 5, 6), us=5)


def middle(n, rows, z1, prod, mots, pmask, m5ts, deps=()):
    def kernel(z1, prod, mots, pmask, m5ts, z2, ab, sa, sb, sp):
        gatet, mot, m5t = m5ts.at[0, 512:640], mots.at[0], m5ts.at[1]
        sp[...] = f32(prod[...])

        def body(r):
            z = gated_product(z1[:, cols(r)], r, rows, gatet, mot, sp)
            z2[:, cols(r)] = z
            project_pair(z, r, rows, m5t, pmask, sa, sb)

        each_row(rows // U, body)
        put_pair(n, ab, sa, sb)

    part = C * rows // n
    return call(
        kernel,
        [((C, rows * L), F32), ((n, 2 * part, L), BF)],
        [((C * rows, L), F32)] * 3,
        (z1, prod, mots, pmask, m5ts), deps=deps, raw=(0, 1, 2, 3, 4), far=(0,), us=4)


def start_front(n, rows, z2, prod, m5ts, mots, abts, deps=()):
    def kernel(z2, prod, m5ts, mots, abts, z3, tb, sp, st):
        gatet, mot, abt = m5ts.at[1, 512:640], mots.at[1], abts.at[0]
        sp[...] = f32(prod[...])

        def body(r):
            z = gated_product(z2[:, cols(r)], r, rows, gatet, mot, sp)
            z3[:, cols(r)] = z
            xh, _ = norm_cols(z)
            put_rows(st, r, HPAD, rows, dot(abt[...], b16(xh)))

        each_row(rows // U, body)
        for d in range(n):
            tb[d] = b16(st[0 : TH * rows])

    return call(
        kernel,
        [((C, rows * L), F32), ((n, TH * rows, L), BF)],
        [((C * rows, L), F32), ((HPAD * rows, L), F32)],
        (z2, prod, m5ts, mots, abts), deps=deps, raw=(0, 1, 2, 3, 4), far=(0,), us=4)


def channel_product(n, rows, outgoing, ab):
    def kernel(ab, out):
        part = C * rows // n
        for ch in range(C // n):
            a = ab[:, ch * rows : (ch + 1) * rows, :].reshape(L, L)
            b = ab[:, part + ch * rows : part + (ch + 1) * rows, :].reshape(L, L)
            prod = dot_nt(a, b) if outgoing else dot_tn(a, b)
            out[:, ch * rows : (ch + 1) * rows, :] = b16(prod).reshape(n, rows, L)

    return call(kernel, [((n, C * rows // n, L), BF)], [], (ab,), raw=(0,), us=1)[0]


def channel_product_back(n, rows, outgoing, ab, dprod, deps=()):
    def kernel(ab, dprod, out):
        part = C * rows // n
        for ch in range(C // n):
            low, high = ch * rows, (ch + 1) * rows
            a = ab[:, low:high, :].reshape(L, L)
            b = ab[:, part + low : part + high, :].reshape(L, L)
            g = dprod[:, low:high, :].reshape(L, L)
            if outgoing:
                da, db = dot(g, b), dot_tn(g, a)
            else:
                da, db = dot_nt(b, g), dot(a, g)
            out[:, low:high, :] = b16(da).reshape(n, rows, L)
            out[:, part + low : part + high, :] = b16(db).reshape(n, rows, L)

    return call(kernel, [((n, 2 * C * rows // n, L), BF)], [], (ab, dprod), deps=deps, raw=(0,), us=2)[0]


def head_masks():
    lane = lax.broadcasted_iota(jnp.int32, (1, C), 1)
    return [b16(jnp.where((lane >= h * HD) & (lane < (h + 1) * HD), 1.0, 0.0)) for h in range(TH)]


def by_head(x):
    pm = b16(x.T)
    return jnp.concatenate([pm * m for m in head_masks()], 0)


def attend(x16, a4t, bias):
    p4 = dot(a4t[...], x16)
    gate = sig(p4[3 * C : 4 * C])
    each, mixed = [], []
    for u in range(U):
        q, k, v = (lanes(p4[m * C : (m + 1) * C], u) for m in range(3))
        logits = dot(by_head(k), b16(q)) + bias[...]
        raised, outs = [], []
        v16 = b16(v)
        for h in range(TH):
            s = logits[h * L : (h + 1) * L]
            e = jnp.exp(s - jnp.max(s, 0, keepdims=True))
            inv = 1.0 / jnp.sum(e, 0, keepdims=True)
            raised.append((e, inv))
            outs.append(dot(v16[h * HD : (h + 1) * HD], b16(e)) * inv)
        each.append((q, k, v, raised))
        mixed.append(jnp.concatenate(outs, 0))
    return each, gate, side(mixed)


def attend_back(state, dy16, ao, dbias):
    each, gate, mixed = state
    du = dot(ao[...], dy16)
    do = du * gate
    dgate = du * mixed * gate * (1.0 - gate)
    both = do * mixed
    parts = []
    for u in range(U):
        q, k, v, raised = each[u]
        do16, q16, k16 = b16(lanes(do, u)), b16(q), b16(k)
        dp = dot(by_head(v), do16)
        row = lanes(both, u)
        dq, dk, dv = [], [], []
        for h in range(TH):
            s = slice(h * HD, (h + 1) * HD)
            w = slice(h * L, (h + 1) * L)
            e, inv = raised[h]
            p = e * inv
            ds = p * (dp[w] - jnp.sum(row[s], 0, keepdims=True))
            dbias[w, :] += ds
            ds16, p16 = b16(ds), b16(p)
            dv.append(dot_nt(do16[s], p16))
            dq.append(dot(k16[s], ds16))
            dk.append(dot_nt(q16[s], ds16))
        parts.append(jnp.concatenate([b16(x) for x in dq + dk + dv], 0))
    return jnp.concatenate([side(parts), b16(dgate)], 0)


def start_attention(n, rows, z3, tb_all, key_row, a4ts, aots, abts, deps=()):
    def kernel(z3, tb_all, key_row, a4ts, aots, abts, z4, send, bias, st, se):
        a4t, aot, abt = a4ts.at[0], aots.at[0], abts.at[1]
        for h in range(TH):
            b = f32(tb_all[:, h * rows : (h + 1) * rows, :].reshape(L, L)) + key_row[...]
            bias[h * L : (h + 1) * L, :] = b.T

        def body(r):
            z = z3[:, cols(r)]
            xh, _ = norm_cols(z)
            _, gate, mixed = attend(b16(xh), a4t, bias)
            z = z + dot(aot[...], b16(mixed * gate))
            z4[:, cols(r)] = z
            put_turned(st, r, rows, z)
            xe, _ = norm_cols(z)
            put_rows(se, r, HPAD, rows, dot(abt[...], b16(xe)))

        each_row(rows // U, body)
        part = L * rows // n
        for d in range(n):
            send[d, 0:part] = b16(st[d * part : (d + 1) * part])
            send[d, part : part + TH * rows] = b16(se[0 : TH * rows])

    part = L * rows // n
    return call(
        kernel,
        [((C, rows * L), F32), ((n, part + TH * rows, L), BF)],
        [((TH * L, L), F32), ((L * rows, C), F32), ((HPAD * rows, L), F32)],
        (z3, tb_all, key_row, a4ts, aots, abts), deps=deps, raw=(0, 1, 2, 3, 4, 5), far=(0,), us=12)


def end_both(n, rows, where, recv, cots, key_row, a4ts, a4s, aots, aos, upt, up, dnt, dn, deps=()):
    part = L * rows // n

    def kernel(where, recv, *refs):
        cots, refs = refs[:n], refs[n:]
        run(where, recv, cots, *refs)

    def run(
        where, recv, cots, key_row, a4ts, a4s, aots, aos, upt, up, dnt, dn,
        p0, p1, p2, p3, p4, p5, p6, p7, send, m_up, m_dn, m_a4, m_ao,
        bias, dbias, scot, sout, sdz, o_h, o_dh, o_x5, o_cot, o_x4, o_d4, o_u, o_dy,
    ):
        a4t, a4, aot, ao = a4ts.at[1], a4s.at[1], aots.at[1], aos.at[1]
        kb = jnp.broadcast_to(key_row[...], (L, L)).T
        for h in range(TH):
            b = recv[:, part + h * rows : part + (h + 1) * rows, :].reshape(L, L)
            bias[h * L : (h + 1) * L, :] = f32(b) + kb
        dbias[...] = jnp.zeros_like(dbias)
        for k in range(n):
            block = lax.rem(where[1] + n - k, n)
            scot[pl.ds(pl.multiple_of(block * part, part), part), :] = f32(cots[k][...])

        def body(r):
            w = cols(r)
            z4 = get_turned(recv, r, rows)
            x4, scale4 = norm_cols(z4)
            x16 = b16(x4)
            state = attend(x16, a4t, bias)
            gated = b16(state[2] * state[1])
            z5 = z4 + dot(aot[...], gated)
            x5, scale5 = norm_cols(z5)
            x516 = b16(x5)
            hid, slope = gelu_parts(dot(upt[...], x516))
            h16 = b16(hid)
            z6 = z5 + dot(dnt[...], h16)
            put_turned(sout, r, rows, z6)
            dz6 = side([scot[pl.ds(r * U + u, L, stride=rows), :].T for u in range(U)])
            c16 = b16(dz6)
            dh16 = b16(dot(dn[...], c16) * slope)
            dz5 = dz6 + norm_cols_back(dot(up[...], dh16), x5, scale5)
            dy16 = b16(dz5)
            d4 = attend_back(state, dy16, ao, dbias)
            dz4 = dz5 + norm_cols_back(dot(a4[...], d4), x4, scale4)
            put_turned(sdz, r, rows, dz4)
            o_h[:, w] = h16
            o_dh[:, w] = dh16
            o_x5[:, w] = x516
            o_cot[:, w] = c16
            o_x4[:, w] = x16
            o_d4[:, w] = d4
            o_u[:, w] = gated
            o_dy[:, w] = dy16

        each_row(rows // U, body)
        for d in range(n):
            send[d, 0:part] = b16(sdz[d * part : (d + 1) * part])
            for h in range(TH):
                send[d, part + h * rows : part + (h + 1) * rows] = b16(
                    dbias[h * L + d * rows : h * L + (d + 1) * rows]
                )
        for k, pout in enumerate((p0, p1, p2, p3, p4, p5, p6, p7)):
            block = lax.rem(where[1] + k, n)
            pout[...] = b16(sout[pl.ds(pl.multiple_of(block * part, part), part), :])
        for k in range(4):
            s = slice(k * C, (k + 1) * C)
            m_up[s] = dot_nt(o_x5[...], o_dh[s])
            m_a4[s] = dot_nt(o_x4[...], o_d4[s])
        m_dn[...] = dot_nt(o_h[...], o_cot[...])
        m_ao[...] = dot_nt(o_u[...], o_dy[...])

    wide = rows * L
    return call(
        kernel,
        [
            *[((part, C), BF)] * n, ((n, part + TH * rows, L), BF),
            ((512, C), F32), ((512, C), F32), ((512, C), F32), ((C, C), F32),
        ],
        [
            ((TH * L, L), F32), ((TH * L, L), F32), ((L * rows, C), F32), ((L * rows, C), F32),
            ((L * rows, C), F32),
            ((512, wide), BF), ((512, wide), BF), ((C, wide), BF), ((C, wide), BF),
            ((C, wide), BF), ((512, wide), BF), ((C, wide), BF), ((C, wide), BF),
        ],
        (where, recv, *cots, key_row, a4ts, a4s, aots, aos, upt, up, dnt, dn),
        deps=deps,
        raw=tuple(range(2, n + 11)),
        far=(0, 1, 2, 3, 4, 5, 6, 7, 9, 10, 11, 12),
        step=8, us=18,
    )


def start_back(n, rows, z3, z4, recv, tb_all, key_row, a4ts, a4s, aos, abts, deps=()):
    part = L * rows // n

    def kernel(
        z3, z4, recv, tb_all, key_row, a4ts, a4s, aos, abts,
        dz4_out, dxs, dtb, m_a4, m_ao, m_ab,
        bias, dbias, seb, o_x3, o_d4, o_u, o_dy, o_x4, o_eb,
    ):
        a4t, a4, ao, abt = a4ts.at[0], a4s.at[0], aos.at[0], abts.at[1]
        for h in range(TH):
            b = f32(tb_all[:, h * rows : (h + 1) * rows, :].reshape(L, L)) + key_row[...]
            bias[h * L : (h + 1) * L, :] = b.T
        dbias[...] = jnp.zeros_like(dbias)
        seb[...] = jnp.zeros_like(seb)
        total = f32(recv[0, part : part + TH * rows])
        for d in range(1, n):
            total = total + f32(recv[d, part : part + TH * rows])
        seb[0 : TH * rows, :] = total

        def body(r):
            w = cols(r)
            x4, scale4 = norm_cols(z4[:, w])
            eb16 = b16(get_rows(seb, r, HPAD, rows))
            dz4 = get_turned(recv, r, rows)
            dz4 = dz4 + norm_cols_back(dot_tn(abt[...], eb16), x4, scale4)
            dz4_out[:, w] = dz4
            x3, _ = norm_cols(z3[:, w])
            x16 = b16(x3)
            state = attend(x16, a4t, bias)
            dy16 = b16(dz4)
            d4 = attend_back(state, dy16, ao, dbias)
            dxs[:, w] = dot(a4[...], d4)
            o_x3[:, w] = x16
            o_d4[:, w] = d4
            o_u[:, w] = b16(state[2] * state[1])
            o_dy[:, w] = dy16
            o_x4[:, w] = b16(x4)
            o_eb[:, w] = eb16

        each_row(rows // U, body)
        for h in range(TH):
            turned = b16(dbias[h * L : (h + 1) * L, :].T)
            for d in range(n):
                dtb[d, h * rows : (h + 1) * rows] = turned[d * rows : (d + 1) * rows]
        for k in range(4):
            s = slice(k * C, (k + 1) * C)
            m_a4[s] = dot_nt(o_x3[...], o_d4[s])
        m_ao[...] = dot_nt(o_u[...], o_dy[...])
        m_ab[...] = dot_nt(o_eb[...], o_x4[...])

    wide = rows * L
    return call(
        kernel,
        [
            ((C, wide), F32), ((C, wide), F32), ((n, TH * rows, L), BF),
            ((512, C), F32), ((C, C), F32), ((HPAD, C), F32),
        ],
        [
            ((TH * L, L), F32), ((TH * L, L), F32), ((HPAD * rows, L), F32),
            ((C, wide), BF), ((512, wide), BF), ((C, wide), BF), ((C, wide), BF),
            ((C, wide), BF), ((HPAD, wide), BF),
        ],
        (z3, z4, recv, tb_all, key_row, a4ts, a4s, aos, abts),
        deps=deps, raw=(0, 1, 3, 4, 5, 6, 7, 8), far=(0, 1, 3, 4, 5), us=20)


def product_back(z, dz, r, rows, sp, gatet, mot, mof, sdp, dgp_out, o_ph, o_do):
    w = cols(r)
    xh, _ = norm_cols(z)
    gate = sig(dot(gatet[...], b16(xh)))
    ph, scale = norm_cols(get_rows(sp, r, C, rows))
    ph16 = b16(ph)
    out = dot(mot[...], ph16)
    dgp_out[:, w] = b16(dz * out * gate * (1.0 - gate))
    do16 = b16(dz * gate)
    put_rows(sdp, r, C, rows, norm_cols_back(dot(mof[...], do16), ph, scale))
    o_ph[:, w] = ph16
    o_do[:, w] = do16


def third_back(n, rows, z3, dz4, dxs, recv, abts, z2, prod, m5ts, mots, mofs, deps=()):
    def kernel(
        z3, dz4, dxs, recv, abts, z2, prod, m5ts, mots, mofs,
        dz3, dgp, dp, m_ab, m_mo,
        stb, sp, sdp, o_x3, o_tb, o_ph, o_do,
    ):
        abt, gatet, mot, mof = abts.at[0], m5ts.at[1, 512:640], mots.at[1], mofs.at[1]
        sp[...] = f32(prod[...])
        stb[...] = jnp.zeros_like(stb)
        total = f32(recv[0])
        for d in range(1, n):
            total = total + f32(recv[d])
        stb[0 : TH * rows, :] = total

        def body(r):
            w = cols(r)
            x3, scale3 = norm_cols(z3[:, w])
            tb16 = b16(get_rows(stb, r, HPAD, rows))
            dx = dxs[:, w] + dot_tn(abt[...], tb16)
            dz = dz4[:, w] + norm_cols_back(dx, x3, scale3)
            dz3[:, w] = dz
            o_x3[:, w] = b16(x3)
            o_tb[:, w] = tb16
            product_back(z2[:, w], dz, r, rows, sp, gatet, mot, mof, sdp, dgp, o_ph, o_do)

        each_row(rows // U, body)
        dp[...] = b16(sdp[...])
        m_ab[...] = dot_nt(o_tb[...], o_x3[...])
        m_mo[...] = dot_nt(o_ph[...], o_do[...])

    wide = rows * L
    return call(
        kernel,
        [
            ((C, wide), F32), ((C, wide), BF), ((C * rows, L), BF),
            ((HPAD, C), F32), ((C, C), F32),
        ],
        [
            ((HPAD * rows, L), F32), ((C * rows, L), F32), ((C * rows, L), F32),
            ((C, wide), BF), ((HPAD, wide), BF), ((C, wide), BF), ((C, wide), BF),
        ],
        (z3, dz4, dxs, recv, abts, z2, prod, m5ts, mots, mofs), deps=deps, raw=(0, 1, 2, 4, 5, 6, 7, 8, 9), far=(0, 1, 3, 4), us=7)


def projections_back(n, rows, z, dz, dgp, r, pmask, m5t, m5, sa, sb, o_x, o_d5):
    w = cols(r)
    xh, scale = norm_cols(z)
    x16 = b16(xh)
    p = dot(m5t[0:512], x16)
    mk = get_rows(pmask, r, 1, 1)
    da = get_rows(sa, r, C, rows) * mk
    db = get_rows(sb, r, C, rows) * mk
    ga, gb = sig(p[0:C]), sig(p[2 * C : 3 * C])
    va, vb = p[C : 2 * C], p[3 * C : 4 * C]
    d5 = jnp.concatenate(
        [
            b16(da * va * ga * (1.0 - ga)),
            b16(da * ga),
            b16(db * vb * gb * (1.0 - gb)),
            b16(db * gb),
            dgp[:, w],
        ],
        0,
    )
    o_x[:, w] = x16
    o_d5[:, w] = d5
    return dz + norm_cols_back(dot(m5[...], d5), xh, scale)


def take_pair(n, dab, sa, sb):
    part = sa.shape[0] // n
    for d in range(n):
        sa[d * part : (d + 1) * part, :] = f32(dab[d, 0:part])
        sb[d * part : (d + 1) * part, :] = f32(dab[d, part : 2 * part])


def second_back(n, rows, z2, dz3, dgp, dab, pmask, m5ts, m5s, z1, prod, mots, mofs, deps=()):
    def kernel(
        z2, dz3, dgp, dab, pmask, m5ts, m5s, z1, prod, mots, mofs,
        dz2, dgp_out, dp, m_m5, m_mo,
        sa, sb, sp, sdp, o_x, o_d5, o_ph, o_do,
    ):
        m5t, m5, gatet = m5ts.at[1], m5s.at[1], m5ts.at[0, 512:640]
        mot, mof = mots.at[0], mofs.at[0]
        sp[...] = f32(prod[...])
        take_pair(n, dab, sa, sb)

        def body(r):
            w = cols(r)
            dz = projections_back(
                n, rows, z2[:, w], dz3[:, w], dgp, r, pmask, m5t, m5, sa, sb, o_x, o_d5
            )
            dz2[:, w] = dz
            product_back(z1[:, w], dz, r, rows, sp, gatet, mot, mof, sdp, dgp_out, o_ph, o_do)

        each_row(rows // U, body)
        dp[...] = b16(sdp[...])
        for k in range(5):
            s = slice(k * C, (k + 1) * C)
            m_m5[s] = dot_nt(o_x[...], o_d5[s])
        m_mo[...] = dot_nt(o_ph[...], o_do[...])

    wide = rows * L
    return call(
        kernel,
        [
            ((C, wide), F32), ((C, wide), BF), ((C * rows, L), BF),
            ((640, C), F32), ((C, C), F32),
        ],
        [
            ((C * rows, L), F32), ((C * rows, L), F32), ((C * rows, L), F32), ((C * rows, L), F32),
            ((C, wide), BF), ((640, wide), BF), ((C, wide), BF), ((C, wide), BF),
        ],
        (z2, dz3, dgp, dab, pmask, m5ts, m5s, z1, prod, mots, mofs), deps=deps, raw=(0, 1, 2, 4, 5, 6, 7, 8, 9, 10), far=(0, 1, 3, 4), us=11)


def first_back(n, rows, copies, where, z1, dz2, dgp, dab, pmask, m5ts, m5s, inner, lrt, left_own, outer_w, deps=()):
    opm = outer_w.shape[0]

    def kernel(
        where, z1, dz2, dgp, dab, pmask, m5ts, m5s, inner, lrt, left_own, outer_w,
        dz1, ends, m_oo, m_m5,
        sa, sb, o_x, o_d5, sdi, sdr,
    ):
        m5t, m5 = m5ts.at[0], m5s.at[0]
        take_pair(n, dab, sa, sb)
        sdr[...] = jnp.zeros_like(sdr)
        right_t = b16(lrt[opm : 2 * opm])

        def body(r):
            w = cols(r)
            dz = projections_back(
                n, rows, z1[:, w], dz2[:, w], dgp, r, pmask, m5t, m5, sa, sb, o_x, o_d5
            )
            for u in range(U):
                dz16 = b16(lanes(dz, u).T)
                dz1[r * U + u] = dz16
                at = pl.ds(r * U + u, opm, stride=rows)
                sdi[at, :] = dot(right_t, dz16)
                sdr[...] += dot_nt(b16(inner[at, :]), dz16)

        each_row(rows // U, body)
        left = left_own[:, 0:opm]
        d16 = side([b16(sdi[b * rows : (b + 1) * rows]) for b in range(opm)])
        outers = dot_tn(left, d16)
        for b in range(opm):
            m_oo[b * opm : (b + 1) * opm] = lanes(outers, b)
        dleft = dot_nt(side([outer_w[b] for b in range(opm)]), d16)
        lane = lax.broadcasted_iota(jnp.int32, (rows, L), 1)
        spot = lax.broadcasted_iota(jnp.int32, (rows, L), 0) + where[1] * rows
        dleft = dot(b16(dleft), b16(jnp.where(lane == spot, 1.0, 0.0)))
        both = jnp.concatenate([dleft, sdr[...]], 0) * lrt[2 * opm : 2 * opm + 1]
        for d in range(copies):
            ends[d] = b16(both)
        for k in range(5):
            s = slice(k * C, (k + 1) * C)
            m_m5[s] = dot_nt(o_x[...], o_d5[s])

    wide = rows * L
    return call(
        kernel,
        [
            ((rows, L, C), BF), ((copies, 2 * opm, L), BF), ((opm * opm, C), F32), ((640, C), F32),
        ],
        [
            ((C * rows, L), F32), ((C * rows, L), F32), ((C, wide), BF), ((640, wide), BF),
            ((opm * rows, C), F32), ((opm, L), F32),
        ],
        (where, z1, dz2, dgp, dab, pmask, m5ts, m5s, inner, lrt, left_own, outer_w), deps=deps, raw=(1, 2, 3, 5, 6, 7, 8, 9, 10, 11), far=(2, 3), us=11)


def last_back(rows, pair, drb, dz1, sbt, deps=()):
    def kernel(pair, drb, dz1, sbt, grad, m_sb, o_x, o_d):
        def body(r):
            w = cols(r)
            xh, scale = norm_cols(side([f32(pair[r * U + u]).T for u in range(U)]))
            d = get_rows(drb, r, 8, rows)
            d16 = b16(jnp.concatenate([d, jnp.zeros_like(d)], 0))
            back = norm_cols_back(dot_tn(sbt[...], d16), xh, scale)
            for u in range(U):
                grad[r * U + u] = f32(dz1[r * U + u]) + lanes(back, u).T
            o_x[:, w] = b16(xh)
            o_d[:, w] = d16

        each_row(rows // U, body)
        m_sb[...] = dot_nt(o_d[...], o_x[...])

    wide = rows * L
    return call(
        kernel,
        [((rows, L, C), F32), ((HPAD, C), F32)],
        [((C, wide), BF), ((HPAD, wide), BF)],
        (pair, drb, dz1, sbt), deps=deps, raw=(0, 1, 2, 3), far=(0,), us=3)


def collect(where, parts, half, deps):
    def kernel(where, *refs):
        sources, (kept, given, rows) = refs[: len(parts)], refs[len(parts) :]
        core = where[3] % 2
        at = 0
        for ref in sources:
            rows[at : at + ref.shape[0]] = ref[...]
            at += ref.shape[0]
        if at < 2 * half:
            rows[at : 2 * half] = jnp.zeros((2 * half - at, C), F32)
        kept[...] = rows[pl.ds(pl.multiple_of(core * half, half), half), :]
        given[...] = b16(rows[pl.ds(pl.multiple_of((1 - core) * half, half), half), :])

    return call(
        kernel,
        [((half, C), F32), ((half, C), BF)],
        [((2 * half, C), F32)],
        (where, *parts),
        deps=deps,
        raw=tuple(range(1, len(parts) + 1)),
        us=0,
    )


def sum_copies(x, extra, count):
    rows, more = x.shape[1], extra.shape[0]

    def kernel(x, extra, out):
        total = b16(jnp.sum(f32(x[...]), 0))
        for d in range(count):
            out[d, 0:rows] = total
            out[d, rows : rows + more] = b16(extra[...])

    return call(kernel, [((count, rows + more, C), BF)], [], (x, extra), us=2)[0]


def finish(where, near, far, gp, gm, mp, mg, mo, ap, ab, pu, sb, places, half, opm, deps):
    def kernel(
        where, near, far, gp, gm, mp, mg, mo, ap, ab, pu, sb,
        g_pg, g_mg, g_sb, g_oo, g_mp, g_mgt, g_mo, g_ap, g_ab, g_ao, g_pu, g_pd,
        rows,
    ):
        core = where[3] % 2
        chips = near.shape[0]
        size = half // chips
        for k in range(chips):
            at = pl.multiple_of(core * half + k * size, 8)
            rows[pl.ds(at, size), :] = f32(near[k, 0:size])
            at = pl.multiple_of((1 - core) * half + k * size, 8)
            rows[pl.ds(at, size), :] = f32(far[k, 0:size])

        def take(name, count, skip=0):
            at = places[name] + skip
            return rows[at : at + count]

        gpv, gmv = f32(gp[...]), f32(gm[...])

        def column(row):
            return jnp.broadcast_to(row, (C, C)).T

        def over_lanes(x):
            return jnp.sum(x.T, 0, keepdims=True)

        def padded(w):
            return jnp.concatenate([f32(w), jnp.zeros((HPAD - w.shape[0], C), F32)], 0)

        total = jnp.zeros((8, C), F32)
        for k in range(chips):
            total = total + (f32(near[k, size : size + 8]) + f32(far[k, size : size + 8]))
        g_pg[0:1] = jnp.sum(f32(sb[...]) * total, 0, keepdims=True)
        g_sb[...] = total * gpv[0:1]
        for t in range(2):
            g = column(gpv[1 + t : 2 + t])
            both = jnp.zeros((C, C), F32)
            for k in range(5):
                m = take("m5%d" % t, C, k * C)
                both = both + m * f32(mp[t, k] if k < 4 else mg[t])
                if k < 4:
                    g_mp[t, k] = m * g
                else:
                    g_mgt[t] = m * g
            g_pg[1 + t : 2 + t] = over_lanes(both)
            m = take("mo%d" % t, C)
            g_mo[t] = m * column(gmv[t : t + 1])
            g_mg[t : t + 1] = over_lanes(m * f32(mo[t]))
            g = column(gpv[3 + t : 4 + t])
            both = jnp.zeros((C, C), F32)
            for k in range(4):
                m = take("a4%d" % t, C, k * C)
                if k == 0:
                    m = m * HD**-0.5
                both = both + m * f32(ap[t, k])
                g_ap[t, k] = m * g
            m = take("ab%d" % t, HPAD)
            g_pg[3 + t : 4 + t] = over_lanes(both) + jnp.sum(padded(ab[t]) * m, 0, keepdims=True)
            g_ab[t] = (m * gpv[3 + t : 4 + t])[0:TH]
            g_ao[t] = take("ao%d" % t, C)
        g = column(gpv[5:6])
        both = jnp.zeros((C, C), F32)
        for k in range(4):
            s = slice(k * C, (k + 1) * C)
            m = take("up", C, k * C)
            both = both + m * f32(pu[:, s])
            g_pu[:, s] = m * g
        g_pg[5:6] = over_lanes(both)
        g_pd[...] = take("dn", 512)
        for b in range(opm):
            g_oo[:, b, :] = take("oo", opm, b * opm)

    outs = [
        (6, C), (2, C), (8, C), (opm, opm, C), (2, 4, C, C), (2, C, C), (2, C, C), (2, 4, C, C),
        (2, TH, C), (2, C, C), (C, 512), (512, C),
    ]
    return call(
        kernel,
        [(s, F32) for s in outs],
        [((2 * half, C), F32)],
        (where, near, far, gp, gm, mp, mg, mo, ap, ab, pu, sb),

        raw=(3, 4, 5, 6, 7, 8, 9, 10, 11), deps=deps, far=tuple(range(12)), us=4,
    )


PRECISE = lax.Precision.HIGHEST


def for_sending(shard):

    def short(part):
        return part.astype(jnp.bfloat16) if part.dtype == jnp.float32 else part

    return jax.tree.map(short, shard)


def widen(operand):
    return operand.astype(jnp.float32)


def narrow(operand):
    return operand.astype(jnp.bfloat16)


def rounded(operand):
    return lax.optimization_barrier(operand.astype(jnp.bfloat16)).astype(jnp.float32)


def contract(pattern, first_term, second_term):
    return jnp.einsum(pattern, first_term, second_term, precision=PRECISE)


def low_product(pattern, first_term, second_term):
    return jnp.einsum(pattern, first_term, second_term, preferred_element_type=jnp.float32)


def norm_rows(operand, gain_vec):
    centre = operand - jnp.mean(operand, -1, keepdims=True)
    spread = jnp.mean(centre * centre, -1, keepdims=True)
    return centre * lax.rsqrt(spread + EPSILON) * gain_vec


def soft_weights(logits):
    highest = jnp.max(logits, -1, keepdims=True)
    raised = jnp.exp(logits - highest)
    return raised / jnp.sum(raised, -1, keepdims=True)


def single_attend(queries, key_rows, values, gate_value, pair_bias, key_bias, weight_out):
    head_count = pair_bias.shape[0]
    feature_width = queries.shape[-1]
    head_size = feature_width // head_count
    query_heads = queries.reshape(queries.shape[0], head_count, head_size)
    key_heads = key_rows.reshape(key_rows.shape[0], head_count, head_size)
    value_heads = values.reshape(values.shape[0], head_count, head_size)
    logits = (
        contract("ihd,jhd->hij", query_heads, key_heads) * head_size ** (-0.5)
        + pair_bias
        + key_bias
    )
    mixed = contract("hij,jhd->ihd", soft_weights(logits), value_heads).reshape(
        queries.shape[0], feature_width
    )
    return contract("is,st->it", mixed * jax.nn.sigmoid(gate_value), weight_out)


def tri_attend(normed, pair_bias, weight_four, weight_out, key_bias):
    head_count = pair_bias.shape[0]
    feature_width = normed.shape[-1]
    head_size = feature_width // head_count

    def one_row(row_in):
        projected = contract("lc,ncd->nld", row_in, weight_four)
        shaped = projected[:3].reshape(3, row_in.shape[0], head_count, head_size)
        logits = (
            contract("jhd,khd->hjk", shaped[0], shaped[1]) * head_size ** (-0.5)
            + pair_bias
            + key_bias
        )
        mixed = contract("hjk,khd->jhd", soft_weights(logits), shaped[2]).reshape(
            row_in.shape[0], feature_width
        )
        return contract("lc,cd->ld", mixed * jax.nn.sigmoid(projected[3]), weight_out)

    return lax.map(jax.checkpoint(one_row), normed)


def mult_front(pair_in, gain_vec, weight_four, weight_gate, pair_mask):
    normed = norm_rows(pair_in, gain_vec)
    projected = contract("rlc,ncm->nmrl", normed, weight_four)
    left_side = jax.nn.sigmoid(projected[0]) * projected[1] * pair_mask
    right_side = jax.nn.sigmoid(projected[2]) * projected[3] * pair_mask
    gate_value = jax.nn.sigmoid(contract("rlc,cd->rld", normed, weight_gate))
    return (left_side, right_side, gate_value)


def mult_back(pair_in, product, gate_value, gain_vec, weight_out):
    centre = product - jnp.mean(product, 0, keepdims=True)
    spread = jnp.mean(centre * centre, 0, keepdims=True)
    scaled = centre * lax.rsqrt(spread + EPSILON) * gain_vec[:, None, None]
    return pair_in + contract("mrl,mc->rlc", scaled, weight_out) * gate_value


def outgoing_forward(left_chan, right_chan):
    return low_product("mik,mjk->mij", left_chan, right_chan)


def outgoing_backward(left_chan, right_chan, grad_out):
    return (
        low_product("mij,mjk->mik", grad_out, right_chan),
        low_product("mij,mik->mjk", grad_out, left_chan),
    )


def incoming_forward(left_chan, right_chan):
    return low_product("mki,mkj->mij", left_chan, right_chan)


def incoming_backward(left_chan, right_chan, grad_out):
    return (
        low_product("mij,mkj->mki", grad_out, right_chan),
        low_product("mij,mki->mkj", grad_out, left_chan),
    )


def to_channels(operand):
    return jax.tree.map(
        lambda part, own: part.astype(own.dtype),
        lax.all_to_all(for_sending(operand), "rows", split_axis=0, concat_axis=1, tiled=True),
        operand,
    )


def to_rows(operand):
    return jax.tree.map(
        lambda part, own: part.astype(own.dtype),
        lax.all_to_all(for_sending(operand), "rows", split_axis=1, concat_axis=0, tiled=True),
        operand,
    )


def turn_cols(operand):
    return jnp.swapaxes(
        lax.all_to_all(operand, "rows", split_axis=1, concat_axis=0, tiled=True), 0, 1
    )


def turn_rows(operand):
    return lax.all_to_all(
        jnp.swapaxes(operand, 0, 1), "rows", split_axis=0, concat_axis=1, tiled=True
    )


def gather_bias(operand):
    return lax.all_gather(operand, "rows", axis=1, tiled=True)


def scatter_bias(operand):
    return lax.psum_scatter(operand, "rows", scatter_dimension=1, tiled=True)


def general_local(
    single_rep,
    pair_rep,
    residue_mask,
    single_gains,
    pair_gains,
    mult_gains,
    single_proj,
    single_bias,
    single_up,
    single_down,
    opm_proj,
    opm_out,
    mult_proj,
    mult_gate,
    mult_out,
    att_proj,
    att_bias,
    att_out,
    pair_up,
    pair_down,
    single_cot,
    pair_cot,
):
    gains_s = widen(single_gains)
    gains_p = widen(pair_gains)
    gains_m = widen(mult_gains)
    proj_s = widen(single_proj)
    bias_sw = widen(single_bias)
    up_s = widen(single_up)
    down_s = widen(single_down)
    proj_o = widen(opm_proj)
    outer_w = widen(opm_out)
    proj_m = widen(mult_proj)
    gate_m = widen(mult_gate)
    out_m = widen(mult_out)
    proj_a = widen(att_proj)
    bias_a = widen(att_bias)
    out_a = widen(att_out)
    up_p = widen(pair_up)
    down_p = widen(pair_down)
    mask_all = widen(residue_mask[0])
    shard_rows = pair_rep.shape[1]
    first_row = lax.axis_index("rows") * shard_rows
    mask_own = lax.dynamic_slice_in_dim(mask_all, first_row, shard_rows, 0)
    key_bias = (mask_all - 1.0) * MASKED
    pair_mask = mask_own[:, None] * mask_all[None, :]
    single_own = widen(single_rep[0])
    pair_own = widen(pair_rep[0])

    def front_single(
        single_in, pair_in, gain_s, gain_z, proj_query, proj_key, proj_value, proj_gate, bias_w
    ):
        normed = norm_rows(single_in, gain_s)
        pair_normed = norm_rows(pair_in, gain_z)
        return (
            contract("rs,st->rt", normed, proj_query),
            contract("rs,st->rt", normed, proj_key),
            contract("rs,st->rt", normed, proj_value),
            contract("rs,st->rt", normed, proj_gate),
            contract("rlc,ch->hrl", pair_normed, bias_w),
        )

    def back_single(
        queries,
        key_rows,
        values,
        gate_value,
        row_bias,
        single_in,
        proj_out,
        gain_t,
        weight_up,
        weight_down,
        gain_o,
        left_w,
        right_w,
    ):
        first_sum = single_in + single_attend(
            queries, key_rows, values, gate_value, row_bias, key_bias, proj_out
        )
        hidden = jax.nn.gelu(contract("rs,st->rt", norm_rows(first_sum, gain_t), weight_up))
        second_sum = first_sum + contract("rt,ts->rs", hidden, weight_down)
        outer_in = norm_rows(second_sum, gain_o)
        left_side = contract("rs,sa->ra", outer_in, left_w) * mask_own[:, None]
        right_side = contract("rs,sa->ra", outer_in, right_w) * mask_own[:, None]
        return (second_sum, left_side, right_side)

    def outer_front(left_side, right_all, pair_in, weight_outer, gain_in, weight_four, weight_gate):
        inner = contract("ia,abc->ibc", left_side, weight_outer)
        updated = pair_in + contract("ibc,jb->ijc", inner, right_all)
        left_m, right_m, gate_value = mult_front(
            updated, gain_in, weight_four, weight_gate, pair_mask
        )
        return (updated, left_m, right_m, gate_value)

    def middle_mult(
        pair_in, product, gate_value, gain_out, weight_out, gain_in, weight_four, weight_gate
    ):
        updated = mult_back(pair_in, product, gate_value, gain_out, weight_out)
        left_m, right_m, gate_next = mult_front(
            updated, gain_in, weight_four, weight_gate, pair_mask
        )
        return (updated, left_m, right_m, gate_next)

    def start_front_general(pair_in, product, gate_value, gain_out, weight_out, gain_start, bias_w):
        updated = mult_back(pair_in, product, gate_value, gain_out, weight_out)
        normed = norm_rows(updated, gain_start)
        return (updated, normed, contract("rlc,ch->hrl", normed, bias_w))

    def start_core(pair_in, normed, bias_all, weight_four, weight_out, gain_end):
        updated = pair_in + tri_attend(normed, bias_all, weight_four, weight_out, key_bias)
        return (updated, norm_rows(updated, gain_end))

    def end_bias(turned, bias_w):
        return contract("rlc,ch->hrl", turned, bias_w)

    def end_core(turned, bias_all, weight_four, weight_out):
        return tri_attend(turned, bias_all, weight_four, weight_out, key_bias)

    def final_pair(pair_in, update, gain_vec, weight_up, weight_down):
        summed = pair_in + update
        hidden = jax.nn.gelu(contract("rlc,cd->rld", norm_rows(summed, gain_vec), weight_up))
        return summed + contract("rld,dc->rlc", hidden, weight_down)

    outs_one, back_one = jax.vjp(
        front_single,
        single_own,
        pair_own,
        gains_s[0],
        gains_p[0],
        proj_s[0],
        proj_s[1],
        proj_s[2],
        proj_s[3],
        bias_sw,
    )
    queries, keys_own, values_own, gate_single, row_bias = outs_one
    keys_all, values_all = (
        lax.all_gather(narrow(keys_own), "rows", axis=0, tiled=True),
        lax.all_gather(narrow(values_own), "rows", axis=0, tiled=True),
    )
    outs_two, back_two = jax.vjp(
        back_single,
        queries,
        widen(keys_all),
        widen(values_all),
        gate_single,
        row_bias,
        single_own,
        proj_s[4],
        gains_s[1],
        up_s,
        down_s,
        gains_s[2],
        proj_o[0],
        proj_o[1],
    )
    single_next, left_outer, right_outer = outs_two
    right_all = widen(lax.all_gather(narrow(right_outer), "rows", axis=0, tiled=True))
    outs_three, back_three = jax.vjp(
        outer_front,
        rounded(left_outer),
        right_all,
        pair_own,
        outer_w,
        gains_p[1],
        proj_m[0],
        gate_m[0],
    )
    pair_one, left_first, right_first, gate_first = outs_three
    chan_left, chan_right = to_channels((narrow(left_first), narrow(right_first)))
    product_one = outgoing_forward(chan_left, chan_right)
    rows_one = widen(to_rows(narrow(product_one)))
    outs_five, back_five = jax.vjp(
        middle_mult,
        pair_one,
        rows_one,
        gate_first,
        gains_m[0],
        out_m[0],
        gains_p[2],
        proj_m[1],
        gate_m[1],
    )
    pair_two, left_second, right_second, gate_second = outs_five
    chan_left_two, chan_right_two = to_channels((narrow(left_second), narrow(right_second)))
    product_two = incoming_forward(chan_left_two, chan_right_two)
    rows_two = widen(to_rows(narrow(product_two)))
    outs_seven, back_seven = jax.vjp(
        start_front_general, pair_two, rows_two, gate_second, gains_m[1], out_m[1], gains_p[3], bias_a[0]
    )
    pair_three, normed_start, bias_start = outs_seven
    bias_start_all = widen(gather_bias(narrow(bias_start)))
    outs_eight, back_eight = jax.vjp(
        start_core, pair_three, normed_start, bias_start_all, proj_a[0], out_a[0], gains_p[4]
    )
    pair_four, normed_end = outs_eight
    turned = widen(turn_cols(narrow(normed_end)))
    bias_end, back_nine = jax.vjp(end_bias, turned, bias_a[1])
    bias_end_all = widen(gather_bias(narrow(bias_end)))
    update_turned, back_ten = jax.vjp(end_core, turned, bias_end_all, proj_a[1], out_a[1])
    update = widen(turn_rows(narrow(update_turned)))
    pair_six, back_eleven = jax.vjp(final_pair, pair_four, update, gains_p[5], up_p, down_p)
    grad_four, grad_update, g_pg5, g_pu, g_pd = back_eleven(widen(pair_cot[0]))
    g_pg5, g_pu, g_pd = (g_pg5, g_pu, g_pd)
    grad_turned_update = widen(turn_cols(narrow(grad_update)))
    grad_turned_a, grad_bias_end_all, g_ap1, g_ao1 = back_ten(grad_turned_update)
    g_ap1, g_ao1 = (g_ap1, g_ao1)
    grad_bias_end = rounded(scatter_bias(grad_bias_end_all))
    grad_turned_b, g_ab1 = back_nine(grad_bias_end)
    grad_normed_end = widen(turn_rows(narrow(grad_turned_a + grad_turned_b)))
    grad_three, grad_normed_start, grad_bias_start_all, g_ap0, g_ao0, g_pg4 = back_eight(
        (grad_four, grad_normed_end)
    )
    g_ap0, g_ao0, g_pg4 = (g_ap0, g_ao0, g_pg4)
    grad_bias_start = rounded(scatter_bias(grad_bias_start_all))
    grad_two, grad_rows_two, grad_gate_second, g_mg1, g_mo1, g_pg3, g_ab0 = back_seven(
        (grad_three, grad_normed_start, grad_bias_start)
    )
    g_mg1, g_mo1, g_pg3, g_ab0 = (g_mg1, g_mo1, g_pg3, g_ab0)
    grad_chan_left_two, grad_chan_right_two = incoming_backward(
        chan_left_two, chan_right_two, to_channels(narrow(grad_rows_two))
    )
    grad_left_second, grad_right_second = to_rows(
        (narrow(grad_chan_left_two), narrow(grad_chan_right_two))
    )
    grad_one, grad_rows_one, grad_gate_first, g_mg0, g_mo0, g_pg2, g_mp1, g_mgt1 = back_five(
        (grad_two, widen(grad_left_second), widen(grad_right_second), grad_gate_second)
    )
    g_mg0, g_mo0, g_pg2, g_mp1, g_mgt1 = (g_mg0, g_mo0, g_pg2, g_mp1, g_mgt1)
    grad_chan_left, grad_chan_right = outgoing_backward(
        chan_left, chan_right, to_channels(narrow(grad_rows_one))
    )
    grad_left_first, grad_right_first = to_rows((narrow(grad_chan_left), narrow(grad_chan_right)))
    grad_left_outer, grad_right_all, grad_pair_a, g_oo, g_pg1, g_mp0, g_mgt0 = back_three(
        (grad_one, widen(grad_left_first), widen(grad_right_first), grad_gate_first)
    )
    g_oo, g_pg1, g_mp0, g_mgt0 = (g_oo, g_pg1, g_mp0, g_mgt0)
    grad_right_outer = rounded(
        lax.psum_scatter(grad_right_all, "rows", scatter_dimension=0, tiled=True)
    )
    two_grads = back_two((widen(single_cot[0]), rounded(grad_left_outer), grad_right_outer))
    grad_query, grad_keys_all, grad_values_all, grad_gate_single, grad_row_bias, grad_single_a = (
        two_grads[:6]
    )
    g_sp4, g_sg1, g_su, g_sd, g_sg2, g_op0, g_op1 = tuple(two_grads[6:])
    grad_keys, grad_values = (
        lax.psum_scatter(grad_keys_all, "rows", scatter_dimension=0, tiled=True),
        lax.psum_scatter(grad_values_all, "rows", scatter_dimension=0, tiled=True),
    )
    grad_single_b, grad_pair_b, g_sg0, g_pg0, g_sp0, g_sp1, g_sp2, g_sp3, g_sb = back_one(
        (grad_query, rounded(grad_keys), rounded(grad_values), grad_gate_single, grad_row_bias)
    )
    g_sg0, g_pg0, g_sp0, g_sp1, g_sp2, g_sp3, g_sb = (
        g_sg0,
        g_pg0,
        g_sp0,
        g_sp1,
        g_sp2,
        g_sp3,
        g_sb,
    )
    weight_totals = (
        jnp.stack([g_sg0, g_sg1, g_sg2]),
        jnp.stack([g_pg0, g_pg1, g_pg2, g_pg3, g_pg4, g_pg5]),
        jnp.stack([g_mg0, g_mg1]),
        jnp.stack([g_sp0, g_sp1, g_sp2, g_sp3, g_sp4]),
        g_sb,
        g_su,
        g_sd,
        jnp.stack([g_op0, g_op1]),
        g_oo,
        jnp.stack([g_mp0, g_mp1]),
        jnp.stack([g_mgt0, g_mgt1]),
        jnp.stack([g_mo0, g_mo1]),
        jnp.stack([g_ap0, g_ap1]),
        jnp.stack([g_ab0, g_ab1]),
        jnp.stack([g_ao0, g_ao1]),
        g_pu,
        g_pd,
    )
    weight_totals = lax.psum(
        (
            weight_totals[0],
            weight_totals[1],
            weight_totals[2],
            weight_totals[3],
            weight_totals[4],
            weight_totals[5],
            weight_totals[6],
            weight_totals[7],
            weight_totals[8],
            weight_totals[9],
            weight_totals[10],
            weight_totals[11],
            weight_totals[12],
            weight_totals[13],
            weight_totals[14],
            weight_totals[15],
            weight_totals[16],
        ),
        ("grp", "rows"),
    )
    return (
        narrow(single_next)[None],
        narrow(pair_six)[None],
        (grad_single_a + grad_single_b)[None],
        (grad_pair_a + grad_pair_b)[None],
    ) + tuple(weight_totals)


def pad_rows(x, count):
    return jnp.concatenate([x, jnp.zeros((count - x.shape[0],) + x.shape[1:], x.dtype)], 0)


def fast_local(square, row_count):
    n = row_count
    rows = L // n
    part = L * rows // n
    crops = 4
    total = crops * n

    def home(g, r):
        if square:
            x, z = g % 2, r // 2
            near = 3 - z if x else z
            side_of, level = ((x, 0), (1 - x, 1), (x, 1), (1 - x, 0))[near]
            g, r = g - x + side_of, (3 - level if x else level) * 2 + r % 2
        return g * n + r

    groups = [[home(g, r) for r in range(n)] for g in range(crops)]

    def swap(x, back=False):
        if not square:
            return x
        pairs = [(g * n + r, home(g, r)) for g in range(crops) for r in range(n)]
        return lax.ppermute(x, AX, [(b, a) for a, b in pairs] if back else pairs)

    def to_home(k, x):
        pairs = [(g * n + r, home(g, (r + k) % n)) for g in range(crops) for r in range(n)]
        return lax.ppermute(x, AX, pairs)

    def from_home(k, x):
        pairs = [(home(g, r), g * n + (r + k) % n) for g in range(crops) for r in range(n)]
        return lax.ppermute(x, AX, pairs)

    def exchange(x):
        if square:
            return lax.all_to_all(x, AX, 0, 0, tiled=True, axis_index_groups=groups)
        return lax.all_to_all(x, "rows", 0, 0, tiled=True)

    def to_all(copies):
        return lax.all_to_all(copies, AX, 0, 0, tiled=True)

    chips = total // 2
    same_core = [[g * n + z * 2 + c for g in range(crops) for z in range(n // 2)] for c in range(2)]
    members = [sorted(set(d // 2 for d in group)) for group in groups]

    def other_core(x):
        return lax.ppermute(x, "rows", [(i, i ^ 1) for i in range(n)])

    def to_chips(copies):
        return lax.all_to_all(copies, AX, 0, 0, tiled=True, axis_index_groups=same_core)

    def local(
        single_rep, pair_rep, residue_mask, single_gains, pair_gains, mult_gains, single_proj,
        single_bias, single_up, single_down, opm_proj, opm_out, mult_proj, mult_gate, mult_out,
        att_proj, att_bias, att_out, pair_up, pair_down, single_cot, pair_cot,
    ):
        grp, row = lax.axis_index("grp"), lax.axis_index("rows")
        crop, block = grp, row
        if square:
            half = row // 4
            level = jnp.where(half == 1, 3 - row // 2, row // 2)
            near = jnp.where(grp % 2 == half, 2 * level, 3 - 2 * level)
            crop = grp - grp % 2 + half
            block = jnp.where(half == 1, 3 - near, near) * 2 + row % 2
        where = jnp.stack([crop, block, grp, row]).astype(jnp.int32)
        single, width = single_rep[0], single_rep.shape[2]
        gathered = lax.all_to_all(
            jnp.broadcast_to(single, (n,) + single.shape), "rows", 0, 0, tiled=True
        )
        pair = swap(pair_rep[0])
        att_b, single_b = jnp.swapaxes(att_bias, 1, 2), single_bias.T
        m5t, m5, mot, mof, a4t, a4, aot, abt, upt, up, dnt, sbt = prep_weights(
            pair_gains, mult_gains, mult_proj, mult_gate, mult_out, att_proj, att_b, att_out,
            pair_up, pair_down, single_b,
        )
        opm = opm_proj.shape[2]
        outer = jnp.swapaxes(opm_proj, 0, 1).reshape(width, 2 * opm)
        outer = jnp.pad(outer, ((0, 0), (0, L - 2 * opm)))
        outer_w = jnp.swapaxes(opm_out, 0, 1)
        mask_row = f32(residue_mask)
        mine, mask_col = pack(rows, single, single_cot[0], pair_rep[0], mask_row, sbt, where)
        single_out, lr = single_own(
            n, rows, total, gathered, mine, mask_col, single_gains, single_proj, single_up,
            single_down, outer,
        )
        lr = to_all(lr)

        z1, ab1, pmask, key_row, inner, lrt, left_own = front(
            n, rows, where, lr, pair, outer_w, m5t
        )
        dealt = deal(n, rows, where, pair_cot[0], (mine,))
        cots = {}

        def send_cots(offsets, ahead, behind):
            for k in offsets:
                block, _ = lax.optimization_barrier((dealt[k], behind))
                cots[k] = to_home(k, block)
            return lax.optimization_barrier((ahead, *[cots[k] for k in offsets]))[0]

        ab1 = send_cots((0, 1), ab1, lr)
        ab1 = exchange(ab1)
        p1 = exchange(channel_product(n, rows, True, ab1)).reshape(C * rows, L)
        z2, ab2 = middle(n, rows, z1, p1, mot, pmask, m5t)
        ab2 = send_cots((2, 3), ab2, p1)
        ab2 = exchange(ab2)
        p2 = exchange(channel_product(n, rows, False, ab2)).reshape(C * rows, L)
        z3, tb = start_front(n, rows, z2, p2, m5t, mot, abt)
        tb = send_cots((4, 5), tb, p2)
        tb_all = exchange(tb)
        z4, turn = start_attention(n, rows, z3, tb_all, key_row, a4t, aot, abt)
        turn = send_cots((6, 7), turn, tb_all)
        turn = exchange(turn)
        copies = to_chips(copies_of(mine, chips, (turn,)))
        others = other_core(copies)

        *pouts, back, m_up, m_dn, m_a41, m_ao1 = end_both(
            n, rows, where, turn, [cots[k] for k in range(n)], key_row, a4t, a4, aot, att_out, upt,
            up, dnt, pair_down,
        )
        back = exchange(back)
        sent = {}

        def send_pouts(offsets, ahead, behind):
            for k in offsets:
                block, _ = lax.optimization_barrier((pouts[k], behind))
                sent[k] = from_home(k, block)
            return lax.optimization_barrier((ahead, *[sent[k] for k in offsets]))[0]

        dz4, dxs, dtb, m_a40, m_ao0, m_ab1 = start_back(
            n, rows, z3, z4, back, tb_all, key_row, a4t, a4, att_out, abt, deps=(copies, others)
        )
        dtb = send_pouts((0, 1, 2, 3), dtb, back)
        dtb = exchange(dtb)
        dz3, dgp2, dp2, m_ab0, m_mo1 = third_back(
            n, rows, z3, dz4, dxs, dtb, abt, z2, p2, m5t, mot, mof
        )
        dp2 = send_pouts((4, 5), dp2, dtb)
        dp2 = exchange(dp2.reshape(n, part, L))
        dab2 = channel_product_back(n, rows, False, ab2, dp2)
        kept = single_every(
            n, rows, where, copies, others, single_gains, single_proj, single_up, single_down,
            deps=(dab2,),
        )
        dab2 = exchange(dab2)
        dz2, dgp1, dp1, m_m51, m_mo0 = second_back(
            n, rows, z2, dz3, dgp2, dab2, pmask, m5t, m5, z1, p1, mot, mof, deps=(kept[0],)
        )
        dp1 = send_pouts((6, 7), dp1, dab2)
        pair_six = undeal(n, rows, where, [sent[k] for k in range(n)])
        dp1 = exchange(dp1.reshape(n, part, L))
        dab1 = exchange(channel_product_back(n, rows, True, ab1, dp1))
        dz1, ends, m_oo, m_m50 = first_back(
            n, rows, chips, where, z1, dz2, dgp1, dab1, pmask, m5t, m5, inner, lrt, left_own,
            outer_w,
        )
        names = [
            "up", "dn", "a41", "ao1", "a40", "ao0", "m51", "mo1", "mo0", "m50", "oo", "ab1", "ab0",
        ]
        sums = [
            m_up, m_dn, m_a41, m_ao1, m_a40, m_ao0, m_m51, m_mo1, m_mo0, m_m50, m_oo, m_ab1, m_ab0,
        ]
        places, at = {}, 0
        for name, m in zip(names, sums):
            places[name] = at
            at += m.shape[0]
        half = -(-at // (total * 16)) * total * 8
        near, far = collect(where, sums, half, ())
        near = b16(near + f32(other_core(far)))
        ends = to_chips(ends)
        ends, near = lax.optimization_barrier((ends, near))
        others_ends = other_core(ends)
        dz1 = swap(copies_of(dz1, 1, (others_ends,))[0], True)
        near, others_ends = lax.optimization_barrier((near, others_ends))
        near = to_chips(near.reshape(chips, half // chips, C))
        ys, g_sg, d_own, drb, m_op = single_back(
            members, rows, where, ends, others_ends, kept, single_gains, single_proj,
            single_up, single_down, outer,
        )
        pair_grad, m_sb = last_back(rows, pair_rep[0], drb, dz1, sbt)
        near_sums = sum_copies(near, m_sb, chips)
        g_sp, g_su, g_sd = weight_grads(kept[2], ys, width, single_up.shape[1], near_sums)
        g_op = jnp.swapaxes(m_op[:, : 2 * opm].reshape(width, 2, opm), 0, 1)

        near = copies_of(to_chips(near_sums), 1, (g_sp, g_su, g_sd, pair_six))[0]
        grads = finish(
            where, near, other_core(near), pair_gains, mult_gains, mult_proj, mult_gate,
            mult_out, att_proj, att_b, pair_up, single_b, places, half, opm, (),
        )
        g_pg, g_mg, g_sb, g_oo, g_mp, g_mgt, g_mo, g_ap, g_ab, g_ao, g_pu, g_pd = grads
        return (
            single_out[None],
            pair_six[None],
            d_own[None],
            pair_grad[None],
            g_sg,
            g_pg,
            g_mg,
            g_sp,
            g_sb.T,
            g_su,
            g_sd,
            g_op,
            g_oo,
            g_mp,
            g_mgt,
            g_mo,
            g_ap,
            jnp.swapaxes(g_ab, 1, 2),
            g_ao,
            g_pu,
            g_pd,
        )

    return local


def solution(mesh):
    groups_of, n = mesh.shape["grp"], mesh.shape["rows"]
    whole = P()
    in_specs = (
        (P("grp", "rows", None), P("grp", "rows", None, None), P("grp", None))
        + (whole,) * 17
        + (P("grp", "rows", None), P("grp", "rows", None, None))
    )
    out_specs = (
        P("grp", "rows", None),
        P("grp", "rows", None, None),
        P("grp", "rows", None),
        P("grp", "rows", None, None),
    ) + (whole,) * 17
    if L % n == 0 and (L // n) % 16 == 0:
        body = fast_local((groups_of, n) == (4, 8), n)
    else:
        body = general_local
    return jax.shard_map(body, mesh=mesh, in_specs=in_specs, out_specs=out_specs, check_vma=False)
```

```python
import math

import jax
import jax.numpy as jnp
from jax import lax
from jax.experimental import pallas as pl
from jax.experimental.pallas import tpu as pltpu
from jax.sharding import PartitionSpec as P

BF = jnp.bfloat16
F32 = jnp.float32
EPSILON = 1e-05
MASKED = 1000000000.0
AX = ("grp", "rows")
L = 128
C = 128
TH = 4
HD = 32
HPAD = 16


def dot(a, b):
    return lax.dot_general(a, b, (((1,), (0,)), ((), ())), preferred_element_type=F32)


def dot_nt(a, b):
    return lax.dot_general(a, b, (((1,), (1,)), ((), ())), preferred_element_type=F32)


def dot_tn(a, b):
    return lax.dot_general(a, b, (((0,), (0,)), ((), ())), preferred_element_type=F32)


def b16(x):
    return x.astype(BF)


def f32(x):
    return x.astype(F32)


def sig(x):
    return 0.5 * jnp.tanh(0.5 * x) + 0.5


GELU_A = 0.7978845608028654
GELU_B = 0.044715


def gelu_parts(x):
    t = jnp.tanh(GELU_A * (x + GELU_B * x * x * x))
    half = 0.5 * (1.0 + t)
    slope = half + 0.5 * x * (1.0 - t * t) * (GELU_A * (1.0 + 3.0 * GELU_B * x * x))
    return x * half, slope


def norm_cols(z):
    c = z - jnp.mean(z, 0, keepdims=True)
    scale = lax.rsqrt(jnp.mean(c * c, 0, keepdims=True) + EPSILON)
    return c * scale, scale


def norm_cols_back(dx, xh, scale):
    return scale * (
        dx - jnp.mean(dx, 0, keepdims=True) - xh * jnp.mean(dx * xh, 0, keepdims=True)
    )


U = 16


def cols(r):
    return pl.ds(pl.multiple_of(r * U * L, U * L), U * L)


def side(parts):
    return jnp.concatenate(parts, 1)


def lanes(x, u):
    return x[:, u * L : (u + 1) * L]


def get_rows(ref, r, count, rows):
    return side([ref[pl.ds(r * U + u, count, stride=rows), :] for u in range(U)])


def put_rows(ref, r, count, rows, x):
    for u in range(U):
        ref[pl.ds(r * U + u, count, stride=rows), :] = lanes(x, u)


def put_turned(ref, r, rows, x):
    for u in range(U):
        ref[pl.ds(r * U + u, L, stride=rows), :] = lanes(x, u).T


def get_turned(ref, r, rows):
    return side(
        [
            f32(ref[:, pl.ds(pl.multiple_of((r * U + u) * rows, rows), rows), :].reshape(L, C)).T
            for u in range(U)
        ]
    )


def each_row(count, body):
    def step(r, carry):
        body(r)
        return carry

    lax.fori_loop(0, count, step, 0, unroll=4 if count == 4 else 1)


def call(kernel, outs, scratch, args, deps=(), raw=(), late=(), far=(), step=16, us=5):
    global U
    U = step
    count, more, given = len(args), len(deps), len(outs)
    fetched = [args[k] for k in raw]

    def body(*refs):
        mine = list(refs[:count])
        results = list(refs[count + more : count + more + given])
        rest = list(refs[count + more + given :])
        sems = rest.pop() if raw or far else None
        stores = [rest.pop() for _ in far][::-1]
        held = [rest.pop() for _ in raw][::-1]
        moves = {}
        for i, k in enumerate(raw):
            moves[k] = pltpu.make_async_copy(mine[k], held[i], sems.at[i])
            moves[k].start()
        for k in raw:
            if k not in late:
                moves[k].wait()
        for i, k in enumerate(raw):
            mine[k] = held[i]
        ends = []
        for i, k in enumerate(far):
            ends.append(pltpu.make_async_copy(stores[i], results[k], sems.at[len(raw) + i]))
            results[k] = stores[i]
        early = set()

        def arrive(k):
            moves[k].wait()

        def leave(k):
            early.add(far.index(k))
            ends[far.index(k)].start()

        if late:
            kernel((arrive, leave), *mine, *results, *rest)
        else:
            kernel(*mine, *results, *rest)
        for i, end in enumerate(ends):
            if i not in early:
                end.start()
        for end in ends:
            end.wait()

    vm = pl.BlockSpec(memory_space=pltpu.VMEM)
    sm = pl.BlockSpec(memory_space=pltpu.SMEM)
    away = pl.BlockSpec(memory_space=pl.ANY)
    moved = sum(a.size * a.dtype.itemsize for a in args)
    buffers = [pltpu.VMEM(s, d) for s, d in scratch]
    buffers += [pltpu.VMEM(a.shape, a.dtype) for a in fetched]
    buffers += [pltpu.VMEM(*outs[k]) for k in far]
    placed = sum(math.prod(b.shape) * jnp.dtype(b.dtype).itemsize for b in buffers)
    if raw or far:
        buffers.append(pltpu.SemaphoreType.DMA((len(raw) + len(far),)))
    return pl.pallas_call(
        body,
        out_shape=[
            pltpu.HBM(s, d) if k in far else jax.ShapeDtypeStruct(s, d)
            for k, (s, d) in enumerate(outs)
        ],
        in_specs=[
            away if k in raw else sm if a.dtype == jnp.int32 else vm for k, a in enumerate(args)
        ]
        + [away] * more,
        out_specs=[away if k in far else vm for k in range(given)],
        scratch_shapes=buffers,
        compiler_params=pltpu.CompilerParams(vmem_limit_bytes=(30 << 20) + placed),
        cost_estimate=pl.CostEstimate(flops=us * 10**9, bytes_accessed=moved if us else 0, transcendentals=0),
    )(
        *[
            pltpu.with_memory_space_constraint(a, pltpu.HBM) if k in raw else a
            for k, a in enumerate(args)
        ],
        *[pltpu.with_memory_space_constraint(d, pltpu.HBM) for d in deps],
    )


def prep_weights(gp, gm, mp, mg, mo, ap, ab, ao, pu, pd, sb):
    def kernel(
        gp, gm, mp, mg, mo, ap, ab, ao, pu, pd, sb,
        m5t, m5, mot, mof, a4t, a4, aot, abt, upt, up, dnt, sbt,
    ):
        gpv = f32(gp[...])
        gmv = f32(gm[...])

        def padded(w):
            return jnp.concatenate([f32(w), jnp.zeros((HPAD - w.shape[0], C), F32)], 0)

        for t in range(2):
            g = gpv[1 + t : 2 + t]
            for k in range(5):
                w = f32(mp[t, k] if k < 4 else mg[t]).T * g
                m5t[t, k * C : (k + 1) * C] = b16(w)
                m5[t, :, k * C : (k + 1) * C] = b16(w.T)
            w = f32(mo[t]).T * gmv[t : t + 1]
            mot[t] = b16(w)
            mof[t] = b16(w.T)
            g = gpv[3 + t : 4 + t]
            for k in range(4):
                w = f32(ap[t, k]).T * (g * HD**-0.5 if k == 0 else g)
                a4t[t, k * C : (k + 1) * C] = b16(w)
                a4[t, :, k * C : (k + 1) * C] = b16(w.T)
            aot[t] = b16(f32(ao[t]).T)
            abt[t] = b16(padded(ab[t]) * g)
        g = gpv[5:6]
        for k in range(4):
            s = slice(k * C, (k + 1) * C)
            w = f32(pu[:, s]).T * g
            upt[s] = b16(w)
            up[:, s] = b16(w.T)
            dnt[:, s] = b16(f32(pd[s]).T)
        sbt[...] = b16(padded(sb[...]) * gpv[0:1])

    outs = [
        ((2, 640, C), BF), ((2, C, 640), BF), ((2, C, C), BF), ((2, C, C), BF),
        ((2, 512, C), BF), ((2, C, 512), BF), ((2, C, C), BF), ((2, HPAD, C), BF),
        ((512, C), BF), ((C, 512), BF), ((C, 512), BF), ((HPAD, C), BF),
    ]
    return call(kernel, outs, [], (gp, gm, mp, mg, mo, ap, ab, ao, pu, pd, sb), raw=(0, 1, 2, 3, 4, 5, 6, 7, 8, 9, 10), far=(0, 1, 2, 3, 4, 5, 6, 7, 8, 9, 10, 11), us=3)


def pack(rows, single, cot, pair, mask, sbt, where):
    def kernel(single, cot, pair, mask, sbt, where, mine, mask_col, s, sm):
        sm[...] = jnp.broadcast_to(mask[...], (L, L)).T
        mask_col[...] = sm[pl.ds(pl.multiple_of(where[3] * rows, rows), rows), :]
        key_row = (mask[...] - 1.0) * MASKED

        def body(r):
            xh, _ = norm_cols(side([f32(pair[r * U + u]).T for u in range(U)]))
            put_rows(s, r, HPAD, rows, dot(sbt[...], b16(xh)) + side([key_row] * U))

        each_row(rows // U, body)
        mine[0:rows] = single[...]
        mine[rows : 2 * rows] = cot[...]
        for h in range(8):
            mine[rows * (2 + h // 4) : rows * (3 + h // 4), (h % 4) * L : (h % 4 + 1) * L] = b16(
                s[h * rows : (h + 1) * rows]
            )

    width = single.shape[1]
    return call(
        kernel,
        [((4 * rows, width), BF), ((rows, L), F32)],
        [((HPAD * rows, L), F32), ((L, L), F32)],
        (single, cot, pair, mask, sbt, where), raw=(0, 1, 2, 4), us=2)


def copies_of(x, count, deps):
    def kernel(x, out):
        for d in range(count):
            out[d] = x[...]

    return call(kernel, [((count,) + x.shape, x.dtype)], [], (x,), deps=deps)[0]


def deal(n, rows, where, x, deps):
    def kernel(where, x, *outs):
        for k in range(n):
            block = lax.rem(where[3] + k, n)
            at = pl.ds(pl.multiple_of(block * rows, rows), rows)
            outs[k][...] = x[:, at, :].reshape(rows * rows, C)

    return call(
        kernel, [((rows * rows, C), BF)] * n, [], (where, x), deps=deps, raw=(1,),
        far=tuple(range(n)), us=1,
    )


def undeal(n, rows, where, parts):
    def kernel(where, *refs):
        out = refs[n]
        for k in range(n):
            block = lax.rem(where[3] + n - k, n)
            at = pl.ds(pl.multiple_of(block * rows, rows), rows)
            out[:, at, :] = refs[k][...].reshape(rows, rows, C)

    return call(
        kernel, [((rows, L, C), BF)], [], (where, *parts), raw=tuple(range(1, n + 1)), far=(0,),
        us=1,
    )[0]


def part_of(x, first, last, deps):
    def kernel(x, out):
        out[...] = x[first:last]

    return call(
        kernel, [((last - first,) + x.shape[1:], x.dtype)], [], (x,), deps=deps, raw=(0,), us=1
    )[0]


def norm_rows16(x):
    c = x - jnp.mean(x, -1, keepdims=True)
    scale = lax.rsqrt(jnp.mean(c * c, -1, keepdims=True) + EPSILON)
    return c * scale, scale


def norm_rows16_back(dx, xh, scale):
    return scale * (
        dx - jnp.mean(dx, -1, keepdims=True) - xh * jnp.mean(dx * xh, -1, keepdims=True)
    )


def halves():
    lane = lax.broadcasted_iota(jnp.int32, (1, L), 1)
    low = jnp.where(lane < L // 2, 1.0, 0.0)
    return b16(low), b16(1.0 - low)


def pair_weights(q, k, bias0, bias1):
    out = []
    for m, bias in zip(halves(), (bias0, bias1)):
        s = dot_nt(q * m, k) + bias
        e = jnp.exp(s - jnp.max(s, -1, keepdims=True))
        out.append(b16(e / jnp.sum(e, -1, keepdims=True)))
    return out


def on_halves(x, axis=0):
    return jnp.concatenate([x * m for m in halves()], axis)


def single_own(n, rows, copies, gathered, mine, mask_col, gains, proj, up, down, outer):
    width = up.shape[0]
    opm2 = 64

    def kernel(moves, gathered, mine, mask_col, gains, proj, up, down, outer, out, lr):
        g = f32(gains[...])
        sn = b16(norm_rows16(f32(gathered[...].reshape(n * rows, width)))[0] * g[0:1])
        arrive, _ = moves
        arrive(4)
        keys, vals = b16(dot(sn, proj[1])), b16(dot(sn, proj[2]))
        x = f32(mine[0:rows])
        sn = b16(norm_rows16(x)[0] * g[0:1])
        query = b16(dot(sn, proj[0]) * 0.125)
        gate = sig(dot(sn, proj[3]))
        mixed = []
        for t in range(4):
            s = slice(t * L, (t + 1) * L)
            bias = [
                f32(mine[rows * (2 + h // 4) : rows * (3 + h // 4), (h % 4) * L : (h % 4 + 1) * L])
                for h in (2 * t, 2 * t + 1)
            ]
            p = pair_weights(query[:, s], keys[:, s], *bias)
            mixed.append(dot(jnp.concatenate(p, 1), on_halves(vals[:, s])))
        mixed = jnp.concatenate(mixed, 1)
        first = x + dot(b16(mixed * gate), proj[4])
        x1 = b16(norm_rows16(first)[0] * g[1:2])
        arrive(5)
        hidden = b16(gelu_parts(dot(x1, up[...]))[0])
        arrive(6)
        second = first + dot(hidden, down[...])
        out[...] = b16(second)
        x2 = b16(norm_rows16(second)[0] * g[2:3])
        both = dot(x2, outer[...]) * mask_col[...]
        lane = lax.broadcasted_iota(jnp.int32, (rows, L), 1)
        both = b16(jnp.where(lane >= opm2, mask_col[...], both))
        for d in range(copies):
            lr[d] = both

    return call(
        kernel,
        [((rows, width), BF), ((copies, rows, L), BF)],
        [],
        (gathered, mine, mask_col, gains, proj, up, down, outer), raw=(3, 4, 5, 6, 7), late=(4, 5, 6), us=6)


def single_every(n, rows, where, ga, gb, gains, proj, up, down, deps=()):
    width, wide = up.shape
    tokens = 4 * L
    half = ga.shape[0]

    def kernel(
        moves, where, ga, gb, gains, proj, up, down,
        x_all, cot_all, xs, qkv, gm, probs, slope, first_out, second_out, held,
    ):
        arrive, leave = moves
        core = where[3] % 2
        for k in range(half):
            held[2 * k + core] = ga[k]
            held[2 * k + 1 - core] = gb[k]
        g = f32(gains[...])
        x16 = held[:, 0:rows, :].reshape(tokens, width)
        x_all[...] = x16
        cot_all[...] = held[:, rows : 2 * rows, :].reshape(tokens, width)
        leave(0)
        leave(1)
        x = f32(x16)
        sn = b16(norm_rows16(x)[0] * g[0:1])
        xs[:, 0:width] = sn
        arrive(4)
        qkv[:, 0:width] = b16(dot(sn, proj[0]) * 0.125)
        qkv[:, width : 2 * width] = b16(dot(sn, proj[1]))
        qkv[:, 2 * width : 3 * width] = b16(dot(sn, proj[2]))
        leave(3)
        gate = sig(dot(sn, proj[3]))
        gm[:, 0:width] = b16(gate)

        def body(crop):
            own = pl.ds(pl.multiple_of(crop * L, L), L)
            part = pl.ds(crop * n, n)
            for t in range(4):
                q = qkv[own, t * L : (t + 1) * L]
                k = qkv[own, width + t * L : width + (t + 1) * L]
                v = qkv[own, 2 * width + t * L : 2 * width + (t + 1) * L]
                bias = [
                    f32(
                        held[
                            part,
                            rows * (2 + h // 4) : rows * (3 + h // 4),
                            (h % 4) * L : (h % 4 + 1) * L,
                        ].reshape(L, L)
                    )
                    for h in (2 * t, 2 * t + 1)
                ]
                p = pair_weights(q, k, *bias)
                for m in range(2):
                    at = pl.multiple_of((crop * 8 + 2 * t + m) * L, L)
                    probs[pl.ds(at, L), :] = p[m]
                mixed = dot(jnp.concatenate(p, 1), on_halves(v))
                gm[own, width + t * L : width + (t + 1) * L] = b16(mixed)

        each_row(4, body)
        leave(5)
        leave(4)
        u = b16(f32(gm[:, width : 2 * width]) * f32(gm[:, 0:width]))
        xs[:, width : 2 * width] = u
        first = x + dot(u, proj[4])
        first_out[...] = first
        leave(7)
        x1 = b16(norm_rows16(first)[0] * g[1:2])
        xs[:, 2 * width : 3 * width] = x1
        arrive(5)
        total = first
        arrive(6)
        for m in range(wide // width):
            s = slice(m * width, (m + 1) * width)
            hid, slp = gelu_parts(dot(x1, up[:, s]))
            h16 = b16(hid)
            xs[:, (3 + m) * width : (4 + m) * width] = h16
            slope[:, s] = b16(slp)
            total = total + dot(h16, down[s])
        second_out[...] = total

    return call(
        kernel,
        [
            ((tokens, width), BF), ((tokens, width), BF), ((tokens, 3 * width + wide), BF),
            ((tokens, 3 * width), BF), ((tokens, 2 * width), BF), ((4 * 8 * L, L), BF),
            ((tokens, wide), BF), ((tokens, width), F32), ((tokens, width), F32),
        ],
        [((2 * half, 4 * rows, width), BF)],
        (where, ga, gb, gains, proj, up, down),
        deps=deps, raw=(1, 2, 3, 4, 5, 6), late=(4, 5, 6), far=(0, 1, 2, 3, 4, 5, 6, 7, 8), us=19)


def single_back(members, rows, where, ea, eb, kept, gains, proj, up, down, outer, deps=()):
    width, wide = up.shape
    tokens = 4 * L
    x_all, cot_all, _, qkv, gm, probs, slope, first_in, second_in = kept

    def kernel(
        moves, where, ea, eb, x_all, cot_all, qkv, gm, probs, slope, first_in, second_in,
        gains, proj, up, down, outer,
        ys, gain_grad, d_own, drb, m_op,
        dlr, o_do, sdrb, sds, srow,
    ):
        arrive, _ = moves
        g = f32(gains[...])
        for crop in range(4):
            total = f32(ea[members[crop][0]]) + f32(eb[members[crop][0]])
            for k in members[crop][1:]:
                total = total + (f32(ea[k]) + f32(eb[k]))
            total = jnp.concatenate([total, jnp.zeros_like(total)], 0)
            dlr[crop * L : (crop + 1) * L] = b16(total.T)
        x2, sc2 = norm_rows16(second_in[...])
        m_op[...] = dot_tn(b16(x2 * g[2:3]), dlr[...])
        dx = dot_nt(dlr[...], outer[...])
        gain_grad[2:3] = jnp.sum(dx * x2, 0, keepdims=True)
        ds2 = f32(cot_all[...]) + norm_rows16_back(dx * g[2:3], x2, sc2)
        ds2_16 = b16(ds2)
        ys[:, 5 * width + wide :] = ds2_16
        for k in (14, 8, 13, 9):
            arrive(k)
        dx = jnp.zeros((tokens, width), F32)
        for m in range(wide // width):
            s = slice(m * width, (m + 1) * width)
            dhp = b16(dot_nt(ds2_16, down[s]) * f32(slope[:, s]))
            ys[:, (5 + m) * width : (6 + m) * width] = dhp
            dx = dx + dot_nt(dhp, up[:, s])
        x1, sc1 = norm_rows16(first_in[...])
        gain_grad[1:2] = jnp.sum(dx * x1, 0, keepdims=True)
        df = ds2 + norm_rows16_back(dx * g[1:2], x1, sc1)
        sds[...] = df
        df16 = b16(df)
        ys[:, 4 * width : 5 * width] = df16
        for k in (12, 6, 5, 7):
            arrive(k)
        du = dot_nt(df16, proj[4])
        gate, mixed = f32(gm[:, 0:width]), f32(gm[:, width : 2 * width])
        do = du * gate
        o_do[...] = b16(do)
        srow[...] = do * mixed
        ys[:, 3 * width : 4 * width] = b16(du * mixed * gate * (1.0 - gate))
        lane = lax.broadcasted_iota(jnp.int32, (1, L), 1)
        low = jnp.where(lane < L // 2, 1.0, 0.0)

        def body(crop):
            own = pl.ds(pl.multiple_of(crop * L, L), L)
            for t in range(4):
                s = slice(t * L, (t + 1) * L)
                q = qkv[own, t * L : (t + 1) * L]
                k = qkv[own, width + t * L : width + (t + 1) * L]
                v = qkv[own, 2 * width + t * L : 2 * width + (t + 1) * L]
                do16, row = o_do[own, s], srow[own, s]
                grads, weights = [], []
                for j, (m, mf) in enumerate(zip(halves(), (low, 1.0 - low))):
                    at = pl.multiple_of((crop * 8 + 2 * t + j) * L, L)
                    p16 = probs[pl.ds(at, L), :]
                    dp = dot_nt(do16 * m, v)
                    e = f32(p16) * (dp - jnp.sum(row * mf, -1, keepdims=True))
                    sdrb[pl.ds(at, L), :] = e
                    grads.append(b16(e))
                    weights.append(p16)
                dq = dot(jnp.concatenate(grads, 1), on_halves(k)) * 0.125
                dk = dot_tn(jnp.concatenate(grads, 0), on_halves(q))
                dv = dot_tn(jnp.concatenate(weights, 0), on_halves(do16))
                ys[own, t * L : (t + 1) * L] = b16(dq)
                ys[own, width + t * L : width + (t + 1) * L] = b16(dk)
                ys[own, 2 * width + t * L : 2 * width + (t + 1) * L] = b16(dv)

        each_row(4, body)
        dx = dot_nt(ys[:, 0:width], proj[0])
        for k in range(1, 4):
            dx = dx + dot_nt(ys[:, k * width : (k + 1) * width], proj[k])
        x0, sc0 = norm_rows16(f32(x_all[...]))
        gain_grad[0:1] = jnp.sum(dx * x0, 0, keepdims=True)
        sds[...] = sds[...] + norm_rows16_back(dx * g[0:1], x0, sc0)
        grp, row = where[2], where[3]
        d_own[...] = sds[pl.ds(pl.multiple_of(grp * L + row * rows, rows), rows), :]
        for h in range(8):
            at = pl.multiple_of((grp * 8 + h) * L + row * rows, rows)
            drb[h * rows : (h + 1) * rows] = sdrb[pl.ds(at, rows), :]

    return call(
        kernel,
        [
            ((tokens, 6 * width + wide), BF), ((3, width), F32), ((rows, width), F32),
            ((8 * rows, L), F32), ((width, L), F32),
        ],
        [
            ((tokens, L), BF), ((tokens, width), BF), ((4 * 8 * L, L), F32), ((tokens, width), F32),
            ((tokens, width), F32),
        ],
        (
            where, ea, eb, x_all, cot_all, qkv, gm, probs, slope, first_in, second_in,
            gains, proj, up, down, outer,
        ), deps=deps, raw=(10, 15, 4, 11, 14, 8, 13, 9, 12, 6, 5, 7, 3), late=(5, 6, 7, 8, 9, 12, 13, 14), far=(0, 1, 2, 3, 4), us=22)


def weight_grads(xs, ys, width, wide, after):
    tokens = xs.shape[0]
    blocks = wide // width

    def kernel(x, y, after, out):
        out[...] = dot_tn(x[...], y[...]).reshape(out.shape)

    def run(steps, x_at, y_at, shape, block, out_at):
        return pl.pallas_call(
            kernel,
            grid=(steps,),
            out_shape=pltpu.HBM(shape, F32),
            in_specs=[
                pl.BlockSpec((tokens, width), x_at),
                pl.BlockSpec((tokens, width), y_at),
                pl.BlockSpec(memory_space=pl.ANY),
            ],
            out_specs=pl.BlockSpec(block, out_at),
            compiler_params=pltpu.CompilerParams(vmem_limit_bytes=32 << 20),
            cost_estimate=pl.CostEstimate(
                flops=2 * 10**9,
                bytes_accessed=steps * width * width * 8,
                transcendentals=0,
            ),
        )(
            pltpu.with_memory_space_constraint(xs, pltpu.HBM),
            pltpu.with_memory_space_constraint(ys, pltpu.HBM),
            pltpu.with_memory_space_constraint(after, pltpu.HBM),
        )

    proj = run(
        5, lambda i: (0, i // 4), lambda i: (0, i), (5, width, width), (1, width, width),
        lambda i: (i, 0, 0),
    )
    up = run(
        blocks, lambda i: (0, 2), lambda i: (0, 5 + i), (width, wide), (width, width),
        lambda i: (0, i),
    )
    down = run(
        blocks, lambda i: (0, 3 + i), lambda i: (0, 5 + blocks), (wide, width), (width, width),
        lambda i: (i, 0),
    )
    return proj, up, down


def project_pair(z, r, rows, m5t, pmask, sa, sb):
    xh, _ = norm_cols(z)
    p = dot(m5t[0:512], b16(xh))
    mk = get_rows(pmask, r, 1, 1)
    put_rows(sa, r, C, rows, sig(p[0:C]) * p[C : 2 * C] * mk)
    put_rows(sb, r, C, rows, sig(p[2 * C : 3 * C]) * p[3 * C : 4 * C] * mk)


def put_pair(n, ab, sa, sb):
    part = sa.shape[0] // n
    for d in range(n):
        ab[d, 0:part] = b16(sa[d * part : (d + 1) * part])
        ab[d, part : 2 * part] = b16(sb[d * part : (d + 1) * part])


def gated_product(z, r, rows, gatet, mot, sp):
    xh, _ = norm_cols(z)
    gate = sig(dot(gatet[...], b16(xh)))
    ph, _ = norm_cols(get_rows(sp, r, C, rows))
    return z + dot(mot[...], b16(ph)) * gate


def front(n, rows, where, lr_all, pair, outer_w, m5ts, deps=()):
    opm = outer_w.shape[0]

    def kernel(
        where, lr_all, pair, outer_w, m5ts,
        z1, ab, pmask, key_row, inner, lrt, left_own, sa, sb, slr, spm,
    ):
        m5t = m5ts.at[0]
        crop, block = where[0], where[1]
        lr16 = lr_all[pl.ds(crop * n, n)].reshape(L, C)
        lr = f32(lr16)
        turned = lr.T
        lrt[...] = turned
        mrow = turned[2 * opm : 2 * opm + 1]
        key_row[...] = (mrow - 1.0) * MASKED
        first = pl.multiple_of(block * rows, rows)
        spm[...] = jnp.broadcast_to(mrow, (L, L)).T * mrow
        pmask[...] = spm[pl.ds(first, rows), :]
        slr[...] = lr
        left = b16(slr[pl.ds(first, rows), :])
        left_own[...] = left
        inners = dot(left[:, 0:opm], side([outer_w[b] for b in range(opm)]))
        for b in range(opm):
            inner[b * rows : (b + 1) * rows] = lanes(inners, b)
        edge = jnp.zeros((opm, C), BF)

        def body(r):
            parts = []
            for u in range(U):
                mine = b16(inner[pl.ds(r * U + u, opm, stride=rows), :])
                mine = jnp.concatenate([edge, mine, edge, edge], 0)
                parts.append((f32(pair[r * U + u]) + dot(lr16, mine)).T)
            z = side(parts)
            z1[:, cols(r)] = z
            project_pair(z, r, rows, m5t, pmask, sa, sb)

        each_row(rows // U, body)
        put_pair(n, ab, sa, sb)

    part = C * rows // n
    return call(
        kernel,
        [
            ((C, rows * L), F32), ((n, 2 * part, L), BF), ((rows, L), F32), ((1, L), F32),
            ((opm * rows, C), F32), ((C, L), F32), ((rows, C), BF),
        ],
        [((C * rows, L), F32)] * 2 + [((L, C), F32), ((L, L), F32)],
        (where, lr_all, pair, outer_w, m5ts), deps=deps, raw=(2, 3, 4), far=(0, 2, 3, 4, 5, 6), us=5)


def middle(n, rows, z1, prod, mots, pmask, m5ts, deps=()):
    def kernel(z1, prod, mots, pmask, m5ts, z2, ab, sa, sb, sp):
        gatet, mot, m5t = m5ts.at[0, 512:640], mots.at[0], m5ts.at[1]
        sp[...] = f32(prod[...])

        def body(r):
            z = gated_product(z1[:, cols(r)], r, rows, gatet, mot, sp)
            z2[:, cols(r)] = z
            project_pair(z, r, rows, m5t, pmask, sa, sb)

        each_row(rows // U, body)
        put_pair(n, ab, sa, sb)

    part = C * rows // n
    return call(
        kernel,
        [((C, rows * L), F32), ((n, 2 * part, L), BF)],
        [((C * rows, L), F32)] * 3,
        (z1, prod, mots, pmask, m5ts), deps=deps, raw=(0, 2, 3, 4), far=(0,), us=4)


def start_front(n, rows, z2, prod, m5ts, mots, abts, deps=()):
    def kernel(z2, prod, m5ts, mots, abts, z3, tb, sp, st):
        gatet, mot, abt = m5ts.at[1, 512:640], mots.at[1], abts.at[0]
        sp[...] = f32(prod[...])

        def body(r):
            z = gated_product(z2[:, cols(r)], r, rows, gatet, mot, sp)
            z3[:, cols(r)] = z
            xh, _ = norm_cols(z)
            put_rows(st, r, HPAD, rows, dot(abt[...], b16(xh)))

        each_row(rows // U, body)
        for d in range(n):
            tb[d] = b16(st[0 : TH * rows])

    return call(
        kernel,
        [((C, rows * L), F32), ((n, TH * rows, L), BF)],
        [((C * rows, L), F32), ((HPAD * rows, L), F32)],
        (z2, prod, m5ts, mots, abts), deps=deps, raw=(0, 2, 3, 4), far=(0,), us=4)


def channel_product(n, rows, outgoing, ab):
    def kernel(ab, out):
        part = C * rows // n
        for ch in range(C // n):
            a = ab[:, ch * rows : (ch + 1) * rows, :].reshape(L, L)
            b = ab[:, part + ch * rows : part + (ch + 1) * rows, :].reshape(L, L)
            prod = dot_nt(a, b) if outgoing else dot_tn(a, b)
            out[:, ch * rows : (ch + 1) * rows, :] = b16(prod).reshape(n, rows, L)

    return call(kernel, [((n, C * rows // n, L), BF)], [], (ab,), us=1)[0]


def channel_product_back(n, rows, outgoing, ab, dprod, deps=()):
    def kernel(ab, dprod, out):
        part = C * rows // n
        for ch in range(C // n):
            low, high = ch * rows, (ch + 1) * rows
            a = ab[:, low:high, :].reshape(L, L)
            b = ab[:, part + low : part + high, :].reshape(L, L)
            g = dprod[:, low:high, :].reshape(L, L)
            if outgoing:
                da, db = dot(g, b), dot_tn(g, a)
            else:
                da, db = dot_nt(b, g), dot(a, g)
            out[:, low:high, :] = b16(da).reshape(n, rows, L)
            out[:, part + low : part + high, :] = b16(db).reshape(n, rows, L)

    return call(kernel, [((n, 2 * C * rows // n, L), BF)], [], (ab, dprod), deps=deps, us=2)[0]


def head_masks():
    lane = lax.broadcasted_iota(jnp.int32, (1, C), 1)
    return [b16(jnp.where((lane >= h * HD) & (lane < (h + 1) * HD), 1.0, 0.0)) for h in range(TH)]


def by_head(x):
    pm = b16(x.T)
    return jnp.concatenate([pm * m for m in head_masks()], 0)


def attend(x16, a4t, bias):
    p4 = dot(a4t[...], x16)
    gate = sig(p4[3 * C : 4 * C])
    each, mixed = [], []
    for u in range(U):
        q, k, v = (lanes(p4[m * C : (m + 1) * C], u) for m in range(3))
        logits = dot(by_head(k), b16(q)) + bias[...]
        raised, outs = [], []
        v16 = b16(v)
        for h in range(TH):
            s = logits[h * L : (h + 1) * L]
            e = jnp.exp(s - jnp.max(s, 0, keepdims=True))
            inv = 1.0 / jnp.sum(e, 0, keepdims=True)
            raised.append((e, inv))
            outs.append(dot(v16[h * HD : (h + 1) * HD], b16(e)) * inv)
        each.append((q, k, v, raised))
        mixed.append(jnp.concatenate(outs, 0))
    return each, gate, side(mixed)


def attend_back(state, dy16, ao, dbias):
    each, gate, mixed = state
    du = dot(ao[...], dy16)
    do = du * gate
    dgate = du * mixed * gate * (1.0 - gate)
    both = do * mixed
    parts = []
    for u in range(U):
        q, k, v, raised = each[u]
        do16, q16, k16 = b16(lanes(do, u)), b16(q), b16(k)
        dp = dot(by_head(v), do16)
        row = lanes(both, u)
        dq, dk, dv = [], [], []
        for h in range(TH):
            s = slice(h * HD, (h + 1) * HD)
            w = slice(h * L, (h + 1) * L)
            e, inv = raised[h]
            p = e * inv
            ds = p * (dp[w] - jnp.sum(row[s], 0, keepdims=True))
            dbias[w, :] += ds
            ds16, p16 = b16(ds), b16(p)
            dv.append(dot_nt(do16[s], p16))
            dq.append(dot(k16[s], ds16))
            dk.append(dot_nt(q16[s], ds16))
        parts.append(jnp.concatenate([b16(x) for x in dq + dk + dv], 0))
    return jnp.concatenate([side(parts), b16(dgate)], 0)


def start_attention(n, rows, z3, tb_all, key_row, a4ts, aots, abts, deps=()):
    def kernel(z3, tb_all, key_row, a4ts, aots, abts, z4, send, bias, st, se):
        a4t, aot, abt = a4ts.at[0], aots.at[0], abts.at[1]
        for h in range(TH):
            b = f32(tb_all[:, h * rows : (h + 1) * rows, :].reshape(L, L)) + key_row[...]
            bias[h * L : (h + 1) * L, :] = b.T

        def body(r):
            z = z3[:, cols(r)]
            xh, _ = norm_cols(z)
            _, gate, mixed = attend(b16(xh), a4t, bias)
            z = z + dot(aot[...], b16(mixed * gate))
            z4[:, cols(r)] = z
            put_turned(st, r, rows, z)
            xe, _ = norm_cols(z)
            put_rows(se, r, HPAD, rows, dot(abt[...], b16(xe)))

        each_row(rows // U, body)
        part = L * rows // n
        for d in range(n):
            send[d, 0:part] = b16(st[d * part : (d + 1) * part])
            send[d, part : part + TH * rows] = b16(se[0 : TH * rows])

    part = L * rows // n
    return call(
        kernel,
        [((C, rows * L), F32), ((n, part + TH * rows, L), BF)],
        [((TH * L, L), F32), ((L * rows, C), F32), ((HPAD * rows, L), F32)],
        (z3, tb_all, key_row, a4ts, aots, abts), deps=deps, raw=(0, 2, 3, 4, 5), far=(0,), us=12)


def end_both(n, rows, where, recv, cots, key_row, a4ts, a4s, aots, aos, upt, up, dnt, dn, deps=()):
    part = L * rows // n

    def kernel(where, recv, *refs):
        cots, refs = refs[:n], refs[n:]
        run(where, recv, cots, *refs)

    def run(
        where, recv, cots, key_row, a4ts, a4s, aots, aos, upt, up, dnt, dn,
        p0, p1, p2, p3, p4, p5, p6, p7, send, m_up, m_dn, m_a4, m_ao,
        bias, dbias, scot, sout, sdz, o_h, o_dh, o_x5, o_cot, o_x4, o_d4, o_u, o_dy,
    ):
        a4t, a4, aot, ao = a4ts.at[1], a4s.at[1], aots.at[1], aos.at[1]
        kb = jnp.broadcast_to(key_row[...], (L, L)).T
        for h in range(TH):
            b = recv[:, part + h * rows : part + (h + 1) * rows, :].reshape(L, L)
            bias[h * L : (h + 1) * L, :] = f32(b) + kb
        dbias[...] = jnp.zeros_like(dbias)
        for k in range(n):
            block = lax.rem(where[1] + n - k, n)
            scot[pl.ds(pl.multiple_of(block * part, part), part), :] = f32(cots[k][...])

        def body(r):
            w = cols(r)
            z4 = get_turned(recv, r, rows)
            x4, scale4 = norm_cols(z4)
            x16 = b16(x4)
            state = attend(x16, a4t, bias)
            gated = b16(state[2] * state[1])
            z5 = z4 + dot(aot[...], gated)
            x5, scale5 = norm_cols(z5)
            x516 = b16(x5)
            hid, slope = gelu_parts(dot(upt[...], x516))
            h16 = b16(hid)
            z6 = z5 + dot(dnt[...], h16)
            put_turned(sout, r, rows, z6)
            dz6 = side([scot[pl.ds(r * U + u, L, stride=rows), :].T for u in range(U)])
            c16 = b16(dz6)
            dh16 = b16(dot(dn[...], c16) * slope)
            dz5 = dz6 + norm_cols_back(dot(up[...], dh16), x5, scale5)
            dy16 = b16(dz5)
            d4 = attend_back(state, dy16, ao, dbias)
            dz4 = dz5 + norm_cols_back(dot(a4[...], d4), x4, scale4)
            put_turned(sdz, r, rows, dz4)
            o_h[:, w] = h16
            o_dh[:, w] = dh16
            o_x5[:, w] = x516
            o_cot[:, w] = c16
            o_x4[:, w] = x16
            o_d4[:, w] = d4
            o_u[:, w] = gated
            o_dy[:, w] = dy16

        each_row(rows // U, body)
        for d in range(n):
            send[d, 0:part] = b16(sdz[d * part : (d + 1) * part])
            for h in range(TH):
                send[d, part + h * rows : part + (h + 1) * rows] = b16(
                    dbias[h * L + d * rows : h * L + (d + 1) * rows]
                )
        for k, pout in enumerate((p0, p1, p2, p3, p4, p5, p6, p7)):
            block = lax.rem(where[1] + k, n)
            pout[...] = b16(sout[pl.ds(pl.multiple_of(block * part, part), part), :])
        for k in range(4):
            s = slice(k * C, (k + 1) * C)
            m_up[s] = dot_nt(o_x5[...], o_dh[s])
            m_a4[s] = dot_nt(o_x4[...], o_d4[s])
        m_dn[...] = dot_nt(o_h[...], o_cot[...])
        m_ao[...] = dot_nt(o_u[...], o_dy[...])

    wide = rows * L
    return call(
        kernel,
        [
            *[((part, C), BF)] * n, ((n, part + TH * rows, L), BF),
            ((512, C), F32), ((512, C), F32), ((512, C), F32), ((C, C), F32),
        ],
        [
            ((TH * L, L), F32), ((TH * L, L), F32), ((L * rows, C), F32), ((L * rows, C), F32),
            ((L * rows, C), F32),
            ((512, wide), BF), ((512, wide), BF), ((C, wide), BF), ((C, wide), BF),
            ((C, wide), BF), ((512, wide), BF), ((C, wide), BF), ((C, wide), BF),
        ],
        (where, recv, *cots, key_row, a4ts, a4s, aots, aos, upt, up, dnt, dn),
        deps=deps,
        raw=tuple(range(2, n + 11)),
        far=(0, 1, 2, 3, 4, 5, 6, 7, 9, 10, 11, 12),
        step=8, us=18,
    )


def start_back(n, rows, z3, z4, recv, tb_all, key_row, a4ts, a4s, aos, abts, deps=()):
    part = L * rows // n

    def kernel(
        z3, z4, recv, tb_all, key_row, a4ts, a4s, aos, abts,
        dz4_out, dxs, dtb, m_a4, m_ao, m_ab,
        bias, dbias, seb, o_x3, o_d4, o_u, o_dy, o_x4, o_eb,
    ):
        a4t, a4, ao, abt = a4ts.at[0], a4s.at[0], aos.at[0], abts.at[1]
        for h in range(TH):
            b = f32(tb_all[:, h * rows : (h + 1) * rows, :].reshape(L, L)) + key_row[...]
            bias[h * L : (h + 1) * L, :] = b.T
        dbias[...] = jnp.zeros_like(dbias)
        seb[...] = jnp.zeros_like(seb)
        total = f32(recv[0, part : part + TH * rows])
        for d in range(1, n):
            total = total + f32(recv[d, part : part + TH * rows])
        seb[0 : TH * rows, :] = total

        def body(r):
            w = cols(r)
            x4, scale4 = norm_cols(z4[:, w])
            eb16 = b16(get_rows(seb, r, HPAD, rows))
            dz4 = get_turned(recv, r, rows)
            dz4 = dz4 + norm_cols_back(dot_tn(abt[...], eb16), x4, scale4)
            dz4_out[:, w] = dz4
            x3, _ = norm_cols(z3[:, w])
            x16 = b16(x3)
            state = attend(x16, a4t, bias)
            dy16 = b16(dz4)
            d4 = attend_back(state, dy16, ao, dbias)
            dxs[:, w] = dot(a4[...], d4)
            o_x3[:, w] = x16
            o_d4[:, w] = d4
            o_u[:, w] = b16(state[2] * state[1])
            o_dy[:, w] = dy16
            o_x4[:, w] = b16(x4)
            o_eb[:, w] = eb16

        each_row(rows // U, body)
        for h in range(TH):
            turned = b16(dbias[h * L : (h + 1) * L, :].T)
            for d in range(n):
                dtb[d, h * rows : (h + 1) * rows] = turned[d * rows : (d + 1) * rows]
        for k in range(4):
            s = slice(k * C, (k + 1) * C)
            m_a4[s] = dot_nt(o_x3[...], o_d4[s])
        m_ao[...] = dot_nt(o_u[...], o_dy[...])
        m_ab[...] = dot_nt(o_eb[...], o_x4[...])

    wide = rows * L
    return call(
        kernel,
        [
            ((C, wide), F32), ((C, wide), F32), ((n, TH * rows, L), BF),
            ((512, C), F32), ((C, C), F32), ((HPAD, C), F32),
        ],
        [
            ((TH * L, L), F32), ((TH * L, L), F32), ((HPAD * rows, L), F32),
            ((C, wide), BF), ((512, wide), BF), ((C, wide), BF), ((C, wide), BF),
            ((C, wide), BF), ((HPAD, wide), BF),
        ],
        (z3, z4, recv, tb_all, key_row, a4ts, a4s, aos, abts),
        deps=deps, raw=(0, 1, 3, 4, 5, 6, 7, 8), far=(0, 1, 3, 4, 5), us=20)


def product_back(z, dz, r, rows, sp, gatet, mot, mof, sdp, dgp_out, o_ph, o_do):
    w = cols(r)
    xh, _ = norm_cols(z)
    gate = sig(dot(gatet[...], b16(xh)))
    ph, scale = norm_cols(get_rows(sp, r, C, rows))
    ph16 = b16(ph)
    out = dot(mot[...], ph16)
    dgp_out[:, w] = b16(dz * out * gate * (1.0 - gate))
    do16 = b16(dz * gate)
    put_rows(sdp, r, C, rows, norm_cols_back(dot(mof[...], do16), ph, scale))
    o_ph[:, w] = ph16
    o_do[:, w] = do16


def third_back(n, rows, z3, dz4, dxs, recv, abts, z2, prod, m5ts, mots, mofs, deps=()):
    def kernel(
        z3, dz4, dxs, recv, abts, z2, prod, m5ts, mots, mofs,
        dz3, dgp, dp, m_ab, m_mo,
        stb, sp, sdp, o_x3, o_tb, o_ph, o_do,
    ):
        abt, gatet, mot, mof = abts.at[0], m5ts.at[1, 512:640], mots.at[1], mofs.at[1]
        sp[...] = f32(prod[...])
        stb[...] = jnp.zeros_like(stb)
        total = f32(recv[0])
        for d in range(1, n):
            total = total + f32(recv[d])
        stb[0 : TH * rows, :] = total

        def body(r):
            w = cols(r)
            x3, scale3 = norm_cols(z3[:, w])
            tb16 = b16(get_rows(stb, r, HPAD, rows))
            dx = dxs[:, w] + dot_tn(abt[...], tb16)
            dz = dz4[:, w] + norm_cols_back(dx, x3, scale3)
            dz3[:, w] = dz
            o_x3[:, w] = b16(x3)
            o_tb[:, w] = tb16
            product_back(z2[:, w], dz, r, rows, sp, gatet, mot, mof, sdp, dgp, o_ph, o_do)

        each_row(rows // U, body)
        dp[...] = b16(sdp[...])
        m_ab[...] = dot_nt(o_tb[...], o_x3[...])
        m_mo[...] = dot_nt(o_ph[...], o_do[...])

    wide = rows * L
    return call(
        kernel,
        [
            ((C, wide), F32), ((C, wide), BF), ((C * rows, L), BF),
            ((HPAD, C), F32), ((C, C), F32),
        ],
        [
            ((HPAD * rows, L), F32), ((C * rows, L), F32), ((C * rows, L), F32),
            ((C, wide), BF), ((HPAD, wide), BF), ((C, wide), BF), ((C, wide), BF),
        ],
        (z3, dz4, dxs, recv, abts, z2, prod, m5ts, mots, mofs), deps=deps, raw=(0, 1, 2, 4, 5, 6, 7, 8, 9), far=(0, 1, 3, 4), us=7)


def projections_back(n, rows, z, dz, dgp, r, pmask, m5t, m5, sa, sb, o_x, o_d5):
    w = cols(r)
    xh, scale = norm_cols(z)
    x16 = b16(xh)
    p = dot(m5t[0:512], x16)
    mk = get_rows(pmask, r, 1, 1)
    da = get_rows(sa, r, C, rows) * mk
    db = get_rows(sb, r, C, rows) * mk
    ga, gb = sig(p[0:C]), sig(p[2 * C : 3 * C])
    va, vb = p[C : 2 * C], p[3 * C : 4 * C]
    d5 = jnp.concatenate(
        [
            b16(da * va * ga * (1.0 - ga)),
            b16(da * ga),
            b16(db * vb * gb * (1.0 - gb)),
            b16(db * gb),
            dgp[:, w],
        ],
        0,
    )
    o_x[:, w] = x16
    o_d5[:, w] = d5
    return dz + norm_cols_back(dot(m5[...], d5), xh, scale)


def take_pair(n, dab, sa, sb):
    part = sa.shape[0] // n
    for d in range(n):
        sa[d * part : (d + 1) * part, :] = f32(dab[d, 0:part])
        sb[d * part : (d + 1) * part, :] = f32(dab[d, part : 2 * part])


def second_back(n, rows, z2, dz3, dgp, dab, pmask, m5ts, m5s, z1, prod, mots, mofs, deps=()):
    def kernel(
        z2, dz3, dgp, dab, pmask, m5ts, m5s, z1, prod, mots, mofs,
        dz2, dgp_out, dp, m_m5, m_mo,
        sa, sb, sp, sdp, o_x, o_d5, o_ph, o_do,
    ):
        m5t, m5, gatet = m5ts.at[1], m5s.at[1], m5ts.at[0, 512:640]
        mot, mof = mots.at[0], mofs.at[0]
        sp[...] = f32(prod[...])
        take_pair(n, dab, sa, sb)

        def body(r):
            w = cols(r)
            dz = projections_back(
                n, rows, z2[:, w], dz3[:, w], dgp, r, pmask, m5t, m5, sa, sb, o_x, o_d5
            )
            dz2[:, w] = dz
            product_back(z1[:, w], dz, r, rows, sp, gatet, mot, mof, sdp, dgp_out, o_ph, o_do)

        each_row(rows // U, body)
        dp[...] = b16(sdp[...])
        for k in range(5):
            s = slice(k * C, (k + 1) * C)
            m_m5[s] = dot_nt(o_x[...], o_d5[s])
        m_mo[...] = dot_nt(o_ph[...], o_do[...])

    wide = rows * L
    return call(
        kernel,
        [
            ((C, wide), F32), ((C, wide), BF), ((C * rows, L), BF),
            ((640, C), F32), ((C, C), F32),
        ],
        [
            ((C * rows, L), F32), ((C * rows, L), F32), ((C * rows, L), F32), ((C * rows, L), F32),
            ((C, wide), BF), ((640, wide), BF), ((C, wide), BF), ((C, wide), BF),
        ],
        (z2, dz3, dgp, dab, pmask, m5ts, m5s, z1, prod, mots, mofs), deps=deps, raw=(0, 1, 2, 4, 5, 6, 7, 8, 9, 10), far=(0, 1, 3, 4), us=11)


def first_back(n, rows, copies, where, z1, dz2, dgp, dab, pmask, m5ts, m5s, inner, lrt, left_own, outer_w, deps=()):
    opm = outer_w.shape[0]

    def kernel(
        where, z1, dz2, dgp, dab, pmask, m5ts, m5s, inner, lrt, left_own, outer_w,
        dz1, ends, m_oo, m_m5,
        sa, sb, o_x, o_d5, sdi, sdr,
    ):
        m5t, m5 = m5ts.at[0], m5s.at[0]
        take_pair(n, dab, sa, sb)
        sdr[...] = jnp.zeros_like(sdr)
        right_t = b16(lrt[opm : 2 * opm])

        def body(r):
            w = cols(r)
            dz = projections_back(
                n, rows, z1[:, w], dz2[:, w], dgp, r, pmask, m5t, m5, sa, sb, o_x, o_d5
            )
            for u in range(U):
                dz16 = b16(lanes(dz, u).T)
                dz1[r * U + u] = dz16
                at = pl.ds(r * U + u, opm, stride=rows)
                sdi[at, :] = dot(right_t, dz16)
                sdr[...] += dot_nt(b16(inner[at, :]), dz16)

        each_row(rows // U, body)
        left = left_own[:, 0:opm]
        d16 = side([b16(sdi[b * rows : (b + 1) * rows]) for b in range(opm)])
        outers = dot_tn(left, d16)
        for b in range(opm):
            m_oo[b * opm : (b + 1) * opm] = lanes(outers, b)
        dleft = dot_nt(side([outer_w[b] for b in range(opm)]), d16)
        lane = lax.broadcasted_iota(jnp.int32, (rows, L), 1)
        spot = lax.broadcasted_iota(jnp.int32, (rows, L), 0) + where[1] * rows
        dleft = dot(b16(dleft), b16(jnp.where(lane == spot, 1.0, 0.0)))
        both = jnp.concatenate([dleft, sdr[...]], 0) * lrt[2 * opm : 2 * opm + 1]
        for d in range(copies):
            ends[d] = b16(both)
        for k in range(5):
            s = slice(k * C, (k + 1) * C)
            m_m5[s] = dot_nt(o_x[...], o_d5[s])

    wide = rows * L
    return call(
        kernel,
        [
            ((rows, L, C), BF), ((copies, 2 * opm, L), BF), ((opm * opm, C), F32), ((640, C), F32),
        ],
        [
            ((C * rows, L), F32), ((C * rows, L), F32), ((C, wide), BF), ((640, wide), BF),
            ((opm * rows, C), F32), ((opm, L), F32),
        ],
        (where, z1, dz2, dgp, dab, pmask, m5ts, m5s, inner, lrt, left_own, outer_w), deps=deps, raw=(1, 2, 3, 5, 6, 7, 8, 9, 10, 11), far=(2, 3), us=11)


def last_back(rows, pair, drb, dz1, sbt, deps=()):
    def kernel(pair, drb, dz1, sbt, grad, m_sb, o_x, o_d):
        def body(r):
            w = cols(r)
            xh, scale = norm_cols(side([f32(pair[r * U + u]).T for u in range(U)]))
            d = get_rows(drb, r, 8, rows)
            d16 = b16(jnp.concatenate([d, jnp.zeros_like(d)], 0))
            back = norm_cols_back(dot_tn(sbt[...], d16), xh, scale)
            for u in range(U):
                grad[r * U + u] = f32(dz1[r * U + u]) + lanes(back, u).T
            o_x[:, w] = b16(xh)
            o_d[:, w] = d16

        each_row(rows // U, body)
        m_sb[...] = dot_nt(o_d[...], o_x[...])

    wide = rows * L
    return call(
        kernel,
        [((rows, L, C), F32), ((HPAD, C), F32)],
        [((C, wide), BF), ((HPAD, wide), BF)],
        (pair, drb, dz1, sbt), deps=deps, raw=(0, 1, 2, 3), far=(0,), us=3)


def collect(where, parts, half, deps):
    def kernel(where, *refs):
        sources, (kept, given, rows) = refs[: len(parts)], refs[len(parts) :]
        core = where[3] % 2
        at = 0
        for ref in sources:
            rows[at : at + ref.shape[0]] = ref[...]
            at += ref.shape[0]
        if at < 2 * half:
            rows[at : 2 * half] = jnp.zeros((2 * half - at, C), F32)
        kept[...] = rows[pl.ds(pl.multiple_of(core * half, half), half), :]
        given[...] = b16(rows[pl.ds(pl.multiple_of((1 - core) * half, half), half), :])

    return call(
        kernel,
        [((half, C), F32), ((half, C), BF)],
        [((2 * half, C), F32)],
        (where, *parts),
        deps=deps,
        raw=tuple(range(1, len(parts) + 1)),
        us=0,
    )


def sum_copies(x, extra, count):
    rows, more = x.shape[1], extra.shape[0]

    def kernel(x, extra, out):
        total = b16(jnp.sum(f32(x[...]), 0))
        for d in range(count):
            out[d, 0:rows] = total
            out[d, rows : rows + more] = b16(extra[...])

    return call(kernel, [((count, rows + more, C), BF)], [], (x, extra), us=2)[0]


def finish(where, near, far, gp, gm, mp, mg, mo, ap, ab, pu, sb, places, half, opm, deps):
    def kernel(
        where, near, far, gp, gm, mp, mg, mo, ap, ab, pu, sb,
        g_pg, g_mg, g_sb, g_oo, g_mp, g_mgt, g_mo, g_ap, g_ab, g_ao, g_pu, g_pd,
        rows,
    ):
        core = where[3] % 2
        chips = near.shape[0]
        size = half // chips
        for k in range(chips):
            at = pl.multiple_of(core * half + k * size, 8)
            rows[pl.ds(at, size), :] = f32(near[k, 0:size])
            at = pl.multiple_of((1 - core) * half + k * size, 8)
            rows[pl.ds(at, size), :] = f32(far[k, 0:size])

        def take(name, count, skip=0):
            at = places[name] + skip
            return rows[at : at + count]

        gpv, gmv = f32(gp[...]), f32(gm[...])

        def column(row):
            return jnp.broadcast_to(row, (C, C)).T

        def over_lanes(x):
            return jnp.sum(x.T, 0, keepdims=True)

        def padded(w):
            return jnp.concatenate([f32(w), jnp.zeros((HPAD - w.shape[0], C), F32)], 0)

        total = jnp.zeros((8, C), F32)
        for k in range(chips):
            total = total + (f32(near[k, size : size + 8]) + f32(far[k, size : size + 8]))
        g_pg[0:1] = jnp.sum(f32(sb[...]) * total, 0, keepdims=True)
        g_sb[...] = total * gpv[0:1]
        for t in range(2):
            g = column(gpv[1 + t : 2 + t])
            both = jnp.zeros((C, C), F32)
            for k in range(5):
                m = take("m5%d" % t, C, k * C)
                both = both + m * f32(mp[t, k] if k < 4 else mg[t])
                if k < 4:
                    g_mp[t, k] = m * g
                else:
                    g_mgt[t] = m * g
            g_pg[1 + t : 2 + t] = over_lanes(both)
            m = take("mo%d" % t, C)
            g_mo[t] = m * column(gmv[t : t + 1])
            g_mg[t : t + 1] = over_lanes(m * f32(mo[t]))
            g = column(gpv[3 + t : 4 + t])
            both = jnp.zeros((C, C), F32)
            for k in range(4):
                m = take("a4%d" % t, C, k * C)
                if k == 0:
                    m = m * HD**-0.5
                both = both + m * f32(ap[t, k])
                g_ap[t, k] = m * g
            m = take("ab%d" % t, HPAD)
            g_pg[3 + t : 4 + t] = over_lanes(both) + jnp.sum(padded(ab[t]) * m, 0, keepdims=True)
            g_ab[t] = (m * gpv[3 + t : 4 + t])[0:TH]
            g_ao[t] = take("ao%d" % t, C)
        g = column(gpv[5:6])
        both = jnp.zeros((C, C), F32)
        for k in range(4):
            s = slice(k * C, (k + 1) * C)
            m = take("up", C, k * C)
            both = both + m * f32(pu[:, s])
            g_pu[:, s] = m * g
        g_pg[5:6] = over_lanes(both)
        g_pd[...] = take("dn", 512)
        for b in range(opm):
            g_oo[:, b, :] = take("oo", opm, b * opm)

    outs = [
        (6, C), (2, C), (8, C), (opm, opm, C), (2, 4, C, C), (2, C, C), (2, C, C), (2, 4, C, C),
        (2, TH, C), (2, C, C), (C, 512), (512, C),
    ]
    return call(
        kernel,
        [(s, F32) for s in outs],
        [((2 * half, C), F32)],
        (where, near, far, gp, gm, mp, mg, mo, ap, ab, pu, sb),

        raw=(3, 4, 5, 6, 7, 8, 9, 10, 11), deps=deps, far=tuple(range(12)), us=4,
    )


PRECISE = lax.Precision.HIGHEST


def for_sending(shard):

    def short(part):
        return part.astype(jnp.bfloat16) if part.dtype == jnp.float32 else part

    return jax.tree.map(short, shard)


def widen(operand):
    return operand.astype(jnp.float32)


def narrow(operand):
    return operand.astype(jnp.bfloat16)


def rounded(operand):
    return lax.optimization_barrier(operand.astype(jnp.bfloat16)).astype(jnp.float32)


def contract(pattern, first_term, second_term):
    return jnp.einsum(pattern, first_term, second_term, precision=PRECISE)


def low_product(pattern, first_term, second_term):
    return jnp.einsum(pattern, first_term, second_term, preferred_element_type=jnp.float32)


def norm_rows(operand, gain_vec):
    centre = operand - jnp.mean(operand, -1, keepdims=True)
    spread = jnp.mean(centre * centre, -1, keepdims=True)
    return centre * lax.rsqrt(spread + EPSILON) * gain_vec


def soft_weights(logits):
    highest = jnp.max(logits, -1, keepdims=True)
    raised = jnp.exp(logits - highest)
    return raised / jnp.sum(raised, -1, keepdims=True)


def single_attend(queries, key_rows, values, gate_value, pair_bias, key_bias, weight_out):
    head_count = pair_bias.shape[0]
    feature_width = queries.shape[-1]
    head_size = feature_width // head_count
    query_heads = queries.reshape(queries.shape[0], head_count, head_size)
    key_heads = key_rows.reshape(key_rows.shape[0], head_count, head_size)
    value_heads = values.reshape(values.shape[0], head_count, head_size)
    logits = (
        contract("ihd,jhd->hij", query_heads, key_heads) * head_size ** (-0.5)
        + pair_bias
        + key_bias
    )
    mixed = contract("hij,jhd->ihd", soft_weights(logits), value_heads).reshape(
        queries.shape[0], feature_width
    )
    return contract("is,st->it", mixed * jax.nn.sigmoid(gate_value), weight_out)


def tri_attend(normed, pair_bias, weight_four, weight_out, key_bias):
    head_count = pair_bias.shape[0]
    feature_width = normed.shape[-1]
    head_size = feature_width // head_count

    def one_row(row_in):
        projected = contract("lc,ncd->nld", row_in, weight_four)
        shaped = projected[:3].reshape(3, row_in.shape[0], head_count, head_size)
        logits = (
            contract("jhd,khd->hjk", shaped[0], shaped[1]) * head_size ** (-0.5)
            + pair_bias
            + key_bias
        )
        mixed = contract("hjk,khd->jhd", soft_weights(logits), shaped[2]).reshape(
            row_in.shape[0], feature_width
        )
        return contract("lc,cd->ld", mixed * jax.nn.sigmoid(projected[3]), weight_out)

    return lax.map(jax.checkpoint(one_row), normed)


def mult_front(pair_in, gain_vec, weight_four, weight_gate, pair_mask):
    normed = norm_rows(pair_in, gain_vec)
    projected = contract("rlc,ncm->nmrl", normed, weight_four)
    left_side = jax.nn.sigmoid(projected[0]) * projected[1] * pair_mask
    right_side = jax.nn.sigmoid(projected[2]) * projected[3] * pair_mask
    gate_value = jax.nn.sigmoid(contract("rlc,cd->rld", normed, weight_gate))
    return (left_side, right_side, gate_value)


def mult_back(pair_in, product, gate_value, gain_vec, weight_out):
    centre = product - jnp.mean(product, 0, keepdims=True)
    spread = jnp.mean(centre * centre, 0, keepdims=True)
    scaled = centre * lax.rsqrt(spread + EPSILON) * gain_vec[:, None, None]
    return pair_in + contract("mrl,mc->rlc", scaled, weight_out) * gate_value


def outgoing_forward(left_chan, right_chan):
    return low_product("mik,mjk->mij", left_chan, right_chan)


def outgoing_backward(left_chan, right_chan, grad_out):
    return (
        low_product("mij,mjk->mik", grad_out, right_chan),
        low_product("mij,mik->mjk", grad_out, left_chan),
    )


def incoming_forward(left_chan, right_chan):
    return low_product("mki,mkj->mij", left_chan, right_chan)


def incoming_backward(left_chan, right_chan, grad_out):
    return (
        low_product("mij,mkj->mki", grad_out, right_chan),
        low_product("mij,mki->mkj", grad_out, left_chan),
    )


def to_channels(operand):
    return jax.tree.map(
        lambda part, own: part.astype(own.dtype),
        lax.all_to_all(for_sending(operand), "rows", split_axis=0, concat_axis=1, tiled=True),
        operand,
    )


def to_rows(operand):
    return jax.tree.map(
        lambda part, own: part.astype(own.dtype),
        lax.all_to_all(for_sending(operand), "rows", split_axis=1, concat_axis=0, tiled=True),
        operand,
    )


def turn_cols(operand):
    return jnp.swapaxes(
        lax.all_to_all(operand, "rows", split_axis=1, concat_axis=0, tiled=True), 0, 1
    )


def turn_rows(operand):
    return lax.all_to_all(
        jnp.swapaxes(operand, 0, 1), "rows", split_axis=0, concat_axis=1, tiled=True
    )


def gather_bias(operand):
    return lax.all_gather(operand, "rows", axis=1, tiled=True)


def scatter_bias(operand):
    return lax.psum_scatter(operand, "rows", scatter_dimension=1, tiled=True)


def general_local(
    single_rep,
    pair_rep,
    residue_mask,
    single_gains,
    pair_gains,
    mult_gains,
    single_proj,
    single_bias,
    single_up,
    single_down,
    opm_proj,
    opm_out,
    mult_proj,
    mult_gate,
    mult_out,
    att_proj,
    att_bias,
    att_out,
    pair_up,
    pair_down,
    single_cot,
    pair_cot,
):
    gains_s = widen(single_gains)
    gains_p = widen(pair_gains)
    gains_m = widen(mult_gains)
    proj_s = widen(single_proj)
    bias_sw = widen(single_bias)
    up_s = widen(single_up)
    down_s = widen(single_down)
    proj_o = widen(opm_proj)
    outer_w = widen(opm_out)
    proj_m = widen(mult_proj)
    gate_m = widen(mult_gate)
    out_m = widen(mult_out)
    proj_a = widen(att_proj)
    bias_a = widen(att_bias)
    out_a = widen(att_out)
    up_p = widen(pair_up)
    down_p = widen(pair_down)
    mask_all = widen(residue_mask[0])
    shard_rows = pair_rep.shape[1]
    first_row = lax.axis_index("rows") * shard_rows
    mask_own = lax.dynamic_slice_in_dim(mask_all, first_row, shard_rows, 0)
    key_bias = (mask_all - 1.0) * MASKED
    pair_mask = mask_own[:, None] * mask_all[None, :]
    single_own = widen(single_rep[0])
    pair_own = widen(pair_rep[0])

    def front_single(
        single_in, pair_in, gain_s, gain_z, proj_query, proj_key, proj_value, proj_gate, bias_w
    ):
        normed = norm_rows(single_in, gain_s)
        pair_normed = norm_rows(pair_in, gain_z)
        return (
            contract("rs,st->rt", normed, proj_query),
            contract("rs,st->rt", normed, proj_key),
            contract("rs,st->rt", normed, proj_value),
            contract("rs,st->rt", normed, proj_gate),
            contract("rlc,ch->hrl", pair_normed, bias_w),
        )

    def back_single(
        queries,
        key_rows,
        values,
        gate_value,
        row_bias,
        single_in,
        proj_out,
        gain_t,
        weight_up,
        weight_down,
        gain_o,
        left_w,
        right_w,
    ):
        first_sum = single_in + single_attend(
            queries, key_rows, values, gate_value, row_bias, key_bias, proj_out
        )
        hidden = jax.nn.gelu(contract("rs,st->rt", norm_rows(first_sum, gain_t), weight_up))
        second_sum = first_sum + contract("rt,ts->rs", hidden, weight_down)
        outer_in = norm_rows(second_sum, gain_o)
        left_side = contract("rs,sa->ra", outer_in, left_w) * mask_own[:, None]
        right_side = contract("rs,sa->ra", outer_in, right_w) * mask_own[:, None]
        return (second_sum, left_side, right_side)

    def outer_front(left_side, right_all, pair_in, weight_outer, gain_in, weight_four, weight_gate):
        inner = contract("ia,abc->ibc", left_side, weight_outer)
        updated = pair_in + contract("ibc,jb->ijc", inner, right_all)
        left_m, right_m, gate_value = mult_front(
            updated, gain_in, weight_four, weight_gate, pair_mask
        )
        return (updated, left_m, right_m, gate_value)

    def middle_mult(
        pair_in, product, gate_value, gain_out, weight_out, gain_in, weight_four, weight_gate
    ):
        updated = mult_back(pair_in, product, gate_value, gain_out, weight_out)
        left_m, right_m, gate_next = mult_front(
            updated, gain_in, weight_four, weight_gate, pair_mask
        )
        return (updated, left_m, right_m, gate_next)

    def start_front_general(pair_in, product, gate_value, gain_out, weight_out, gain_start, bias_w):
        updated = mult_back(pair_in, product, gate_value, gain_out, weight_out)
        normed = norm_rows(updated, gain_start)
        return (updated, normed, contract("rlc,ch->hrl", normed, bias_w))

    def start_core(pair_in, normed, bias_all, weight_four, weight_out, gain_end):
        updated = pair_in + tri_attend(normed, bias_all, weight_four, weight_out, key_bias)
        return (updated, norm_rows(updated, gain_end))

    def end_bias(turned, bias_w):
        return contract("rlc,ch->hrl", turned, bias_w)

    def end_core(turned, bias_all, weight_four, weight_out):
        return tri_attend(turned, bias_all, weight_four, weight_out, key_bias)

    def final_pair(pair_in, update, gain_vec, weight_up, weight_down):
        summed = pair_in + update
        hidden = jax.nn.gelu(contract("rlc,cd->rld", norm_rows(summed, gain_vec), weight_up))
        return summed + contract("rld,dc->rlc", hidden, weight_down)

    outs_one, back_one = jax.vjp(
        front_single,
        single_own,
        pair_own,
        gains_s[0],
        gains_p[0],
        proj_s[0],
        proj_s[1],
        proj_s[2],
        proj_s[3],
        bias_sw,
    )
    queries, keys_own, values_own, gate_single, row_bias = outs_one
    keys_all, values_all = (
        lax.all_gather(narrow(keys_own), "rows", axis=0, tiled=True),
        lax.all_gather(narrow(values_own), "rows", axis=0, tiled=True),
    )
    outs_two, back_two = jax.vjp(
        back_single,
        queries,
        widen(keys_all),
        widen(values_all),
        gate_single,
        row_bias,
        single_own,
        proj_s[4],
        gains_s[1],
        up_s,
        down_s,
        gains_s[2],
        proj_o[0],
        proj_o[1],
    )
    single_next, left_outer, right_outer = outs_two
    right_all = widen(lax.all_gather(narrow(right_outer), "rows", axis=0, tiled=True))
    outs_three, back_three = jax.vjp(
        outer_front,
        rounded(left_outer),
        right_all,
        pair_own,
        outer_w,
        gains_p[1],
        proj_m[0],
        gate_m[0],
    )
    pair_one, left_first, right_first, gate_first = outs_three
    chan_left, chan_right = to_channels((narrow(left_first), narrow(right_first)))
    product_one = outgoing_forward(chan_left, chan_right)
    rows_one = widen(to_rows(narrow(product_one)))
    outs_five, back_five = jax.vjp(
        middle_mult,
        pair_one,
        rows_one,
        gate_first,
        gains_m[0],
        out_m[0],
        gains_p[2],
        proj_m[1],
        gate_m[1],
    )
    pair_two, left_second, right_second, gate_second = outs_five
    chan_left_two, chan_right_two = to_channels((narrow(left_second), narrow(right_second)))
    product_two = incoming_forward(chan_left_two, chan_right_two)
    rows_two = widen(to_rows(narrow(product_two)))
    outs_seven, back_seven = jax.vjp(
        start_front_general, pair_two, rows_two, gate_second, gains_m[1], out_m[1], gains_p[3], bias_a[0]
    )
    pair_three, normed_start, bias_start = outs_seven
    bias_start_all = widen(gather_bias(narrow(bias_start)))
    outs_eight, back_eight = jax.vjp(
        start_core, pair_three, normed_start, bias_start_all, proj_a[0], out_a[0], gains_p[4]
    )
    pair_four, normed_end = outs_eight
    turned = widen(turn_cols(narrow(normed_end)))
    bias_end, back_nine = jax.vjp(end_bias, turned, bias_a[1])
    bias_end_all = widen(gather_bias(narrow(bias_end)))
    update_turned, back_ten = jax.vjp(end_core, turned, bias_end_all, proj_a[1], out_a[1])
    update = widen(turn_rows(narrow(update_turned)))
    pair_six, back_eleven = jax.vjp(final_pair, pair_four, update, gains_p[5], up_p, down_p)
    grad_four, grad_update, g_pg5, g_pu, g_pd = back_eleven(widen(pair_cot[0]))
    g_pg5, g_pu, g_pd = (g_pg5, g_pu, g_pd)
    grad_turned_update = widen(turn_cols(narrow(grad_update)))
    grad_turned_a, grad_bias_end_all, g_ap1, g_ao1 = back_ten(grad_turned_update)
    g_ap1, g_ao1 = (g_ap1, g_ao1)
    grad_bias_end = rounded(scatter_bias(grad_bias_end_all))
    grad_turned_b, g_ab1 = back_nine(grad_bias_end)
    grad_normed_end = widen(turn_rows(narrow(grad_turned_a + grad_turned_b)))
    grad_three, grad_normed_start, grad_bias_start_all, g_ap0, g_ao0, g_pg4 = back_eight(
        (grad_four, grad_normed_end)
    )
    g_ap0, g_ao0, g_pg4 = (g_ap0, g_ao0, g_pg4)
    grad_bias_start = rounded(scatter_bias(grad_bias_start_all))
    grad_two, grad_rows_two, grad_gate_second, g_mg1, g_mo1, g_pg3, g_ab0 = back_seven(
        (grad_three, grad_normed_start, grad_bias_start)
    )
    g_mg1, g_mo1, g_pg3, g_ab0 = (g_mg1, g_mo1, g_pg3, g_ab0)
    grad_chan_left_two, grad_chan_right_two = incoming_backward(
        chan_left_two, chan_right_two, to_channels(narrow(grad_rows_two))
    )
    grad_left_second, grad_right_second = to_rows(
        (narrow(grad_chan_left_two), narrow(grad_chan_right_two))
    )
    grad_one, grad_rows_one, grad_gate_first, g_mg0, g_mo0, g_pg2, g_mp1, g_mgt1 = back_five(
        (grad_two, widen(grad_left_second), widen(grad_right_second), grad_gate_second)
    )
    g_mg0, g_mo0, g_pg2, g_mp1, g_mgt1 = (g_mg0, g_mo0, g_pg2, g_mp1, g_mgt1)
    grad_chan_left, grad_chan_right = outgoing_backward(
        chan_left, chan_right, to_channels(narrow(grad_rows_one))
    )
    grad_left_first, grad_right_first = to_rows((narrow(grad_chan_left), narrow(grad_chan_right)))
    grad_left_outer, grad_right_all, grad_pair_a, g_oo, g_pg1, g_mp0, g_mgt0 = back_three(
        (grad_one, widen(grad_left_first), widen(grad_right_first), grad_gate_first)
    )
    g_oo, g_pg1, g_mp0, g_mgt0 = (g_oo, g_pg1, g_mp0, g_mgt0)
    grad_right_outer = rounded(
        lax.psum_scatter(grad_right_all, "rows", scatter_dimension=0, tiled=True)
    )
    two_grads = back_two((widen(single_cot[0]), rounded(grad_left_outer), grad_right_outer))
    grad_query, grad_keys_all, grad_values_all, grad_gate_single, grad_row_bias, grad_single_a = (
        two_grads[:6]
    )
    g_sp4, g_sg1, g_su, g_sd, g_sg2, g_op0, g_op1 = tuple(two_grads[6:])
    grad_keys, grad_values = (
        lax.psum_scatter(grad_keys_all, "rows", scatter_dimension=0, tiled=True),
        lax.psum_scatter(grad_values_all, "rows", scatter_dimension=0, tiled=True),
    )
    grad_single_b, grad_pair_b, g_sg0, g_pg0, g_sp0, g_sp1, g_sp2, g_sp3, g_sb = back_one(
        (grad_query, rounded(grad_keys), rounded(grad_values), grad_gate_single, grad_row_bias)
    )
    g_sg0, g_pg0, g_sp0, g_sp1, g_sp2, g_sp3, g_sb = (
        g_sg0,
        g_pg0,
        g_sp0,
        g_sp1,
        g_sp2,
        g_sp3,
        g_sb,
    )
    weight_totals = (
        jnp.stack([g_sg0, g_sg1, g_sg2]),
        jnp.stack([g_pg0, g_pg1, g_pg2, g_pg3, g_pg4, g_pg5]),
        jnp.stack([g_mg0, g_mg1]),
        jnp.stack([g_sp0, g_sp1, g_sp2, g_sp3, g_sp4]),
        g_sb,
        g_su,
        g_sd,
        jnp.stack([g_op0, g_op1]),
        g_oo,
        jnp.stack([g_mp0, g_mp1]),
        jnp.stack([g_mgt0, g_mgt1]),
        jnp.stack([g_mo0, g_mo1]),
        jnp.stack([g_ap0, g_ap1]),
        jnp.stack([g_ab0, g_ab1]),
        jnp.stack([g_ao0, g_ao1]),
        g_pu,
        g_pd,
    )
    weight_totals = lax.psum(
        (
            weight_totals[0],
            weight_totals[1],
            weight_totals[2],
            weight_totals[3],
            weight_totals[4],
            weight_totals[5],
            weight_totals[6],
            weight_totals[7],
            weight_totals[8],
            weight_totals[9],
            weight_totals[10],
            weight_totals[11],
            weight_totals[12],
            weight_totals[13],
            weight_totals[14],
            weight_totals[15],
            weight_totals[16],
        ),
        ("grp", "rows"),
    )
    return (
        narrow(single_next)[None],
        narrow(pair_six)[None],
        (grad_single_a + grad_single_b)[None],
        (grad_pair_a + grad_pair_b)[None],
    ) + tuple(weight_totals)


def pad_rows(x, count):
    return jnp.concatenate([x, jnp.zeros((count - x.shape[0],) + x.shape[1:], x.dtype)], 0)


def fast_local(square, row_count):
    n = row_count
    rows = L // n
    part = L * rows // n
    crops = 4
    total = crops * n

    def home(g, r):
        if square:
            x, z = g % 2, r // 2
            near = 3 - z if x else z
            side_of, level = ((x, 0), (1 - x, 1), (x, 1), (1 - x, 0))[near]
            g, r = g - x + side_of, (3 - level if x else level) * 2 + r % 2
        return g * n + r

    groups = [[home(g, r) for r in range(n)] for g in range(crops)]

    def swap(x, back=False):
        if not square:
            return x
        pairs = [(g * n + r, home(g, r)) for g in range(crops) for r in range(n)]
        return lax.ppermute(x, AX, [(b, a) for a, b in pairs] if back else pairs)

    def to_home(k, x):
        pairs = [(g * n + r, home(g, (r + k) % n)) for g in range(crops) for r in range(n)]
        return lax.ppermute(x, AX, pairs)

    def from_home(k, x):
        pairs = [(home(g, r), g * n + (r + k) % n) for g in range(crops) for r in range(n)]
        return lax.ppermute(x, AX, pairs)

    def exchange(x):
        if square:
            return lax.all_to_all(x, AX, 0, 0, tiled=True, axis_index_groups=groups)
        return lax.all_to_all(x, "rows", 0, 0, tiled=True)

    def to_all(copies):
        return lax.all_to_all(copies, AX, 0, 0, tiled=True)

    chips = total // 2
    same_core = [[g * n + z * 2 + c for g in range(crops) for z in range(n // 2)] for c in range(2)]
    members = [sorted(set(d // 2 for d in group)) for group in groups]

    def other_core(x):
        return lax.ppermute(x, "rows", [(i, i ^ 1) for i in range(n)])

    def to_chips(copies):
        return lax.all_to_all(copies, AX, 0, 0, tiled=True, axis_index_groups=same_core)

    def local(
        single_rep, pair_rep, residue_mask, single_gains, pair_gains, mult_gains, single_proj,
        single_bias, single_up, single_down, opm_proj, opm_out, mult_proj, mult_gate, mult_out,
        att_proj, att_bias, att_out, pair_up, pair_down, single_cot, pair_cot,
    ):
        grp, row = lax.axis_index("grp"), lax.axis_index("rows")
        crop, block = grp, row
        if square:
            half = row // 4
            level = jnp.where(half == 1, 3 - row // 2, row // 2)
            near = jnp.where(grp % 2 == half, 2 * level, 3 - 2 * level)
            crop = grp - grp % 2 + half
            block = jnp.where(half == 1, 3 - near, near) * 2 + row % 2
        where = jnp.stack([crop, block, grp, row]).astype(jnp.int32)
        single, width = single_rep[0], single_rep.shape[2]
        gathered = lax.all_to_all(
            jnp.broadcast_to(single, (n,) + single.shape), "rows", 0, 0, tiled=True
        )
        pair = swap(pair_rep[0])
        att_b, single_b = jnp.swapaxes(att_bias, 1, 2), single_bias.T
        m5t, m5, mot, mof, a4t, a4, aot, abt, upt, up, dnt, sbt = prep_weights(
            pair_gains, mult_gains, mult_proj, mult_gate, mult_out, att_proj, att_b, att_out,
            pair_up, pair_down, single_b,
        )
        opm = opm_proj.shape[2]
        outer = jnp.swapaxes(opm_proj, 0, 1).reshape(width, 2 * opm)
        outer = jnp.pad(outer, ((0, 0), (0, L - 2 * opm)))
        outer_w = jnp.swapaxes(opm_out, 0, 1)
        mask_row = f32(residue_mask)
        mine, mask_col = pack(rows, single, single_cot[0], pair_rep[0], mask_row, sbt, where)
        single_out, lr = single_own(
            n, rows, total, gathered, mine, mask_col, single_gains, single_proj, single_up,
            single_down, outer,
        )
        lr = to_all(lr)

        z1, ab1, pmask, key_row, inner, lrt, left_own = front(
            n, rows, where, lr, pair, outer_w, m5t
        )
        dealt = deal(n, rows, where, pair_cot[0], (mine,))
        cots = {}

        def send_cots(offsets, ahead, behind):
            for k in offsets:
                block, _ = lax.optimization_barrier((dealt[k], behind))
                cots[k] = to_home(k, block)
            return lax.optimization_barrier((ahead, *[cots[k] for k in offsets]))[0]

        ab1 = send_cots((0, 1), ab1, lr)
        ab1 = exchange(ab1)
        p1 = exchange(channel_product(n, rows, True, ab1)).reshape(C * rows, L)
        z2, ab2 = middle(n, rows, z1, p1, mot, pmask, m5t)
        ab2 = send_cots((2, 3), ab2, p1)
        ab2 = exchange(ab2)
        p2 = exchange(channel_product(n, rows, False, ab2)).reshape(C * rows, L)
        z3, tb = start_front(n, rows, z2, p2, m5t, mot, abt)
        tb = send_cots((4, 5), tb, p2)
        tb_all = exchange(tb)
        z4, turn = start_attention(n, rows, z3, tb_all, key_row, a4t, aot, abt)
        turn = send_cots((6, 7), turn, tb_all)
        turn = exchange(turn)
        copies = to_chips(copies_of(mine, chips, (turn,)))
        others = other_core(copies)

        *pouts, back, m_up, m_dn, m_a41, m_ao1 = end_both(
            n, rows, where, turn, [cots[k] for k in range(n)], key_row, a4t, a4, aot, att_out, upt,
            up, dnt, pair_down,
        )
        back = exchange(back)
        sent = {}

        def send_pouts(offsets, ahead, behind):
            for k in offsets:
                block, _ = lax.optimization_barrier((pouts[k], behind))
                sent[k] = from_home(k, block)
            return lax.optimization_barrier((ahead, *[sent[k] for k in offsets]))[0]

        dz4, dxs, dtb, m_a40, m_ao0, m_ab1 = start_back(
            n, rows, z3, z4, back, tb_all, key_row, a4t, a4, att_out, abt, deps=(copies, others)
        )
        dtb = send_pouts((0, 1, 2, 3), dtb, back)
        dtb = exchange(dtb)
        dz3, dgp2, dp2, m_ab0, m_mo1 = third_back(
            n, rows, z3, dz4, dxs, dtb, abt, z2, p2, m5t, mot, mof
        )
        dp2 = send_pouts((4, 5), dp2, dtb)
        dp2 = exchange(dp2.reshape(n, part, L))
        dab2 = channel_product_back(n, rows, False, ab2, dp2)
        kept = single_every(
            n, rows, where, copies, others, single_gains, single_proj, single_up, single_down,
            deps=(dab2,),
        )
        dab2 = exchange(dab2)
        dz2, dgp1, dp1, m_m51, m_mo0 = second_back(
            n, rows, z2, dz3, dgp2, dab2, pmask, m5t, m5, z1, p1, mot, mof, deps=(kept[0],)
        )
        dp1 = send_pouts((6, 7), dp1, dab2)
        pair_six = undeal(n, rows, where, [sent[k] for k in range(n)])
        dp1 = exchange(dp1.reshape(n, part, L))
        dab1 = exchange(channel_product_back(n, rows, True, ab1, dp1))
        dz1, ends, m_oo, m_m50 = first_back(
            n, rows, chips, where, z1, dz2, dgp1, dab1, pmask, m5t, m5, inner, lrt, left_own,
            outer_w,
        )
        names = [
            "up", "dn", "a41", "ao1", "a40", "ao0", "m51", "mo1", "mo0", "m50", "oo", "ab1", "ab0",
        ]
        sums = [
            m_up, m_dn, m_a41, m_ao1, m_a40, m_ao0, m_m51, m_mo1, m_mo0, m_m50, m_oo, m_ab1, m_ab0,
        ]
        places, at = {}, 0
        for name, m in zip(names, sums):
            places[name] = at
            at += m.shape[0]
        half = -(-at // (total * 16)) * total * 8
        near, far = collect(where, sums, half, ())
        near = b16(near + f32(other_core(far)))
        ends = to_chips(ends)
        ends, near = lax.optimization_barrier((ends, near))
        others_ends = other_core(ends)
        dz1 = swap(copies_of(dz1, 1, (others_ends,))[0], True)
        near, others_ends = lax.optimization_barrier((near, others_ends))
        near = to_chips(near.reshape(chips, half // chips, C))
        ys, g_sg, d_own, drb, m_op = single_back(
            members, rows, where, ends, others_ends, kept, single_gains, single_proj,
            single_up, single_down, outer,
        )
        pair_grad, m_sb = last_back(rows, pair_rep[0], drb, dz1, sbt)
        near_sums = sum_copies(near, m_sb, chips)
        g_sp, g_su, g_sd = weight_grads(kept[2], ys, width, single_up.shape[1], near_sums)
        g_op = jnp.swapaxes(m_op[:, : 2 * opm].reshape(width, 2, opm), 0, 1)

        near = copies_of(to_chips(near_sums), 1, (g_sp, g_su, g_sd, pair_six))[0]
        grads = finish(
            where, near, other_core(near), pair_gains, mult_gains, mult_proj, mult_gate,
            mult_out, att_proj, att_b, pair_up, single_b, places, half, opm, (),
        )
        g_pg, g_mg, g_sb, g_oo, g_mp, g_mgt, g_mo, g_ap, g_ab, g_ao, g_pu, g_pd = grads
        return (
            single_out[None],
            pair_six[None],
            d_own[None],
            pair_grad[None],
            g_sg,
            g_pg,
            g_mg,
            g_sp,
            g_sb.T,
            g_su,
            g_sd,
            g_op,
            g_oo,
            g_mp,
            g_mgt,
            g_mo,
            g_ap,
            jnp.swapaxes(g_ab, 1, 2),
            g_ao,
            g_pu,
            g_pd,
        )

    return local


def solution(mesh):
    groups_of, n = mesh.shape["grp"], mesh.shape["rows"]
    whole = P()
    in_specs = (
        (P("grp", "rows", None), P("grp", "rows", None, None), P("grp", None))
        + (whole,) * 17
        + (P("grp", "rows", None), P("grp", "rows", None, None))
    )
    out_specs = (
        P("grp", "rows", None),
        P("grp", "rows", None, None),
        P("grp", "rows", None),
        P("grp", "rows", None, None),
    ) + (whole,) * 17
    if L % n == 0 and (L // n) % 16 == 0:
        body = fast_local((groups_of, n) == (4, 8), n)
    else:
        body = general_local
    return jax.shard_map(body, mesh=mesh, in_specs=in_specs, out_specs=out_specs, check_vma=False)
```

```python
import math

import jax
import jax.numpy as jnp
from jax import lax
from jax.experimental import pallas as pl
from jax.experimental.pallas import tpu as pltpu
from jax.sharding import PartitionSpec as P

BF = jnp.bfloat16
F32 = jnp.float32
EPSILON = 1e-05
MASKED = 1000000000.0
AX = ("grp", "rows")
L = 128
C = 128
TH = 4
HD = 32
HPAD = 16


def dot(a, b):
    return lax.dot_general(a, b, (((1,), (0,)), ((), ())), preferred_element_type=F32)


def dot_nt(a, b):
    return lax.dot_general(a, b, (((1,), (1,)), ((), ())), preferred_element_type=F32)


def dot_tn(a, b):
    return lax.dot_general(a, b, (((0,), (0,)), ((), ())), preferred_element_type=F32)


def b16(x):
    return x.astype(BF)


def f32(x):
    return x.astype(F32)


def sig(x):
    return 0.5 * jnp.tanh(0.5 * x) + 0.5


GELU_A = 0.7978845608028654
GELU_B = 0.044715


def gelu_parts(x):
    t = jnp.tanh(GELU_A * (x + GELU_B * x * x * x))
    half = 0.5 * (1.0 + t)
    slope = half + 0.5 * x * (1.0 - t * t) * (GELU_A * (1.0 + 3.0 * GELU_B * x * x))
    return x * half, slope


def norm_cols(z):
    c = z - jnp.mean(z, 0, keepdims=True)
    scale = lax.rsqrt(jnp.mean(c * c, 0, keepdims=True) + EPSILON)
    return c * scale, scale


def norm_cols_back(dx, xh, scale):
    return scale * (
        dx - jnp.mean(dx, 0, keepdims=True) - xh * jnp.mean(dx * xh, 0, keepdims=True)
    )


U = 16


def cols(r):
    return pl.ds(pl.multiple_of(r * U * L, U * L), U * L)


def side(parts):
    return jnp.concatenate(parts, 1)


def lanes(x, u):
    return x[:, u * L : (u + 1) * L]


def get_rows(ref, r, count, rows):
    return side([ref[pl.ds(r * U + u, count, stride=rows), :] for u in range(U)])


def put_rows(ref, r, count, rows, x):
    for u in range(U):
        ref[pl.ds(r * U + u, count, stride=rows), :] = lanes(x, u)


def put_turned(ref, r, rows, x):
    for u in range(U):
        ref[pl.ds(r * U + u, L, stride=rows), :] = lanes(x, u).T


def get_turned(ref, r, rows):
    return side(
        [
            f32(ref[:, pl.ds(pl.multiple_of((r * U + u) * rows, rows), rows), :].reshape(L, C)).T
            for u in range(U)
        ]
    )


def each_row(count, body):
    def step(r, carry):
        body(r)
        return carry

    lax.fori_loop(0, count, step, 0, unroll=4 if count == 4 else 1)


def call(kernel, outs, scratch, args, deps=(), raw=(), late=(), far=(), step=16, us=5):
    global U
    U = step
    count, more, given = len(args), len(deps), len(outs)
    fetched = [args[k] for k in raw]

    def body(*refs):
        mine = list(refs[:count])
        results = list(refs[count + more : count + more + given])
        rest = list(refs[count + more + given :])
        sems = rest.pop() if raw or far else None
        stores = [rest.pop() for _ in far][::-1]
        held = [rest.pop() for _ in raw][::-1]
        moves = {}
        for i, k in enumerate(raw):
            moves[k] = pltpu.make_async_copy(mine[k], held[i], sems.at[i])
            moves[k].start()
        for k in raw:
            if k not in late:
                moves[k].wait()
        for i, k in enumerate(raw):
            mine[k] = held[i]
        ends = []
        for i, k in enumerate(far):
            ends.append(pltpu.make_async_copy(stores[i], results[k], sems.at[len(raw) + i]))
            results[k] = stores[i]
        early = set()

        def arrive(k):
            moves[k].wait()

        def leave(k):
            early.add(far.index(k))
            ends[far.index(k)].start()

        if late:
            kernel((arrive, leave), *mine, *results, *rest)
        else:
            kernel(*mine, *results, *rest)
        for i, end in enumerate(ends):
            if i not in early:
                end.start()
        for end in ends:
            end.wait()

    vm = pl.BlockSpec(memory_space=pltpu.VMEM)
    sm = pl.BlockSpec(memory_space=pltpu.SMEM)
    away = pl.BlockSpec(memory_space=pl.ANY)
    moved = sum(a.size * a.dtype.itemsize for a in args)
    buffers = [pltpu.VMEM(s, d) for s, d in scratch]
    buffers += [pltpu.VMEM(a.shape, a.dtype) for a in fetched]
    buffers += [pltpu.VMEM(*outs[k]) for k in far]
    placed = sum(math.prod(b.shape) * jnp.dtype(b.dtype).itemsize for b in buffers)
    if raw or far:
        buffers.append(pltpu.SemaphoreType.DMA((len(raw) + len(far),)))
    return pl.pallas_call(
        body,
        out_shape=[
            pltpu.HBM(s, d) if k in far else jax.ShapeDtypeStruct(s, d)
            for k, (s, d) in enumerate(outs)
        ],
        in_specs=[
            away if k in raw else sm if a.dtype == jnp.int32 else vm for k, a in enumerate(args)
        ]
        + [away] * more,
        out_specs=[away if k in far else vm for k in range(given)],
        scratch_shapes=buffers,
        compiler_params=pltpu.CompilerParams(vmem_limit_bytes=(30 << 20) + placed),
        cost_estimate=pl.CostEstimate(flops=us * 10**9, bytes_accessed=moved if us else 0, transcendentals=0),
    )(
        *[
            pltpu.with_memory_space_constraint(a, pltpu.HBM) if k in raw else a
            for k, a in enumerate(args)
        ],
        *[pltpu.with_memory_space_constraint(d, pltpu.HBM) for d in deps],
    )


def prep_weights(gp, gm, mp, mg, mo, ap, ab, ao, pu, pd, sb):
    def kernel(
        gp, gm, mp, mg, mo, ap, ab, ao, pu, pd, sb,
        m5t, m5, mot, mof, a4t, a4, aot, abt, upt, up, dnt, sbt,
    ):
        gpv = f32(gp[...])
        gmv = f32(gm[...])

        def padded(w):
            return jnp.concatenate([f32(w), jnp.zeros((HPAD - w.shape[0], C), F32)], 0)

        for t in range(2):
            g = gpv[1 + t : 2 + t]
            for k in range(5):
                w = f32(mp[t, k] if k < 4 else mg[t]).T * g
                m5t[t, k * C : (k + 1) * C] = b16(w)
                m5[t, :, k * C : (k + 1) * C] = b16(w.T)
            w = f32(mo[t]).T * gmv[t : t + 1]
            mot[t] = b16(w)
            mof[t] = b16(w.T)
            g = gpv[3 + t : 4 + t]
            for k in range(4):
                w = f32(ap[t, k]).T * (g * HD**-0.5 if k == 0 else g)
                a4t[t, k * C : (k + 1) * C] = b16(w)
                a4[t, :, k * C : (k + 1) * C] = b16(w.T)
            aot[t] = b16(f32(ao[t]).T)
            abt[t] = b16(padded(ab[t]) * g)
        g = gpv[5:6]
        for k in range(4):
            s = slice(k * C, (k + 1) * C)
            w = f32(pu[:, s]).T * g
            upt[s] = b16(w)
            up[:, s] = b16(w.T)
            dnt[:, s] = b16(f32(pd[s]).T)
        sbt[...] = b16(padded(sb[...]) * gpv[0:1])

    outs = [
        ((2, 640, C), BF), ((2, C, 640), BF), ((2, C, C), BF), ((2, C, C), BF),
        ((2, 512, C), BF), ((2, C, 512), BF), ((2, C, C), BF), ((2, HPAD, C), BF),
        ((512, C), BF), ((C, 512), BF), ((C, 512), BF), ((HPAD, C), BF),
    ]
    return call(kernel, outs, [], (gp, gm, mp, mg, mo, ap, ab, ao, pu, pd, sb), raw=(0, 1, 2, 3, 4, 5, 6, 7, 8, 9, 10), far=(0, 1, 2, 3, 4, 5, 6, 7, 8, 9, 10, 11), us=3)


def pack(rows, single, cot, pair, mask, sbt, where):
    def kernel(single, cot, pair, mask, sbt, where, mine, mask_col, s, sm):
        sm[...] = jnp.broadcast_to(mask[...], (L, L)).T
        mask_col[...] = sm[pl.ds(pl.multiple_of(where[3] * rows, rows), rows), :]
        key_row = (mask[...] - 1.0) * MASKED

        def body(r):
            xh, _ = norm_cols(side([f32(pair[r * U + u]).T for u in range(U)]))
            put_rows(s, r, HPAD, rows, dot(sbt[...], b16(xh)) + side([key_row] * U))

        each_row(rows // U, body)
        mine[0:rows] = single[...]
        mine[rows : 2 * rows] = cot[...]
        for h in range(8):
            mine[rows * (2 + h // 4) : rows * (3 + h // 4), (h % 4) * L : (h % 4 + 1) * L] = b16(
                s[h * rows : (h + 1) * rows]
            )

    width = single.shape[1]
    return call(
        kernel,
        [((4 * rows, width), BF), ((rows, L), F32)],
        [((HPAD * rows, L), F32), ((L, L), F32)],
        (single, cot, pair, mask, sbt, where), raw=(0, 1, 2, 4), us=2)


def copies_of(x, count, deps):
    def kernel(x, out):
        for d in range(count):
            out[d] = x[...]

    return call(kernel, [((count,) + x.shape, x.dtype)], [], (x,), deps=deps)[0]


def deal(n, rows, where, x, deps):
    def kernel(where, x, *outs):
        for k in range(n):
            block = lax.rem(where[3] + k, n)
            at = pl.ds(pl.multiple_of(block * rows, rows), rows)
            outs[k][...] = x[:, at, :].reshape(rows * rows, C)

    return call(
        kernel, [((rows * rows, C), BF)] * n, [], (where, x), deps=deps, raw=(1,),
        far=tuple(range(n)), us=1,
    )


def undeal(n, rows, where, parts):
    def kernel(where, *refs):
        out = refs[n]
        for k in range(n):
            block = lax.rem(where[3] + n - k, n)
            at = pl.ds(pl.multiple_of(block * rows, rows), rows)
            out[:, at, :] = refs[k][...].reshape(rows, rows, C)

    return call(
        kernel, [((rows, L, C), BF)], [], (where, *parts), raw=tuple(range(1, n + 1)), far=(0,),
        us=1,
    )[0]


def part_of(x, first, last, deps):
    def kernel(x, out):
        out[...] = x[first:last]

    return call(
        kernel, [((last - first,) + x.shape[1:], x.dtype)], [], (x,), deps=deps, raw=(0,), us=1
    )[0]


def norm_rows16(x):
    c = x - jnp.mean(x, -1, keepdims=True)
    scale = lax.rsqrt(jnp.mean(c * c, -1, keepdims=True) + EPSILON)
    return c * scale, scale


def norm_rows16_back(dx, xh, scale):
    return scale * (
        dx - jnp.mean(dx, -1, keepdims=True) - xh * jnp.mean(dx * xh, -1, keepdims=True)
    )


def halves():
    lane = lax.broadcasted_iota(jnp.int32, (1, L), 1)
    low = jnp.where(lane < L // 2, 1.0, 0.0)
    return b16(low), b16(1.0 - low)


def pair_weights(q, k, bias0, bias1):
    out = []
    for m, bias in zip(halves(), (bias0, bias1)):
        s = dot_nt(q * m, k) + bias
        e = jnp.exp(s - jnp.max(s, -1, keepdims=True))
        out.append(b16(e / jnp.sum(e, -1, keepdims=True)))
    return out


def on_halves(x, axis=0):
    return jnp.concatenate([x * m for m in halves()], axis)


def single_own(n, rows, copies, gathered, mine, mask_col, gains, proj, up, down, outer):
    width = up.shape[0]
    opm2 = 64

    def kernel(moves, gathered, mine, mask_col, gains, proj, up, down, outer, out, lr):
        g = f32(gains[...])
        sn = b16(norm_rows16(f32(gathered[...].reshape(n * rows, width)))[0] * g[0:1])
        arrive, _ = moves
        arrive(4)
        keys, vals = b16(dot(sn, proj[1])), b16(dot(sn, proj[2]))
        x = f32(mine[0:rows])
        sn = b16(norm_rows16(x)[0] * g[0:1])
        query = b16(dot(sn, proj[0]) * 0.125)
        gate = sig(dot(sn, proj[3]))
        mixed = []
        for t in range(4):
            s = slice(t * L, (t + 1) * L)
            bias = [
                f32(mine[rows * (2 + h // 4) : rows * (3 + h // 4), (h % 4) * L : (h % 4 + 1) * L])
                for h in (2 * t, 2 * t + 1)
            ]
            p = pair_weights(query[:, s], keys[:, s], *bias)
            mixed.append(dot(jnp.concatenate(p, 1), on_halves(vals[:, s])))
        mixed = jnp.concatenate(mixed, 1)
        first = x + dot(b16(mixed * gate), proj[4])
        x1 = b16(norm_rows16(first)[0] * g[1:2])
        arrive(5)
        hidden = b16(gelu_parts(dot(x1, up[...]))[0])
        arrive(6)
        second = first + dot(hidden, down[...])
        out[...] = b16(second)
        x2 = b16(norm_rows16(second)[0] * g[2:3])
        both = dot(x2, outer[...]) * mask_col[...]
        lane = lax.broadcasted_iota(jnp.int32, (rows, L), 1)
        both = b16(jnp.where(lane >= opm2, mask_col[...], both))
        for d in range(copies):
            lr[d] = both

    return call(
        kernel,
        [((rows, width), BF), ((copies, rows, L), BF)],
        [],
        (gathered, mine, mask_col, gains, proj, up, down, outer), raw=(3, 4, 5, 6, 7), late=(4, 5, 6), us=6)


def single_every(n, rows, where, ga, gb, gains, proj, up, down, deps=()):
    width, wide = up.shape
    tokens = 4 * L
    half = ga.shape[0]

    def kernel(
        moves, where, ga, gb, gains, proj, up, down,
        x_all, cot_all, xs, qkv, gm, probs, slope, first_out, second_out, held,
    ):
        arrive, leave = moves
        core = where[3] % 2
        for k in range(half):
            held[2 * k + core] = ga[k]
            held[2 * k + 1 - core] = gb[k]
        g = f32(gains[...])
        x16 = held[:, 0:rows, :].reshape(tokens, width)
        x_all[...] = x16
        cot_all[...] = held[:, rows : 2 * rows, :].reshape(tokens, width)
        leave(0)
        leave(1)
        x = f32(x16)
        sn = b16(norm_rows16(x)[0] * g[0:1])
        xs[:, 0:width] = sn
        arrive(4)
        qkv[:, 0:width] = b16(dot(sn, proj[0]) * 0.125)
        qkv[:, width : 2 * width] = b16(dot(sn, proj[1]))
        qkv[:, 2 * width : 3 * width] = b16(dot(sn, proj[2]))
        leave(3)
        gate = sig(dot(sn, proj[3]))
        gm[:, 0:width] = b16(gate)

        def body(crop):
            own = pl.ds(pl.multiple_of(crop * L, L), L)
            part = pl.ds(crop * n, n)
            for t in range(4):
                q = qkv[own, t * L : (t + 1) * L]
                k = qkv[own, width + t * L : width + (t + 1) * L]
                v = qkv[own, 2 * width + t * L : 2 * width + (t + 1) * L]
                bias = [
                    f32(
                        held[
                            part,
                            rows * (2 + h // 4) : rows * (3 + h // 4),
                            (h % 4) * L : (h % 4 + 1) * L,
                        ].reshape(L, L)
                    )
                    for h in (2 * t, 2 * t + 1)
                ]
                p = pair_weights(q, k, *bias)
                for m in range(2):
                    at = pl.multiple_of((crop * 8 + 2 * t + m) * L, L)
                    probs[pl.ds(at, L), :] = p[m]
                mixed = dot(jnp.concatenate(p, 1), on_halves(v))
                gm[own, width + t * L : width + (t + 1) * L] = b16(mixed)

        each_row(4, body)
        leave(5)
        leave(4)
        u = b16(f32(gm[:, width : 2 * width]) * f32(gm[:, 0:width]))
        xs[:, width : 2 * width] = u
        first = x + dot(u, proj[4])
        first_out[...] = first
        leave(7)
        x1 = b16(norm_rows16(first)[0] * g[1:2])
        xs[:, 2 * width : 3 * width] = x1
        arrive(5)
        total = first
        arrive(6)
        for m in range(wide // width):
            s = slice(m * width, (m + 1) * width)
            hid, slp = gelu_parts(dot(x1, up[:, s]))
            h16 = b16(hid)
            xs[:, (3 + m) * width : (4 + m) * width] = h16
            slope[:, s] = b16(slp)
            total = total + dot(h16, down[s])
        second_out[...] = total

    return call(
        kernel,
        [
            ((tokens, width), BF), ((tokens, width), BF), ((tokens, 3 * width + wide), BF),
            ((tokens, 3 * width), BF), ((tokens, 2 * width), BF), ((4 * 8 * L, L), BF),
            ((tokens, wide), BF), ((tokens, width), F32), ((tokens, width), F32),
        ],
        [((2 * half, 4 * rows, width), BF)],
        (where, ga, gb, gains, proj, up, down),
        deps=deps, raw=(1, 2, 3, 4, 5, 6), late=(4, 5, 6), far=(0, 1, 2, 3, 4, 5, 6, 7, 8), us=19)


def single_back(members, rows, where, ea, eb, kept, gains, proj, up, down, outer, deps=()):
    width, wide = up.shape
    tokens = 4 * L
    x_all, cot_all, _, qkv, gm, probs, slope, first_in, second_in = kept

    def kernel(
        moves, where, ea, eb, x_all, cot_all, qkv, gm, probs, slope, first_in, second_in,
        gains, proj, up, down, outer,
        ys, gain_grad, d_own, drb, m_op,
        dlr, o_do, sdrb, sds, srow,
    ):
        arrive, _ = moves
        g = f32(gains[...])
        for crop in range(4):
            total = f32(ea[members[crop][0]]) + f32(eb[members[crop][0]])
            for k in members[crop][1:]:
                total = total + (f32(ea[k]) + f32(eb[k]))
            total = jnp.concatenate([total, jnp.zeros_like(total)], 0)
            dlr[crop * L : (crop + 1) * L] = b16(total.T)
        x2, sc2 = norm_rows16(second_in[...])
        m_op[...] = dot_tn(b16(x2 * g[2:3]), dlr[...])
        dx = dot_nt(dlr[...], outer[...])
        gain_grad[2:3] = jnp.sum(dx * x2, 0, keepdims=True)
        ds2 = f32(cot_all[...]) + norm_rows16_back(dx * g[2:3], x2, sc2)
        ds2_16 = b16(ds2)
        ys[:, 5 * width + wide :] = ds2_16
        for k in (14, 8, 13, 9):
            arrive(k)
        dx = jnp.zeros((tokens, width), F32)
        for m in range(wide // width):
            s = slice(m * width, (m + 1) * width)
            dhp = b16(dot_nt(ds2_16, down[s]) * f32(slope[:, s]))
            ys[:, (5 + m) * width : (6 + m) * width] = dhp
            dx = dx + dot_nt(dhp, up[:, s])
        x1, sc1 = norm_rows16(first_in[...])
        gain_grad[1:2] = jnp.sum(dx * x1, 0, keepdims=True)
        df = ds2 + norm_rows16_back(dx * g[1:2], x1, sc1)
        sds[...] = df
        df16 = b16(df)
        ys[:, 4 * width : 5 * width] = df16
        for k in (12, 6, 5, 7):
            arrive(k)
        du = dot_nt(df16, proj[4])
        gate, mixed = f32(gm[:, 0:width]), f32(gm[:, width : 2 * width])
        do = du * gate
        o_do[...] = b16(do)
        srow[...] = do * mixed
        ys[:, 3 * width : 4 * width] = b16(du * mixed * gate * (1.0 - gate))
        lane = lax.broadcasted_iota(jnp.int32, (1, L), 1)
        low = jnp.where(lane < L // 2, 1.0, 0.0)

        def body(crop):
            own = pl.ds(pl.multiple_of(crop * L, L), L)
            for t in range(4):
                s = slice(t * L, (t + 1) * L)
                q = qkv[own, t * L : (t + 1) * L]
                k = qkv[own, width + t * L : width + (t + 1) * L]
                v = qkv[own, 2 * width + t * L : 2 * width + (t + 1) * L]
                do16, row = o_do[own, s], srow[own, s]
                grads, weights = [], []
                for j, (m, mf) in enumerate(zip(halves(), (low, 1.0 - low))):
                    at = pl.multiple_of((crop * 8 + 2 * t + j) * L, L)
                    p16 = probs[pl.ds(at, L), :]
                    dp = dot_nt(do16 * m, v)
                    e = f32(p16) * (dp - jnp.sum(row * mf, -1, keepdims=True))
                    sdrb[pl.ds(at, L), :] = e
                    grads.append(b16(e))
                    weights.append(p16)
                dq = dot(jnp.concatenate(grads, 1), on_halves(k)) * 0.125
                dk = dot_tn(jnp.concatenate(grads, 0), on_halves(q))
                dv = dot_tn(jnp.concatenate(weights, 0), on_halves(do16))
                ys[own, t * L : (t + 1) * L] = b16(dq)
                ys[own, width + t * L : width + (t + 1) * L] = b16(dk)
                ys[own, 2 * width + t * L : 2 * width + (t + 1) * L] = b16(dv)

        each_row(4, body)
        dx = dot_nt(ys[:, 0:width], proj[0])
        for k in range(1, 4):
            dx = dx + dot_nt(ys[:, k * width : (k + 1) * width], proj[k])
        x0, sc0 = norm_rows16(f32(x_all[...]))
        gain_grad[0:1] = jnp.sum(dx * x0, 0, keepdims=True)
        sds[...] = sds[...] + norm_rows16_back(dx * g[0:1], x0, sc0)
        grp, row = where[2], where[3]
        d_own[...] = sds[pl.ds(pl.multiple_of(grp * L + row * rows, rows), rows), :]
        for h in range(8):
            at = pl.multiple_of((grp * 8 + h) * L + row * rows, rows)
            drb[h * rows : (h + 1) * rows] = sdrb[pl.ds(at, rows), :]

    return call(
        kernel,
        [
            ((tokens, 6 * width + wide), BF), ((3, width), F32), ((rows, width), F32),
            ((8 * rows, L), F32), ((width, L), F32),
        ],
        [
            ((tokens, L), BF), ((tokens, width), BF), ((4 * 8 * L, L), F32), ((tokens, width), F32),
            ((tokens, width), F32),
        ],
        (
            where, ea, eb, x_all, cot_all, qkv, gm, probs, slope, first_in, second_in,
            gains, proj, up, down, outer,
        ), deps=deps, raw=(10, 15, 4, 11, 14, 8, 13, 9, 12, 6, 5, 7, 3), late=(5, 6, 7, 8, 9, 12, 13, 14), far=(0, 1, 2, 3, 4), us=22)


def weight_grads(xs, ys, width, wide, after):
    tokens = xs.shape[0]
    blocks = wide // width

    def kernel(x, y, after, out):
        out[...] = dot_tn(x[...], y[...]).reshape(out.shape)

    def run(steps, x_at, y_at, shape, block, out_at):
        return pl.pallas_call(
            kernel,
            grid=(steps,),
            out_shape=pltpu.HBM(shape, F32),
            in_specs=[
                pl.BlockSpec((tokens, width), x_at),
                pl.BlockSpec((tokens, width), y_at),
                pl.BlockSpec(memory_space=pl.ANY),
            ],
            out_specs=pl.BlockSpec(block, out_at),
            compiler_params=pltpu.CompilerParams(vmem_limit_bytes=32 << 20),
            cost_estimate=pl.CostEstimate(
                flops=2 * 10**9,
                bytes_accessed=steps * width * width * 8,
                transcendentals=0,
            ),
        )(
            pltpu.with_memory_space_constraint(xs, pltpu.HBM),
            pltpu.with_memory_space_constraint(ys, pltpu.HBM),
            pltpu.with_memory_space_constraint(after, pltpu.HBM),
        )

    proj = run(
        5, lambda i: (0, i // 4), lambda i: (0, i), (5, width, width), (1, width, width),
        lambda i: (i, 0, 0),
    )
    up = run(
        blocks, lambda i: (0, 2), lambda i: (0, 5 + i), (width, wide), (width, width),
        lambda i: (0, i),
    )
    down = run(
        blocks, lambda i: (0, 3 + i), lambda i: (0, 5 + blocks), (wide, width), (width, width),
        lambda i: (i, 0),
    )
    return proj, up, down


def project_pair(z, r, rows, m5t, pmask, sa, sb):
    xh, _ = norm_cols(z)
    p = dot(m5t[0:512], b16(xh))
    mk = get_rows(pmask, r, 1, 1)
    put_rows(sa, r, C, rows, sig(p[0:C]) * p[C : 2 * C] * mk)
    put_rows(sb, r, C, rows, sig(p[2 * C : 3 * C]) * p[3 * C : 4 * C] * mk)


def put_pair(n, ab, sa, sb):
    part = sa.shape[0] // n
    for d in range(n):
        ab[d, 0:part] = b16(sa[d * part : (d + 1) * part])
        ab[d, part : 2 * part] = b16(sb[d * part : (d + 1) * part])


def gated_product(z, r, rows, gatet, mot, sp):
    xh, _ = norm_cols(z)
    gate = sig(dot(gatet[...], b16(xh)))
    ph, _ = norm_cols(get_rows(sp, r, C, rows))
    return z + dot(mot[...], b16(ph)) * gate


def front(n, rows, where, lr_all, pair, outer_w, m5ts, deps=()):
    opm = outer_w.shape[0]

    def kernel(
        where, lr_all, pair, outer_w, m5ts,
        z1, ab, pmask, key_row, inner, lrt, left_own, sa, sb, slr, spm,
    ):
        m5t = m5ts.at[0]
        crop, block = where[0], where[1]
        lr16 = lr_all[pl.ds(crop * n, n)].reshape(L, C)
        lr = f32(lr16)
        turned = lr.T
        lrt[...] = turned
        mrow = turned[2 * opm : 2 * opm + 1]
        key_row[...] = (mrow - 1.0) * MASKED
        first = pl.multiple_of(block * rows, rows)
        spm[...] = jnp.broadcast_to(mrow, (L, L)).T * mrow
        pmask[...] = spm[pl.ds(first, rows), :]
        slr[...] = lr
        left = b16(slr[pl.ds(first, rows), :])
        left_own[...] = left
        inners = dot(left[:, 0:opm], side([outer_w[b] for b in range(opm)]))
        for b in range(opm):
            inner[b * rows : (b + 1) * rows] = lanes(inners, b)
        edge = jnp.zeros((opm, C), BF)

        def body(r):
            parts = []
            for u in range(U):
                mine = b16(inner[pl.ds(r * U + u, opm, stride=rows), :])
                mine = jnp.concatenate([edge, mine, edge, edge], 0)
                parts.append((f32(pair[r * U + u]) + dot(lr16, mine)).T)
            z = side(parts)
            z1[:, cols(r)] = z
            project_pair(z, r, rows, m5t, pmask, sa, sb)

        each_row(rows // U, body)
        put_pair(n, ab, sa, sb)

    part = C * rows // n
    return call(
        kernel,
        [
            ((C, rows * L), F32), ((n, 2 * part, L), BF), ((rows, L), F32), ((1, L), F32),
            ((opm * rows, C), F32), ((C, L), F32), ((rows, C), BF),
        ],
        [((C * rows, L), F32)] * 2 + [((L, C), F32), ((L, L), F32)],
        (where, lr_all, pair, outer_w, m5ts), deps=deps, raw=(2, 3, 4), far=(0, 2, 3, 4, 5, 6), us=5)


def middle(n, rows, z1, prod, mots, pmask, m5ts, deps=()):
    def kernel(z1, prod, mots, pmask, m5ts, z2, ab, sa, sb, sp):
        gatet, mot, m5t = m5ts.at[0, 512:640], mots.at[0], m5ts.at[1]
        sp[...] = f32(prod[...])

        def body(r):
            z = gated_product(z1[:, cols(r)], r, rows, gatet, mot, sp)
            z2[:, cols(r)] = z
            project_pair(z, r, rows, m5t, pmask, sa, sb)

        each_row(rows // U, body)
        put_pair(n, ab, sa, sb)

    part = C * rows // n
    return call(
        kernel,
        [((C, rows * L), F32), ((n, 2 * part, L), BF)],
        [((C * rows, L), F32)] * 3,
        (z1, prod, mots, pmask, m5ts), deps=deps, raw=(0, 2, 3, 4), far=(0,), us=4)


def start_front(n, rows, z2, prod, m5ts, mots, abts, deps=()):
    def kernel(z2, prod, m5ts, mots, abts, z3, tb, sp, st):
        gatet, mot, abt = m5ts.at[1, 512:640], mots.at[1], abts.at[0]
        sp[...] = f32(prod[...])

        def body(r):
            z = gated_product(z2[:, cols(r)], r, rows, gatet, mot, sp)
            z3[:, cols(r)] = z
            xh, _ = norm_cols(z)
            put_rows(st, r, HPAD, rows, dot(abt[...], b16(xh)))

        each_row(rows // U, body)
        for d in range(n):
            tb[d] = b16(st[0 : TH * rows])

    return call(
        kernel,
        [((C, rows * L), F32), ((n, TH * rows, L), BF)],
        [((C * rows, L), F32), ((HPAD * rows, L), F32)],
        (z2, prod, m5ts, mots, abts), deps=deps, raw=(0, 2, 3, 4), far=(0,), us=4)


def channel_product(n, rows, outgoing, ab):
    def kernel(ab, out):
        part = C * rows // n
        for ch in range(C // n):
            a = ab[:, ch * rows : (ch + 1) * rows, :].reshape(L, L)
            b = ab[:, part + ch * rows : part + (ch + 1) * rows, :].reshape(L, L)
            prod = dot_nt(a, b) if outgoing else dot_tn(a, b)
            out[:, ch * rows : (ch + 1) * rows, :] = b16(prod).reshape(n, rows, L)

    return call(kernel, [((n, C * rows // n, L), BF)], [], (ab,), us=1)[0]


def channel_product_back(n, rows, outgoing, ab, dprod, deps=()):
    def kernel(ab, dprod, out):
        part = C * rows // n
        for ch in range(C // n):
            low, high = ch * rows, (ch + 1) * rows
            a = ab[:, low:high, :].reshape(L, L)
            b = ab[:, part + low : part + high, :].reshape(L, L)
            g = dprod[:, low:high, :].reshape(L, L)
            if outgoing:
                da, db = dot(g, b), dot_tn(g, a)
            else:
                da, db = dot_nt(b, g), dot(a, g)
            out[:, low:high, :] = b16(da).reshape(n, rows, L)
            out[:, part + low : part + high, :] = b16(db).reshape(n, rows, L)

    return call(kernel, [((n, 2 * C * rows // n, L), BF)], [], (ab, dprod), deps=deps, us=2)[0]


def head_masks():
    lane = lax.broadcasted_iota(jnp.int32, (1, C), 1)
    return [b16(jnp.where((lane >= h * HD) & (lane < (h + 1) * HD), 1.0, 0.0)) for h in range(TH)]


def by_head(x):
    pm = b16(x.T)
    return jnp.concatenate([pm * m for m in head_masks()], 0)


def attend(x16, a4t, bias):
    p4 = dot(a4t[...], x16)
    gate = sig(p4[3 * C : 4 * C])
    each, mixed = [], []
    for u in range(U):
        q, k, v = (lanes(p4[m * C : (m + 1) * C], u) for m in range(3))
        logits = dot(by_head(k), b16(q)) + bias[...]
        raised, outs = [], []
        v16 = b16(v)
        for h in range(TH):
            s = logits[h * L : (h + 1) * L]
            e = jnp.exp(s - jnp.max(s, 0, keepdims=True))
            inv = 1.0 / jnp.sum(e, 0, keepdims=True)
            raised.append((e, inv))
            outs.append(dot(v16[h * HD : (h + 1) * HD], b16(e)) * inv)
        each.append((q, k, v, raised))
        mixed.append(jnp.concatenate(outs, 0))
    return each, gate, side(mixed)


def attend_back(state, dy16, ao, dbias):
    each, gate, mixed = state
    du = dot(ao[...], dy16)
    do = du * gate
    dgate = du * mixed * gate * (1.0 - gate)
    both = do * mixed
    parts = []
    for u in range(U):
        q, k, v, raised = each[u]
        do16, q16, k16 = b16(lanes(do, u)), b16(q), b16(k)
        dp = dot(by_head(v), do16)
        row = lanes(both, u)
        dq, dk, dv = [], [], []
        for h in range(TH):
            s = slice(h * HD, (h + 1) * HD)
            w = slice(h * L, (h + 1) * L)
            e, inv = raised[h]
            p = e * inv
            ds = p * (dp[w] - jnp.sum(row[s], 0, keepdims=True))
            dbias[w, :] += ds
            ds16, p16 = b16(ds), b16(p)
            dv.append(dot_nt(do16[s], p16))
            dq.append(dot(k16[s], ds16))
            dk.append(dot_nt(q16[s], ds16))
        parts.append(jnp.concatenate([b16(x) for x in dq + dk + dv], 0))
    return jnp.concatenate([side(parts), b16(dgate)], 0)


def start_attention(n, rows, z3, tb_all, key_row, a4ts, aots, abts, deps=()):
    def kernel(z3, tb_all, key_row, a4ts, aots, abts, z4, send, bias, st, se):
        a4t, aot, abt = a4ts.at[0], aots.at[0], abts.at[1]
        for h in range(TH):
            b = f32(tb_all[:, h * rows : (h + 1) * rows, :].reshape(L, L)) + key_row[...]
            bias[h * L : (h + 1) * L, :] = b.T

        def body(r):
            z = z3[:, cols(r)]
            xh, _ = norm_cols(z)
            _, gate, mixed = attend(b16(xh), a4t, bias)
            z = z + dot(aot[...], b16(mixed * gate))
            z4[:, cols(r)] = z
            put_turned(st, r, rows, z)
            xe, _ = norm_cols(z)
            put_rows(se, r, HPAD, rows, dot(abt[...], b16(xe)))

        each_row(rows // U, body)
        part = L * rows // n
        for d in range(n):
            send[d, 0:part] = b16(st[d * part : (d + 1) * part])
            send[d, part : part + TH * rows] = b16(se[0 : TH * rows])

    part = L * rows // n
    return call(
        kernel,
        [((C, rows * L), F32), ((n, part + TH * rows, L), BF)],
        [((TH * L, L), F32), ((L * rows, C), F32), ((HPAD * rows, L), F32)],
        (z3, tb_all, key_row, a4ts, aots, abts), deps=deps, raw=(0, 2, 3, 4, 5), far=(0,), us=12)


def end_both(n, rows, where, recv, cots, key_row, a4ts, a4s, aots, aos, upt, up, dnt, dn, deps=()):
    part = L * rows // n

    def kernel(where, recv, *refs):
        cots, refs = refs[:n], refs[n:]
        run(where, recv, cots, *refs)

    def run(
        where, recv, cots, key_row, a4ts, a4s, aots, aos, upt, up, dnt, dn,
        p0, p1, p2, p3, p4, p5, p6, p7, send, m_up, m_dn, m_a4, m_ao,
        bias, dbias, scot, sout, sdz, o_h, o_dh, o_x5, o_cot, o_x4, o_d4, o_u, o_dy,
    ):
        a4t, a4, aot, ao = a4ts.at[1], a4s.at[1], aots.at[1], aos.at[1]
        kb = jnp.broadcast_to(key_row[...], (L, L)).T
        for h in range(TH):
            b = recv[:, part + h * rows : part + (h + 1) * rows, :].reshape(L, L)
            bias[h * L : (h + 1) * L, :] = f32(b) + kb
        dbias[...] = jnp.zeros_like(dbias)
        for k in range(n):
            block = lax.rem(where[1] + n - k, n)
            scot[pl.ds(pl.multiple_of(block * part, part), part), :] = f32(cots[k][...])

        def body(r):
            w = cols(r)
            z4 = get_turned(recv, r, rows)
            x4, scale4 = norm_cols(z4)
            x16 = b16(x4)
            state = attend(x16, a4t, bias)
            gated = b16(state[2] * state[1])
            z5 = z4 + dot(aot[...], gated)
            x5, scale5 = norm_cols(z5)
            x516 = b16(x5)
            hid, slope = gelu_parts(dot(upt[...], x516))
            h16 = b16(hid)
            z6 = z5 + dot(dnt[...], h16)
            put_turned(sout, r, rows, z6)
            dz6 = side([scot[pl.ds(r * U + u, L, stride=rows), :].T for u in range(U)])
            c16 = b16(dz6)
            dh16 = b16(dot(dn[...], c16) * slope)
            dz5 = dz6 + norm_cols_back(dot(up[...], dh16), x5, scale5)
            dy16 = b16(dz5)
            d4 = attend_back(state, dy16, ao, dbias)
            dz4 = dz5 + norm_cols_back(dot(a4[...], d4), x4, scale4)
            put_turned(sdz, r, rows, dz4)
            o_h[:, w] = h16
            o_dh[:, w] = dh16
            o_x5[:, w] = x516
            o_cot[:, w] = c16
            o_x4[:, w] = x16
            o_d4[:, w] = d4
            o_u[:, w] = gated
            o_dy[:, w] = dy16

        each_row(rows // U, body)
        for d in range(n):
            send[d, 0:part] = b16(sdz[d * part : (d + 1) * part])
            for h in range(TH):
                send[d, part + h * rows : part + (h + 1) * rows] = b16(
                    dbias[h * L + d * rows : h * L + (d + 1) * rows]
                )
        for k, pout in enumerate((p0, p1, p2, p3, p4, p5, p6, p7)):
            block = lax.rem(where[1] + k, n)
            pout[...] = b16(sout[pl.ds(pl.multiple_of(block * part, part), part), :])
        for k in range(4):
            s = slice(k * C, (k + 1) * C)
            m_up[s] = dot_nt(o_x5[...], o_dh[s])
            m_a4[s] = dot_nt(o_x4[...], o_d4[s])
        m_dn[...] = dot_nt(o_h[...], o_cot[...])
        m_ao[...] = dot_nt(o_u[...], o_dy[...])

    wide = rows * L
    return call(
        kernel,
        [
            *[((part, C), BF)] * n, ((n, part + TH * rows, L), BF),
            ((512, C), F32), ((512, C), F32), ((512, C), F32), ((C, C), F32),
        ],
        [
            ((TH * L, L), F32), ((TH * L, L), F32), ((L * rows, C), F32), ((L * rows, C), F32),
            ((L * rows, C), F32),
            ((512, wide), BF), ((512, wide), BF), ((C, wide), BF), ((C, wide), BF),
            ((C, wide), BF), ((512, wide), BF), ((C, wide), BF), ((C, wide), BF),
        ],
        (where, recv, *cots, key_row, a4ts, a4s, aots, aos, upt, up, dnt, dn),
        deps=deps,
        raw=tuple(range(2, n + 11)),
        far=(0, 1, 2, 3, 4, 5, 6, 7, 9, 10, 11, 12),
        step=8, us=18,
    )


def start_back(n, rows, z3, z4, recv, tb_all, key_row, a4ts, a4s, aos, abts, deps=()):
    part = L * rows // n

    def kernel(
        z3, z4, recv, tb_all, key_row, a4ts, a4s, aos, abts,
        dz4_out, dxs, dtb, m_a4, m_ao, m_ab,
        bias, dbias, seb, o_x3, o_d4, o_u, o_dy, o_x4, o_eb,
    ):
        a4t, a4, ao, abt = a4ts.at[0], a4s.at[0], aos.at[0], abts.at[1]
        for h in range(TH):
            b = f32(tb_all[:, h * rows : (h + 1) * rows, :].reshape(L, L)) + key_row[...]
            bias[h * L : (h + 1) * L, :] = b.T
        dbias[...] = jnp.zeros_like(dbias)
        seb[...] = jnp.zeros_like(seb)
        total = f32(recv[0, part : part + TH * rows])
        for d in range(1, n):
            total = total + f32(recv[d, part : part + TH * rows])
        seb[0 : TH * rows, :] = total

        def body(r):
            w = cols(r)
            x4, scale4 = norm_cols(z4[:, w])
            eb16 = b16(get_rows(seb, r, HPAD, rows))
            dz4 = get_turned(recv, r, rows)
            dz4 = dz4 + norm_cols_back(dot_tn(abt[...], eb16), x4, scale4)
            dz4_out[:, w] = dz4
            x3, _ = norm_cols(z3[:, w])
            x16 = b16(x3)
            state = attend(x16, a4t, bias)
            dy16 = b16(dz4)
            d4 = attend_back(state, dy16, ao, dbias)
            dxs[:, w] = dot(a4[...], d4)
            o_x3[:, w] = x16
            o_d4[:, w] = d4
            o_u[:, w] = b16(state[2] * state[1])
            o_dy[:, w] = dy16
            o_x4[:, w] = b16(x4)
            o_eb[:, w] = eb16

        each_row(rows // U, body)
        for h in range(TH):
            turned = b16(dbias[h * L : (h + 1) * L, :].T)
            for d in range(n):
                dtb[d, h * rows : (h + 1) * rows] = turned[d * rows : (d + 1) * rows]
        for k in range(4):
            s = slice(k * C, (k + 1) * C)
            m_a4[s] = dot_nt(o_x3[...], o_d4[s])
        m_ao[...] = dot_nt(o_u[...], o_dy[...])
        m_ab[...] = dot_nt(o_eb[...], o_x4[...])

    wide = rows * L
    return call(
        kernel,
        [
            ((C, wide), F32), ((C, wide), F32), ((n, TH * rows, L), BF),
            ((512, C), F32), ((C, C), F32), ((HPAD, C), F32),
        ],
        [
            ((TH * L, L), F32), ((TH * L, L), F32), ((HPAD * rows, L), F32),
            ((C, wide), BF), ((512, wide), BF), ((C, wide), BF), ((C, wide), BF),
            ((C, wide), BF), ((HPAD, wide), BF),
        ],
        (z3, z4, recv, tb_all, key_row, a4ts, a4s, aos, abts),
        deps=deps, raw=(0, 1, 3, 4, 5, 6, 7, 8), far=(0, 1, 3, 4, 5), us=20)


def product_back(z, dz, r, rows, sp, gatet, mot, mof, sdp, dgp_out, o_ph, o_do):
    w = cols(r)
    xh, _ = norm_cols(z)
    gate = sig(dot(gatet[...], b16(xh)))
    ph, scale = norm_cols(get_rows(sp, r, C, rows))
    ph16 = b16(ph)
    out = dot(mot[...], ph16)
    dgp_out[:, w] = b16(dz * out * gate * (1.0 - gate))
    do16 = b16(dz * gate)
    put_rows(sdp, r, C, rows, norm_cols_back(dot(mof[...], do16), ph, scale))
    o_ph[:, w] = ph16
    o_do[:, w] = do16


def third_back(n, rows, z3, dz4, dxs, recv, abts, z2, prod, m5ts, mots, mofs, deps=()):
    def kernel(
        z3, dz4, dxs, recv, abts, z2, prod, m5ts, mots, mofs,
        dz3, dgp, dp, m_ab, m_mo,
        stb, sp, sdp, o_x3, o_tb, o_ph, o_do,
    ):
        abt, gatet, mot, mof = abts.at[0], m5ts.at[1, 512:640], mots.at[1], mofs.at[1]
        sp[...] = f32(prod[...])
        stb[...] = jnp.zeros_like(stb)
        total = f32(recv[0])
        for d in range(1, n):
            total = total + f32(recv[d])
        stb[0 : TH * rows, :] = total

        def body(r):
            w = cols(r)
            x3, scale3 = norm_cols(z3[:, w])
            tb16 = b16(get_rows(stb, r, HPAD, rows))
            dx = dxs[:, w] + dot_tn(abt[...], tb16)
            dz = dz4[:, w] + norm_cols_back(dx, x3, scale3)
            dz3[:, w] = dz
            o_x3[:, w] = b16(x3)
            o_tb[:, w] = tb16
            product_back(z2[:, w], dz, r, rows, sp, gatet, mot, mof, sdp, dgp, o_ph, o_do)

        each_row(rows // U, body)
        dp[...] = b16(sdp[...])
        m_ab[...] = dot_nt(o_tb[...], o_x3[...])
        m_mo[...] = dot_nt(o_ph[...], o_do[...])

    wide = rows * L
    return call(
        kernel,
        [
            ((C, wide), F32), ((C, wide), BF), ((C * rows, L), BF),
            ((HPAD, C), F32), ((C, C), F32),
        ],
        [
            ((HPAD * rows, L), F32), ((C * rows, L), F32), ((C * rows, L), F32),
            ((C, wide), BF), ((HPAD, wide), BF), ((C, wide), BF), ((C, wide), BF),
        ],
        (z3, dz4, dxs, recv, abts, z2, prod, m5ts, mots, mofs), deps=deps, raw=(0, 1, 2, 4, 5, 6, 7, 8, 9), far=(0, 1, 3, 4), us=7)


def projections_back(n, rows, z, dz, dgp, r, pmask, m5t, m5, sa, sb, o_x, o_d5):
    w = cols(r)
    xh, scale = norm_cols(z)
    x16 = b16(xh)
    p = dot(m5t[0:512], x16)
    mk = get_rows(pmask, r, 1, 1)
    da = get_rows(sa, r, C, rows) * mk
    db = get_rows(sb, r, C, rows) * mk
    ga, gb = sig(p[0:C]), sig(p[2 * C : 3 * C])
    va, vb = p[C : 2 * C], p[3 * C : 4 * C]
    d5 = jnp.concatenate(
        [
            b16(da * va * ga * (1.0 - ga)),
            b16(da * ga),
            b16(db * vb * gb * (1.0 - gb)),
            b16(db * gb),
            dgp[:, w],
        ],
        0,
    )
    o_x[:, w] = x16
    o_d5[:, w] = d5
    return dz + norm_cols_back(dot(m5[...], d5), xh, scale)


def take_pair(n, dab, sa, sb):
    part = sa.shape[0] // n
    for d in range(n):
        sa[d * part : (d + 1) * part, :] = f32(dab[d, 0:part])
        sb[d * part : (d + 1) * part, :] = f32(dab[d, part : 2 * part])


def second_back(n, rows, z2, dz3, dgp, dab, pmask, m5ts, m5s, z1, prod, mots, mofs, deps=()):
    def kernel(
        z2, dz3, dgp, dab, pmask, m5ts, m5s, z1, prod, mots, mofs,
        dz2, dgp_out, dp, m_m5, m_mo,
        sa, sb, sp, sdp, o_x, o_d5, o_ph, o_do,
    ):
        m5t, m5, gatet = m5ts.at[1], m5s.at[1], m5ts.at[0, 512:640]
        mot, mof = mots.at[0], mofs.at[0]
        sp[...] = f32(prod[...])
        take_pair(n, dab, sa, sb)

        def body(r):
            w = cols(r)
            dz = projections_back(
                n, rows, z2[:, w], dz3[:, w], dgp, r, pmask, m5t, m5, sa, sb, o_x, o_d5
            )
            dz2[:, w] = dz
            product_back(z1[:, w], dz, r, rows, sp, gatet, mot, mof, sdp, dgp_out, o_ph, o_do)

        each_row(rows // U, body)
        dp[...] = b16(sdp[...])
        for k in range(5):
            s = slice(k * C, (k + 1) * C)
            m_m5[s] = dot_nt(o_x[...], o_d5[s])
        m_mo[...] = dot_nt(o_ph[...], o_do[...])

    wide = rows * L
    return call(
        kernel,
        [
            ((C, wide), F32), ((C, wide), BF), ((C * rows, L), BF),
            ((640, C), F32), ((C, C), F32),
        ],
        [
            ((C * rows, L), F32), ((C * rows, L), F32), ((C * rows, L), F32), ((C * rows, L), F32),
            ((C, wide), BF), ((640, wide), BF), ((C, wide), BF), ((C, wide), BF),
        ],
        (z2, dz3, dgp, dab, pmask, m5ts, m5s, z1, prod, mots, mofs), deps=deps, raw=(0, 1, 2, 4, 5, 6, 7, 8, 9, 10), far=(0, 1, 3, 4), us=11)


def first_back(n, rows, copies, where, z1, dz2, dgp, dab, pmask, m5ts, m5s, inner, lrt, left_own, outer_w, deps=()):
    opm = outer_w.shape[0]

    def kernel(
        where, z1, dz2, dgp, dab, pmask, m5ts, m5s, inner, lrt, left_own, outer_w,
        dz1, ends, m_oo, m_m5,
        sa, sb, o_x, o_d5, sdi, sdr,
    ):
        m5t, m5 = m5ts.at[0], m5s.at[0]
        take_pair(n, dab, sa, sb)
        sdr[...] = jnp.zeros_like(sdr)
        right_t = b16(lrt[opm : 2 * opm])

        def body(r):
            w = cols(r)
            dz = projections_back(
                n, rows, z1[:, w], dz2[:, w], dgp, r, pmask, m5t, m5, sa, sb, o_x, o_d5
            )
            for u in range(U):
                dz16 = b16(lanes(dz, u).T)
                dz1[r * U + u] = dz16
                at = pl.ds(r * U + u, opm, stride=rows)
                sdi[at, :] = dot(right_t, dz16)
                sdr[...] += dot_nt(b16(inner[at, :]), dz16)

        each_row(rows // U, body)
        left = left_own[:, 0:opm]
        d16 = side([b16(sdi[b * rows : (b + 1) * rows]) for b in range(opm)])
        outers = dot_tn(left, d16)
        for b in range(opm):
            m_oo[b * opm : (b + 1) * opm] = lanes(outers, b)
        dleft = dot_nt(side([outer_w[b] for b in range(opm)]), d16)
        lane = lax.broadcasted_iota(jnp.int32, (rows, L), 1)
        spot = lax.broadcasted_iota(jnp.int32, (rows, L), 0) + where[1] * rows
        dleft = dot(b16(dleft), b16(jnp.where(lane == spot, 1.0, 0.0)))
        both = jnp.concatenate([dleft, sdr[...]], 0) * lrt[2 * opm : 2 * opm + 1]
        for d in range(copies):
            ends[d] = b16(both)
        for k in range(5):
            s = slice(k * C, (k + 1) * C)
            m_m5[s] = dot_nt(o_x[...], o_d5[s])

    wide = rows * L
    return call(
        kernel,
        [
            ((rows, L, C), BF), ((copies, 2 * opm, L), BF), ((opm * opm, C), F32), ((640, C), F32),
        ],
        [
            ((C * rows, L), F32), ((C * rows, L), F32), ((C, wide), BF), ((640, wide), BF),
            ((opm * rows, C), F32), ((opm, L), F32),
        ],
        (where, z1, dz2, dgp, dab, pmask, m5ts, m5s, inner, lrt, left_own, outer_w), deps=deps, raw=(1, 2, 3, 5, 6, 7, 8, 9, 10, 11), far=(2, 3), us=11)


def last_back(rows, pair, drb, dz1, sbt, deps=()):
    def kernel(pair, drb, dz1, sbt, grad, m_sb, o_x, o_d):
        def body(r):
            w = cols(r)
            xh, scale = norm_cols(side([f32(pair[r * U + u]).T for u in range(U)]))
            d = get_rows(drb, r, 8, rows)
            d16 = b16(jnp.concatenate([d, jnp.zeros_like(d)], 0))
            back = norm_cols_back(dot_tn(sbt[...], d16), xh, scale)
            for u in range(U):
                grad[r * U + u] = f32(dz1[r * U + u]) + lanes(back, u).T
            o_x[:, w] = b16(xh)
            o_d[:, w] = d16

        each_row(rows // U, body)
        m_sb[...] = dot_nt(o_d[...], o_x[...])

    wide = rows * L
    return call(
        kernel,
        [((rows, L, C), F32), ((HPAD, C), F32)],
        [((C, wide), BF), ((HPAD, wide), BF)],
        (pair, drb, dz1, sbt), deps=deps, raw=(0, 1, 2, 3), far=(0,), us=3)


def collect(where, parts, half, deps):
    def kernel(where, *refs):
        sources, (kept, given, rows) = refs[: len(parts)], refs[len(parts) :]
        core = where[3] % 2
        at = 0
        for ref in sources:
            rows[at : at + ref.shape[0]] = ref[...]
            at += ref.shape[0]
        if at < 2 * half:
            rows[at : 2 * half] = jnp.zeros((2 * half - at, C), F32)
        kept[...] = rows[pl.ds(pl.multiple_of(core * half, half), half), :]
        given[...] = b16(rows[pl.ds(pl.multiple_of((1 - core) * half, half), half), :])

    return call(
        kernel,
        [((half, C), F32), ((half, C), BF)],
        [((2 * half, C), F32)],
        (where, *parts),
        deps=deps,
        raw=tuple(range(1, len(parts) + 1)),
        us=0,
    )


def sum_copies(x, extra, count):
    rows, more = x.shape[1], extra.shape[0]

    def kernel(x, extra, out):
        total = b16(jnp.sum(f32(x[...]), 0))
        for d in range(count):
            out[d, 0:rows] = total
            out[d, rows : rows + more] = b16(extra[...])

    return call(kernel, [((count, rows + more, C), BF)], [], (x, extra), us=2)[0]


def finish(where, near, far, gp, gm, mp, mg, mo, ap, ab, pu, sb, places, half, opm, deps):
    def kernel(
        where, near, far, gp, gm, mp, mg, mo, ap, ab, pu, sb,
        g_pg, g_mg, g_sb, g_oo, g_mp, g_mgt, g_mo, g_ap, g_ab, g_ao, g_pu, g_pd,
        rows,
    ):
        core = where[3] % 2
        chips = near.shape[0]
        size = half // chips
        for k in range(chips):
            at = pl.multiple_of(core * half + k * size, 8)
            rows[pl.ds(at, size), :] = f32(near[k, 0:size])
            at = pl.multiple_of((1 - core) * half + k * size, 8)
            rows[pl.ds(at, size), :] = f32(far[k, 0:size])

        def take(name, count, skip=0):
            at = places[name] + skip
            return rows[at : at + count]

        gpv, gmv = f32(gp[...]), f32(gm[...])

        def column(row):
            return jnp.broadcast_to(row, (C, C)).T

        def over_lanes(x):
            return jnp.sum(x.T, 0, keepdims=True)

        def padded(w):
            return jnp.concatenate([f32(w), jnp.zeros((HPAD - w.shape[0], C), F32)], 0)

        total = jnp.zeros((8, C), F32)
        for k in range(chips):
            total = total + (f32(near[k, size : size + 8]) + f32(far[k, size : size + 8]))
        g_pg[0:1] = jnp.sum(f32(sb[...]) * total, 0, keepdims=True)
        g_sb[...] = total * gpv[0:1]
        for t in range(2):
            g = column(gpv[1 + t : 2 + t])
            both = jnp.zeros((C, C), F32)
            for k in range(5):
                m = take("m5%d" % t, C, k * C)
                both = both + m * f32(mp[t, k] if k < 4 else mg[t])
                if k < 4:
                    g_mp[t, k] = m * g
                else:
                    g_mgt[t] = m * g
            g_pg[1 + t : 2 + t] = over_lanes(both)
            m = take("mo%d" % t, C)
            g_mo[t] = m * column(gmv[t : t + 1])
            g_mg[t : t + 1] = over_lanes(m * f32(mo[t]))
            g = column(gpv[3 + t : 4 + t])
            both = jnp.zeros((C, C), F32)
            for k in range(4):
                m = take("a4%d" % t, C, k * C)
                if k == 0:
                    m = m * HD**-0.5
                both = both + m * f32(ap[t, k])
                g_ap[t, k] = m * g
            m = take("ab%d" % t, HPAD)
            g_pg[3 + t : 4 + t] = over_lanes(both) + jnp.sum(padded(ab[t]) * m, 0, keepdims=True)
            g_ab[t] = (m * gpv[3 + t : 4 + t])[0:TH]
            g_ao[t] = take("ao%d" % t, C)
        g = column(gpv[5:6])
        both = jnp.zeros((C, C), F32)
        for k in range(4):
            s = slice(k * C, (k + 1) * C)
            m = take("up", C, k * C)
            both = both + m * f32(pu[:, s])
            g_pu[:, s] = m * g
        g_pg[5:6] = over_lanes(both)
        g_pd[...] = take("dn", 512)
        for b in range(opm):
            g_oo[:, b, :] = take("oo", opm, b * opm)

    outs = [
        (6, C), (2, C), (8, C), (opm, opm, C), (2, 4, C, C), (2, C, C), (2, C, C), (2, 4, C, C),
        (2, TH, C), (2, C, C), (C, 512), (512, C),
    ]
    return call(
        kernel,
        [(s, F32) for s in outs],
        [((2 * half, C), F32)],
        (where, near, far, gp, gm, mp, mg, mo, ap, ab, pu, sb),

        raw=(3, 4, 5, 6, 7, 8, 9, 10, 11), deps=deps, far=tuple(range(12)), us=4,
    )


PRECISE = lax.Precision.HIGHEST


def for_sending(shard):

    def short(part):
        return part.astype(jnp.bfloat16) if part.dtype == jnp.float32 else part

    return jax.tree.map(short, shard)


def widen(operand):
    return operand.astype(jnp.float32)


def narrow(operand):
    return operand.astype(jnp.bfloat16)


def rounded(operand):
    return lax.optimization_barrier(operand.astype(jnp.bfloat16)).astype(jnp.float32)


def contract(pattern, first_term, second_term):
    return jnp.einsum(pattern, first_term, second_term, precision=PRECISE)


def low_product(pattern, first_term, second_term):
    return jnp.einsum(pattern, first_term, second_term, preferred_element_type=jnp.float32)


def norm_rows(operand, gain_vec):
    centre = operand - jnp.mean(operand, -1, keepdims=True)
    spread = jnp.mean(centre * centre, -1, keepdims=True)
    return centre * lax.rsqrt(spread + EPSILON) * gain_vec


def soft_weights(logits):
    highest = jnp.max(logits, -1, keepdims=True)
    raised = jnp.exp(logits - highest)
    return raised / jnp.sum(raised, -1, keepdims=True)


def single_attend(queries, key_rows, values, gate_value, pair_bias, key_bias, weight_out):
    head_count = pair_bias.shape[0]
    feature_width = queries.shape[-1]
    head_size = feature_width // head_count
    query_heads = queries.reshape(queries.shape[0], head_count, head_size)
    key_heads = key_rows.reshape(key_rows.shape[0], head_count, head_size)
    value_heads = values.reshape(values.shape[0], head_count, head_size)
    logits = (
        contract("ihd,jhd->hij", query_heads, key_heads) * head_size ** (-0.5)
        + pair_bias
        + key_bias
    )
    mixed = contract("hij,jhd->ihd", soft_weights(logits), value_heads).reshape(
        queries.shape[0], feature_width
    )
    return contract("is,st->it", mixed * jax.nn.sigmoid(gate_value), weight_out)


def tri_attend(normed, pair_bias, weight_four, weight_out, key_bias):
    head_count = pair_bias.shape[0]
    feature_width = normed.shape[-1]
    head_size = feature_width // head_count

    def one_row(row_in):
        projected = contract("lc,ncd->nld", row_in, weight_four)
        shaped = projected[:3].reshape(3, row_in.shape[0], head_count, head_size)
        logits = (
            contract("jhd,khd->hjk", shaped[0], shaped[1]) * head_size ** (-0.5)
            + pair_bias
            + key_bias
        )
        mixed = contract("hjk,khd->jhd", soft_weights(logits), shaped[2]).reshape(
            row_in.shape[0], feature_width
        )
        return contract("lc,cd->ld", mixed * jax.nn.sigmoid(projected[3]), weight_out)

    return lax.map(jax.checkpoint(one_row), normed)


def mult_front(pair_in, gain_vec, weight_four, weight_gate, pair_mask):
    normed = norm_rows(pair_in, gain_vec)
    projected = contract("rlc,ncm->nmrl", normed, weight_four)
    left_side = jax.nn.sigmoid(projected[0]) * projected[1] * pair_mask
    right_side = jax.nn.sigmoid(projected[2]) * projected[3] * pair_mask
    gate_value = jax.nn.sigmoid(contract("rlc,cd->rld", normed, weight_gate))
    return (left_side, right_side, gate_value)


def mult_back(pair_in, product, gate_value, gain_vec, weight_out):
    centre = product - jnp.mean(product, 0, keepdims=True)
    spread = jnp.mean(centre * centre, 0, keepdims=True)
    scaled = centre * lax.rsqrt(spread + EPSILON) * gain_vec[:, None, None]
    return pair_in + contract("mrl,mc->rlc", scaled, weight_out) * gate_value


def outgoing_forward(left_chan, right_chan):
    return low_product("mik,mjk->mij", left_chan, right_chan)


def outgoing_backward(left_chan, right_chan, grad_out):
    return (
        low_product("mij,mjk->mik", grad_out, right_chan),
        low_product("mij,mik->mjk", grad_out, left_chan),
    )


def incoming_forward(left_chan, right_chan):
    return low_product("mki,mkj->mij", left_chan, right_chan)


def incoming_backward(left_chan, right_chan, grad_out):
    return (
        low_product("mij,mkj->mki", grad_out, right_chan),
        low_product("mij,mki->mkj", grad_out, left_chan),
    )


def to_channels(operand):
    return jax.tree.map(
        lambda part, own: part.astype(own.dtype),
        lax.all_to_all(for_sending(operand), "rows", split_axis=0, concat_axis=1, tiled=True),
        operand,
    )


def to_rows(operand):
    return jax.tree.map(
        lambda part, own: part.astype(own.dtype),
        lax.all_to_all(for_sending(operand), "rows", split_axis=1, concat_axis=0, tiled=True),
        operand,
    )


def turn_cols(operand):
    return jnp.swapaxes(
        lax.all_to_all(operand, "rows", split_axis=1, concat_axis=0, tiled=True), 0, 1
    )


def turn_rows(operand):
    return lax.all_to_all(
        jnp.swapaxes(operand, 0, 1), "rows", split_axis=0, concat_axis=1, tiled=True
    )


def gather_bias(operand):
    return lax.all_gather(operand, "rows", axis=1, tiled=True)


def scatter_bias(operand):
    return lax.psum_scatter(operand, "rows", scatter_dimension=1, tiled=True)


def general_local(
    single_rep,
    pair_rep,
    residue_mask,
    single_gains,
    pair_gains,
    mult_gains,
    single_proj,
    single_bias,
    single_up,
    single_down,
    opm_proj,
    opm_out,
    mult_proj,
    mult_gate,
    mult_out,
    att_proj,
    att_bias,
    att_out,
    pair_up,
    pair_down,
    single_cot,
    pair_cot,
):
    gains_s = widen(single_gains)
    gains_p = widen(pair_gains)
    gains_m = widen(mult_gains)
    proj_s = widen(single_proj)
    bias_sw = widen(single_bias)
    up_s = widen(single_up)
    down_s = widen(single_down)
    proj_o = widen(opm_proj)
    outer_w = widen(opm_out)
    proj_m = widen(mult_proj)
    gate_m = widen(mult_gate)
    out_m = widen(mult_out)
    proj_a = widen(att_proj)
    bias_a = widen(att_bias)
    out_a = widen(att_out)
    up_p = widen(pair_up)
    down_p = widen(pair_down)
    mask_all = widen(residue_mask[0])
    shard_rows = pair_rep.shape[1]
    first_row = lax.axis_index("rows") * shard_rows
    mask_own = lax.dynamic_slice_in_dim(mask_all, first_row, shard_rows, 0)
    key_bias = (mask_all - 1.0) * MASKED
    pair_mask = mask_own[:, None] * mask_all[None, :]
    single_own = widen(single_rep[0])
    pair_own = widen(pair_rep[0])

    def front_single(
        single_in, pair_in, gain_s, gain_z, proj_query, proj_key, proj_value, proj_gate, bias_w
    ):
        normed = norm_rows(single_in, gain_s)
        pair_normed = norm_rows(pair_in, gain_z)
        return (
            contract("rs,st->rt", normed, proj_query),
            contract("rs,st->rt", normed, proj_key),
            contract("rs,st->rt", normed, proj_value),
            contract("rs,st->rt", normed, proj_gate),
            contract("rlc,ch->hrl", pair_normed, bias_w),
        )

    def back_single(
        queries,
        key_rows,
        values,
        gate_value,
        row_bias,
        single_in,
        proj_out,
        gain_t,
        weight_up,
        weight_down,
        gain_o,
        left_w,
        right_w,
    ):
        first_sum = single_in + single_attend(
            queries, key_rows, values, gate_value, row_bias, key_bias, proj_out
        )
        hidden = jax.nn.gelu(contract("rs,st->rt", norm_rows(first_sum, gain_t), weight_up))
        second_sum = first_sum + contract("rt,ts->rs", hidden, weight_down)
        outer_in = norm_rows(second_sum, gain_o)
        left_side = contract("rs,sa->ra", outer_in, left_w) * mask_own[:, None]
        right_side = contract("rs,sa->ra", outer_in, right_w) * mask_own[:, None]
        return (second_sum, left_side, right_side)

    def outer_front(left_side, right_all, pair_in, weight_outer, gain_in, weight_four, weight_gate):
        inner = contract("ia,abc->ibc", left_side, weight_outer)
        updated = pair_in + contract("ibc,jb->ijc", inner, right_all)
        left_m, right_m, gate_value = mult_front(
            updated, gain_in, weight_four, weight_gate, pair_mask
        )
        return (updated, left_m, right_m, gate_value)

    def middle_mult(
        pair_in, product, gate_value, gain_out, weight_out, gain_in, weight_four, weight_gate
    ):
        updated = mult_back(pair_in, product, gate_value, gain_out, weight_out)
        left_m, right_m, gate_next = mult_front(
            updated, gain_in, weight_four, weight_gate, pair_mask
        )
        return (updated, left_m, right_m, gate_next)

    def start_front_general(pair_in, product, gate_value, gain_out, weight_out, gain_start, bias_w):
        updated = mult_back(pair_in, product, gate_value, gain_out, weight_out)
        normed = norm_rows(updated, gain_start)
        return (updated, normed, contract("rlc,ch->hrl", normed, bias_w))

    def start_core(pair_in, normed, bias_all, weight_four, weight_out, gain_end):
        updated = pair_in + tri_attend(normed, bias_all, weight_four, weight_out, key_bias)
        return (updated, norm_rows(updated, gain_end))

    def end_bias(turned, bias_w):
        return contract("rlc,ch->hrl", turned, bias_w)

    def end_core(turned, bias_all, weight_four, weight_out):
        return tri_attend(turned, bias_all, weight_four, weight_out, key_bias)

    def final_pair(pair_in, update, gain_vec, weight_up, weight_down):
        summed = pair_in + update
        hidden = jax.nn.gelu(contract("rlc,cd->rld", norm_rows(summed, gain_vec), weight_up))
        return summed + contract("rld,dc->rlc", hidden, weight_down)

    outs_one, back_one = jax.vjp(
        front_single,
        single_own,
        pair_own,
        gains_s[0],
        gains_p[0],
        proj_s[0],
        proj_s[1],
        proj_s[2],
        proj_s[3],
        bias_sw,
    )
    queries, keys_own, values_own, gate_single, row_bias = outs_one
    keys_all, values_all = (
        lax.all_gather(narrow(keys_own), "rows", axis=0, tiled=True),
        lax.all_gather(narrow(values_own), "rows", axis=0, tiled=True),
    )
    outs_two, back_two = jax.vjp(
        back_single,
        queries,
        widen(keys_all),
        widen(values_all),
        gate_single,
        row_bias,
        single_own,
        proj_s[4],
        gains_s[1],
        up_s,
        down_s,
        gains_s[2],
        proj_o[0],
        proj_o[1],
    )
    single_next, left_outer, right_outer = outs_two
    right_all = widen(lax.all_gather(narrow(right_outer), "rows", axis=0, tiled=True))
    outs_three, back_three = jax.vjp(
        outer_front,
        rounded(left_outer),
        right_all,
        pair_own,
        outer_w,
        gains_p[1],
        proj_m[0],
        gate_m[0],
    )
    pair_one, left_first, right_first, gate_first = outs_three
    chan_left, chan_right = to_channels((narrow(left_first), narrow(right_first)))
    product_one = outgoing_forward(chan_left, chan_right)
    rows_one = widen(to_rows(narrow(product_one)))
    outs_five, back_five = jax.vjp(
        middle_mult,
        pair_one,
        rows_one,
        gate_first,
        gains_m[0],
        out_m[0],
        gains_p[2],
        proj_m[1],
        gate_m[1],
    )
    pair_two, left_second, right_second, gate_second = outs_five
    chan_left_two, chan_right_two = to_channels((narrow(left_second), narrow(right_second)))
    product_two = incoming_forward(chan_left_two, chan_right_two)
    rows_two = widen(to_rows(narrow(product_two)))
    outs_seven, back_seven = jax.vjp(
        start_front_general, pair_two, rows_two, gate_second, gains_m[1], out_m[1], gains_p[3], bias_a[0]
    )
    pair_three, normed_start, bias_start = outs_seven
    bias_start_all = widen(gather_bias(narrow(bias_start)))
    outs_eight, back_eight = jax.vjp(
        start_core, pair_three, normed_start, bias_start_all, proj_a[0], out_a[0], gains_p[4]
    )
    pair_four, normed_end = outs_eight
    turned = widen(turn_cols(narrow(normed_end)))
    bias_end, back_nine = jax.vjp(end_bias, turned, bias_a[1])
    bias_end_all = widen(gather_bias(narrow(bias_end)))
    update_turned, back_ten = jax.vjp(end_core, turned, bias_end_all, proj_a[1], out_a[1])
    update = widen(turn_rows(narrow(update_turned)))
    pair_six, back_eleven = jax.vjp(final_pair, pair_four, update, gains_p[5], up_p, down_p)
    grad_four, grad_update, g_pg5, g_pu, g_pd = back_eleven(widen(pair_cot[0]))
    g_pg5, g_pu, g_pd = (g_pg5, g_pu, g_pd)
    grad_turned_update = widen(turn_cols(narrow(grad_update)))
    grad_turned_a, grad_bias_end_all, g_ap1, g_ao1 = back_ten(grad_turned_update)
    g_ap1, g_ao1 = (g_ap1, g_ao1)
    grad_bias_end = rounded(scatter_bias(grad_bias_end_all))
    grad_turned_b, g_ab1 = back_nine(grad_bias_end)
    grad_normed_end = widen(turn_rows(narrow(grad_turned_a + grad_turned_b)))
    grad_three, grad_normed_start, grad_bias_start_all, g_ap0, g_ao0, g_pg4 = back_eight(
        (grad_four, grad_normed_end)
    )
    g_ap0, g_ao0, g_pg4 = (g_ap0, g_ao0, g_pg4)
    grad_bias_start = rounded(scatter_bias(grad_bias_start_all))
    grad_two, grad_rows_two, grad_gate_second, g_mg1, g_mo1, g_pg3, g_ab0 = back_seven(
        (grad_three, grad_normed_start, grad_bias_start)
    )
    g_mg1, g_mo1, g_pg3, g_ab0 = (g_mg1, g_mo1, g_pg3, g_ab0)
    grad_chan_left_two, grad_chan_right_two = incoming_backward(
        chan_left_two, chan_right_two, to_channels(narrow(grad_rows_two))
    )
    grad_left_second, grad_right_second = to_rows(
        (narrow(grad_chan_left_two), narrow(grad_chan_right_two))
    )
    grad_one, grad_rows_one, grad_gate_first, g_mg0, g_mo0, g_pg2, g_mp1, g_mgt1 = back_five(
        (grad_two, widen(grad_left_second), widen(grad_right_second), grad_gate_second)
    )
    g_mg0, g_mo0, g_pg2, g_mp1, g_mgt1 = (g_mg0, g_mo0, g_pg2, g_mp1, g_mgt1)
    grad_chan_left, grad_chan_right = outgoing_backward(
        chan_left, chan_right, to_channels(narrow(grad_rows_one))
    )
    grad_left_first, grad_right_first = to_rows((narrow(grad_chan_left), narrow(grad_chan_right)))
    grad_left_outer, grad_right_all, grad_pair_a, g_oo, g_pg1, g_mp0, g_mgt0 = back_three(
        (grad_one, widen(grad_left_first), widen(grad_right_first), grad_gate_first)
    )
    g_oo, g_pg1, g_mp0, g_mgt0 = (g_oo, g_pg1, g_mp0, g_mgt0)
    grad_right_outer = rounded(
        lax.psum_scatter(grad_right_all, "rows", scatter_dimension=0, tiled=True)
    )
    two_grads = back_two((widen(single_cot[0]), rounded(grad_left_outer), grad_right_outer))
    grad_query, grad_keys_all, grad_values_all, grad_gate_single, grad_row_bias, grad_single_a = (
        two_grads[:6]
    )
    g_sp4, g_sg1, g_su, g_sd, g_sg2, g_op0, g_op1 = tuple(two_grads[6:])
    grad_keys, grad_values = (
        lax.psum_scatter(grad_keys_all, "rows", scatter_dimension=0, tiled=True),
        lax.psum_scatter(grad_values_all, "rows", scatter_dimension=0, tiled=True),
    )
    grad_single_b, grad_pair_b, g_sg0, g_pg0, g_sp0, g_sp1, g_sp2, g_sp3, g_sb = back_one(
        (grad_query, rounded(grad_keys), rounded(grad_values), grad_gate_single, grad_row_bias)
    )
    g_sg0, g_pg0, g_sp0, g_sp1, g_sp2, g_sp3, g_sb = (
        g_sg0,
        g_pg0,
        g_sp0,
        g_sp1,
        g_sp2,
        g_sp3,
        g_sb,
    )
    weight_totals = (
        jnp.stack([g_sg0, g_sg1, g_sg2]),
        jnp.stack([g_pg0, g_pg1, g_pg2, g_pg3, g_pg4, g_pg5]),
        jnp.stack([g_mg0, g_mg1]),
        jnp.stack([g_sp0, g_sp1, g_sp2, g_sp3, g_sp4]),
        g_sb,
        g_su,
        g_sd,
        jnp.stack([g_op0, g_op1]),
        g_oo,
        jnp.stack([g_mp0, g_mp1]),
        jnp.stack([g_mgt0, g_mgt1]),
        jnp.stack([g_mo0, g_mo1]),
        jnp.stack([g_ap0, g_ap1]),
        jnp.stack([g_ab0, g_ab1]),
        jnp.stack([g_ao0, g_ao1]),
        g_pu,
        g_pd,
    )
    weight_totals = lax.psum(
        (
            weight_totals[0],
            weight_totals[1],
            weight_totals[2],
            weight_totals[3],
            weight_totals[4],
            weight_totals[5],
            weight_totals[6],
            weight_totals[7],
            weight_totals[8],
            weight_totals[9],
            weight_totals[10],
            weight_totals[11],
            weight_totals[12],
            weight_totals[13],
            weight_totals[14],
            weight_totals[15],
            weight_totals[16],
        ),
        ("grp", "rows"),
    )
    return (
        narrow(single_next)[None],
        narrow(pair_six)[None],
        (grad_single_a + grad_single_b)[None],
        (grad_pair_a + grad_pair_b)[None],
    ) + tuple(weight_totals)


def pad_rows(x, count):
    return jnp.concatenate([x, jnp.zeros((count - x.shape[0],) + x.shape[1:], x.dtype)], 0)


def fast_local(square, row_count):
    n = row_count
    rows = L // n
    part = L * rows // n
    crops = 4
    total = crops * n

    def home(g, r):
        if square:
            x, z = g % 2, r // 2
            near = 3 - z if x else z
            side_of, level = ((x, 0), (1 - x, 1), (x, 1), (1 - x, 0))[near]
            g, r = g - x + side_of, (3 - level if x else level) * 2 + r % 2
        return g * n + r

    groups = [[home(g, r) for r in range(n)] for g in range(crops)]

    def swap(x, back=False):
        if not square:
            return x
        pairs = [(g * n + r, home(g, r)) for g in range(crops) for r in range(n)]
        return lax.ppermute(x, AX, [(b, a) for a, b in pairs] if back else pairs)

    def to_home(k, x):
        pairs = [(g * n + r, home(g, (r + k) % n)) for g in range(crops) for r in range(n)]
        return lax.ppermute(x, AX, pairs)

    def from_home(k, x):
        pairs = [(home(g, r), g * n + (r + k) % n) for g in range(crops) for r in range(n)]
        return lax.ppermute(x, AX, pairs)

    def exchange(x):
        if square:
            return lax.all_to_all(x, AX, 0, 0, tiled=True, axis_index_groups=groups)
        return lax.all_to_all(x, "rows", 0, 0, tiled=True)

    def to_all(copies):
        return lax.all_to_all(copies, AX, 0, 0, tiled=True)

    chips = total // 2
    same_core = [[g * n + z * 2 + c for g in range(crops) for z in range(n // 2)] for c in range(2)]
    members = [sorted(set(d // 2 for d in group)) for group in groups]

    def other_core(x):
        return lax.ppermute(x, "rows", [(i, i ^ 1) for i in range(n)])

    def to_chips(copies):
        return lax.all_to_all(copies, AX, 0, 0, tiled=True, axis_index_groups=same_core)

    def local(
        single_rep, pair_rep, residue_mask, single_gains, pair_gains, mult_gains, single_proj,
        single_bias, single_up, single_down, opm_proj, opm_out, mult_proj, mult_gate, mult_out,
        att_proj, att_bias, att_out, pair_up, pair_down, single_cot, pair_cot,
    ):
        grp, row = lax.axis_index("grp"), lax.axis_index("rows")
        crop, block = grp, row
        if square:
            half = row // 4
            level = jnp.where(half == 1, 3 - row // 2, row // 2)
            near = jnp.where(grp % 2 == half, 2 * level, 3 - 2 * level)
            crop = grp - grp % 2 + half
            block = jnp.where(half == 1, 3 - near, near) * 2 + row % 2
        where = jnp.stack([crop, block, grp, row]).astype(jnp.int32)
        single, width = single_rep[0], single_rep.shape[2]
        gathered = lax.all_to_all(
            jnp.broadcast_to(single, (n,) + single.shape), "rows", 0, 0, tiled=True
        )
        pair = swap(pair_rep[0])
        att_b, single_b = jnp.swapaxes(att_bias, 1, 2), single_bias.T
        m5t, m5, mot, mof, a4t, a4, aot, abt, upt, up, dnt, sbt = prep_weights(
            pair_gains, mult_gains, mult_proj, mult_gate, mult_out, att_proj, att_b, att_out,
            pair_up, pair_down, single_b,
        )
        opm = opm_proj.shape[2]
        outer = jnp.swapaxes(opm_proj, 0, 1).reshape(width, 2 * opm)
        outer = jnp.pad(outer, ((0, 0), (0, L - 2 * opm)))
        outer_w = jnp.swapaxes(opm_out, 0, 1)
        mask_row = f32(residue_mask)
        mine, mask_col = pack(rows, single, single_cot[0], pair_rep[0], mask_row, sbt, where)
        single_out, lr = single_own(
            n, rows, total, gathered, mine, mask_col, single_gains, single_proj, single_up,
            single_down, outer,
        )
        lr = to_all(lr)

        z1, ab1, pmask, key_row, inner, lrt, left_own = front(
            n, rows, where, lr, pair, outer_w, m5t
        )
        dealt = deal(n, rows, where, pair_cot[0], (mine,))
        cots = {}

        def send_cots(offsets, ahead, behind):
            for k in offsets:
                block, _ = lax.optimization_barrier((dealt[k], behind))
                cots[k] = to_home(k, block)
            return lax.optimization_barrier((ahead, *[cots[k] for k in offsets]))[0]

        ab1 = send_cots((0, 1), ab1, lr)
        ab1 = exchange(ab1)
        p1 = exchange(channel_product(n, rows, True, ab1)).reshape(C * rows, L)
        z2, ab2 = middle(n, rows, z1, p1, mot, pmask, m5t)
        ab2 = send_cots((2, 3), ab2, p1)
        ab2 = exchange(ab2)
        p2 = exchange(channel_product(n, rows, False, ab2)).reshape(C * rows, L)
        z3, tb = start_front(n, rows, z2, p2, m5t, mot, abt)
        tb = send_cots((4, 5), tb, p2)
        tb_all = exchange(tb)
        z4, turn = start_attention(n, rows, z3, tb_all, key_row, a4t, aot, abt)
        turn = send_cots((6, 7), turn, tb_all)
        turn = exchange(turn)
        copies = to_chips(copies_of(mine, chips, (turn,)))
        others = other_core(copies)

        *pouts, back, m_up, m_dn, m_a41, m_ao1 = end_both(
            n, rows, where, turn, [cots[k] for k in range(n)], key_row, a4t, a4, aot, att_out, upt,
            up, dnt, pair_down,
        )
        back = exchange(back)
        sent = {}

        def send_pouts(offsets, ahead, behind):
            for k in offsets:
                block, _ = lax.optimization_barrier((pouts[k], behind))
                sent[k] = from_home(k, block)
            return lax.optimization_barrier((ahead, *[sent[k] for k in offsets]))[0]

        dz4, dxs, dtb, m_a40, m_ao0, m_ab1 = start_back(
            n, rows, z3, z4, back, tb_all, key_row, a4t, a4, att_out, abt, deps=(copies, others)
        )
        dtb = send_pouts((0, 1, 2, 3), dtb, back)
        dtb = exchange(dtb)
        dz3, dgp2, dp2, m_ab0, m_mo1 = third_back(
            n, rows, z3, dz4, dxs, dtb, abt, z2, p2, m5t, mot, mof
        )
        dp2 = send_pouts((4, 5, 6, 7), dp2, dtb)
        dp2 = exchange(dp2.reshape(n, part, L))
        dab2 = channel_product_back(n, rows, False, ab2, dp2)
        kept = single_every(
            n, rows, where, copies, others, single_gains, single_proj, single_up, single_down,
            deps=(dab2,),
        )
        dab2 = exchange(dab2)
        dz2, dgp1, dp1, m_m51, m_mo0 = second_back(
            n, rows, z2, dz3, dgp2, dab2, pmask, m5t, m5, z1, p1, mot, mof, deps=(kept[0],)
        )
        pair_six = undeal(n, rows, where, [sent[k] for k in range(n)])
        dp1 = exchange(dp1.reshape(n, part, L))
        dab1 = exchange(channel_product_back(n, rows, True, ab1, dp1))
        dz1, ends, m_oo, m_m50 = first_back(
            n, rows, chips, where, z1, dz2, dgp1, dab1, pmask, m5t, m5, inner, lrt, left_own,
            outer_w,
        )
        names = [
            "up", "dn", "a41", "ao1", "a40", "ao0", "m51", "mo1", "mo0", "m50", "oo", "ab1", "ab0",
        ]
        sums = [
            m_up, m_dn, m_a41, m_ao1, m_a40, m_ao0, m_m51, m_mo1, m_mo0, m_m50, m_oo, m_ab1, m_ab0,
        ]
        places, at = {}, 0
        for name, m in zip(names, sums):
            places[name] = at
            at += m.shape[0]
        half = -(-at // (total * 16)) * total * 8
        near, far = collect(where, sums, half, ())
        near = b16(near + f32(other_core(far)))
        ends = to_chips(ends)
        ends, near = lax.optimization_barrier((ends, near))
        others_ends = other_core(ends)
        dz1 = swap(copies_of(dz1, 1, (others_ends,))[0], True)
        near, others_ends = lax.optimization_barrier((near, others_ends))
        near = to_chips(near.reshape(chips, half // chips, C))
        ys, g_sg, d_own, drb, m_op = single_back(
            members, rows, where, ends, others_ends, kept, single_gains, single_proj,
            single_up, single_down, outer,
        )
        pair_grad, m_sb = last_back(rows, pair_rep[0], drb, dz1, sbt)
        near_sums = sum_copies(near, m_sb, chips)
        g_sp, g_su, g_sd = weight_grads(kept[2], ys, width, single_up.shape[1], near_sums)
        g_op = jnp.swapaxes(m_op[:, : 2 * opm].reshape(width, 2, opm), 0, 1)

        near = copies_of(to_chips(near_sums), 1, (g_sp, g_su, g_sd, pair_six))[0]
        grads = finish(
            where, near, other_core(near), pair_gains, mult_gains, mult_proj, mult_gate,
            mult_out, att_proj, att_b, pair_up, single_b, places, half, opm, (),
        )
        g_pg, g_mg, g_sb, g_oo, g_mp, g_mgt, g_mo, g_ap, g_ab, g_ao, g_pu, g_pd = grads
        return (
            single_out[None],
            pair_six[None],
            d_own[None],
            pair_grad[None],
            g_sg,
            g_pg,
            g_mg,
            g_sp,
            g_sb.T,
            g_su,
            g_sd,
            g_op,
            g_oo,
            g_mp,
            g_mgt,
            g_mo,
            g_ap,
            jnp.swapaxes(g_ab, 1, 2),
            g_ao,
            g_pu,
            g_pd,
        )

    return local


def solution(mesh):
    groups_of, n = mesh.shape["grp"], mesh.shape["rows"]
    whole = P()
    in_specs = (
        (P("grp", "rows", None), P("grp", "rows", None, None), P("grp", None))
        + (whole,) * 17
        + (P("grp", "rows", None), P("grp", "rows", None, None))
    )
    out_specs = (
        P("grp", "rows", None),
        P("grp", "rows", None, None),
        P("grp", "rows", None),
        P("grp", "rows", None, None),
    ) + (whole,) * 17
    if L % n == 0 and (L // n) % 16 == 0:
        body = fast_local((groups_of, n) == (4, 8), n)
    else:
        body = general_local
    return jax.shard_map(body, mesh=mesh, in_specs=in_specs, out_specs=out_specs, check_vma=False)
```
